32 devices in a mesh: pipe: 2 (over core), dp: 16 (over z, y, x).
Axes of the slice: x: 2, y: 2, z: 4, core: 2. Of those that a mesh axis runs over, the one named last changes fastest.
Arguments:
- images: bfloat16 [128, 16, 16, 1024], P('dp'), may hold values from -25 to 25
- extents: int32 [128, 2], P('dp'), may hold values from 8 to 16, as said below
- views: int32 [128], P('dp'), may hold values from 0 to 1, as said below
- params: bfloat16 [2, 6029312], P('pipe'), may hold values from -0.1875 to 0.1875
- norms: float32 [2, 2, 5120], P('pipe'), may hold values from -2 to 2, as said below
- cotangent: bfloat16 [128, 8, 8, 2048], P('dp'), may hold values from -6 to 6
Outputs:
- boundary: bfloat16 [2, 128, 262144], P('pipe', 'dp')
- weight_grads: float32 [2, 6029312], P('pipe')
- norm_grads: float32 [2, 2, 5120], P('pipe')
The draws below stay inside these ranges and needn't reach their ends.
Inputs may be any that keep to these rules, and one draw needn't show every extreme that they name: `extents`: entry [i, 0] is image i's valid height and [i, 1] its valid width, even numbers from 8 to 16 and from 8 to 16; the valid region is the top-left corner. The first of every dp index's images is whole. Images 2 k and 2 k + 1 have different views. `norms`: gains lie in 0.5 to 1.5.
All inputs are finite; a program needn't handle non-finite values.
Results may differ from the reference program's by a relative error of at most 0.014.
Values may be sent and summed in bfloat16 or wider, within the bound.
No kernel may reach another device: no remote copies, remote signals or barrier semaphores. Data moves between devices by JAX's collectives and lax.ppermute only.
A program may use at most 384 MiB of HBM per device.

```python
import jax
import jax.numpy as jnp
from jax import lax

C0 = 1024
M0 = 256
M1 = 512
C1 = 2048
HB = 16
WB = 16
IMG_MB = 2
MB = 4
IMG_DEV = 8
IMAGES = 128
P_SIZE = 6029312
CN = 5120
ELEMS = 262144
N_DP = 16


def draw_images(key, part):
    key = jax.random.fold_in(key, 11)
    base_key, jitter_key = jax.random.split(key)
    position = jnp.arange(IMAGES, dtype=jnp.float32) / max(IMAGES - 1, 1)
    jitter = jax.random.uniform(jitter_key, (IMAGES,), minval=-0.3, maxval=0.3)
    rising = jnp.exp(jnp.log(3.0) * position + jitter)
    values = jnp.clip(jax.random.normal(base_key, (IMAGES, HB, WB, C0)), -6.0, 6.0)
    return (values * rising[:, None, None, None]).astype(jnp.bfloat16)


def draw_extents(key, part):
    key = jax.random.fold_in(key, 12)
    high_key, wide_key = jax.random.split(key)
    heights = HB // 2 + 2 * jax.random.randint(high_key, (IMAGES,), 0, HB // 4 + 1)
    widths = WB // 2 + 2 * jax.random.randint(wide_key, (IMAGES,), 0, WB // 4 + 1)
    leading = jnp.arange(IMAGES) % IMG_DEV == 0
    heights = jnp.where(leading, HB, heights)
    widths = jnp.where(leading, WB, widths)
    return jnp.stack([heights, widths], axis=1).astype(jnp.int32)


def draw_views(key, part):
    key = jax.random.fold_in(key, 13)
    flips = jax.random.randint(key, (IMAGES // 2,), 0, 2)
    return jnp.stack([flips, 1 - flips], axis=1).reshape(IMAGES).astype(jnp.int32)


def draw_norms(key, part):
    key = jax.random.fold_in(key, 14)
    gain_key, shift_key = jax.random.split(key)
    gains = jax.random.uniform(gain_key, (2, 1, CN), minval=0.5, maxval=1.5)
    shifts = jnp.clip(0.5 * jax.random.normal(shift_key, (2, 1, CN)), -2.0, 2.0)
    return jnp.concatenate([gains, shifts], axis=1).astype(jnp.float32)


def level_of(key, extent, cuts, low, largest):
    level, own = 1.0, jax.random.fold_in(key, 6)
    for dim, parts in cuts:
        steps = jnp.exp(jax.random.uniform(jax.random.fold_in(own, dim), (parts,), jnp.float32, low / len(cuts), largest / len(cuts)))
        level = level * jnp.repeat(steps, extent[dim] // parts).reshape([-1 if axis == dim else 1 for axis in range(len(extent))])
    return level


def gaussian(rng, dims, scale, most, cuts=(), kind=jnp.bfloat16):
    factor_of = level_of(rng, dims, cuts, -0.22, 0.18) if cuts else 1.0
    array = jax.random.normal(rng, dims, jnp.float32) * scale * factor_of
    return jnp.minimum(jnp.maximum(array, -most), most).astype(kind)


def setup_inputs(seed: int = 0) -> dict:
    keys = jax.random.split(jax.random.key(seed), 7)
    images = draw_images(jax.random.fold_in(keys[6], 71), 0)
    extents = draw_extents(jax.random.fold_in(keys[6], 71), 0)
    views = draw_views(jax.random.fold_in(keys[6], 71), 0)
    params = gaussian(keys[3], (2, P_SIZE), C0 ** -0.5, 0.1875, ((0, 2),))
    norms = draw_norms(jax.random.fold_in(keys[6], 71), 0)
    cotangent = gaussian(keys[5], (IMAGES, HB // 2, WB // 2, C1), 1.0, 6.0, ((0, 16),))
    return {"images": images, "extents": extents, "views": views, "params": params, "norms": norms, "cotangent": cotangent}


EPSILON = 1e-05
PRECISE = lax.Precision.HIGHEST

@jax.custom_vjp
def low(v):
    return lax.optimization_barrier(v.astype(jnp.bfloat16)).astype(jnp.float32)

@jax.custom_vjp
def low_back(v):
    return v

def low_keep(v):
    return (low(v), None)

def low_pass(kept, grad):
    return (grad,)

def back_keep(v):
    return (v, None)

def back_low(kept, grad):
    return (low(grad),)
low.defvjp(low_keep, low_pass)
low_back.defvjp(back_keep, back_low)

def silu_value(values):
    return values * jax.nn.sigmoid(values)

def section_shape(section_id):
    if section_id == 0:
        return (M0, C0)
    return (M1, C1)

def unpack_weights(packed, section_id):
    middle, outward = section_shape(section_id)
    shapes = [(C0, middle), (9 * middle, middle), (middle, outward)]
    if section_id == 1:
        shapes.append((C0, C1))
    pieces = []
    offset = 0
    for first_dim, second_dim in shapes:
        pieces.append(packed[offset:offset + first_dim * second_dim].reshape(first_dim, second_dim))
        offset = offset + first_dim * second_dim
    return pieces

def norm_slices(norm_row, section_id):
    middle, outward = section_shape(section_id)
    bounds = [0, middle, 2 * middle, 2 * middle + outward, 2 * middle + outward + C1]
    count_bn = 3 if section_id == 0 else 4
    return [(norm_row[0, bounds[k]:bounds[k + 1]], norm_row[1, bounds[k]:bounds[k + 1]]) for k in range(count_bn)]

def layout(extents, views, height, breadth):
    row_ids = jnp.arange(height, dtype=jnp.int32)
    col_ids = jnp.arange(breadth, dtype=jnp.int32)
    inside = (row_ids[None, :, None] < extents[:, 0, None, None]) & (col_ids[None, None, :] < extents[:, 1, None, None])
    pixel_mask = inside.astype(jnp.float32)
    onehot = (views[:, None] == jnp.arange(2, dtype=jnp.int32)[None, :]).astype(jnp.float32)
    weighted = (pixel_mask[:, :, :, None] * onehot[:, None, None, :]).reshape(-1, 2)
    selector = jnp.broadcast_to(onehot[:, None, None, :], pixel_mask.shape + (2,)).reshape(-1, 2)
    return (pixel_mask.reshape(-1, 1), weighted, selector)

def moments(values, weighted):
    return jnp.stack([jnp.dot(weighted.T, values, precision=PRECISE), jnp.dot(weighted.T, values * values, precision=PRECISE)])

def normalize(values, totals, counts, selector):
    average = totals[0] / counts[:, None]
    spread = totals[1] / counts[:, None] - average * average
    inverse_dev = lax.rsqrt(spread + EPSILON)
    scale_pix = jnp.dot(selector, inverse_dev, precision=PRECISE)
    return (values - jnp.dot(selector, average, precision=PRECISE)) * scale_pix

def patches(act):
    image_count, height, breadth, channels = act.shape
    padded = jnp.pad(act, ((0, 0), (1, 1), (1, 1), (0, 0)))
    pieces = [padded[:, a:a + height, b:b + breadth, :] for a in range(3) for b in range(3)]
    return jnp.concatenate(pieces, axis=3).reshape(image_count * height * breadth, 9 * channels)

def block(inputs, packed, norm_row, extents, views, section_id):
    middle, outward = section_shape(section_id)
    if section_id == 1:
        source = inputs[:, ::2, ::2, :]
        extents = extents // 2
    else:
        source = inputs
    image_count, height, breadth, channels = source.shape
    pixel_mask, weighted, selector = layout(extents, views, height, breadth)
    counts = lax.optimization_barrier(jnp.sum(weighted, axis=0))
    weights = unpack_weights(packed, section_id)
    slices = norm_slices(norm_row, section_id)
    rows_in = source.reshape(-1, C0)

    def norm_of(values, index):
        return normalize(values, moments(values, weighted), counts, selector) * slices[index][0] + slices[index][1]
    first_z = low_back(jnp.dot(rows_in, weights[0], precision=PRECISE))
    act_one = low(silu_value(norm_of(first_z, 0)) * pixel_mask)
    second_z = low_back(jnp.dot(patches(act_one.reshape(image_count, height, breadth, middle)), weights[1], precision=PRECISE))
    act_two = low(silu_value(norm_of(second_z, 1)) * pixel_mask)
    third_z = low_back(jnp.dot(act_two, weights[2], precision=PRECISE))
    if section_id == 1:
        side_z = low_back(jnp.dot(rows_in, weights[3], precision=PRECISE))
        residual = norm_of(side_z, 3)
    else:
        residual = rows_in
    result = silu_value(norm_of(third_z, 2) + residual) * pixel_mask
    return result.reshape(image_count, height, breadth, outward)

def reference(images, extents, views, params, norms, cotangent):
    ext_grouped = extents.reshape(N_DP, MB, IMG_MB, 2)
    view_grouped = views.reshape(N_DP, MB, IMG_MB)

    def forward(images_f, packed_all, norm_all):
        grouped = images_f.reshape(N_DP, MB, IMG_MB, HB, WB, C0)
        outputs = []
        for micro_no in range(MB):
            inputs = grouped[:, micro_no].reshape(N_DP * IMG_MB, HB, WB, C0)
            ext_now = ext_grouped[:, micro_no].reshape(N_DP * IMG_MB, 2)
            view_now = view_grouped[:, micro_no].reshape(N_DP * IMG_MB)
            middle_out = block(inputs, packed_all[0], norm_all[0], ext_now, view_now, 0)
            handed = low_back(low(middle_out))
            final = block(handed, packed_all[1], norm_all[1], ext_now, view_now, 1)
            outputs.append(final.reshape(N_DP, IMG_MB, HB // 2, WB // 2, C1))
        return jnp.stack(outputs, axis=1).reshape(IMAGES, HB // 2, WB // 2, C1)
    result, pullback = jax.vjp(forward, images.astype(jnp.float32), params.astype(jnp.float32), norms)
    grad_images, grad_params, grad_norms = pullback(cotangent.astype(jnp.float32))
    input_rows = grad_images.astype(jnp.bfloat16).reshape(IMAGES, ELEMS)
    output_rows = result.astype(jnp.bfloat16).reshape(IMAGES, ELEMS // 2)
    output_rows = jnp.pad(output_rows, ((0, 0), (0, ELEMS - ELEMS // 2)))
    boundary = jnp.stack([input_rows, output_rows])
    return (boundary, grad_params, grad_norms)
```

```python
import functools

import jax
import jax.numpy as jnp
from jax import lax
from jax.experimental import pallas as pl
from jax.experimental.pallas import tpu as pltpu
from jax.sharding import PartitionSpec as P

C0 = 1024
M0 = 256
M1 = 512
C1 = 2048
HB = 16
WB = 16
IMG_MB = 2
MB = 4
P_SIZE = 6029312
CN = 5120
SLOTS = 4
PIX0 = 256
PIX1 = 64
EPSILON = 1e-05
MIB = 1 << 20

F32 = jnp.float32
BF16 = jnp.bfloat16


def shape_of(dims, kind):
    return jax.ShapeDtypeStruct(dims, kind)


def dot_nn(left, right):
    return lax.dot_general(left, right, (((1,), (0,)), ((), ())), preferred_element_type=F32)


def dot_nt(left, right):
    return lax.dot_general(left, right, (((1,), (1,)), ((), ())), preferred_element_type=F32)


def over_lanes(column, width):
    return jnp.concatenate([column] * (width // 128), axis=1)


def pixel_mask(high, wide, breadth, rows):
    index = lax.broadcasted_iota(jnp.int32, (rows, 128), 0)
    shift = breadth.bit_length() - 1
    inside = ((index >> shift) < high) & ((index & (breadth - 1)) < wide)
    return jnp.where(inside, 1.0, 0.0).astype(F32)


def column_of(breadth, rows, width):
    return lax.broadcasted_iota(jnp.int32, (rows, width), 0) & (breadth - 1)


def sigmoid(values):
    return 1.0 / (1.0 + jnp.exp(-values))


def silu(values):
    return values * sigmoid(values)


def slope(values):
    sig = sigmoid(values)
    return sig * (1.0 + values * (1.0 - sig))


def row_at(table, row):
    if isinstance(row, int):
        return table[row : row + 1, :]
    rows = lax.broadcasted_iota(jnp.int32, table.shape, 0)
    return jnp.sum(jnp.where(rows == row, table, 0.0), axis=0, keepdims=True)


def put_rows(ref, slot, first, second):
    if isinstance(slot, int):
        ref[2 * slot : 2 * slot + 1, :] = first
        ref[2 * slot + 1 : 2 * slot + 2, :] = second
        return
    rows = lax.broadcasted_iota(jnp.int32, ref.shape, 0)
    kept = jnp.where(rows == 2 * slot, first, ref[...])
    ref[...] = jnp.where(rows == 2 * slot + 1, second, kept)


def total_rows(values):
    return jnp.sum(values, axis=0, keepdims=True)


def mean_scale(table, slot, count):
    mean = row_at(table, 2 * slot) / count
    spread = row_at(table, 2 * slot + 1) / count - mean * mean
    return mean, lax.rsqrt(spread + EPSILON)


def back_means(table, slot, count):
    return row_at(table, 2 * slot) / count, row_at(table, 2 * slot + 1) / count


def count_of(table, slot):
    return row_at(table, 2 * slot)[:, M0 : M0 + 1]


def side_columns(values, breadth):
    rows, width = values.shape
    column = column_of(breadth, rows, width)
    left = jnp.where(column == 0, 0.0, pltpu.roll(values, 1, 0))
    right = jnp.where(column == breadth - 1, 0.0, pltpu.roll(values, rows - 1, 0))
    return left, right


def later_rows(values, step, height, breadth):
    if step == 0:
        return values
    rows, width = values.shape
    images = values.reshape(rows // (height * breadth), height * breadth, width)
    gap = jnp.zeros((images.shape[0], breadth, width), values.dtype)
    if step > 0:
        moved = jnp.concatenate([gap, images[:, :-breadth]], axis=1)
    else:
        moved = jnp.concatenate([images[:, breadth:], gap], axis=1)
    return moved.reshape(rows, width)


def even_picker():
    row = lax.broadcasted_iota(jnp.int32, (PIX1, PIX0), 0)
    col = lax.broadcasted_iota(jnp.int32, (PIX1, PIX0), 1)
    return jnp.where(col == 32 * (row >> 3) + 2 * (row & 7), 1.0, 0.0).astype(BF16)


def even_placer():
    row = lax.broadcasted_iota(jnp.int32, (PIX0, PIX1), 0)
    col = lax.broadcasted_iota(jnp.int32, (PIX0, PIX1), 1)
    return jnp.where(row == 32 * (col >> 3) + 2 * (col & 7), 1.0, 0.0).astype(BF16)


def placed(values):
    placer = even_placer()
    high = values.astype(BF16)
    rest = (values - high.astype(F32)).astype(BF16)
    return dot_nn(placer, high) + dot_nn(placer, rest)


def call(body, outs, grid, in_specs, out_specs, scratch=(), limit=40):
    return pl.pallas_call(
        body,
        out_shape=outs,
        grid_spec=pltpu.PrefetchScalarGridSpec(
            num_scalar_prefetch=1,
            grid=grid,
            in_specs=in_specs,
            out_specs=out_specs,
            scratch_shapes=list(scratch),
        ),
        compiler_params=pltpu.CompilerParams(vmem_limit_bytes=limit * MIB),
    )


def full(*dims):
    return pl.BlockSpec(dims, lambda *_: (0,) * len(dims))


def per_slot(*dims):
    return pl.BlockSpec((1,) + dims, lambda s, meta: (s,) + (0,) * len(dims))


def per_image(*dims):
    return pl.BlockSpec((1,) + dims, lambda s, meta: (meta[s],) + (0,) * len(dims))


def slot_mask0(meta, slot):
    return pixel_mask(meta[SLOTS + slot], meta[2 * SLOTS + slot], WB, PIX0)


def slot_mask1(meta, slot):
    return pixel_mask(meta[SLOTS + slot] >> 1, meta[2 * SLOTS + slot] >> 1, WB // 2, PIX1)


def front_one(meta, x_ref, w_ref, z_ref, st_ref):
    slot = pl.program_id(0)
    z = dot_nn(x_ref[0].reshape(PIX0, C0), w_ref[...])
    z_ref[0] = z
    zm = z * over_lanes(slot_mask0(meta, slot), M0)
    count = (meta[SLOTS + slot] * meta[2 * SLOTS + slot]).astype(F32)
    extra = jnp.full((1, 128), 1.0, F32) * count
    put_rows(
        st_ref,
        slot,
        jnp.concatenate([total_rows(zm), extra], axis=1),
        jnp.concatenate([total_rows(zm * z), extra], axis=1),
    )


def front_two(meta, r_ref, z_ref, n_ref, w_ref, tot_ref, act_ref, z2_ref, st_ref):
    slot = pl.program_id(0)

    @pl.when(slot == 0)
    def _():
        tot_ref[...] = jnp.sum(r_ref[...], axis=0)

    table = tot_ref[...]
    count = count_of(table, slot)
    mean, scale = mean_scale(table[:, :M0], slot, count)
    mask = over_lanes(slot_mask0(meta, slot), M0)
    pre = (z_ref[0] - mean) * scale * n_ref[0:1, :M0] + n_ref[1:2, :M0]
    act = silu(pre) * mask
    left, right = side_columns(act, WB)
    act_ref[0, 0:WB, :] = jnp.zeros((WB, 3 * M0), BF16)
    act_ref[0, WB + PIX0 : 2 * WB + PIX0, :] = jnp.zeros((WB, 3 * M0), BF16)
    act_ref[0, WB : WB + PIX0, :] = jnp.concatenate([left, act, right], axis=1).astype(BF16)
    z2 = dot_nn(act_ref[0, 0:PIX0, :], w_ref[0 : 3 * M0, :])
    z2 = z2 + dot_nn(act_ref[0, WB : WB + PIX0, :], w_ref[3 * M0 : 6 * M0, :])
    z2 = z2 + dot_nn(act_ref[0, 2 * WB : 2 * WB + PIX0, :], w_ref[6 * M0 :, :])
    z2_ref[0] = z2
    zm = z2 * mask
    put_rows(st_ref, slot, total_rows(zm), total_rows(zm * z2))


def front_three(meta, r_ref, tot_ref, z2_ref, n_ref, w_ref, tot2_ref, a2_ref, st_ref):
    slot = pl.program_id(0)

    @pl.when(slot == 0)
    def _():
        tot2_ref[...] = jnp.sum(r_ref[...], axis=0)

    count = count_of(tot_ref[...], slot)
    mean, scale = mean_scale(tot2_ref[...], slot, count)
    pre = (z2_ref[0] - mean) * scale * n_ref[0:1, M0 : 2 * M0] + n_ref[1:2, M0 : 2 * M0]
    act = (silu(pre) * over_lanes(slot_mask0(meta, slot), M0)).astype(BF16)
    a2_ref[0] = act
    z3 = dot_nn(act, w_ref[...])
    put_rows(st_ref, slot, total_rows(z3), total_rows(z3 * z3))


def join(
    meta, tot3_ref, tot_ref, a2_ref, x_ref, n_ref, w3_ref, w1_ref, ws_ref,
    s_ref, p_ref, z3_ref, z1_ref, zs_ref, st_ref, sts_ref,
):
    step = pl.program_id(0)

    @pl.when(step < SLOTS)
    def _():
        count = count_of(tot_ref[...], step)
        mean, scale = mean_scale(tot3_ref[...], step, count)
        picker = even_picker()
        act = dot_nn(picker, a2_ref[0]).astype(BF16)
        z3 = dot_nn(act, w3_ref[...])
        here = pl.ds(pl.multiple_of(step * PIX1, PIX1), PIX1)
        z3_ref[here, :] = z3
        pre = (z3 - mean) * scale * n_ref[0:1, 2 * M0 : 2 * M0 + C0]
        pre = pre + n_ref[1:2, 2 * M0 : 2 * M0 + C0]
        pre = pre + dot_nn(picker, x_ref[0].reshape(PIX0, C0))
        p_ref[here, :] = pre
        s_ref[here, :] = (silu(pre) * over_lanes(slot_mask1(meta, step), C0)).astype(BF16)

    @pl.when(step == SLOTS)
    def _():
        z1 = dot_nn(s_ref[...], w1_ref[...])
        z1_ref[...] = z1
        for slot in range(SLOTS):
            part = z1[slot * PIX1 : (slot + 1) * PIX1]
            put_rows(st_ref, slot, total_rows(part), total_rows(part * part))

    @pl.when(step >= SLOTS)
    def _():
        zs = dot_nn(s_ref[...], ws_ref[...])
        zs_ref[...] = zs
        for slot in range(SLOTS):
            part = zs[slot * PIX1 : (slot + 1) * PIX1]
            put_rows(sts_ref, slot, total_rows(part), total_rows(part * part))


def by_slot(pieces):
    return jnp.concatenate(pieces, axis=0)


def normed_slots(values, table, counts, width):
    pieces = []
    for slot in range(SLOTS):
        mean, scale = mean_scale(table, slot, counts[slot])
        pieces.append((values[slot * PIX1 : (slot + 1) * PIX1] - mean) * scale)
    return by_slot(pieces)


def counts1(tot_ref):
    table = tot_ref[...]
    return [count_of(table, slot) * 0.25 for slot in range(SLOTS)]


def mask1_all(meta, width):
    return over_lanes(by_slot([slot_mask1(meta, slot) for slot in range(SLOTS)]), width)


def slot_sums(st_ref, first, second):
    for slot in range(SLOTS):
        here = slice(slot * PIX1, (slot + 1) * PIX1)
        put_rows(st_ref, slot, total_rows(first[here]), total_rows(second[here]))


def mid_one(meta, r_ref, tot_ref, z1_ref, n_ref, w_ref, tot4_ref, act_ref, z2_ref, st_ref):
    tot4_ref[...] = jnp.sum(r_ref[...], axis=0)
    counts = counts1(tot_ref)
    mask = mask1_all(meta, M1)
    pre = normed_slots(z1_ref[...], tot4_ref[...], counts, M1) * n_ref[0:1, :M1] + n_ref[1:2, :M1]
    act = silu(pre) * mask
    left, right = side_columns(act, WB // 2)
    wide = jnp.concatenate([left, act, right], axis=1).astype(BF16)
    act_ref[...] = wide
    z2 = dot_nn(wide, w_ref[3 * M1 : 6 * M1, :])
    z2 = z2 + later_rows(dot_nn(wide, w_ref[0 : 3 * M1, :]), 1, HB // 2, WB // 2)
    z2 = z2 + later_rows(dot_nn(wide, w_ref[6 * M1 :, :]), -1, HB // 2, WB // 2)
    z2_ref[...] = z2
    zm = z2 * mask
    slot_sums(st_ref, zm, zm * z2)


def mid_two(meta, r_ref, tot_ref, z2_ref, n_ref, w_ref, tot5_ref, a2_ref, z3_ref, st_ref):
    tot5_ref[...] = jnp.sum(r_ref[...], axis=0)
    counts = counts1(tot_ref)
    pre = normed_slots(z2_ref[...], tot5_ref[...], counts, M1)
    pre = pre * n_ref[0:1, M1 : 2 * M1] + n_ref[1:2, M1 : 2 * M1]
    act = (silu(pre) * mask1_all(meta, M1)).astype(BF16)
    a2_ref[...] = act
    z3 = dot_nn(act, w_ref[...])
    z3_ref[...] = z3
    slot_sums(st_ref, z3, z3 * z3)


def turn(
    meta, tot6_ref, tots_ref, tot_ref, z3_ref, zs_ref, n_ref, cot_ref,
    y_ref, g_ref, st_ref, sts_ref,
):
    slot = pl.program_id(0)
    count = count_of(tot_ref[...], slot) * 0.25
    mask = over_lanes(slot_mask1(meta, slot), C1)
    mean, scale = mean_scale(tot6_ref[...], slot, count)
    normed = (z3_ref[0] - mean) * scale
    mean_s, scale_s = mean_scale(tots_ref[...], slot, count)
    normed_s = (zs_ref[0] - mean_s) * scale_s
    at3, ats = 2 * M1, 2 * M1 + C1
    pre = normed * n_ref[0:1, at3:ats] + n_ref[1:2, at3:ats]
    pre = pre + (normed_s * n_ref[0:1, ats : ats + C1] + n_ref[1:2, ats : ats + C1])
    sig = sigmoid(pre)
    y_ref[0] = (pre * sig * mask).astype(BF16).reshape(HB // 2, WB // 2, C1)
    grad = cot_ref[0].reshape(PIX1, C1).astype(F32) * (sig * (1.0 + pre * (1.0 - sig))) * mask
    g_ref[0] = grad
    put_rows(st_ref, slot, total_rows(grad), total_rows(grad * normed))
    put_rows(sts_ref, slot, total_rows(grad), total_rows(grad * normed_s))


def norm_back_slots(grad, normed, scales, gain, table, counts, mask):
    pieces = []
    for slot in range(SLOTS):
        here = slice(slot * PIX1, (slot + 1) * PIX1)
        first, second = back_means(table, slot, counts[slot])
        pieces.append(
            mask[here] * scales[slot] * gain * (grad[here] - first - normed[here] * second)
        )
    return by_slot(pieces).astype(BF16)


def scales_of(table, counts):
    return [mean_scale(table, slot, counts[slot])[1] for slot in range(SLOTS)]


def back_one(
    meta, tot7_ref, tot6_ref, tot5_ref, tot_ref, z3_ref, g_ref, z2_ref, n_ref, w_ref,
    d3_ref, g2_ref, st_ref,
):
    counts = counts1(tot_ref)
    mask = mask1_all(meta, C1)
    normed = normed_slots(z3_ref[...], tot6_ref[...], counts, C1)
    d3 = norm_back_slots(
        g_ref[...], normed, scales_of(tot6_ref[...], counts), n_ref[0:1, 2 * M1 : 2 * M1 + C1],
        tot7_ref[...], counts, mask,
    )
    d3_ref[...] = d3
    normed2 = normed_slots(z2_ref[...], tot5_ref[...], counts, M1)
    pre2 = normed2 * n_ref[0:1, M1 : 2 * M1] + n_ref[1:2, M1 : 2 * M1]
    g2 = dot_nt(d3, w_ref[...]) * mask[:, :M1] * slope(pre2)
    g2_ref[...] = g2
    slot_sums(st_ref, g2, g2 * normed2)


def back_two(
    meta, r_ref, tot5_ref, tot4_ref, tot_ref, z2_ref, g2_ref, z1_ref, n_ref, w_ref,
    tot8_ref, d2_ref, g1_ref, st_ref,
):
    tot8_ref[...] = jnp.sum(r_ref[...], axis=0)
    counts = counts1(tot_ref)
    mask = mask1_all(meta, M1)
    normed = normed_slots(z2_ref[...], tot5_ref[...], counts, M1)
    d2 = norm_back_slots(
        g2_ref[...], normed, scales_of(tot5_ref[...], counts), n_ref[0:1, M1 : 2 * M1],
        tot8_ref[...], counts, mask,
    )
    d2_ref[...] = d2
    wide = dot_nt(d2, w_ref[3 * M1 : 6 * M1, :])
    wide = wide + later_rows(dot_nt(d2, w_ref[0 : 3 * M1, :]), -1, HB // 2, WB // 2)
    wide = wide + later_rows(dot_nt(d2, w_ref[6 * M1 :, :]), 1, HB // 2, WB // 2)
    left, _ = side_columns(wide[:, 2 * M1 :], WB // 2)
    _, right = side_columns(wide[:, :M1], WB // 2)
    normed1 = normed_slots(z1_ref[...], tot4_ref[...], counts, M1)
    pre1 = normed1 * n_ref[0:1, :M1] + n_ref[1:2, :M1]
    g1 = (wide[:, M1 : 2 * M1] + left + right) * mask * slope(pre1)
    g1_ref[...] = g1
    slot_sums(st_ref, g1, g1 * normed1)


def back_three(
    meta, r_ref, tot4_ref, tot_ref, z1_ref, g1_ref, totg_ref, tots_ref, zs_ref, g_ref,
    tot3_ref, p_ref, z3_ref, n0_ref, n_ref, w1_ref, ws_ref,
    tot9_ref, d1_ref, ds_ref, g0_ref, st_ref,
):
    tot9_ref[...] = jnp.sum(r_ref[...], axis=0)
    counts = counts1(tot_ref)
    mask = mask1_all(meta, C1)
    normed = normed_slots(z1_ref[...], tot4_ref[...], counts, M1)
    d1 = norm_back_slots(
        g1_ref[...], normed, scales_of(tot4_ref[...], counts), n_ref[0:1, :M1],
        tot9_ref[...], counts, mask[:, :M1],
    )
    d1_ref[...] = d1
    normed_s = normed_slots(zs_ref[...], tots_ref[...], counts, C1)
    ats = 2 * M1 + C1
    ds = norm_back_slots(
        g_ref[...], normed_s, scales_of(tots_ref[...], counts), n_ref[0:1, ats : ats + C1],
        totg_ref[...], counts, mask,
    )
    ds_ref[...] = ds
    grad = dot_nt(d1, w1_ref[...]) + dot_nt(ds, ws_ref[...])
    grad = grad.astype(BF16).astype(F32)
    g0 = grad * slope(p_ref[...]) * mask[:, :C0]
    g0_ref[...] = g0
    counts0 = [count * 4.0 for count in counts]
    normed3 = normed_slots(z3_ref[...], tot3_ref[...], counts0, C0)
    slot_sums(st_ref, g0, g0 * normed3)


def norm_back(grad, normed, scale, gain, table, slot, count, mask):
    first, second = back_means(table, slot, count)
    return (mask * scale * gain * (grad - first - normed * second)).astype(BF16)


def last_one(
    meta, tot10_ref, tot3_ref, tot2_ref, tot_ref, a2_ref, g0_ref, z2_ref, n_ref, w_ref,
    d3_ref, g2_ref, st_ref,
):
    slot = pl.program_id(0)
    count = count_of(tot_ref[...], slot)
    mask = over_lanes(slot_mask0(meta, slot), C0)
    mean, scale = mean_scale(tot3_ref[...], slot, count)
    normed = (dot_nn(a2_ref[0], w_ref[...]) - mean) * scale
    grad = placed(g0_ref[0])
    d3 = norm_back(
        grad, normed, scale, n_ref[0:1, 2 * M0 : 2 * M0 + C0], tot10_ref[...], slot, count, mask
    )
    d3_ref[0] = d3
    mean2, scale2 = mean_scale(tot2_ref[...], slot, count)
    normed2 = (z2_ref[0] - mean2) * scale2
    pre2 = normed2 * n_ref[0:1, M0 : 2 * M0] + n_ref[1:2, M0 : 2 * M0]
    g2 = dot_nt(d3, w_ref[...]) * mask[:, :M0] * slope(pre2)
    g2_ref[0] = g2
    put_rows(st_ref, slot, total_rows(g2), total_rows(g2 * normed2))


def last_two(
    meta, r_ref, tot2_ref, tot_ref, z2_ref, g2_ref, z1_ref, n_ref, w_ref,
    tot11_ref, d2_ref, g1_ref, st_ref,
):
    slot = pl.program_id(0)

    @pl.when(slot == 0)
    def _():
        tot11_ref[...] = jnp.sum(r_ref[...], axis=0)

    table = tot_ref[...]
    count = count_of(table, slot)
    mask = over_lanes(slot_mask0(meta, slot), M0)
    mean2, scale2 = mean_scale(tot2_ref[...], slot, count)
    normed2 = (z2_ref[0] - mean2) * scale2
    d2 = norm_back(
        g2_ref[0], normed2, scale2, n_ref[0:1, M0 : 2 * M0], tot11_ref[...], slot, count, mask
    )
    d2_ref[0] = d2
    wide = dot_nt(d2, w_ref[3 * M0 : 6 * M0, :])
    wide = wide + later_rows(dot_nt(d2, w_ref[0 : 3 * M0, :]), -1, HB, WB)
    wide = wide + later_rows(dot_nt(d2, w_ref[6 * M0 :, :]), 1, HB, WB)
    left, _ = side_columns(wide[:, 2 * M0 :], WB)
    _, right = side_columns(wide[:, :M0], WB)
    mean1, scale1 = mean_scale(table[:, :M0], slot, count)
    normed1 = (z1_ref[0] - mean1) * scale1
    pre1 = normed1 * n_ref[0:1, :M0] + n_ref[1:2, :M0]
    g1 = (wide[:, M0 : 2 * M0] + left + right) * mask * slope(pre1)
    g1_ref[0] = g1
    put_rows(st_ref, slot, total_rows(g1), total_rows(g1 * normed1))


def last_three(meta, r_ref, tot_ref, z1_ref, g1_ref, g0_ref, n_ref, w_ref, tot12_ref, d1_ref, gx_ref):
    slot = pl.program_id(0)

    @pl.when(slot == 0)
    def _():
        tot12_ref[...] = jnp.sum(r_ref[...], axis=0)

    table = tot_ref[...]
    count = count_of(table, slot)
    mask = over_lanes(slot_mask0(meta, slot), M0)
    mean1, scale1 = mean_scale(table[:, :M0], slot, count)
    normed1 = (z1_ref[0] - mean1) * scale1
    d1 = norm_back(g1_ref[0], normed1, scale1, n_ref[0:1, :M0], tot12_ref[...], slot, count, mask)
    d1_ref[0] = d1
    grad = dot_nt(d1, w_ref[...]) + placed(g0_ref[0])
    gx_ref[0] = grad.astype(BF16).reshape(HB, WB, C0)


def unpack_body(cols, rows, i_ref, o_ref):
    tiles = cols // 128
    for tile in range(tiles):
        part = i_ref[pl.ds(tile, rows, stride=tiles), :]
        o_ref[:, tile * 128 : (tile + 1) * 128] = part.astype(BF16)


def unpack(packed, offset, rows, cols, steps):
    flat = packed[:, offset : offset + rows * cols].astype(F32).reshape(-1, 128)
    part = rows // steps
    return pl.pallas_call(
        functools.partial(unpack_body, cols, part),
        out_shape=shape_of((rows, cols), BF16),
        grid=(steps,),
        in_specs=[pl.BlockSpec((part * cols // 128, 128), lambda i: (i, 0))],
        out_specs=pl.BlockSpec((part, cols), lambda i: (i, 0)),
    )(flat)


def pack_body(cols, rows, i_ref, o_ref):
    tiles = cols // 128
    for tile in range(tiles):
        o_ref[pl.ds(tile, rows, stride=tiles), :] = i_ref[:, tile * 128 : (tile + 1) * 128].astype(F32)


def pack(matrix, steps):
    rows, cols = matrix.shape
    part = rows // steps
    return pl.pallas_call(
        functools.partial(pack_body, cols, part),
        out_shape=shape_of((rows * cols // 128, 128), F32),
        grid=(steps,),
        in_specs=[pl.BlockSpec((part, cols), lambda i: (i, 0))],
        out_specs=pl.BlockSpec((part * cols // 128, 128), lambda i: (i, 0)),
    )(matrix).reshape(-1)


def swap_cores(value):
    return lax.ppermute(value, "pipe", [(0, 1), (1, 0)])


def spread(value):
    count = lax.axis_size("dp")
    copies = jnp.broadcast_to(value[None], (count,) + value.shape)
    return lax.all_to_all(copies, "dp", 0, 0)


def summed(value):
    count = lax.axis_size("dp")
    if count != 16:
        return lax.psum(value, "dp")
    for step in (1, 4):
        parts = [
            lax.ppermute(value, "dp", [(i, i ^ (k * step)) for i in range(count)]) for k in (1, 2, 3)
        ]
        value = (value + parts[0]) + (parts[1] + parts[2])
    return value


def halved(value, axis_bits):
    count = lax.axis_size("dp")
    me = lax.axis_index("dp")
    for bit in axis_bits:
        half = value.shape[0] // 2
        mine = (me & bit) != 0
        kept = jnp.where(mine, value[half:], value[:half])
        sent = jnp.where(mine, value[:half], value[half:])
        got = lax.ppermute(sent, "dp", [(i, i ^ bit) for i in range(count)])
        value = (kept.astype(F32) + got.astype(F32)).astype(BF16)
    return value


def doubled(value, axis_bits):
    count = lax.axis_size("dp")
    me = lax.axis_index("dp")
    for bit in reversed(axis_bits):
        got = lax.ppermute(value, "dp", [(i, i ^ bit) for i in range(count)])
        mine = (me & bit) != 0
        value = jnp.concatenate([jnp.where(mine, got, value), jnp.where(mine, value, got)], axis=0)
    return value


def panels(matrix):
    return [matrix[:, k : k + 256] for k in range(0, matrix.shape[1], 256)]


def grad_of(left, right):
    return lax.dot_general(
        left, right, (((0,), (0,)), ((), ())), preferred_element_type=F32
    ).astype(BF16)


def conv_grad(padded_rows, delta, breadth, pixels):
    pieces = [
        grad_of(padded_rows[:, a * breadth : a * breadth + pixels].reshape(-1, padded_rows.shape[2]), delta)
        for a in range(3)
    ]
    return jnp.concatenate(pieces, axis=0)


def on_device(images, extents, views, params, norms, cotangent):
    core = lax.axis_index("pipe")
    first_core = core == 0
    count = lax.axis_size("dp")
    bits = [1 << k for k in range(count.bit_length() - 1)]

    own_views = lax.dynamic_slice(views, (core * SLOTS,), (SLOTS,))
    own_ext = lax.dynamic_slice(extents, (core * SLOTS, 0), (SLOTS, 2))
    order = []
    for mb in range(SLOTS // IMG_MB):
        flipped = own_views[2 * mb] != 0
        order += [jnp.where(flipped, 2 * mb + 1, 2 * mb), jnp.where(flipped, 2 * mb, 2 * mb + 1)]
    order = jnp.stack(order).astype(jnp.int32)
    hot = (order[:, None] == jnp.arange(SLOTS, dtype=jnp.int32)[None, :]).astype(jnp.int32)
    sizes = jnp.sum(hot[:, :, None] * own_ext[None], axis=1)
    meta = jnp.concatenate([order + core * SLOTS, sizes[:, 0], sizes[:, 1], order]).astype(jnp.int32)

    norms_there = swap_cores(norms[0])
    norms0 = jnp.where(first_core, norms[0], norms_there)
    norms1 = jnp.where(first_core, norms_there, norms[0])

    def from_core(owner, matrix):
        got = lax.ppermute(matrix, "pipe", [(owner, 1 - owner)])
        return jnp.where(core == owner, matrix, got)

    w1 = from_core(0, unpack(params, 0, C0, M0, 2))
    w2 = from_core(0, unpack(params, 262144, 9 * M0, M0, 3))
    w3 = from_core(0, unpack(params, 851968, M0, C0, 2))
    v1 = from_core(1, unpack(params, 0, C0, M1, 2))
    v2 = from_core(1, unpack(params, 524288, 9 * M1, M1, 6))
    v3 = from_core(1, unpack(params, 2883584, M1, C1, 4))
    vs = from_core(1, unpack(params, 3932160, C0, C1, 8))

    image = per_image(HB, WB, C0)
    z1, st = call(
        front_one,
        [shape_of((SLOTS, PIX0, M0), F32), shape_of((8, M0 + 128), F32)],
        (SLOTS,),
        [image, full(C0, M0)],
        [per_slot(PIX0, M0), full(8, M0 + 128)],
    )(meta, images, w1)
    tot1, act, z2, st = call(
        front_two,
        [
            shape_of((8, M0 + 128), F32),
            shape_of((SLOTS, PIX0 + 2 * WB, 3 * M0), BF16),
            shape_of((SLOTS, PIX0, M0), F32),
            shape_of((8, M0), F32),
        ],
        (SLOTS,),
        [full(count, 8, M0 + 128), per_slot(PIX0, M0), full(2, CN), full(9 * M0, M0)],
        [full(8, M0 + 128), per_slot(PIX0 + 2 * WB, 3 * M0), per_slot(PIX0, M0), full(8, M0)],
    )(meta, spread(st), z1, norms0, w2)
    tot2, a2, st = call(
        front_three,
        [shape_of((8, M0), F32), shape_of((SLOTS, PIX0, M0), BF16), shape_of((8, C0), F32)],
        (SLOTS,),
        [
            full(count, 8, M0),
            full(8, M0 + 128),
            per_slot(PIX0, M0),
            full(2, CN),
            full(M0, C0),
        ],
        [full(8, M0), per_slot(PIX0, M0), full(8, C0)],
    )(meta, spread(st), tot1, z2, norms0, w3)
    tot3 = summed(st)

    clamp = lambda s: jnp.minimum(s, SLOTS - 1)
    tile = lambda s: jnp.maximum(s - SLOTS, 0)
    rows1 = SLOTS * PIX1
    src, p_even, z3_even, y1, ys, st, sts = call(
        join,
        [
            shape_of((rows1, C0), BF16),
            shape_of((rows1, C0), F32),
            shape_of((rows1, C0), F32),
            shape_of((rows1, M1), F32),
            shape_of((rows1, C1), F32),
            shape_of((8, M1), F32),
            shape_of((8, C1), F32),
        ],
        (SLOTS + 4,),
        [
            full(8, C0),
            full(8, M0 + 128),
            pl.BlockSpec((1, PIX0, M0), lambda s, meta: (clamp(s), 0, 0)),
            pl.BlockSpec((1, HB, WB, C0), lambda s, meta: (meta[clamp(s)], 0, 0, 0)),
            full(2, CN),
            full(M0, C0),
            full(C0, M1),
            pl.BlockSpec((C0, C1 // 4), lambda s, meta: (0, tile(s))),
        ],
        [
            full(rows1, C0),
            full(rows1, C0),
            full(rows1, C0),
            full(rows1, M1),
            pl.BlockSpec((rows1, C1 // 4), lambda s, meta: (0, tile(s))),
            full(8, M1),
            pl.BlockSpec((8, C1 // 4), lambda s, meta: (0, tile(s))),
        ],
    )(meta, tot3, tot1, a2, images, norms0, w3, v1, vs)
    tots = summed(sts)

    one = (1,)
    tot4, act1, y2, st = call(
        mid_one,
        [
            shape_of((8, M1), F32),
            shape_of((rows1, 3 * M1), BF16),
            shape_of((rows1, M1), F32),
            shape_of((8, M1), F32),
        ],
        one,
        [full(count, 8, M1), full(8, M0 + 128), full(rows1, M1), full(2, CN), full(9 * M1, M1)],
        [full(8, M1), full(rows1, 3 * M1), full(rows1, M1), full(8, M1)],
    )(meta, spread(st), tot1, y1, norms1, v2)
    tot5, b2, y3, st = call(
        mid_two,
        [
            shape_of((8, M1), F32),
            shape_of((rows1, M1), BF16),
            shape_of((rows1, C1), F32),
            shape_of((8, C1), F32),
        ],
        one,
        [full(count, 8, M1), full(8, M0 + 128), full(rows1, M1), full(2, CN), full(M1, C1)],
        [full(8, M1), full(rows1, M1), full(rows1, C1), full(8, C1)],
    )(meta, spread(st), tot1, y2, norms1, v3)
    tot6 = summed(st)

    by_image = pl.BlockSpec(
        (1, HB // 2, WB // 2, C1), lambda s, meta: (meta[3 * SLOTS + s], 0, 0, 0)
    )
    y_out, grad_y, st, stg = call(
        turn,
        [
            shape_of((SLOTS, HB // 2, WB // 2, C1), BF16),
            shape_of((SLOTS, PIX1, C1), F32),
            shape_of((8, C1), F32),
            shape_of((8, C1), F32),
        ],
        (SLOTS,),
        [
            full(8, C1),
            full(8, C1),
            full(8, M0 + 128),
            per_slot(PIX1, C1),
            per_slot(PIX1, C1),
            full(2, CN),
            per_image(HB // 2, WB // 2, C1),
        ],
        [by_image, per_slot(PIX1, C1), full(8, C1), full(8, C1)],
    )(
        meta, tot6, tots, tot1, y3.reshape(SLOTS, PIX1, C1), ys.reshape(SLOTS, PIX1, C1),
        norms1, cotangent,
    )
    tot7 = summed(st)
    totg = summed(stg)
    grad_y = grad_y.reshape(rows1, C1)

    e3, g2, st = call(
        back_one,
        [shape_of((rows1, C1), BF16), shape_of((rows1, M1), F32), shape_of((8, M1), F32)],
        one,
        [
            full(8, C1), full(8, C1), full(8, M1), full(8, M0 + 128), full(rows1, C1),
            full(rows1, C1), full(rows1, M1), full(2, CN), full(M1, C1),
        ],
        [full(rows1, C1), full(rows1, M1), full(8, M1)],
    )(meta, tot7, tot6, tot5, tot1, y3, grad_y, y2, norms1, v3)
    tot8, e2, g1, st = call(
        back_two,
        [
            shape_of((8, M1), F32),
            shape_of((rows1, M1), BF16),
            shape_of((rows1, M1), F32),
            shape_of((8, M1), F32),
        ],
        one,
        [
            full(count, 8, M1), full(8, M1), full(8, M1), full(8, M0 + 128), full(rows1, M1),
            full(rows1, M1), full(rows1, M1), full(2, CN), full(9 * M1, M1),
        ],
        [full(8, M1), full(rows1, M1), full(rows1, M1), full(8, M1)],
    )(meta, spread(st), tot5, tot4, tot1, y2, g2, y1, norms1, v2)
    tot9, e1, es, g0, st = call(
        back_three,
        [
            shape_of((8, M1), F32),
            shape_of((rows1, M1), BF16),
            shape_of((rows1, C1), BF16),
            shape_of((rows1, C0), F32),
            shape_of((8, C0), F32),
        ],
        one,
        [
            full(count, 8, M1), full(8, M1), full(8, M0 + 128), full(rows1, M1), full(rows1, M1),
            full(8, C1), full(8, C1), full(rows1, C1), full(rows1, C1), full(8, C0),
            full(rows1, C0), full(rows1, C0), full(2, CN), full(2, CN), full(C0, M1), full(C0, C1),
        ],
        [full(8, M1), full(rows1, M1), full(rows1, C1), full(rows1, C0), full(8, C0)],
    )(
        meta, spread(st), tot4, tot1, y1, g1, totg, tots, ys, grad_y, tot3, p_even, z3_even,
        norms0, norms1, v1, vs,
    )
    tot10 = summed(st)
    g0 = g0.reshape(SLOTS, PIX1, C0)

    d3, g2, st = call(
        last_one,
        [
            shape_of((SLOTS, PIX0, C0), BF16),
            shape_of((SLOTS, PIX0, M0), F32),
            shape_of((8, M0), F32),
        ],
        (SLOTS,),
        [
            full(8, C0), full(8, C0), full(8, M0), full(8, M0 + 128), per_slot(PIX0, M0),
            per_slot(PIX1, C0), per_slot(PIX0, M0), full(2, CN), full(M0, C0),
        ],
        [per_slot(PIX0, C0), per_slot(PIX0, M0), full(8, M0)],
    )(meta, tot10, tot3, tot2, tot1, a2, g0, z2, norms0, w3)
    tot11, d2, g1, st = call(
        last_two,
        [
            shape_of((8, M0), F32),
            shape_of((SLOTS, PIX0, M0), BF16),
            shape_of((SLOTS, PIX0, M0), F32),
            shape_of((8, M0), F32),
        ],
        (SLOTS,),
        [
            full(count, 8, M0), full(8, M0), full(8, M0 + 128), per_slot(PIX0, M0),
            per_slot(PIX0, M0), per_slot(PIX0, M0), full(2, CN), full(9 * M0, M0),
        ],
        [full(8, M0), per_slot(PIX0, M0), per_slot(PIX0, M0), full(8, M0)],
    )(meta, spread(st), tot2, tot1, z2, g2, z1, norms0, w2)
    own_image = pl.BlockSpec((1, HB, WB, C0), lambda s, meta: (meta[3 * SLOTS + s], 0, 0, 0))
    tot12, d1, gx = call(
        last_three,
        [
            shape_of((8, M0), F32),
            shape_of((SLOTS, PIX0, M0), BF16),
            shape_of((SLOTS, HB, WB, C0), BF16),
        ],
        (SLOTS,),
        [
            full(count, 8, M0), full(8, M0 + 128), per_slot(PIX0, M0), per_slot(PIX0, M0),
            per_slot(PIX1, C0), full(2, CN), full(C0, M0),
        ],
        [full(8, M0), per_slot(PIX0, M0), own_image],
    )(meta, spread(st), tot1, z1, g1, g0, norms0, w1)

    own = lax.dynamic_slice_in_dim(images, core * SLOTS, SLOTS, 0)
    picked = jnp.take(own, order, axis=0).reshape(SLOTS * PIX0, C0)
    flat_d2 = d2.reshape(SLOTS * PIX0, M0)
    wide1 = jnp.pad(act1.reshape(SLOTS, PIX1, 3 * M1), ((0, 0), (8, 8), (0, 0)))
    grads0 = [
        grad_of(picked, d1.reshape(SLOTS * PIX0, M0)),
        conv_grad(act, flat_d2, WB, PIX0),
        grad_of(a2.reshape(SLOTS * PIX0, M0), d3.reshape(SLOTS * PIX0, C0)),
    ]
    grads1 = [
        grad_of(src, e1),
        conv_grad(wide1, e2, WB // 2, PIX1),
        grad_of(b2, e3),
        grad_of(src, es),
    ]
    pieces = []
    for matrix in grads1 + grads0:
        pieces += panels(matrix)
    joined = jnp.concatenate(pieces, axis=0)
    padding = -joined.shape[0] % (64 * count)
    joined = jnp.pad(joined, ((0, padding), (0, 0)))
    half = joined.shape[0] // 2
    kept = jnp.where(first_core, joined[:half], joined[half:])
    other = swap_cores(jnp.where(first_core, joined[half:], joined[:half]))
    shard = (kept.astype(F32) + other.astype(F32)).astype(BF16)
    shard = doubled(halved(shard, bits), bits)
    other = swap_cores(shard)
    whole = jnp.concatenate(
        [jnp.where(first_core, shard, other), jnp.where(first_core, other, shard)], axis=0
    )

    def packed_grads(start, shapes):
        flats = []
        for rows, cols in shapes:
            parts = []
            for _ in range(0, cols, 256):
                parts.append(whole[start : start + rows])
                start += rows
            flats.append(pack(jnp.concatenate(parts, axis=1), max(1, rows * cols // 262144)))
        flat = jnp.concatenate(flats)
        return jnp.pad(flat, (0, P_SIZE - flat.shape[0]))

    shapes1 = [(C0, M1), (9 * M1, M1), (M1, C1), (C0, C1)]
    shapes0 = [(C0, M0), (9 * M0, M0), (M0, C0)]
    rows_one = P_SIZE // 256
    weight_grads = lax.cond(
        first_core,
        lambda: packed_grads(rows_one, shapes0),
        lambda: packed_grads(0, shapes1),
    )

    def gain_shift(table):
        parts = table.reshape(SLOTS, 2, -1).sum(axis=0)
        return jnp.stack([parts[1], parts[0]])

    line0 = jnp.concatenate([gain_shift(tot12), gain_shift(tot11), gain_shift(tot10)], axis=1)
    line0 = jnp.pad(line0, ((0, 0), (0, CN - line0.shape[1])))
    line1 = jnp.concatenate(
        [gain_shift(tot9), gain_shift(tot8), gain_shift(tot7), gain_shift(totg)], axis=1
    )
    got = swap_cores(jnp.where(first_core, line1, line0))
    norm_grads = jnp.where(first_core, line0, line1) + got

    elems = HB * WB * C0
    rows_y = jnp.pad(y_out.reshape(SLOTS, -1), ((0, 0), (0, elems // 2)))
    rows_x = gx.reshape(SLOTS, -1)
    got = swap_cores(jnp.where(first_core, rows_y, rows_x))
    boundary = jnp.concatenate(
        [jnp.where(first_core, rows_x, got), jnp.where(first_core, got, rows_y)], axis=0
    )
    return boundary[None], weight_grads[None], norm_grads[None]


def solution(mesh):
    placed_as = (
        P("dp", None, None, None),
        P("dp", None),
        P("dp"),
        P("pipe", None),
        P("pipe", None, None),
        P("dp", None, None, None),
    )
    return jax.shard_map(
        on_device,
        mesh=mesh,
        in_specs=placed_as,
        out_specs=(P("pipe", "dp", None), P("pipe", None), P("pipe", None, None)),
        check_vma=False,
    )
```

```python
import functools

import jax
import jax.numpy as jnp
from jax import lax
from jax.experimental import pallas as pl
from jax.experimental.pallas import tpu as pltpu
from jax.sharding import PartitionSpec as P

C0 = 1024
M0 = 256
M1 = 512
C1 = 2048
HB = 16
WB = 16
IMG_MB = 2
MB = 4
P_SIZE = 6029312
CN = 5120
SLOTS = 4
PIX0 = 256
PIX1 = 64
EPSILON = 1e-05
MIB = 1 << 20

F32 = jnp.float32
BF16 = jnp.bfloat16


def shape_of(dims, kind):
    return jax.ShapeDtypeStruct(dims, kind)


def dot_nn(left, right):
    return lax.dot_general(left, right, (((1,), (0,)), ((), ())), preferred_element_type=F32)


def dot_nt(left, right):
    return lax.dot_general(left, right, (((1,), (1,)), ((), ())), preferred_element_type=F32)


def over_lanes(column, width):
    return jnp.concatenate([column] * (width // 128), axis=1)


def pixel_mask(high, wide, breadth, rows):
    index = lax.broadcasted_iota(jnp.int32, (rows, 128), 0)
    shift = breadth.bit_length() - 1
    inside = ((index >> shift) < high) & ((index & (breadth - 1)) < wide)
    return jnp.where(inside, 1.0, 0.0).astype(F32)


def column_of(breadth, rows, width):
    return lax.broadcasted_iota(jnp.int32, (rows, width), 0) & (breadth - 1)


def sigmoid(values):
    return 1.0 / (1.0 + jnp.exp(-values))


def silu(values):
    return values * sigmoid(values)


def slope(values):
    sig = sigmoid(values)
    return sig * (1.0 + values * (1.0 - sig))


def row_at(table, row):
    if isinstance(row, int):
        return table[row : row + 1, :]
    rows = lax.broadcasted_iota(jnp.int32, table.shape, 0)
    return jnp.sum(jnp.where(rows == row, table, 0.0), axis=0, keepdims=True)


def put_rows(ref, slot, first, second):
    if isinstance(slot, int):
        ref[2 * slot : 2 * slot + 1, :] = first
        ref[2 * slot + 1 : 2 * slot + 2, :] = second
        return
    rows = lax.broadcasted_iota(jnp.int32, ref.shape, 0)
    kept = jnp.where(rows == 2 * slot, first, ref[...])
    ref[...] = jnp.where(rows == 2 * slot + 1, second, kept)


def total_rows(values):
    return jnp.sum(values, axis=0, keepdims=True)


def mean_scale(table, slot, count):
    mean = row_at(table, 2 * slot) / count
    spread = row_at(table, 2 * slot + 1) / count - mean * mean
    return mean, lax.rsqrt(spread + EPSILON)


def back_means(table, slot, count):
    return row_at(table, 2 * slot) / count, row_at(table, 2 * slot + 1) / count


def count_of(table, slot):
    return row_at(table, 2 * slot)[:, M0 : M0 + 1]


def side_columns(values, breadth):
    rows, width = values.shape
    column = column_of(breadth, rows, width)
    left = jnp.where(column == 0, 0.0, pltpu.roll(values, 1, 0))
    right = jnp.where(column == breadth - 1, 0.0, pltpu.roll(values, rows - 1, 0))
    return left, right


def later_rows(values, step, height, breadth):
    if step == 0:
        return values
    rows, width = values.shape
    images = values.reshape(rows // (height * breadth), height * breadth, width)
    gap = jnp.zeros((images.shape[0], breadth, width), values.dtype)
    if step > 0:
        moved = jnp.concatenate([gap, images[:, :-breadth]], axis=1)
    else:
        moved = jnp.concatenate([images[:, breadth:], gap], axis=1)
    return moved.reshape(rows, width)


def even_picker():
    row = lax.broadcasted_iota(jnp.int32, (PIX1, PIX0), 0)
    col = lax.broadcasted_iota(jnp.int32, (PIX1, PIX0), 1)
    return jnp.where(col == 32 * (row >> 3) + 2 * (row & 7), 1.0, 0.0).astype(BF16)


def even_placer():
    row = lax.broadcasted_iota(jnp.int32, (PIX0, PIX1), 0)
    col = lax.broadcasted_iota(jnp.int32, (PIX0, PIX1), 1)
    return jnp.where(row == 32 * (col >> 3) + 2 * (col & 7), 1.0, 0.0).astype(BF16)


def placed(values):
    placer = even_placer()
    high = values.astype(BF16)
    rest = (values - high.astype(F32)).astype(BF16)
    return dot_nn(placer, high) + dot_nn(placer, rest)


def call(body, outs, grid, in_specs, out_specs, scratch=(), limit=28, aliases={}):
    return pl.pallas_call(
        body,
        out_shape=outs,
        grid_spec=pltpu.PrefetchScalarGridSpec(
            num_scalar_prefetch=1,
            grid=grid,
            in_specs=in_specs,
            out_specs=out_specs,
            scratch_shapes=list(scratch),
        ),
        input_output_aliases=aliases,
        compiler_params=pltpu.CompilerParams(vmem_limit_bytes=limit * MIB),
    )


ANYWHERE = pl.BlockSpec(memory_space=pltpu.HBM)


def in_hbm(array):
    return pltpu.with_memory_space_constraint(array, pltpu.HBM)


DMA = pltpu.SemaphoreType.DMA
CORE, PLANE, LEVEL = 16, 17, 18


def fetch(meta, owner, own_ref, got_ref, here, sem):
    mine = meta[CORE] == owner

    @pl.when(mine)
    def _():
        pltpu.make_async_copy(own_ref, here, sem).start()

    @pl.when(jnp.logical_not(mine))
    def _():
        pltpu.make_async_copy(got_ref, here, sem).start()


def await_copy(ref, here, sem):
    pltpu.make_async_copy(ref, here, sem).wait()


def full(*dims):
    return pl.BlockSpec(dims, lambda *_: (0,) * len(dims), pipeline_mode=pl.Buffered(1))


def per_slot(*dims):
    return pl.BlockSpec((1,) + dims, lambda s, meta: (s,) + (0,) * len(dims))


def per_image(*dims):
    return pl.BlockSpec((1,) + dims, lambda s, meta: (meta[s],) + (0,) * len(dims))


def slot_mask0(meta, slot):
    return pixel_mask(meta[SLOTS + slot], meta[2 * SLOTS + slot], WB, PIX0)


def slot_mask1(meta, slot):
    return pixel_mask(meta[SLOTS + slot] >> 1, meta[2 * SLOTS + slot] >> 1, WB // 2, PIX1)


def front_one(meta, x_ref, wa_ref, wb_ref, z_ref, st_ref, w_ref, sem):
    slot = pl.program_id(0)

    @pl.when(slot == 0)
    def _():
        fetch(meta, 0, wa_ref, wb_ref, w_ref, sem)
        await_copy(wa_ref, w_ref, sem)

    z = dot_nn(x_ref[0].reshape(PIX0, C0), w_ref[...])
    z_ref[0] = z
    zm = z * over_lanes(slot_mask0(meta, slot), M0)
    count = (meta[SLOTS + slot] * meta[2 * SLOTS + slot]).astype(F32)
    extra = jnp.full((1, 128), 1.0, F32) * count
    put_rows(
        st_ref,
        slot,
        jnp.concatenate([total_rows(zm), extra], axis=1),
        jnp.concatenate([total_rows(zm * z), extra], axis=1),
    )


def front_two(
    meta, r_ref, z_ref, n_ref, wa_ref, wb_ref, tot_ref, a1_ref, z2_ref, st_ref, w_ref, act_ref, sem
):
    slot = pl.program_id(0)

    @pl.when(slot == 0)
    def _():
        fetch(meta, 0, wa_ref, wb_ref, w_ref, sem)
        tot_ref[...] = jnp.sum(r_ref[...], axis=0)
        act_ref[0:WB, :] = jnp.zeros((WB, 3 * M0), BF16)
        act_ref[WB + PIX0 : 2 * WB + PIX0, :] = jnp.zeros((WB, 3 * M0), BF16)

    table = tot_ref[...]
    count = count_of(table, slot)
    mean, scale = mean_scale(table[:, :M0], slot, count)
    mask = over_lanes(slot_mask0(meta, slot), M0)
    pre = (z_ref[0] - mean) * scale * n_ref[0:1, :M0] + n_ref[1:2, :M0]
    act = silu(pre) * mask
    left, right = side_columns(act, WB)
    wide = jnp.concatenate([left, act, right], axis=1).astype(BF16)
    act_ref[WB : WB + PIX0, :] = wide
    a1_ref[0] = wide[:, M0 : 2 * M0]

    @pl.when(slot == 0)
    def _():
        await_copy(wa_ref, w_ref, sem)

    z2 = dot_nn(act_ref[0:PIX0, :], w_ref[0 : 3 * M0, :])
    z2 = z2 + dot_nn(act_ref[WB : WB + PIX0, :], w_ref[3 * M0 : 6 * M0, :])
    z2 = z2 + dot_nn(act_ref[2 * WB : 2 * WB + PIX0, :], w_ref[6 * M0 :, :])
    z2_ref[0] = z2
    zm = z2 * mask
    put_rows(st_ref, slot, total_rows(zm), total_rows(zm * z2))


def front_three(
    meta, r_ref, tot_ref, z2_ref, n_ref, wa_ref, wb_ref, tot2_ref, a2_ref, st_ref, w_ref, sem
):
    slot = pl.program_id(0)

    @pl.when(slot == 0)
    def _():
        fetch(meta, 0, wa_ref, wb_ref, w_ref, sem)
        tot2_ref[...] = jnp.sum(r_ref[...], axis=0)

    count = count_of(tot_ref[...], slot)
    mean, scale = mean_scale(tot2_ref[...], slot, count)
    pre = (z2_ref[0] - mean) * scale * n_ref[0:1, M0 : 2 * M0] + n_ref[1:2, M0 : 2 * M0]
    act = (silu(pre) * over_lanes(slot_mask0(meta, slot), M0)).astype(BF16)
    a2_ref[0] = act

    @pl.when(slot == 0)
    def _():
        await_copy(wa_ref, w_ref, sem)

    z3 = dot_nn(act, w_ref[...])
    put_rows(st_ref, slot, total_rows(z3), total_rows(z3 * z3))


def join(
    meta, tot3_ref, tot_ref, a2_ref, x_ref, n_ref, w3a_ref, w3b_ref, w1a_ref, w1b_ref, wsa_ref, wsb_ref,
    s_ref, p_ref, z3_ref, z1_ref, zs_ref, st_ref, sts_ref, w3_ref, w1_ref, ws_ref, sems,
):
    step = pl.program_id(0)
    part = C1 // 4

    @pl.when(step == 0)
    def _():
        fetch(meta, 0, w3a_ref, w3b_ref, w3_ref, sems.at[0])
        fetch(meta, 1, w1a_ref, w1b_ref, w1_ref, sems.at[1])
        for k in range(4):
            cols = pl.ds(k * part, part)
            fetch(meta, 1, wsa_ref.at[:, cols], wsb_ref.at[:, cols], ws_ref.at[k], sems.at[2 + k])
        await_copy(w3a_ref, w3_ref, sems.at[0])

    @pl.when(step < SLOTS)
    def _():
        count = count_of(tot_ref[...], step)
        mean, scale = mean_scale(tot3_ref[...], step, count)
        picker = even_picker()
        act = dot_nn(picker, a2_ref[0]).astype(BF16)
        z3 = dot_nn(act, w3_ref[...])
        here = pl.ds(pl.multiple_of(step * PIX1, PIX1), PIX1)
        z3_ref[here, :] = z3
        pre = (z3 - mean) * scale * n_ref[0:1, 2 * M0 : 2 * M0 + C0]
        pre = pre + n_ref[1:2, 2 * M0 : 2 * M0 + C0]
        pre = pre + dot_nn(picker, x_ref[0].reshape(PIX0, C0))
        p_ref[here, :] = pre
        s_ref[here, :] = (silu(pre) * over_lanes(slot_mask1(meta, step), C0)).astype(BF16)

    @pl.when(step == SLOTS)
    def _():
        await_copy(w1a_ref, w1_ref, sems.at[1])
        z1 = dot_nn(s_ref[...], w1_ref[...])
        z1_ref[...] = z1
        for slot in range(SLOTS):
            rows = z1[slot * PIX1 : (slot + 1) * PIX1]
            put_rows(st_ref, slot, total_rows(rows), total_rows(rows * rows))

    for k in range(4):

        @pl.when(step == SLOTS + k)
        def _(k=k):
            await_copy(wsa_ref.at[:, pl.ds(k * part, part)], ws_ref.at[k], sems.at[2 + k])
            zs = dot_nn(s_ref[...], ws_ref[k])
            zs_ref[...] = zs
            for slot in range(SLOTS):
                rows = zs[slot * PIX1 : (slot + 1) * PIX1]
                put_rows(sts_ref, slot, total_rows(rows), total_rows(rows * rows))


def by_slot(pieces):
    return jnp.concatenate(pieces, axis=0)


def normed_slots(values, table, counts, width):
    pieces = []
    for slot in range(SLOTS):
        mean, scale = mean_scale(table, slot, counts[slot])
        pieces.append((values[slot * PIX1 : (slot + 1) * PIX1] - mean) * scale)
    return by_slot(pieces)


def counts1(tot_ref):
    table = tot_ref[...]
    return [count_of(table, slot) * 0.25 for slot in range(SLOTS)]


def mask1_all(meta, width):
    return over_lanes(by_slot([slot_mask1(meta, slot) for slot in range(SLOTS)]), width)


def slot_sums(st_ref, first, second):
    for slot in range(SLOTS):
        here = slice(slot * PIX1, (slot + 1) * PIX1)
        put_rows(st_ref, slot, total_rows(first[here]), total_rows(second[here]))


def fetch_conv(meta, wa_ref, wb_ref, w_ref, sems):
    for k in range(3):
        rows = pl.ds(k * 3 * M1, 3 * M1)
        fetch(meta, 1, wa_ref.at[rows], wb_ref.at[rows], w_ref.at[rows], sems.at[k])


def await_conv(wa_ref, w_ref, sems, k):
    rows = pl.ds(k * 3 * M1, 3 * M1)
    await_copy(wa_ref.at[rows], w_ref.at[rows], sems.at[k])


def mid_one(
    meta, r_ref, tot_ref, z1_ref, n_ref, wa_ref, wb_ref, tot4_ref, a1_ref, z2_ref, st_ref, w_ref, sems
):
    fetch_conv(meta, wa_ref, wb_ref, w_ref, sems)
    tot4_ref[...] = jnp.sum(r_ref[...], axis=0)
    counts = counts1(tot_ref)
    mask = mask1_all(meta, M1)
    pre = normed_slots(z1_ref[...], tot4_ref[...], counts, M1) * n_ref[0:1, :M1] + n_ref[1:2, :M1]
    act = silu(pre) * mask
    left, right = side_columns(act, WB // 2)
    wide = jnp.concatenate([left, act, right], axis=1).astype(BF16)
    a1_ref[...] = wide[:, M1 : 2 * M1]
    await_conv(wa_ref, w_ref, sems, 0)
    z2 = later_rows(dot_nn(wide, w_ref[0 : 3 * M1, :]), 1, HB // 2, WB // 2)
    await_conv(wa_ref, w_ref, sems, 1)
    z2 = z2 + dot_nn(wide, w_ref[3 * M1 : 6 * M1, :])
    await_conv(wa_ref, w_ref, sems, 2)
    z2 = z2 + later_rows(dot_nn(wide, w_ref[6 * M1 :, :]), -1, HB // 2, WB // 2)
    z2_ref[...] = z2
    zm = z2 * mask
    slot_sums(st_ref, zm, zm * z2)


def mid_two(
    meta, r_ref, tot_ref, z2_ref, n_ref, wa_ref, wb_ref, tot5_ref, a2_ref, z3_ref, st_ref, w_ref, sems
):
    fetch(meta, 1, wa_ref, wb_ref, w_ref, sems)
    tot5_ref[...] = jnp.sum(r_ref[...], axis=0)
    counts = counts1(tot_ref)
    pre = normed_slots(z2_ref[...], tot5_ref[...], counts, M1)
    pre = pre * n_ref[0:1, M1 : 2 * M1] + n_ref[1:2, M1 : 2 * M1]
    act = (silu(pre) * mask1_all(meta, M1)).astype(BF16)
    a2_ref[...] = act
    await_copy(wa_ref, w_ref, sems)
    z3 = dot_nn(act, w_ref[...])
    z3_ref[...] = z3
    slot_sums(st_ref, z3, z3 * z3)


def turn(
    meta, tot6_ref, tots_ref, tot_ref, z3_ref, zs_ref, n_ref, cot_ref,
    y_ref, g_ref, st_ref, sts_ref,
):
    slot = pl.program_id(0)
    count = count_of(tot_ref[...], slot) * 0.25
    mask = over_lanes(slot_mask1(meta, slot), C1)
    mean, scale = mean_scale(tot6_ref[...], slot, count)
    normed = (z3_ref[0] - mean) * scale
    mean_s, scale_s = mean_scale(tots_ref[...], slot, count)
    normed_s = (zs_ref[0] - mean_s) * scale_s
    at3, ats = 2 * M1, 2 * M1 + C1
    pre = normed * n_ref[0:1, at3:ats] + n_ref[1:2, at3:ats]
    pre = pre + (normed_s * n_ref[0:1, ats : ats + C1] + n_ref[1:2, ats : ats + C1])
    sig = sigmoid(pre)
    y_ref[0] = (pre * sig * mask).astype(BF16)
    grad = cot_ref[0].reshape(PIX1, C1).astype(F32) * (sig * (1.0 + pre * (1.0 - sig))) * mask
    g_ref[0] = grad
    put_rows(st_ref, slot, total_rows(grad), total_rows(grad * normed))
    put_rows(sts_ref, slot, total_rows(grad), total_rows(grad * normed_s))


def turn_of(core, mask):
    return jnp.where((core == 1) & ((mask == 1) | (mask == 2)), 3 - mask, mask)


SWAPPED = (0, 2, 1, 3)


def norm_back_slots(grad, normed, scales, gain, table, counts, mask):
    pieces = []
    for slot in range(SLOTS):
        here = slice(slot * PIX1, (slot + 1) * PIX1)
        first, second = back_means(table, slot, counts[slot])
        pieces.append(
            mask[here] * scales[slot] * gain * (grad[here] - first - normed[here] * second)
        )
    return by_slot(pieces).astype(BF16)


def scales_of(table, counts):
    return [mean_scale(table, slot, counts[slot])[1] for slot in range(SLOTS)]


def back_one(
    meta, tot7_ref, totg_ref, tot6_ref, tots_ref, tot5_ref, tot_ref, z3_ref, zs_ref, g_ref, z2_ref,
    n_ref, wa_ref, wb_ref,
    er_ref, es_ref, g2_ref, st_ref, w_ref, sems,
):
    fetch(meta, 1, wa_ref, wb_ref, w_ref, sems)
    counts = counts1(tot_ref)
    mask = mask1_all(meta, C1)
    grad = g_ref[...]
    normed = normed_slots(z3_ref[...], tot6_ref[...], counts, C1)
    d3 = norm_back_slots(
        grad, normed, scales_of(tot6_ref[...], counts), n_ref[0:1, 2 * M1 : 2 * M1 + C1],
        tot7_ref[...], counts, mask,
    )
    normed2 = normed_slots(z2_ref[...], tot5_ref[...], counts, M1)
    pre2 = normed2 * n_ref[0:1, M1 : 2 * M1] + n_ref[1:2, M1 : 2 * M1]
    await_copy(wa_ref, w_ref, sems)
    g2 = dot_nt(d3, w_ref[...]) * mask[:, :M1] * slope(pre2)
    g2_ref[...] = g2
    slot_sums(st_ref, g2, g2 * normed2)
    normed_s = normed_slots(zs_ref[...], tots_ref[...], counts, C1)
    ats = 2 * M1 + C1
    ds = norm_back_slots(
        grad, normed_s, scales_of(tots_ref[...], counts), n_ref[0:1, ats : ats + C1],
        totg_ref[...], counts, mask,
    )
    es_ref[...] = ds
    core, plane = meta[CORE], meta[PLANE]
    for p in range(2):
        for c in range(4):
            cols = slice((4 * p + c) * 256, (4 * p + c + 1) * 256)
            here = 4 * (core ^ p) + turn_of(p, plane ^ c)
            er_ref[here] = jnp.concatenate([d3[:, cols], ds[:, cols]], axis=1)


def back_two(
    meta, r_ref, tot5_ref, tot4_ref, tot_ref, z2_ref, g2_ref, z1_ref, n_ref, wa_ref, wb_ref,
    tot8_ref, e2r_ref, g1_ref, st_ref, w_ref, sems,
):
    fetch_conv(meta, wa_ref, wb_ref, w_ref, sems)
    tot8_ref[...] = jnp.sum(r_ref[...], axis=0)
    counts = counts1(tot_ref)
    mask = mask1_all(meta, M1)
    normed = normed_slots(z2_ref[...], tot5_ref[...], counts, M1)
    d2 = norm_back_slots(
        g2_ref[...], normed, scales_of(tot5_ref[...], counts), n_ref[0:1, M1 : 2 * M1],
        tot8_ref[...], counts, mask,
    )
    for c in range(4):
        e2r_ref[turn_of(meta[CORE], meta[PLANE] ^ c)] = d2[:, 128 * c : 128 * (c + 1)]
    normed1 = normed_slots(z1_ref[...], tot4_ref[...], counts, M1)
    pre1 = normed1 * n_ref[0:1, :M1] + n_ref[1:2, :M1]
    await_conv(wa_ref, w_ref, sems, 0)
    wide = later_rows(dot_nt(d2, w_ref[0 : 3 * M1, :]), -1, HB // 2, WB // 2)
    await_conv(wa_ref, w_ref, sems, 1)
    wide = wide + dot_nt(d2, w_ref[3 * M1 : 6 * M1, :])
    await_conv(wa_ref, w_ref, sems, 2)
    wide = wide + later_rows(dot_nt(d2, w_ref[6 * M1 :, :]), 1, HB // 2, WB // 2)
    left, _ = side_columns(wide[:, 2 * M1 :], WB // 2)
    _, right = side_columns(wide[:, :M1], WB // 2)
    g1 = (wide[:, M1 : 2 * M1] + left + right) * mask * slope(pre1)
    g1_ref[...] = g1
    slot_sums(st_ref, g1, g1 * normed1)


def back_three(
    meta, r_ref, tot4_ref, tot_ref, z1_ref, g1_ref, es_ref, tot3_ref, p_ref, z3_ref, n_ref,
    w1a_ref, w1b_ref, wsa_ref, wsb_ref,
    tot9_ref, e1r_ref, g0_ref, st_ref, w1_ref, ws_ref, sems,
):
    fetch(meta, 1, w1a_ref, w1b_ref, w1_ref, sems.at[0])
    fetch(meta, 1, wsa_ref, wsb_ref, ws_ref, sems.at[1])
    tot9_ref[...] = jnp.sum(r_ref[...], axis=0)
    counts = counts1(tot_ref)
    mask = mask1_all(meta, C0)
    normed = normed_slots(z1_ref[...], tot4_ref[...], counts, M1)
    d1 = norm_back_slots(
        g1_ref[...], normed, scales_of(tot4_ref[...], counts), n_ref[0:1, :M1],
        tot9_ref[...], counts, mask[:, :M1],
    )
    for c in range(4):
        e1r_ref[turn_of(meta[CORE], meta[PLANE] ^ c)] = d1[:, 128 * c : 128 * (c + 1)]
    await_copy(w1a_ref, w1_ref, sems.at[0])
    grad = dot_nt(d1, w1_ref[...])
    await_copy(wsa_ref, ws_ref, sems.at[1])
    grad = grad + dot_nt(es_ref[...], ws_ref[...])
    grad = grad.astype(BF16).astype(F32)
    g0 = grad * slope(p_ref[...]) * mask
    g0_ref[...] = g0
    counts0 = [count * 4.0 for count in counts]
    normed3 = normed_slots(z3_ref[...], tot3_ref[...], counts0, C0)
    slot_sums(st_ref, g0, g0 * normed3)


def norm_back(grad, normed, scale, gain, table, slot, count, mask):
    first, second = back_means(table, slot, count)
    return (mask * scale * gain * (grad - first - normed * second)).astype(BF16)


def last_one(
    meta, tot10_ref, tot3_ref, tot2_ref, tot_ref, a2_ref, g0_ref, z2_ref, n_ref, wa_ref, wb_ref,
    d3_ref, g2_ref, st_ref, w_ref, sem,
):
    slot = pl.program_id(0)

    @pl.when(slot == 0)
    def _():
        fetch(meta, 0, wa_ref, wb_ref, w_ref, sem)
        await_copy(wa_ref, w_ref, sem)

    count = count_of(tot_ref[...], slot)
    mask = over_lanes(slot_mask0(meta, slot), C0)
    mean, scale = mean_scale(tot3_ref[...], slot, count)
    normed = (dot_nn(a2_ref[0], w_ref[...]) - mean) * scale
    grad = placed(g0_ref[0])
    d3 = norm_back(
        grad, normed, scale, n_ref[0:1, 2 * M0 : 2 * M0 + C0], tot10_ref[...], slot, count, mask
    )
    d3_ref[0] = d3
    mean2, scale2 = mean_scale(tot2_ref[...], slot, count)
    normed2 = (z2_ref[0] - mean2) * scale2
    pre2 = normed2 * n_ref[0:1, M0 : 2 * M0] + n_ref[1:2, M0 : 2 * M0]
    g2 = dot_nt(d3, w_ref[...]) * mask[:, :M0] * slope(pre2)
    g2_ref[0] = g2
    put_rows(st_ref, slot, total_rows(g2), total_rows(g2 * normed2))


def last_two(
    meta, r_ref, tot2_ref, tot_ref, z2_ref, g2_ref, z1_ref, n_ref, wa_ref, wb_ref,
    tot11_ref, d2_ref, g1_ref, st_ref, w_ref, sem,
):
    slot = pl.program_id(0)

    @pl.when(slot == 0)
    def _():
        fetch(meta, 0, wa_ref, wb_ref, w_ref, sem)
        tot11_ref[...] = jnp.sum(r_ref[...], axis=0)

    table = tot_ref[...]
    count = count_of(table, slot)
    mask = over_lanes(slot_mask0(meta, slot), M0)
    mean2, scale2 = mean_scale(tot2_ref[...], slot, count)
    normed2 = (z2_ref[0] - mean2) * scale2
    d2 = norm_back(
        g2_ref[0], normed2, scale2, n_ref[0:1, M0 : 2 * M0], tot11_ref[...], slot, count, mask
    )
    d2_ref[0] = d2
    mean1, scale1 = mean_scale(table[:, :M0], slot, count)
    normed1 = (z1_ref[0] - mean1) * scale1
    pre1 = normed1 * n_ref[0:1, :M0] + n_ref[1:2, :M0]

    @pl.when(slot == 0)
    def _():
        await_copy(wa_ref, w_ref, sem)

    wide = dot_nt(d2, w_ref[3 * M0 : 6 * M0, :])
    wide = wide + later_rows(dot_nt(d2, w_ref[0 : 3 * M0, :]), -1, HB, WB)
    wide = wide + later_rows(dot_nt(d2, w_ref[6 * M0 :, :]), 1, HB, WB)
    left, _ = side_columns(wide[:, 2 * M0 :], WB)
    _, right = side_columns(wide[:, :M0], WB)
    g1 = (wide[:, M0 : 2 * M0] + left + right) * mask * slope(pre1)
    g1_ref[0] = g1
    put_rows(st_ref, slot, total_rows(g1), total_rows(g1 * normed1))


def last_three(
    meta, r_ref, tot_ref, z1_ref, g1_ref, g0_ref, n_ref, wa_ref, wb_ref,
    tot12_ref, d1_ref, gx_ref, w_ref, sem,
):
    slot = pl.program_id(0)

    @pl.when(slot == 0)
    def _():
        fetch(meta, 0, wa_ref, wb_ref, w_ref, sem)
        tot12_ref[...] = jnp.sum(r_ref[...], axis=0)

    table = tot_ref[...]
    count = count_of(table, slot)
    mask = over_lanes(slot_mask0(meta, slot), M0)
    mean1, scale1 = mean_scale(table[:, :M0], slot, count)
    normed1 = (z1_ref[0] - mean1) * scale1
    d1 = norm_back(g1_ref[0], normed1, scale1, n_ref[0:1, :M0], tot12_ref[...], slot, count, mask)
    d1_ref[0] = d1

    @pl.when(slot == 0)
    def _():
        await_copy(wa_ref, w_ref, sem)

    grad = dot_nt(d1, w_ref[...]) + placed(g0_ref[0])
    gx_ref[0] = grad.astype(BF16)


def dot_tn(left, right):
    return lax.dot_general(left, right, (((0,), (0,)), ((), ())), preferred_element_type=F32)


def put_tiles(ref, start, values):
    rows, width = values.shape
    for k in range(width // 128):
        ref[start + k * rows : start + (k + 1) * rows, :] = values[:, 128 * k : 128 * (k + 1)].astype(BF16)


def nine_shifts(delta, height, breadth):
    pieces = []
    left, right = side_columns(delta, breadth)
    for a in range(3):
        for moved in (right, delta, left):
            pieces.append(later_rows(moved, a - 1, height, breadth).astype(BF16))
    return jnp.concatenate(pieces, axis=1)


def put_shards(ref, start, shard, values):
    rows = values.shape[0] // 4
    for z in range(4):
        for k in range(values.shape[1] // 128):
            here = z * shard + start + k * rows
            part = values[z * rows : (z + 1) * rows, 128 * k : 128 * (k + 1)]
            ref[here : here + rows, :] = part.astype(BF16)


SIDES, MIDDLE = 768, 704


def sides_grad(meta, sa_ref, sb_ref, la_ref, lb_ref, *refs):
    rights, out_ref = refs[0:4], refs[4]
    total_s, total_3 = 0.0, 0.0
    for core, (source_ref, left_ref) in enumerate(((sa_ref, la_ref), (sb_ref, lb_ref))):
        for k in range(4):
            right = rights[k][core]
            place = SWAPPED[k] if core else k
            total_s = total_s + dot_tn(source_ref[place], right[:, 256:])
            total_3 = total_3 + dot_tn(left_ref[place][:, :M1], right[:, :256])
    put_shards(out_ref, 0, SIDES, total_s)
    put_shards(out_ref, C0 // 2, SIDES, total_3)


def middle_grad(meta, la_ref, lb_ref, sa_ref, sb_ref, ma_ref, mb_ref, out_ref):
    first = meta[CORE] == 0
    total_2, total_1 = 0.0, 0.0
    half, some = M1 // 2, C0 // 2
    for left_ref, source_ref, mid_ref in ((la_ref, sa_ref, ma_ref), (lb_ref, sb_ref, mb_ref)):
        for k in range(4):
            mid = mid_ref[k]
            shifted = nine_shifts(mid[:, :128].astype(F32), HB // 2, WB // 2)
            left = left_ref[k][:, M1:]
            left = jnp.where(first, left[:, :half], left[:, half:])
            total_2 = total_2 + dot_tn(left, shifted)
            source = source_ref[k]
            source = jnp.where(first, source[:, :some], source[:, some:])
            total_1 = total_1 + dot_tn(source, mid[:, 128:])
    put_shards(out_ref, 0, MIDDLE, total_2)
    put_shards(out_ref, 9 * M1 // 8, MIDDLE, total_1)


def front_grad_two(meta, a1_ref, d2_ref, a2_ref, d3_ref, out_ref, acc2_ref, acc3_ref):
    slot = pl.program_id(0)
    conv = dot_tn(a1_ref[0], nine_shifts(d2_ref[0].astype(F32), HB, WB))
    last = dot_tn(a2_ref[0], d3_ref[0])

    @pl.when(slot == 0)
    def _():
        acc2_ref[...] = conv
        acc3_ref[...] = last

    @pl.when(slot > 0)
    def _():
        acc2_ref[...] += conv
        acc3_ref[...] += last

    @pl.when(slot == SLOTS - 1)
    def _():
        for tap in range(9):
            for tile in range(2):
                start = tile * 9 * M0 + tap * M0
                lanes = tap * M0 + tile * 128
                out_ref[start : start + M0, :] = acc2_ref[:, lanes : lanes + 128].astype(BF16)
        put_tiles(out_ref, 2 * 9 * M0, acc3_ref[...])


def front_grad_one(meta, x_ref, d1_ref, out_ref, acc_ref):
    slot = pl.program_id(0)
    first = dot_tn(x_ref[0].reshape(PIX0, C0), d1_ref[0])

    @pl.when(slot == 0)
    def _():
        acc_ref[...] = first

    @pl.when(slot > 0)
    def _():
        acc_ref[...] += first

    @pl.when(slot == SLOTS - 1)
    def _():
        put_tiles(out_ref, 0, acc_ref[...])


CHUNK = 262144


def unpack_kernel(shapes, jobs, meta, raw_ref, *refs):
    outs, refs = refs[: len(shapes)], refs[len(shapes) :]
    raws, flat_ref, sem_in, sem_out = refs[0:2], refs[2], refs[3], refs[4]
    stages = dict(zip(sorted({cols for _, cols in shapes}), refs[5:]))

    def run(listed):
        loads, stores, sizes = [], [], []
        for out, offset in listed:
            rows, cols = shapes[out]
            for row in range(0, rows, CHUNK // cols):
                some = min(CHUNK // cols, rows - row)
                k = len(loads)
                source = raw_ref.at[:, pl.ds(offset + row * cols, some * cols)]
                here = raws[k % 2].at[:, pl.ds(0, some * cols)]
                loads.append(pltpu.make_async_copy(source, here, sem_in.at[k % 2]))
                stage = stages[cols].at[k % 2, pl.ds(0, some)]
                there = outs[out].at[pl.ds(row, some)]
                stores.append(pltpu.make_async_copy(stage, there, sem_out.at[k % 2]))
                sizes.append((some, cols))
        loads[0].start()
        for k, (rows, cols) in enumerate(sizes):
            if k + 1 < len(sizes):
                loads[k + 1].start()
            loads[k].wait()
            flat_ref[:, : rows * cols] = raws[k % 2][:, : rows * cols].astype(F32)
            lines = flat_ref.reshape(CHUNK // 128, 128)
            if k >= 2:
                stores[k - 2].wait()
            for tile in range(cols // 128):
                values = lines[pl.ds(tile, rows, stride=cols // 128), :].astype(BF16)
                stages[cols][k % 2, 0:rows, tile * 128 : (tile + 1) * 128] = values
            stores[k].start()
        for store in stores[-2:]:
            store.wait()

    for core in range(2):
        if jobs[core]:
            pl.when(meta[CORE] == core)(functools.partial(run, jobs[core]))


def unpack(meta, packed, shapes, jobs):
    widths = sorted({cols for _, cols in shapes})
    return call(
        functools.partial(unpack_kernel, shapes, jobs),
        [pltpu.HBM(dims, BF16) for dims in shapes],
        (1,),
        [ANYWHERE],
        [ANYWHERE] * len(shapes),
        [pltpu.VMEM((1, CHUNK), BF16)] * 2
        + [pltpu.VMEM((1, CHUNK), F32), DMA((2,)), DMA((2,))]
        + [pltpu.VMEM((2, CHUNK // cols, cols), BF16) for cols in widths],
    )(meta, in_hbm(packed))


PACK_ROWS = 2048
GRAD_ROWS = P_SIZE // 128
ARRIVED = ((1, (0, 1)), (0, (0, 2)), (0, (1, 3)), (1, (2, 3)))


def quarters(bufs, target):
    found = []
    for buf, (p, masks) in zip(bufs, ARRIVED):
        if target == 0:
            p, masks = 1 - p, tuple(SWAPPED[m] for m in masks)
        for k, mask in enumerate(masks):
            found.append((p, mask, buf, k * (buf.shape[0] // 2)))
    return found


def pack_sides(meta, *refs):
    bufs, out_ref = refs[:4], refs[4]
    step = pl.program_id(0)

    @pl.when(meta[CORE] == 0)
    def _():
        out_ref[...] = jnp.zeros_like(out_ref)

    @pl.when(meta[CORE] == 1)
    def _():
        shard = jnp.where(step < 4, step, (step - 4) >> 1) ^ meta[LEVEL]
        for p, mask, buf, start in quarters(bufs, 1):
            for half in range(2):
                tile = 8 * p + 2 * (meta[PLANE] ^ mask) + half
                row = jnp.where(step < 4, C0 // 2 + 128 * half, 256 * half + 128 * (step & 1))
                here = pl.ds(pl.multiple_of(start + shard * SIDES + row, 128), 128)
                out_ref[pl.ds(tile, 128, stride=16), :] = buf[here, :].astype(F32)


def pack_middle(first_step, meta, *refs):
    bufs, out_ref = refs[1:5], refs[-1]
    step = pl.program_id(0) + first_step
    plane, level = meta[PLANE], meta[LEVEL]

    @pl.when((meta[CORE] == 1) & (step < 2))
    def _():
        for p, mask, buf, start in quarters(bufs, 1):

            @pl.when(step == p)
            def _(mask=mask, buf=buf, start=start):
                for z in range(4):
                    here = start + (level ^ z) * MIDDLE + 9 * M1 // 8
                    rows = buf[pl.ds(pl.multiple_of(here, 64), 128), :].astype(F32)
                    out_ref[pl.ds(512 * z + (plane ^ mask), 128, stride=4), :] = rows

    @pl.when((meta[CORE] == 1) & (step > 1))
    def _():
        for p, mask, buf, start in quarters(bufs, 1):
            for z in range(4):
                here = start + (level ^ z) * MIDDLE + (step - 2) * 64
                rows = buf[pl.ds(pl.multiple_of(here, 64), 64), :].astype(F32)
                at = 1024 * p + 256 * z + (plane ^ mask)
                out_ref[pl.ds(at, 64, stride=4), :] = rows


def pack_rest(meta, *refs):
    out_ref = refs[-1]

    @pl.when(meta[CORE] == 0)
    def _():
        out_ref[...] = jnp.zeros_like(out_ref)

    pack_middle(5, meta, *refs)


def pack_front(meta, *refs):
    fronts, out_ref, whole_ref = refs[5:9], refs[9], refs[10]
    step = pl.program_id(0)
    core, plane, level = meta[CORE], meta[PLANE], meta[LEVEL]
    part = fronts[0].shape[0] // 8

    @pl.when((core == 0) & (step == 0))
    def _():
        for p, mask, buf, start in quarters(fronts, 0):
            for z in range(4):
                there = ((4 * p + (plane ^ mask)) * 4 + (level ^ z)) * part
                rows = buf[start + z * part : start + (z + 1) * part, :]
                whole_ref[pl.ds(pl.multiple_of(there, 16), part), :] = rows

    at2, at3 = 2 * C0, 2 * C0 + 2 * 9 * M0

    def piece(start, rows):
        return whole_ref[start : start + rows, :].astype(F32)

    @pl.when((core == 0) & (step == 0))
    def _():
        for tile in range(2):
            out_ref[pl.ds(tile, C0, stride=2), :] = piece(tile * C0, C0)

    for k in range(2):

        @pl.when((core == 0) & (step == 1 + k))
        def _(k=k):
            for tile in range(2):
                out_ref[pl.ds(tile, C0, stride=2), :] = piece(at2 + tile * 9 * M0 + k * C0, C0)

    @pl.when((core == 0) & (step == 3))
    def _():
        for tile in range(2):
            out_ref[pl.ds(tile, 256, stride=2), :] = piece(at2 + tile * 9 * M0 + 2 * C0, 256)
        for tile in range(8):
            out_ref[pl.ds(512 + tile, 192, stride=8), :] = piece(at3 + tile * 256, 192)

    @pl.when((core == 0) & (step == 4))
    def _():
        out_ref[...] = jnp.zeros_like(out_ref)
        for tile in range(8):
            out_ref[pl.ds(tile, 64, stride=8), :] = piece(at3 + tile * 256 + 192, 64)

    pack_middle(0, meta, *refs[:5], out_ref)


def rows_out(meta, x_ref, xg_ref, y_ref, yg_ref, out_ref):
    step = pl.program_id(0)
    row = lax.broadcasted_iota(jnp.int32, (128, 128), 0)
    col = lax.broadcasted_iota(jnp.int32, (128, 128), 1)
    mover = jnp.where(col == 16 * (row & 7) + (row >> 3), 1.0, 0.0).astype(BF16)

    def put(first, second):
        values = jnp.concatenate([first.reshape(-1, C0), second.reshape(-1, C0)], axis=0)
        moved = dot_nn(mover, values).astype(BF16)
        for k in range(16):
            out_ref[:, k * C0 : (k + 1) * C0] = moved[8 * k : 8 * (k + 1), :]

    @pl.when(meta[CORE] == 0)
    def _():
        put(x_ref[...], xg_ref[...])

    @pl.when((meta[CORE] == 1) & (step < HB // 2))
    def _():
        pieces = []
        for ref in (yg_ref, y_ref):
            for image in range(SLOTS):
                wide = ref[image].astype(F32)
                pieces += [wide[:, :C0], wide[:, C0:]]
        values = jnp.concatenate(pieces, axis=0).astype(BF16)
        source = 16 * (row & 7) + 8 * ((row >> 3) & 1) + (row >> 4)
        mover_y = jnp.where(col == source, 1.0, 0.0).astype(BF16)
        moved = dot_nn(mover_y, values).astype(BF16)
        for k in range(16):
            out_ref[:, k * C0 : (k + 1) * C0] = moved[8 * k : 8 * (k + 1), :]

    @pl.when((meta[CORE] == 1) & (step >= HB // 2))
    def _():
        out_ref[...] = jnp.zeros_like(out_ref)


def pin(value, *others):
    return lax.optimization_barrier((value,) + others)[0]


def swap_cores(value):
    return lax.ppermute(value, "pipe", [(0, 1), (1, 0)])


def spread(value):
    count = lax.axis_size("dp")
    copies = jnp.broadcast_to(value[None], (count,) + value.shape)
    return lax.all_to_all(copies, "dp", 0, 0)


def xor_permute(value, mask):
    count = lax.axis_size("dp")
    return lax.ppermute(value, "dp", [(i, i ^ mask) for i in range(count)])


def levels(count):
    found, step = [], 4
    while step < count:
        radix = 4 if count // step >= 4 else 2
        found.append((step, radix))
        step *= radix
    return found


def summed(value):
    for step, radix in [(1, 4)] + levels(lax.axis_size("dp")):
        parts = [value] + [xor_permute(value, k * step) for k in range(1, radix)]
        while len(parts) > 1:
            parts = [sum(parts[i : i + 2]) for i in range(0, len(parts), 2)]
        value = parts[0]
    return value


def part_at(value, index, parts):
    rows = value.shape[0] // parts
    return lax.dynamic_slice_in_dim(value, index * rows, rows, 0)


def scattered(value, step, radix):
    digit = (lax.axis_index("dp") // step) % radix
    total = part_at(value, digit, radix).astype(F32)
    gots = [xor_permute(part_at(value, digit ^ k, radix), k * step) for k in range(1, radix)]
    for got in gots:
        total = total + got.astype(F32)
    return total.astype(BF16)


def level_sum(value):
    value = scattered(value, 4, 4)
    for step, radix in levels(lax.axis_size("dp"))[1:]:
        for bit in range(radix.bit_length() - 1):
            value = (value.astype(F32) + xor_permute(value, step << bit).astype(F32)).astype(BF16)
    return value


def level_gather(value):
    return jnp.concatenate([value] + [xor_permute(value, 4 * k) for k in (1, 2, 3)], axis=0)


def plane_turn(value, turn):
    count = lax.axis_size("dp")
    pairs = []
    for p in range(2):
        mask = SWAPPED[turn] if p else turn
        pairs += [(p * count + i, p * count + (i ^ mask)) for i in range(count)]
    return lax.ppermute(value, ("pipe", "dp"), pairs)


def plane_gather(value):
    two = jnp.stack([value, plane_turn(value, 1)])
    return two, lambda: jnp.concatenate([two, plane_turn(two, 2)], axis=0)


def to_core(value, target):
    count = lax.axis_size("dp")
    both = jnp.concatenate([value, plane_turn(value, 2)], axis=0)
    other = 1 - target
    near, far = (1, 2) if target == 1 else (2, 1)
    hops = [(other, 0), (other, near), (target, far)]
    arrived = [both]
    for p, mask in hops:
        pairs = [(p * count + i, target * count + (i ^ mask)) for i in range(count)]
        arrived.append(lax.ppermute(both, ("pipe", "dp"), pairs))
    return arrived


def on_device(images, extents, views, params, norms, cotangent):
    images, cotangent, params = in_hbm(images), in_hbm(cotangent), in_hbm(params)
    core = lax.axis_index("pipe")
    first_core = core == 0
    count = lax.axis_size("dp")
    plane = lax.axis_index("dp") % 4

    own_views = lax.dynamic_slice(views, (core * SLOTS,), (SLOTS,))
    own_ext = lax.dynamic_slice(extents, (core * SLOTS, 0), (SLOTS, 2))
    order = []
    for mb in range(SLOTS // IMG_MB):
        flipped = own_views[2 * mb] != 0
        order += [jnp.where(flipped, 2 * mb + 1, 2 * mb), jnp.where(flipped, 2 * mb, 2 * mb + 1)]
    order = jnp.stack(order).astype(jnp.int32)
    hot = (order[:, None] == jnp.arange(SLOTS, dtype=jnp.int32)[None, :]).astype(jnp.int32)
    sizes = jnp.sum(hot[:, :, None] * own_ext[None], axis=1)
    level = (lax.axis_index("dp") // 4) % 4
    place = jnp.stack([core, plane, level]).astype(jnp.int32)
    meta = jnp.concatenate([order + core * SLOTS, sizes[:, 0], sizes[:, 1], order, place])
    meta = meta.astype(jnp.int32)

    def sent_from(owner, matrix):
        return in_hbm(matrix), in_hbm(lax.ppermute(matrix, "pipe", [(owner, 1 - owner)]))

    (w1,) = unpack(meta, params, [(C0, M0)], ([(0, 0)], []))
    w1 = sent_from(0, w1)
    w2, w3, v1 = unpack(
        meta,
        params,
        [(9 * M0, M0), (M0, C0), (C0, M1)],
        ([(0, 262144), (1, 851968)], [(2, 0)]),
    )
    w2, w3, v1 = sent_from(0, w2), sent_from(0, w3), sent_from(1, v1)
    norms_there = swap_cores(norms[0])
    norms0 = jnp.where(first_core, norms[0], norms_there)
    norms1 = jnp.where(first_core, norms_there, norms[0])

    image = per_image(HB, WB, C0)
    vmem = lambda *dims: pltpu.VMEM(dims, BF16)
    z1, st = call(
        front_one,
        [shape_of((SLOTS, PIX0, M0), F32), shape_of((8, M0 + 128), F32)],
        (SLOTS,),
        [image, ANYWHERE, ANYWHERE],
        [per_slot(PIX0, M0), full(8, M0 + 128)],
        [vmem(C0, M0), DMA],
    )(meta, images, *w1)

    r1 = spread(st)
    (vs,) = unpack(meta, pin(params, st), [(C0, C1)], ([], [(0, 3932160)]))
    r1 = pin(r1, vs, w2[1], w3[1], v1[1])
    vs = sent_from(1, vs)
    tot1, a1, z2, st = call(
        front_two,
        [
            shape_of((8, M0 + 128), F32),
            shape_of((SLOTS, PIX0, M0), BF16),
            shape_of((SLOTS, PIX0, M0), F32),
            shape_of((8, M0), F32),
        ],
        (SLOTS,),
        [full(count, 8, M0 + 128), per_slot(PIX0, M0), full(2, CN), ANYWHERE, ANYWHERE],
        [full(8, M0 + 128), per_slot(PIX0, M0), per_slot(PIX0, M0), full(8, M0)],
        [vmem(9 * M0, M0), vmem(PIX0 + 2 * WB, 3 * M0), DMA],
    )(meta, r1, z1, norms0, *w2)

    r2 = spread(st)
    (v2,) = unpack(meta, pin(params, st), [(9 * M1, M1)], ([], [(0, 524288)]))
    r2 = pin(r2, v2, vs[1])
    v2 = sent_from(1, v2)
    tot2, a2, st = call(
        front_three,
        [shape_of((8, M0), F32), shape_of((SLOTS, PIX0, M0), BF16), shape_of((8, C0), F32)],
        (SLOTS,),
        [
            full(count, 8, M0), full(8, M0 + 128), per_slot(PIX0, M0), full(2, CN), ANYWHERE,
            ANYWHERE,
        ],
        [full(8, M0), per_slot(PIX0, M0), full(8, C0)],
        [vmem(M0, C0), DMA],
    )(meta, r2, tot1, z2, norms0, *w3)
    (v3,) = unpack(meta, pin(params, st), [(M1, C1)], ([], [(0, 2883584)]))
    tot3 = pin(summed(st), v3, v2[1])
    v3 = sent_from(1, v3)

    clamp = lambda s: jnp.minimum(s, SLOTS - 1)
    tile = lambda s: jnp.maximum(s - SLOTS, 0)
    rows1 = SLOTS * PIX1
    src, p_even, z3_even, y1, ys, st, sts = call(
        join,
        [
            shape_of((rows1, C0), BF16),
            shape_of((rows1, C0), F32),
            shape_of((rows1, C0), F32),
            shape_of((rows1, M1), F32),
            shape_of((rows1, C1), F32),
            shape_of((8, M1), F32),
            shape_of((8, C1), F32),
        ],
        (SLOTS + 4,),
        [
            full(8, C0),
            full(8, M0 + 128),
            pl.BlockSpec((1, PIX0, M0), lambda s, meta: (clamp(s), 0, 0)),
            pl.BlockSpec((1, HB, WB, C0), lambda s, meta: (meta[clamp(s)], 0, 0, 0)),
            full(2, CN),
        ]
        + [ANYWHERE] * 6,
        [
            full(rows1, C0),
            full(rows1, C0),
            full(rows1, C0),
            full(rows1, M1),
            pl.BlockSpec((rows1, C1 // 4), lambda s, meta: (0, tile(s))),
            full(8, M1),
            pl.BlockSpec((8, C1 // 4), lambda s, meta: (0, tile(s))),
        ],
        [vmem(M0, C0), vmem(C0, M1), vmem(4, C0, C1 // 4), DMA((6,))],
    )(meta, tot3, tot1, a2, images, norms0, *w3, *v1, *vs)
    tots = summed(sts)
    r4 = spread(st)
    two, gather = plane_gather(src)
    r4 = pin(r4, two, v3[1])
    sources = gather()

    one = (1,)
    conv_scratch = [vmem(9 * M1, M1), DMA((3,))]
    last_scratch = [vmem(M1, C1), DMA]
    tot4, b1, y2, st = call(
        mid_one,
        [
            shape_of((8, M1), F32),
            shape_of((rows1, M1), BF16),
            shape_of((rows1, M1), F32),
            shape_of((8, M1), F32),
        ],
        one,
        [full(count, 8, M1), full(8, M0 + 128), full(rows1, M1), full(2, CN), ANYWHERE, ANYWHERE],
        [full(8, M1), full(rows1, M1), full(rows1, M1), full(8, M1)],
        conv_scratch,
    )(meta, r4, tot1, y1, norms1, *v2)
    r5 = pin(spread(st), sources)
    sources = (sources, swap_cores(sources))
    tot5, b2, y3, st = call(
        mid_two,
        [
            shape_of((8, M1), F32),
            shape_of((rows1, M1), BF16),
            shape_of((rows1, C1), F32),
            shape_of((8, C1), F32),
        ],
        one,
        [full(count, 8, M1), full(8, M0 + 128), full(rows1, M1), full(2, CN), ANYWHERE, ANYWHERE],
        [full(8, M1), full(rows1, M1), full(rows1, C1), full(8, C1)],
        last_scratch,
    )(meta, r5, tot1, y2, norms1, *v3)
    tot6 = summed(st)

    left = jnp.concatenate([b2, b1], axis=1)

    by_image = pl.BlockSpec((1, PIX1, C1), lambda s, meta: (meta[3 * SLOTS + s], 0, 0))
    y_out, grad_y, st, stg = call(
        turn,
        [
            shape_of((SLOTS, PIX1, C1), BF16),
            shape_of((SLOTS, PIX1, C1), F32),
            shape_of((8, C1), F32),
            shape_of((8, C1), F32),
        ],
        (SLOTS,),
        [
            full(8, C1),
            full(8, C1),
            full(8, M0 + 128),
            per_slot(PIX1, C1),
            per_slot(PIX1, C1),
            full(2, CN),
            per_image(HB // 2, WB // 2, C1),
        ],
        [by_image, per_slot(PIX1, C1), full(8, C1), full(8, C1)],
    )(
        meta, tot6, tots, tot1, y3.reshape(SLOTS, PIX1, C1), ys.reshape(SLOTS, PIX1, C1),
        norms1, cotangent,
    )
    tots7 = summed(jnp.concatenate([st, stg], axis=0))
    tots7 = pin(tots7, left, sources[1])
    tot7, totg = tots7[:8], tots7[8:]
    grad_y = grad_y.reshape(rows1, C1)
    y_there = lax.ppermute(y_out, "pipe", [(0, 1)])

    er, es, g2, st = call(
        back_one,
        [
            shape_of((8, rows1, 512), BF16),
            shape_of((rows1, C1), BF16),
            shape_of((rows1, M1), F32),
            shape_of((8, M1), F32),
        ],
        one,
        [
            full(8, C1), full(8, C1), full(8, C1), full(8, C1), full(8, M1), full(8, M0 + 128),
            full(rows1, C1), full(rows1, C1), full(rows1, C1), full(rows1, M1), full(2, CN),
            ANYWHERE, ANYWHERE,
        ],
        [full(8, rows1, 512), full(rows1, C1), full(rows1, M1), full(8, M1)],
        last_scratch,
    )(meta, tot7, totg, tot6, tots, tot5, tot1, y3, ys, grad_y, y2, norms1, *v3)

    r8 = spread(st)
    other = swap_cores(er[4:])
    two, gather = plane_gather(pin(left, st))
    rights = [jnp.stack([er[k], other[k]]) for k in range(4)]
    r8 = pin(r8, two, *rights)
    lefts = gather()
    plane_all = lambda width: full(4, rows1, width)
    pair_right = full(2, rows1, 512)

    tot8, e2r, g1, st = call(
        back_two,
        [
            shape_of((8, M1), F32),
            shape_of((4, rows1, 128), BF16),
            shape_of((rows1, M1), F32),
            shape_of((8, M1), F32),
        ],
        one,
        [
            full(count, 8, M1), full(8, M1), full(8, M1), full(8, M0 + 128), full(rows1, M1),
            full(rows1, M1), full(rows1, M1), full(2, CN), ANYWHERE, ANYWHERE,
        ],
        [full(8, M1), full(4, rows1, 128), full(rows1, M1), full(8, M1)],
        conv_scratch,
    )(meta, r8, tot5, tot4, tot1, y2, g2, y1, norms1, *v2)
    r9 = spread(st)
    rights = rights[:1] + [plane_turn(rights[k], k) for k in (1, 2, 3)]
    r9 = pin(r9, lefts)
    lefts = (lefts, swap_cores(lefts))
    tot9, e1r, g0, st = call(
        back_three,
        [
            shape_of((8, M1), F32),
            shape_of((4, rows1, 128), BF16),
            shape_of((rows1, C0), F32),
            shape_of((8, C0), F32),
        ],
        one,
        [
            full(count, 8, M1), full(8, M1), full(8, M0 + 128), full(rows1, M1), full(rows1, M1),
            full(rows1, C1), full(8, C0), full(rows1, C0), full(rows1, C0), full(2, CN),
            ANYWHERE, ANYWHERE, ANYWHERE, ANYWHERE,
        ],
        [full(8, M1), full(4, rows1, 128), full(rows1, C0), full(8, C0)],
        [vmem(C0, M1), vmem(C0, C1), DMA((2,))],
    )(
        meta, r9, tot4, tot1, y1, g1, es, tot3, p_even, z3_even, norms1, *v1, *vs,
    )
    tot10 = summed(st)
    g0 = g0.reshape(SLOTS, PIX1, C0)

    mids = jnp.concatenate([e2r, e1r], axis=2)
    tot10 = pin(tot10, lefts[1], *rights)

    d3, g2, st = call(
        last_one,
        [
            shape_of((SLOTS, PIX0, C0), BF16),
            shape_of((SLOTS, PIX0, M0), F32),
            shape_of((8, M0), F32),
        ],
        (SLOTS,),
        [
            full(8, C0), full(8, C0), full(8, M0), full(8, M0 + 128), per_slot(PIX0, M0),
            per_slot(PIX1, C0), per_slot(PIX0, M0), full(2, CN), ANYWHERE, ANYWHERE,
        ],
        [per_slot(PIX0, C0), per_slot(PIX0, M0), full(8, M0)],
        [vmem(M0, C0), DMA],
    )(meta, tot10, tot3, tot2, tot1, a2, g0, z2, norms0, *w3)
    r11 = spread(st)
    sides = call(
        sides_grad,
        shape_of((4 * SIDES, 128), BF16),
        one,
        [plane_all(C0)] * 2 + [plane_all(2 * M1)] * 2 + [pair_right] * 4,
        full(4 * SIDES, 128),
        limit=40,
    )(meta, *sources, *lefts, *[pin(right, st) for right in rights])
    mids = jnp.stack([mids[0]] + [plane_turn(pin(mids[k], st), k) for k in (1, 2, 3)])
    r11 = pin(r11, sides, mids)
    mids = (mids, swap_cores(mids))
    tot11, d2, g1, st = call(
        last_two,
        [
            shape_of((8, M0), F32),
            shape_of((SLOTS, PIX0, M0), BF16),
            shape_of((SLOTS, PIX0, M0), F32),
            shape_of((8, M0), F32),
        ],
        (SLOTS,),
        [
            full(count, 8, M0), full(8, M0), full(8, M0 + 128), per_slot(PIX0, M0),
            per_slot(PIX0, M0), per_slot(PIX0, M0), full(2, CN), ANYWHERE, ANYWHERE,
        ],
        [full(8, M0), per_slot(PIX0, M0), per_slot(PIX0, M0), full(8, M0)],
        [vmem(9 * M0, M0), DMA],
    )(meta, r11, tot2, tot1, z2, g2, z1, norms0, *w2)
    r12 = spread(st)
    sides = level_sum(pin(sides, st))
    middle = call(
        middle_grad,
        shape_of((4 * MIDDLE, 128), BF16),
        one,
        [plane_all(2 * M1)] * 2 + [plane_all(C0)] * 2 + [plane_all(256)] * 2,
        full(4 * MIDDLE, 128),
        limit=40,
    )(meta, *lefts, *sources, *[pin(mid, st) for mid in mids])
    r12 = pin(r12, sides, middle)
    sides = level_gather(sides)
    middle = level_sum(middle)
    front = call(
        front_grad_two,
        shape_of((2 * 9 * M0 + 8 * M0, 128), BF16),
        (SLOTS,),
        [per_slot(PIX0, M0), per_slot(PIX0, M0), per_slot(PIX0, M0), per_slot(PIX0, C0)],
        full(2 * 9 * M0 + 8 * M0, 128),
        [pltpu.VMEM((M0, 9 * M0), F32), pltpu.VMEM((M0, C0), F32)],
    )(meta, a1, d2, a2, d3)
    own_image = pl.BlockSpec((1, PIX0, C0), lambda s, meta: (meta[3 * SLOTS + s], 0, 0))
    tot12, d1, gx = call(
        last_three,
        [
            shape_of((8, M0), F32),
            shape_of((SLOTS, PIX0, M0), BF16),
            shape_of((SLOTS, PIX0, C0), BF16),
        ],
        (SLOTS,),
        [
            full(count, 8, M0), full(8, M0 + 128), per_slot(PIX0, M0), per_slot(PIX0, M0),
            per_slot(PIX1, C0), full(2, CN), ANYWHERE, ANYWHERE,
        ],
        [full(8, M0), per_slot(PIX0, M0), own_image],
        [vmem(C0, M0), DMA],
    )(meta, pin(r12, front), tot1, z1, g1, g0, norms0, *w1)
    first = call(
        front_grad_one,
        shape_of((2 * C0, 128), BF16),
        (SLOTS,),
        [image, per_slot(PIX0, M0)],
        full(2 * C0, 128),
        [pltpu.VMEM((C0, M0), F32)],
    )(meta, images, d1)

    front = jnp.concatenate([first, front], axis=0)
    half = part_at(front, core, 2).astype(F32) + swap_cores(part_at(front, 1 - core, 2)).astype(F32)
    half = half.astype(BF16)
    total = part_at(half, plane, 4).astype(F32)
    for k in (1, 2, 3):
        mask = jnp.where(first_core, k, SWAPPED[k])
        total = total + plane_turn(part_at(half, plane ^ mask, 4), k).astype(F32)
    front = level_gather(level_sum(total.astype(BF16)))

    sides = to_core(sides, 1)
    middle = to_core(level_gather(middle), 1)
    fronts = to_core(front, 0)

    whole = shape_of((GRAD_ROWS, 128), F32)
    block_at = lambda first: pl.BlockSpec((PACK_ROWS, 128), lambda s, meta: (s + first, 0))
    side_spec, mid_spec = full(8 * SIDES, 128), full(8 * MIDDLE, 128)
    grads = call(pack_sides, whole, (GRAD_ROWS // PACK_ROWS - 11,), [side_spec] * 4, block_at(11))(
        meta, *sides
    )
    grads = call(
        pack_rest, whole, (6,), [ANYWHERE] + [mid_spec] * 4, block_at(5), aliases={1: 0}
    )(meta, grads, *middle)
    front_rows = fronts[0].shape[0]
    grads = call(
        pack_front,
        whole,
        (5,),
        [ANYWHERE] + [mid_spec] * 4 + [full(front_rows, 128)] * 4,
        block_at(0),
        [pltpu.VMEM((4 * front_rows, 128), BF16)],
        aliases={1: 0},
    )(meta, grads, *middle, *fronts)
    weight_grads = grads.reshape(1, P_SIZE)

    def gain_shift(table):
        parts = table.reshape(SLOTS, 2, -1).sum(axis=0)
        return jnp.stack([parts[1], parts[0]])

    line0 = jnp.concatenate([gain_shift(tot12), gain_shift(tot11), gain_shift(tot10)], axis=1)
    line0 = jnp.pad(line0, ((0, 0), (0, CN - line0.shape[1])))
    line1 = jnp.concatenate(
        [gain_shift(tot9), gain_shift(tot8), gain_shift(tot7), gain_shift(totg)], axis=1
    )
    got = swap_cores(jnp.where(first_core, line1, line0))
    norm_grads = jnp.where(first_core, line0, line1) + got

    x_there = lax.ppermute(gx, "pipe", [(1, 0)])
    strip = lambda s, meta: (0, s, 0)
    strip_y = lambda s, meta: (0, jnp.minimum(s, 7), 0)
    boundary = call(
        rows_out,
        shape_of((2 * SLOTS, HB * WB * C0), BF16),
        (HB,),
        [pl.BlockSpec((SLOTS, WB, C0), strip)] * 2
        + [pl.BlockSpec((SLOTS, WB // 2, C1), strip_y)] * 2,
        pl.BlockSpec((2 * SLOTS, WB * C0), lambda s, meta: (0, s)),
    )(meta, gx, x_there, y_out, y_there)
    return boundary[None], weight_grads, norm_grads[None]


def solution(mesh):
    placed_as = (
        P("dp", None, None, None),
        P("dp", None),
        P("dp"),
        P("pipe", None),
        P("pipe", None, None),
        P("dp", None, None, None),
    )
    return jax.shard_map(
        on_device,
        mesh=mesh,
        in_specs=placed_as,
        out_specs=(P("pipe", "dp", None), P("pipe", None), P("pipe", None, None)),
        check_vma=False,
    )
```

```python
import functools

import jax
import jax.numpy as jnp
from jax import lax
from jax.experimental import pallas as pl
from jax.experimental.pallas import tpu as pltpu
from jax.sharding import PartitionSpec as P

C0 = 1024
M0 = 256
M1 = 512
C1 = 2048
HB = 16
WB = 16
P_SIZE = 6029312
CN = 5120
WORK = 4
PIX0 = 256
PIX1 = 64
ROWS0 = WORK * PIX0
ROWS1 = WORK * PIX1
EPSILON = 1e-05
MIB = 1 << 20

F32 = jnp.float32
BF16 = jnp.bfloat16
CORE, PLANE, LEVEL, HIGH, WIDE = 4, 5, 6, 7, 11


def shape_of(dims, kind):
    return jax.ShapeDtypeStruct(dims, kind)


def hbm_of(dims, kind):
    return pltpu.HBM(dims, kind)


def dot_nn(left, right):
    return lax.dot_general(left, right, (((1,), (0,)), ((), ())), preferred_element_type=F32)


def dot_nt(left, right):
    return lax.dot_general(left, right, (((1,), (1,)), ((), ())), preferred_element_type=F32)


def dot_tn(left, right):
    return lax.dot_general(left, right, (((0,), (0,)), ((), ())), preferred_element_type=F32)


def over_lanes(column, width):
    return jnp.concatenate([column] * (width // 128), axis=1)


def pixel_mask(high, wide, breadth, rows):
    index = lax.broadcasted_iota(jnp.int32, (rows, 128), 0)
    row = (index >> (breadth.bit_length() - 1)).astype(F32)
    col = (index & (breadth - 1)).astype(F32)
    return jnp.where((row < high) & (col < wide), 1.0, 0.0)


def mask0(hw_ref, image):
    return pixel_mask(hw_ref[image : image + 1, :], hw_ref[4 + image : 5 + image, :], WB, PIX0)


def mask1(hw_ref, image):
    high, wide = hw_ref[image : image + 1, :] * 0.5, hw_ref[4 + image : 5 + image, :] * 0.5
    return pixel_mask(high, wide, WB // 2, PIX1)


def mask1_all(hw_ref, width):
    return over_lanes(jnp.concatenate([mask1(hw_ref, k) for k in range(WORK)], axis=0), width)


def sigmoid(values):
    return 1.0 / (1.0 + jnp.exp(-values))


def silu(values):
    return values * sigmoid(values)


def slope(values):
    sig = sigmoid(values)
    return sig * (1.0 + values * (1.0 - sig))


def total_rows(values):
    return jnp.sum(values, axis=0, keepdims=True)


def put_sums(ref, first, second):
    ref[0:1, :] = total_rows(first)
    ref[1:2, :] = total_rows(second)


def plane_total(refs):
    return (refs[0][...] + refs[1][...]) + (refs[2][...] + refs[3][...])


def mean_scale(table, count):
    mean = table[0:1, :] / count
    spread = table[1:2, :] / count - mean * mean
    return mean, lax.rsqrt(spread + EPSILON)


def count_of(tot_ref):
    return tot_ref[0:1, M0 : M0 + 1]


def side_columns(values, breadth):
    rows, width = values.shape
    column = lax.broadcasted_iota(jnp.int32, (rows, width), 0) & (breadth - 1)
    left = jnp.where(column == 0, 0.0, pltpu.roll(values, 1, 0))
    right = jnp.where(column == breadth - 1, 0.0, pltpu.roll(values, rows - 1, 0))
    return left, right


def later_rows(values, step, height, breadth):
    if step == 0:
        return values
    rows, width = values.shape
    images = values.reshape(rows // (height * breadth), height * breadth, width)
    gap = jnp.zeros((images.shape[0], breadth, width), values.dtype)
    if step > 0:
        moved = jnp.concatenate([gap, images[:, :-breadth]], axis=1)
    else:
        moved = jnp.concatenate([images[:, breadth:], gap], axis=1)
    return moved.reshape(rows, width)


def even_picker():
    row = lax.broadcasted_iota(jnp.int32, (PIX1, PIX0), 0)
    col = lax.broadcasted_iota(jnp.int32, (PIX1, PIX0), 1)
    return jnp.where(col == 32 * (row >> 3) + 2 * (row & 7), 1.0, 0.0).astype(BF16)


def even_placer():
    row = lax.broadcasted_iota(jnp.int32, (PIX0, PIX1), 0)
    col = lax.broadcasted_iota(jnp.int32, (PIX0, PIX1), 1)
    return jnp.where(row == 32 * (col >> 3) + 2 * (col & 7), 1.0, 0.0).astype(BF16)


def placed(values):
    placer = even_placer()
    high = values.astype(BF16)
    rest = (values - high.astype(F32)).astype(BF16)
    return dot_nn(placer, high) + dot_nn(placer, rest)


def call(body, outs, grid, in_specs, out_specs, scratch=(), limit=28, aliases={}, micros=5):
    size = int(micros * 3.6e6)
    return pl.pallas_call(
        body,
        out_shape=outs,
        grid_spec=pltpu.PrefetchScalarGridSpec(
            num_scalar_prefetch=1,
            grid=grid,
            in_specs=in_specs,
            out_specs=out_specs,
            scratch_shapes=list(scratch),
        ),
        input_output_aliases=aliases,
        cost_estimate=pl.CostEstimate(flops=0, bytes_accessed=size, transcendentals=0),
        compiler_params=pltpu.CompilerParams(vmem_limit_bytes=limit * MIB),
    )


ANYWHERE = pl.BlockSpec(memory_space=pltpu.HBM)
DMA = pltpu.SemaphoreType.DMA


def in_hbm(array):
    return pltpu.with_memory_space_constraint(array, pltpu.HBM)


def vmem(*dims):
    return pltpu.VMEM(dims, BF16)


def full(*dims):
    return pl.BlockSpec(dims, lambda *_: (0,) * len(dims), pipeline_mode=pl.Buffered(1))


def per_image(*dims):
    return pl.BlockSpec((1,) + dims, lambda s, meta: (s,) + (0,) * len(dims))


def own_image(*dims):
    return pl.BlockSpec((1,) + dims, lambda s, meta: (meta[s],) + (0,) * len(dims))


def single(body, meta, ins, outs, scratch=(), limit=28, micros=5):
    in_specs = [ANYWHERE if whole else full(*array.shape) for array, whole in ins]
    shapes = [(hbm_of if far else shape_of)(dims, kind) for dims, kind, far in outs]
    out_specs = [full(*dims) for dims, _, _ in outs]
    made = call(body, shapes, (1,), in_specs, out_specs, scratch, limit, micros=micros)
    return made(meta, *[array for array, _ in ins])


def near(*arrays):
    return [(array, False) for array in arrays]


def far(*arrays):
    return [(in_hbm(array), False) for array in arrays]


def weight(pair):
    return [(array, True) for array in pair]


def fetch(meta, owner, own_ref, got_ref, here, sem):
    mine = meta[CORE] == owner

    @pl.when(mine)
    def _():
        pltpu.make_async_copy(own_ref, here, sem).start()

    @pl.when(jnp.logical_not(mine))
    def _():
        pltpu.make_async_copy(got_ref, here, sem).start()


def await_copy(ref, here, sem):
    pltpu.make_async_copy(ref, here, sem).wait()


def enter(meta, x_ref, cot_ref, wa_ref, wb_ref, *refs):
    pays, evens, cots, w_ref, sem = refs[0:4], refs[4:8], refs[8:12], refs[12], refs[13]
    step = pl.program_id(0)

    @pl.when(step == 0)
    def _():
        fetch(meta, 0, wa_ref, wb_ref, w_ref, sem)
        await_copy(wa_ref, w_ref, sem)

    x = x_ref[0].reshape(PIX0, C0)
    z = dot_nn(x, w_ref[...])
    even = dot_nn(even_picker(), x).astype(BF16)
    row = lax.broadcasted_iota(jnp.int32, (16, M0), 0)
    high, wide = meta[HIGH + step].astype(F32), meta[WIDE + step].astype(F32)
    sizes = jnp.where(row == 0, high, jnp.where(row == 1, wide, 0.0))
    middle = total_rows(z) * (1.0 / PIX0)
    rest = middle
    for k in range(3):
        part = rest.astype(BF16).astype(F32)
        sizes = jnp.where(row == 2 + k, part, sizes)
        rest = rest - part
    z = z - middle
    for k in range(WORK):

        @pl.when(step == k)
        def _(k=k):
            pays[k][0:PIX0, :] = z.astype(BF16)
            pays[k][PIX0 : PIX0 + 16, :] = sizes.astype(BF16)
            evens[k][...] = even
            cots[k][...] = cot_ref[0].reshape(PIX1, C1)


def arrive(meta, *refs):
    pays, z_ref, z_far_ref, hw_ref, st_ref = refs[0:4], *refs[4:]
    first, second, count = 0.0, 0.0, 0.0
    for k in range(WORK):
        rows = pays[k][PIX0 : PIX0 + 16, :].astype(F32)
        sizes = rows[:, 0:128]
        hw_ref[k : k + 1, :] = sizes[0:1, :]
        hw_ref[4 + k : 5 + k, :] = sizes[1:2, :]
        count = count + sizes[0:1, :] * sizes[1:2, :]
        z = pays[k][0:PIX0, :].astype(F32) + ((rows[2:3, :] + rows[3:4, :]) + rows[4:5, :])
        z_ref[k] = z
        z_far_ref[k] = z
        zm = z * over_lanes(pixel_mask(sizes[0:1, :], sizes[1:2, :], WB, PIX0), M0)
        first = first + total_rows(zm)
        second = second + total_rows(zm * z)
    st_ref[0:1, :] = jnp.concatenate([first, count], axis=1)
    st_ref[1:2, :] = jnp.concatenate([second, count], axis=1)


def front_two(meta, *refs):
    stats, (z_ref, hw_ref, n_ref, wa_ref, wb_ref) = refs[0:4], refs[4:9]
    tot_ref, a1_ref, z2_ref, z2b_ref, st_ref, w_ref, act_ref, sem = refs[9:]
    fetch(meta, 0, wa_ref, wb_ref, w_ref, sem)
    table = plane_total(stats)
    tot_ref[...] = table
    mean, scale = mean_scale(table[:, :M0], count_of(tot_ref))
    act_ref[:, 0:WB, :] = jnp.zeros((2, WB, 3 * M0), BF16)
    act_ref[:, WB + PIX0 : 2 * WB + PIX0, :] = jnp.zeros((2, WB, 3 * M0), BF16)
    first, second = 0.0, 0.0
    for k in range(WORK):
        mask = over_lanes(mask0(hw_ref, k), M0)
        pre = (z_ref[k] - mean) * scale * n_ref[0:1, :M0] + n_ref[1:2, :M0]
        act = silu(pre) * mask
        left, right = side_columns(act, WB)
        wide = jnp.concatenate([left, act, right], axis=1).astype(BF16)
        act_ref[k % 2, WB : WB + PIX0, :] = wide
        a1_ref[k] = wide[:, M0 : 2 * M0]
        if k == 0:
            await_copy(wa_ref, w_ref, sem)
        z2 = dot_nn(act_ref[k % 2, 0:PIX0, :], w_ref[0 : 3 * M0, :])
        z2 = z2 + dot_nn(wide, w_ref[3 * M0 : 6 * M0, :])
        z2 = z2 + dot_nn(act_ref[k % 2, 2 * WB : 2 * WB + PIX0, :], w_ref[6 * M0 :, :])
        z2_ref[k] = z2
        z2b_ref[k] = z2
        zm = z2 * mask
        first = first + total_rows(zm)
        second = second + total_rows(zm * z2)
    st_ref[0:1, :] = first
    st_ref[1:2, :] = second


def front_three(meta, *refs):
    stats, (tot_ref, z2_ref, hw_ref, n_ref, wa_ref, wb_ref) = refs[0:4], refs[4:10]
    tot2_ref, a2_ref, a2b_ref, st_ref, w_ref, sem = refs[10:]
    fetch(meta, 0, wa_ref, wb_ref, w_ref, sem)
    table = plane_total(stats)
    tot2_ref[...] = table
    mean, scale = mean_scale(table, count_of(tot_ref))
    first, second = 0.0, 0.0
    for k in range(WORK):
        pre = (z2_ref[k] - mean) * scale * n_ref[0:1, M0 : 2 * M0] + n_ref[1:2, M0 : 2 * M0]
        act = (silu(pre) * over_lanes(mask0(hw_ref, k), M0)).astype(BF16)
        a2_ref[k] = act
        a2b_ref[k] = act
        if k == 0:
            await_copy(wa_ref, w_ref, sem)
        z3 = dot_nn(act, w_ref[...])
        first = first + total_rows(z3)
        second = second + total_rows(z3 * z3)
    st_ref[0:1, :] = first
    st_ref[1:2, :] = second


def even_picker():
    row = lax.broadcasted_iota(jnp.int32, (PIX1, PIX0), 0)
    col = lax.broadcasted_iota(jnp.int32, (PIX1, PIX0), 1)
    return jnp.where(col == 32 * (row >> 3) + 2 * (row & 7), 1.0, 0.0).astype(BF16)


def even_placer():
    row = lax.broadcasted_iota(jnp.int32, (PIX0, PIX1), 0)
    col = lax.broadcasted_iota(jnp.int32, (PIX0, PIX1), 1)
    return jnp.where(row == 32 * (col >> 3) + 2 * (col & 7), 1.0, 0.0).astype(BF16)


def placed(values):
    placer = even_placer()
    high = values.astype(BF16)
    rest = (values - high.astype(F32)).astype(BF16)
    return dot_nn(placer, high) + dot_nn(placer, rest)


SIDE_PART = C1 // 4


def join(meta, *refs):
    stats, (tot_ref, a2_ref), evens, (hw_ref, n_ref) = refs[0:4], refs[4:6], refs[6:10], refs[10:12]
    w3a_ref, w3b_ref, w1a_ref, w1b_ref, wsa_ref, wsb_ref = refs[12:18]
    tot3_ref, s_ref, p_ref, z3_ref, z1_ref, z1b_ref, zs_ref, st_ref, sts_ref = refs[18:27]
    w3_ref, w1_ref, ws_ref, sems = refs[27:]
    step = pl.program_id(0)

    @pl.when(step == 0)
    def _():
        fetch(meta, 0, w3a_ref, w3b_ref, w3_ref, sems.at[0])
        fetch(meta, 1, w1a_ref, w1b_ref, w1_ref, sems.at[1])
        for k in range(4):
            cols = pl.ds(k * SIDE_PART, SIDE_PART)
            fetch(meta, 1, wsa_ref.at[:, cols], wsb_ref.at[:, cols], ws_ref.at[k], sems.at[2 + k])
        table = plane_total(stats)
        tot3_ref[...] = table
        mean, scale = mean_scale(table, count_of(tot_ref))
        picker = even_picker()
        await_copy(w3a_ref, w3_ref, sems.at[0])
        for k in range(WORK):
            act = dot_nn(picker, a2_ref[k]).astype(BF16)
            z3 = dot_nn(act, w3_ref[...])
            here = slice(k * PIX1, (k + 1) * PIX1)
            z3_ref[here, :] = z3
            pre = (z3 - mean) * scale * n_ref[0:1, 2 * M0 : 2 * M0 + C0]
            pre = pre + n_ref[1:2, 2 * M0 : 2 * M0 + C0]
            pre = pre + evens[k][...].astype(F32)
            p_ref[here, :] = pre
            s_ref[here, :] = (silu(pre) * over_lanes(mask1(hw_ref, k), C0)).astype(BF16)
        await_copy(w1a_ref, w1_ref, sems.at[1])
        z1 = dot_nn(s_ref[...], w1_ref[...])
        z1_ref[...] = z1
        z1b_ref[...] = z1
        put_sums(st_ref, z1, z1 * z1)

    for k in range(4):

        @pl.when(step == k)
        def _(k=k):
            await_copy(wsa_ref.at[:, pl.ds(k * SIDE_PART, SIDE_PART)], ws_ref.at[k], sems.at[2 + k])
            zs = dot_nn(s_ref[...], ws_ref[k])
            zs_ref[...] = zs
            put_sums(sts_ref, zs, zs * zs)


def fetch_conv(meta, wa_ref, wb_ref, w_ref, sems):
    for k in range(3):
        rows = pl.ds(k * 3 * M1, 3 * M1)
        fetch(meta, 1, wa_ref.at[rows], wb_ref.at[rows], w_ref.at[rows], sems.at[k])


def await_conv(wa_ref, w_ref, sems, k):
    rows = pl.ds(k * 3 * M1, 3 * M1)
    await_copy(wa_ref.at[rows], w_ref.at[rows], sems.at[k])


def mid_one(meta, *refs):
    stats, (tot_ref, z1_ref, hw_ref, n_ref, wa_ref, wb_ref) = refs[0:4], refs[4:10]
    tot4_ref, a1_ref, z2_ref, z2b_ref, st_ref, w_ref, sems = refs[10:]
    fetch_conv(meta, wa_ref, wb_ref, w_ref, sems)
    table = plane_total(stats)
    tot4_ref[...] = table
    mean, scale = mean_scale(table, count_of(tot_ref) * 0.25)
    mask = mask1_all(hw_ref, M1)
    act = silu((z1_ref[...] - mean) * scale * n_ref[0:1, :M1] + n_ref[1:2, :M1]) * mask
    left, right = side_columns(act, WB // 2)
    wide = jnp.concatenate([left, act, right], axis=1).astype(BF16)
    a1_ref[...] = wide[:, M1 : 2 * M1]
    await_conv(wa_ref, w_ref, sems, 0)
    z2 = later_rows(dot_nn(wide, w_ref[0 : 3 * M1, :]), 1, HB // 2, WB // 2)
    await_conv(wa_ref, w_ref, sems, 1)
    z2 = z2 + dot_nn(wide, w_ref[3 * M1 : 6 * M1, :])
    await_conv(wa_ref, w_ref, sems, 2)
    z2 = z2 + later_rows(dot_nn(wide, w_ref[6 * M1 :, :]), -1, HB // 2, WB // 2)
    z2_ref[...] = z2
    z2b_ref[...] = z2
    zm = z2 * mask
    put_sums(st_ref, zm, zm * z2)


def mid_two(meta, *refs):
    stats, (tot_ref, z2_ref, hw_ref, n_ref, wa_ref, wb_ref) = refs[0:4], refs[4:10]
    tot5_ref, a2_ref, z3_ref, st_ref, w_ref, sem = refs[10:]
    fetch(meta, 1, wa_ref, wb_ref, w_ref, sem)
    table = plane_total(stats)
    tot5_ref[...] = table
    mean, scale = mean_scale(table, count_of(tot_ref) * 0.25)
    pre = (z2_ref[...] - mean) * scale * n_ref[0:1, M1 : 2 * M1] + n_ref[1:2, M1 : 2 * M1]
    act = (silu(pre) * mask1_all(hw_ref, M1)).astype(BF16)
    a2_ref[...] = act
    await_copy(wa_ref, w_ref, sem)
    z3 = dot_nn(act, w_ref[...])
    z3_ref[...] = z3
    put_sums(st_ref, z3, z3 * z3)


AT3, ATS = 2 * M1, 2 * M1 + C1


def turn(meta, *refs):
    stats, sides, (tot_ref, z3_ref, zs_ref, hw_ref, n_ref) = refs[0:4], refs[4:8], refs[8:13]
    cots, (tot6_ref, tots_ref), ys, (g_ref, st_ref) = refs[13:17], refs[17:19], refs[19:23], refs[23:]
    step = pl.program_id(0)

    @pl.when(step == 0)
    def _():
        tot6_ref[...] = plane_total(stats)
        tots_ref[...] = plane_total(sides)
        st_ref[...] = jnp.zeros_like(st_ref)

    count = count_of(tot_ref) * 0.25
    mean, scale = mean_scale(tot6_ref[...], count)
    mean_s, scale_s = mean_scale(tots_ref[...], count)
    normed = (z3_ref[0] - mean) * scale
    normed_s = (zs_ref[0] - mean_s) * scale_s
    pre = normed * n_ref[0:1, AT3:ATS] + n_ref[1:2, AT3:ATS]
    pre = pre + (normed_s * n_ref[0:1, ATS : ATS + C1] + n_ref[1:2, ATS : ATS + C1])
    sig = sigmoid(pre)
    value = pre * sig
    change = sig * (1.0 + pre * (1.0 - sig))
    for k in range(WORK):

        @pl.when(step == k)
        def _(k=k):
            mask = over_lanes(mask1(hw_ref, k), C1)
            ys[k][...] = (value * mask).astype(BF16)
            g_ref[0] = cots[k][...].astype(F32) * change * mask

    grad = g_ref[0]
    st_ref[0:1, :] += total_rows(grad)
    st_ref[1:2, :] += total_rows(grad * normed)
    st_ref[2:3, :] += total_rows(grad * normed_s)


def norm_back(grad, normed, scale, gain, first, second, mask):
    return (mask * (scale * gain) * (grad - first - normed * second)).astype(BF16)


def back_one(meta, *refs):
    stats, (tot6_ref, tots_ref, tot5_ref, tot_ref) = refs[0:4], refs[4:8]
    z3_ref, zs_ref, g_ref, z2_ref, hw_ref, n_ref, wa_ref, wb_ref = refs[8:16]
    tot7_ref, er_ref, es_ref, g2_ref, st_ref, w_ref, sem = refs[16:]
    fetch(meta, 1, wa_ref, wb_ref, w_ref, sem)
    table = plane_total(stats)
    tot7_ref[...] = table
    count = count_of(tot_ref) * 0.25
    table = table / count
    mask = mask1_all(hw_ref, C1)
    grad = g_ref[...]
    mean, scale = mean_scale(tot6_ref[...], count)
    normed = (z3_ref[...] - mean) * scale
    d3 = norm_back(grad, normed, scale, n_ref[0:1, AT3:ATS], table[0:1], table[1:2], mask)
    mean2, scale2 = mean_scale(tot5_ref[...], count)
    normed2 = (z2_ref[...] - mean2) * scale2
    pre2 = normed2 * n_ref[0:1, M1 : 2 * M1] + n_ref[1:2, M1 : 2 * M1]
    await_copy(wa_ref, w_ref, sem)
    g2 = dot_nt(d3, w_ref[...]) * mask[:, :M1] * slope(pre2)
    g2_ref[...] = g2
    put_sums(st_ref, g2, g2 * normed2)
    mean_s, scale_s = mean_scale(tots_ref[...], count)
    normed_s = (zs_ref[...] - mean_s) * scale_s
    ds = norm_back(grad, normed_s, scale_s, n_ref[0:1, ATS : ATS + C1], table[0:1], table[2:3], mask)
    es_ref[...] = ds
    half = C1 // 2
    for p in range(2):
        cols = slice(p * half, (p + 1) * half)
        er_ref[meta[CORE] ^ p] = jnp.concatenate([d3[:, cols], ds[:, cols]], axis=1)


def back_two(meta, *refs):
    stats, (tot5_ref, tot4_ref, tot_ref, z2_ref, g2_ref, z1_ref) = refs[0:4], refs[4:10]
    hw_ref, n_ref, wa_ref, wb_ref, tot8_ref, er_ref, g1_ref, st_ref, w_ref, sems = refs[10:]
    fetch_conv(meta, wa_ref, wb_ref, w_ref, sems)
    table = plane_total(stats)
    tot8_ref[...] = table
    count = count_of(tot_ref) * 0.25
    table = table / count
    mask = mask1_all(hw_ref, M1)
    mean, scale = mean_scale(tot5_ref[...], count)
    normed = (z2_ref[...] - mean) * scale
    d2 = norm_back(
        g2_ref[...], normed, scale, n_ref[0:1, M1 : 2 * M1], table[0:1], table[1:2], mask
    )
    for p in range(2):
        er_ref[meta[CORE] ^ p] = d2[:, p * (M1 // 2) : (p + 1) * (M1 // 2)]
    mean1, scale1 = mean_scale(tot4_ref[...], count)
    normed1 = (z1_ref[...] - mean1) * scale1
    pre1 = normed1 * n_ref[0:1, :M1] + n_ref[1:2, :M1]
    await_conv(wa_ref, w_ref, sems, 0)
    wide = later_rows(dot_nt(d2, w_ref[0 : 3 * M1, :]), -1, HB // 2, WB // 2)
    await_conv(wa_ref, w_ref, sems, 1)
    wide = wide + dot_nt(d2, w_ref[3 * M1 : 6 * M1, :])
    await_conv(wa_ref, w_ref, sems, 2)
    wide = wide + later_rows(dot_nt(d2, w_ref[6 * M1 :, :]), 1, HB // 2, WB // 2)
    left, _ = side_columns(wide[:, 2 * M1 :], WB // 2)
    _, right = side_columns(wide[:, :M1], WB // 2)
    g1 = (wide[:, M1 : 2 * M1] + left + right) * mask * slope(pre1)
    g1_ref[...] = g1
    put_sums(st_ref, g1, g1 * normed1)


def back_three(meta, *refs):
    stats, (tot4_ref, tot_ref, z1_ref, g1_ref, es_ref, tot3_ref, p_ref, z3_ref) = refs[0:4], refs[4:12]
    hw_ref, n_ref, w1a_ref, w1b_ref, wsa_ref, wsb_ref = refs[12:18]
    tot9_ref, er_ref, g0_ref, st_ref, w1_ref, ws_ref, sems = refs[18:]
    fetch(meta, 1, w1a_ref, w1b_ref, w1_ref, sems.at[0])
    fetch(meta, 1, wsa_ref, wsb_ref, ws_ref, sems.at[1])
    table = plane_total(stats)
    tot9_ref[...] = table
    count = count_of(tot_ref) * 0.25
    table = table / count
    mask = mask1_all(hw_ref, C0)
    mean, scale = mean_scale(tot4_ref[...], count)
    normed = (z1_ref[...] - mean) * scale
    d1 = norm_back(
        g1_ref[...], normed, scale, n_ref[0:1, :M1], table[0:1], table[1:2], mask[:, :M1]
    )
    for p in range(2):
        er_ref[meta[CORE] ^ p] = d1[:, p * (M1 // 2) : (p + 1) * (M1 // 2)]
    await_copy(w1a_ref, w1_ref, sems.at[0])
    grad = dot_nt(d1, w1_ref[...])
    await_copy(wsa_ref, ws_ref, sems.at[1])
    grad = grad + dot_nt(es_ref[...], ws_ref[...])
    grad = grad.astype(BF16).astype(F32)
    g0 = grad * slope(p_ref[...]) * mask
    g0_ref[...] = g0
    mean3, scale3 = mean_scale(tot3_ref[...], count * 4.0)
    put_sums(st_ref, g0, g0 * ((z3_ref[...] - mean3) * scale3))


def last_one(meta, *refs):
    stats, (tot3_ref, tot2_ref, tot_ref, a2_ref, g0_ref, z2_ref, hw_ref, n_ref) = refs[0:4], refs[4:12]
    wa_ref, wb_ref, tot10_ref, d3_ref, g2_ref, st_ref, w_ref, sem = refs[12:]
    step = pl.program_id(0)

    @pl.when(step == 0)
    def _():
        fetch(meta, 0, wa_ref, wb_ref, w_ref, sem)
        tot10_ref[...] = plane_total(stats)
        st_ref[...] = jnp.zeros_like(st_ref)
        await_copy(wa_ref, w_ref, sem)

    count = count_of(tot_ref)
    table = tot10_ref[...] / count
    mean, scale = mean_scale(tot3_ref[...], count)
    mean2, scale2 = mean_scale(tot2_ref[...], count)
    high = pl.ds(step, 1)
    wide = pl.ds(4 + step, 1)
    mask = over_lanes(pixel_mask(hw_ref[high, :], hw_ref[wide, :], WB, PIX0), C0)
    normed = (dot_nn(a2_ref[0], w_ref[...]) - mean) * scale
    grad = placed(g0_ref[0])
    gain = n_ref[0:1, 2 * M0 : 2 * M0 + C0]
    d3 = norm_back(grad, normed, scale, gain, table[0:1], table[1:2], mask)
    d3_ref[0] = d3
    normed2 = (z2_ref[0] - mean2) * scale2
    pre2 = normed2 * n_ref[0:1, M0 : 2 * M0] + n_ref[1:2, M0 : 2 * M0]
    g2 = dot_nt(d3, w_ref[...]) * mask[:, :M0] * slope(pre2)
    g2_ref[0] = g2
    st_ref[0:1, :] += total_rows(g2)
    st_ref[1:2, :] += total_rows(g2 * normed2)


def last_two(meta, *refs):
    stats, (tot2_ref, tot_ref, z2_ref, g2_ref, z1_ref, hw_ref, n_ref) = refs[0:4], refs[4:11]
    wa_ref, wb_ref, tot11_ref, d2_ref, g1_ref, st_ref, w_ref, sem = refs[11:]
    step = pl.program_id(0)

    @pl.when(step == 0)
    def _():
        fetch(meta, 0, wa_ref, wb_ref, w_ref, sem)
        tot11_ref[...] = plane_total(stats)
        st_ref[...] = jnp.zeros_like(st_ref)

    count = count_of(tot_ref)
    table = tot11_ref[...] / count
    mask = pixel_mask(hw_ref[pl.ds(step, 1), :], hw_ref[pl.ds(4 + step, 1), :], WB, PIX0)
    mask = over_lanes(mask, M0)
    mean2, scale2 = mean_scale(tot2_ref[...], count)
    normed2 = (z2_ref[0] - mean2) * scale2
    gain = n_ref[0:1, M0 : 2 * M0]
    d2 = norm_back(g2_ref[0], normed2, scale2, gain, table[0:1], table[1:2], mask)
    d2_ref[0] = d2
    mean1, scale1 = mean_scale(tot_ref[:, :M0], count)
    normed1 = (z1_ref[0] - mean1) * scale1
    pre1 = normed1 * n_ref[0:1, :M0] + n_ref[1:2, :M0]

    @pl.when(step == 0)
    def _():
        await_copy(wa_ref, w_ref, sem)

    wide = dot_nt(d2, w_ref[3 * M0 : 6 * M0, :])
    wide = wide + later_rows(dot_nt(d2, w_ref[0 : 3 * M0, :]), -1, HB, WB)
    wide = wide + later_rows(dot_nt(d2, w_ref[6 * M0 :, :]), 1, HB, WB)
    left, _ = side_columns(wide[:, 2 * M0 :], WB)
    _, right = side_columns(wide[:, :M0], WB)
    g1 = (wide[:, M0 : 2 * M0] + left + right) * mask * slope(pre1)
    g1_ref[0] = g1
    st_ref[0:1, :] += total_rows(g1)
    st_ref[1:2, :] += total_rows(g1 * normed1)


def last_three(meta, *refs):
    stats, (tot_ref, z1_ref, g1_ref, g0_ref, hw_ref, n_ref) = refs[0:4], refs[4:10]
    tot12_ref, backs = refs[10], refs[11:15]
    table = plane_total(stats)
    tot12_ref[...] = table
    count = count_of(tot_ref)
    table = table / count
    mean, scale = mean_scale(tot_ref[:, :M0], count)
    for k in range(WORK):
        mask = over_lanes(mask0(hw_ref, k), M0)
        normed = (z1_ref[k] - mean) * scale
        backs[k][0:PIX0, :] = norm_back(
            g1_ref[k], normed, scale, n_ref[0:1, :M0], table[0:1], table[1:2], mask
        )
        grad = g0_ref[k * PIX1 : (k + 1) * PIX1, :].astype(BF16)
        for part in range(C0 // M0):
            here = slice(PIX0 + part * PIX1, PIX0 + (part + 1) * PIX1)
            backs[k][here, :] = grad[:, part * M0 : (part + 1) * M0]


def leave(meta, x_ref, wa_ref, wb_ref, *refs):
    backs, gx_ref, out_ref, w_ref, acc_ref, sem = refs[0:4], *refs[4:]
    step = pl.program_id(0)

    @pl.when(step == 0)
    def _():
        fetch(meta, 0, wa_ref, wb_ref, w_ref, sem)
        acc_ref[...] = jnp.zeros_like(acc_ref)
        await_copy(wa_ref, w_ref, sem)

    for k in range(WORK):

        @pl.when(step == k)
        def _(k=k):
            d1 = backs[k][0:PIX0, :]
            grad = jnp.concatenate(
                [backs[k][PIX0 + n * PIX1 : PIX0 + (n + 1) * PIX1, :] for n in range(C0 // M0)], axis=1
            )
            gx_ref[0] = (dot_nt(d1, w_ref[...]) + dot_nn(even_placer(), grad)).astype(BF16)
            acc_ref[...] += dot_tn(x_ref[0].reshape(PIX0, C0), d1)

    @pl.when(step == WORK - 1)
    def _():
        put_tiles(out_ref, 0, acc_ref[...])


def put_tiles(ref, start, values):
    rows, width = values.shape
    for k in range(width // 128):
        here = slice(start + k * rows, start + (k + 1) * rows)
        ref[here, :] = values[:, 128 * k : 128 * (k + 1)].astype(BF16)


def nine_shifts(delta, height, breadth):
    pieces = []
    left, right = side_columns(delta, breadth)
    for a in range(3):
        for moved in (right, delta, left):
            pieces.append(later_rows(moved, a - 1, height, breadth).astype(BF16))
    return jnp.concatenate(pieces, axis=1)


SIDES, MIDDLE = 768, 704
SWAPPED = (0, 2, 1, 3)


def place_of(core, chip):
    return jnp.where(core == 0, 2 * (chip & 1) + (chip >> 1), chip)


def put_shards(ref, shard, start, core, level_first, values):
    rows = values.shape[0] // 16
    values = values.astype(BF16)
    for chip in range(4):
        place = place_of(core, chip)
        for z in range(4):
            at = (SWAPPED[z] * 4 + place if level_first else place * 4 + z) * shard + start
            part = values[(4 * chip + z) * rows : (4 * chip + z + 1) * rows]
            for k in range(values.shape[1] // 128):
                here = pl.ds(pl.multiple_of(at + k * rows, 16), rows)
                ref[here, :] = part[:, 128 * k : 128 * (k + 1)]


def sides_grad(meta, sa_ref, sb_ref, la_ref, lb_ref, ea_ref, eb_ref, out_ref):
    half = C1 // 2
    side = dot_tn(sa_ref[...], ea_ref[0][:, half:]) + dot_tn(sb_ref[...], eb_ref[0][:, half:])
    put_shards(out_ref, SIDES, 0, meta[CORE], True, side)
    last = dot_tn(la_ref[...], ea_ref[0][:, :half]) + dot_tn(lb_ref[...], eb_ref[0][:, :half])
    put_shards(out_ref, SIDES, C0 // 2, meta[CORE], True, last)


def middle_grad(meta, sa_ref, sb_ref, la_ref, lb_ref, ma_ref, mb_ref, fa_ref, fb_ref, out_ref):
    conv = dot_tn(la_ref[...], nine_shifts(ma_ref[0].astype(F32), HB // 2, WB // 2))
    conv = conv + dot_tn(lb_ref[...], nine_shifts(mb_ref[0].astype(F32), HB // 2, WB // 2))
    put_shards(out_ref, MIDDLE, 0, meta[CORE], False, conv)
    first = dot_tn(sa_ref[...], fa_ref[0]) + dot_tn(sb_ref[...], fb_ref[0])
    put_shards(out_ref, MIDDLE, 9 * M1 // 8, meta[CORE], False, first)


def front_grad_two(meta, a1_ref, d2_ref, a2_ref, d3_ref, out_ref, acc2_ref, acc3_ref):
    slot = pl.program_id(0)
    conv = dot_tn(a1_ref[0], nine_shifts(d2_ref[0].astype(F32), HB, WB))
    last = dot_tn(a2_ref[0], d3_ref[0])

    @pl.when(slot == 0)
    def _():
        acc2_ref[...] = conv
        acc3_ref[...] = last

    @pl.when(slot > 0)
    def _():
        acc2_ref[...] += conv
        acc3_ref[...] += last

    @pl.when(slot == WORK - 1)
    def _():
        for tap in range(9):
            for tile in range(2):
                start = tile * 9 * M0 + tap * M0
                lanes = tap * M0 + tile * 128
                out_ref[start : start + M0, :] = acc2_ref[:, lanes : lanes + 128].astype(BF16)
        put_tiles(out_ref, 2 * 9 * M0, acc3_ref[...])


def unpack_kernel(shapes, jobs, chunk, meta, raw_ref, *refs):
    outs, refs = refs[: len(shapes)], refs[len(shapes) :]
    raws, flat_ref, sem_in, sem_out = refs[0:3], refs[3], refs[4], refs[5]
    stages = dict(zip(sorted({cols for _, cols in shapes}), refs[6:]))

    def run(listed):
        loads, stores, sizes = [], [], []
        for out, offset in listed:
            rows, cols = shapes[out]
            for row in range(0, rows, chunk // cols):
                some = min(chunk // cols, rows - row)
                k = len(loads)
                source = raw_ref.at[:, pl.ds(offset + row * cols, some * cols)]
                here = raws[k % 3].at[:, pl.ds(0, some * cols)]
                loads.append(pltpu.make_async_copy(source, here, sem_in.at[k % 3]))
                stage = stages[cols].at[k % 2, pl.ds(0, some)]
                there = outs[out].at[pl.ds(row, some)]
                stores.append(pltpu.make_async_copy(stage, there, sem_out.at[k % 2]))
                sizes.append((some, cols))
        for load in loads[:2]:
            load.start()
        for k, (rows, cols) in enumerate(sizes):
            if k + 2 < len(sizes):
                loads[k + 2].start()
            loads[k].wait()
            flat_ref[:, : rows * cols] = raws[k % 3][:, : rows * cols].astype(F32)
            lines = flat_ref.reshape(chunk // 128, 128)
            if k >= 2:
                stores[k - 2].wait()
            for tile in range(cols // 128):
                values = lines[pl.ds(tile, rows, stride=cols // 128), :].astype(BF16)
                stages[cols][k % 2, 0:rows, tile * 128 : (tile + 1) * 128] = values
            stores[k].start()
        for store in stores[-2:]:
            store.wait()

    for core in range(2):
        if jobs[core]:
            pl.when(meta[CORE] == core)(functools.partial(run, jobs[core]))


def unpack(meta, packed, shapes, jobs, micros, chunk=262144):
    widths = sorted({cols for _, cols in shapes})
    return call(
        functools.partial(unpack_kernel, shapes, jobs, chunk),
        [pltpu.HBM(dims, BF16) for dims in shapes],
        (1,),
        [ANYWHERE],
        [ANYWHERE] * len(shapes),
        [pltpu.VMEM((1, chunk), BF16)] * 3
        + [pltpu.VMEM((1, chunk), F32), DMA((3,)), DMA((2,))]
        + [pltpu.VMEM((2, chunk // cols, cols), BF16) for cols in widths],
        micros=micros,
    )(meta, in_hbm(packed))


PACK_ROWS = 2048
GRAD_ROWS = P_SIZE // 128
ARRIVED = ((1, (0, 1)), (0, (0, 2)), (0, (1, 3)), (1, (2, 3)))


def quarters(bufs, target):
    found = []
    for buf, (p, masks) in zip(bufs, ARRIVED):
        if target == 0:
            p, masks = 1 - p, tuple(SWAPPED[m] for m in masks)
        for k, mask in enumerate(masks):
            found.append((p, mask, buf, k * (buf.shape[0] // 2)))
    return found


def pack_sides(meta, *refs):
    bufs, out_ref = refs[:4], refs[4]
    step = pl.program_id(0)
    level, plane = meta[LEVEL], meta[PLANE]

    @pl.when(meta[CORE] == 0)
    def _():
        out_ref[...] = jnp.zeros_like(out_ref)

    for p, mask, buf, start in quarters(bufs, 1):
        here = meta[CORE] == 1

        @pl.when(here & (step < 4) & (step == (plane ^ mask)))
        def _(p=p, buf=buf, start=start):
            for z in range(4):
                for k in range(8):
                    row = start + (level ^ z) * SIDES + C0 // 2 + 32 * k
                    rows = buf[pl.ds(pl.multiple_of(row, 32), 32), :].astype(F32)
                    out_ref[pl.ds(512 * z + 8 * p + k, 32, stride=16), :] = rows

        @pl.when(here & (step >= 4) & (((step - 4) >> 1) == (plane ^ mask)))
        def _(p=p, buf=buf, start=start):
            for j in range(2):
                z = 2 * (step & 1) + j
                for k in range(8):
                    row = start + (level ^ z) * SIDES + 64 * k
                    rows = buf[pl.ds(pl.multiple_of(row, 64), 64), :].astype(F32)
                    out_ref[pl.ds(1024 * j + 8 * p + k, 64, stride=16), :] = rows


def pack_middle(first_step, meta, *refs):
    bufs, out_ref = refs[1:5], refs[-1]
    step = pl.program_id(0) + first_step
    plane, level = meta[PLANE], meta[LEVEL]

    for p, mask, buf, start in quarters(bufs, 1):
        chip = plane ^ mask

        @pl.when((meta[CORE] == 1) & (step < 2) & (step == (chip >> 1)))
        def _(p=p, buf=buf, start=start, chip=chip):
            for z in range(4):
                for k in range(2):
                    row = start + (level ^ z) * MIDDLE + 9 * M1 // 8 + 64 * k
                    rows = buf[pl.ds(pl.multiple_of(row, 64), 64), :].astype(F32)
                    at = 256 * (4 * (chip & 1) + z) + 2 * p + k
                    out_ref[pl.ds(at, 64, stride=4), :] = rows

        @pl.when((meta[CORE] == 1) & (step > 1))
        def _(p=p, buf=buf, start=start, chip=chip):
            for z in range(4):
                for k in range(2):
                    row = start + (level ^ z) * MIDDLE + 64 * (step - 2) + 32 * k
                    rows = buf[pl.ds(pl.multiple_of(row, 32), 32), :].astype(F32)
                    at = 128 * (4 * chip + z) + 2 * p + k
                    out_ref[pl.ds(at, 32, stride=4), :] = rows


def pack_rest(meta, *refs):
    out_ref = refs[-1]

    @pl.when(meta[CORE] == 0)
    def _():
        out_ref[...] = jnp.zeros_like(out_ref)

    pack_middle(5, meta, *refs)


def pack_front(meta, *refs):
    fronts, out_ref, whole_ref = refs[5:9], refs[9], refs[10]
    step = pl.program_id(0)
    core, plane, level = meta[CORE], meta[PLANE], meta[LEVEL]
    part = fronts[0].shape[0] // 8

    @pl.when((core == 0) & (step == 0))
    def _():
        for p, mask, buf, start in quarters(fronts, 0):
            for z in range(4):
                there = (16 * p + 4 * place_of(p, plane ^ mask) + (level ^ z)) * part
                rows = buf[start + z * part : start + (z + 1) * part, :]
                whole_ref[pl.ds(pl.multiple_of(there, 16), part), :] = rows

    at2, at3 = 2 * C0, 2 * C0 + 2 * 9 * M0

    def piece(start, rows):
        return whole_ref[start : start + rows, :].astype(F32)

    @pl.when((core == 0) & (step == 0))
    def _():
        for tile in range(2):
            out_ref[pl.ds(tile, C0, stride=2), :] = piece(tile * C0, C0)

    for k in range(2):

        @pl.when((core == 0) & (step == 1 + k))
        def _(k=k):
            for tile in range(2):
                out_ref[pl.ds(tile, C0, stride=2), :] = piece(at2 + tile * 9 * M0 + k * C0, C0)

    @pl.when((core == 0) & (step == 3))
    def _():
        for tile in range(2):
            out_ref[pl.ds(tile, 256, stride=2), :] = piece(at2 + tile * 9 * M0 + 2 * C0, 256)
        for tile in range(8):
            out_ref[pl.ds(512 + tile, 192, stride=8), :] = piece(at3 + tile * 256, 192)

    @pl.when((core == 0) & (step == 4))
    def _():
        out_ref[...] = jnp.zeros_like(out_ref)
        for tile in range(8):
            out_ref[pl.ds(tile, 64, stride=8), :] = piece(at3 + tile * 256 + 192, 64)

    pack_middle(0, meta, *refs[:5], out_ref)


def rows_out(meta, x_ref, xg_ref, y_ref, yg_ref, out_ref):
    step = pl.program_id(0)
    row = lax.broadcasted_iota(jnp.int32, (128, 128), 0)
    col = lax.broadcasted_iota(jnp.int32, (128, 128), 1)

    def put(first, second, source):
        values = jnp.concatenate([first.reshape(-1, C0), second.reshape(-1, C0)], axis=0)
        mover = jnp.where(col == source, 1.0, 0.0).astype(BF16)
        moved = dot_nn(mover, values).astype(BF16)
        for k in range(16):
            out_ref[:, k * C0 : (k + 1) * C0] = moved[8 * k : 8 * (k + 1), :]

    image, stand = row & 7, row * 0
    for k in range(WORK):
        stand = jnp.where(image == meta[k], k, jnp.where(image == (meta[k] ^ 1), WORK + k, stand))

    @pl.when(meta[CORE] == 0)
    def _():
        put(x_ref[...], xg_ref[...], 16 * stand + (row >> 3))

    @pl.when((meta[CORE] == 1) & (step < HB // 2))
    def _():
        def split(ref):
            pieces = []
            for k in range(WORK):
                wide = ref[k].astype(F32)
                pieces += [wide[:, :C0], wide[:, C0:]]
            return jnp.concatenate(pieces, axis=0).astype(BF16)

        put(split(y_ref), split(yg_ref), 16 * stand + 8 * ((row >> 3) & 1) + (row >> 4))

    @pl.when((meta[CORE] == 1) & (step >= HB // 2))
    def _():
        out_ref[...] = jnp.zeros_like(out_ref)


def pin(value, *others):
    return lax.optimization_barrier((value,) + others)[0]


def swap_cores(value):
    return lax.ppermute(value, "pipe", [(0, 1), (1, 0)])


def xor_permute(value, mask):
    count = lax.axis_size("dp")
    return lax.ppermute(value, "dp", [(i, i ^ mask) for i in range(count)])


def upper_bits():
    return [bit for bit in (16, 32, 64, 128, 256, 512) if bit < lax.axis_size("dp")]


def plane_turn(value, turn_no):
    count = lax.axis_size("dp")
    pairs = []
    for p in range(2):
        mask = SWAPPED[turn_no] if p else turn_no
        pairs += [(p * count + i, p * count + (i ^ mask)) for i in range(count)]
    return lax.ppermute(value, ("pipe", "dp"), pairs)


def shared(value):
    for bit in upper_bits():
        value = value + xor_permute(value, bit)
    return [value] + [plane_turn(value, k) for k in (1, 2, 3)]


def over_levels(values):
    return [values[0]] + [xor_permute(values[k], 4 * k) for k in (1, 2, 3)]


def part_at(value, index, parts):
    rows = value.shape[0] // parts
    return lax.dynamic_slice_in_dim(value, index * rows, rows, 0)


def added(*parts):
    total = parts[0].astype(F32)
    for part in parts[1:]:
        total = total + part.astype(F32)
    return total.astype(BF16)


def level_sum(value, level):
    gots = [xor_permute(part_at(value, level ^ k, 4), 4 * k) for k in (1, 2, 3)]
    value = added(part_at(value, level, 4), *gots)
    for bit in upper_bits():
        value = added(value, xor_permute(value, bit))
    return value


def plane_sum(value, place):
    for turn_no, bit in ((1, place >> 1), (2, place & 1)):
        got = plane_turn(part_at(value, 1 - bit, 2), turn_no)
        value = added(part_at(value, bit, 2), got)
    return value


def level_gather(value):
    return jnp.concatenate([value] + [xor_permute(value, 4 * k) for k in (1, 2, 3)], axis=0)


def to_core(both, target):
    count = lax.axis_size("dp")
    other = 1 - target
    close, away = (1, 2) if target == 1 else (2, 1)
    arrived = [both]
    for p, mask in ((other, 0), (other, close), (target, away)):
        pairs = [(p * count + i, target * count + (i ^ mask)) for i in range(count)]
        arrived.append(lax.ppermute(both, ("pipe", "dp"), pairs))
    return arrived


def on_device(images, extents, views, params, norms, cotangent):
    images, cotangent, params = in_hbm(images), in_hbm(cotangent), in_hbm(params)
    core = lax.axis_index("pipe")
    first_core = core == 0
    plane = lax.axis_index("dp") % 4
    level = (lax.axis_index("dp") // 4) % 4
    place = place_of(core, plane)

    pair = 2 * (level ^ jnp.arange(WORK, dtype=jnp.int32))
    hot = (pair[:, None] == jnp.arange(2 * WORK, dtype=jnp.int32)[None, :]).astype(jnp.int32)
    view = jnp.sum(hot * views[None, :], axis=1)
    order = pair + (view != core).astype(jnp.int32)
    hot = (order[:, None] == jnp.arange(2 * WORK, dtype=jnp.int32)[None, :]).astype(jnp.int32)
    sizes = jnp.sum(hot[:, :, None] * extents[None], axis=1)
    spot = jnp.stack([core, plane, level]).astype(jnp.int32)
    meta = jnp.concatenate([order, spot, sizes[:, 0], sizes[:, 1]]).astype(jnp.int32)

    def sent_from(owner, matrix):
        return in_hbm(matrix), in_hbm(lax.ppermute(matrix, "pipe", [(owner, 1 - owner)]))

    (w1,) = unpack(meta, params, [(C0, M0)], ([(0, 0)], []), 3, 65536)
    w1 = sent_from(0, w1)
    norms_there = swap_cores(norms[0])
    n0 = jnp.where(first_core, norms[0], norms_there)
    n1 = jnp.where(first_core, norms_there, norms[0])

    some = lambda dims, kind: [shape_of(dims, kind)] * WORK
    made = call(
        enter,
        some((PIX0 + 16, M0), BF16) + some((PIX1, C0), BF16) + some((PIX1, C1), BF16),
        (WORK,),
        [own_image(HB, WB, C0), own_image(HB // 2, WB // 2, C1), ANYWHERE, ANYWHERE],
        [full(PIX0 + 16, M0)] * 4 + [full(PIX1, C0)] * 4 + [full(PIX1, C1)] * 4,
        [vmem(C0, M0), DMA],
    )(meta, images, cotangent, *w1)
    pays, evens, cots = over_levels(made[0:4]), made[4:8], made[8:12]
    w2, w3, v1, vs = unpack(
        meta,
        pin(params, made[0]),
        [(9 * M0, M0), (M0, C0), (C0, M1), (C0, C1)],
        ([(0, 262144), (1, 851968)], [(2, 0), (3, 3932160)]),
        8,
    )
    pays[0] = pin(pays[0], w2, norms_there)
    w2, w3, v1, vs = sent_from(0, w2), sent_from(0, w3), sent_from(1, v1), sent_from(1, vs)
    evens = over_levels(evens)
    cots = over_levels(cots)
    z1, z1b, hw, st = single(
        arrive,
        meta,
        near(*pays),
        [
            ((WORK, PIX0, M0), F32, False),
            ((WORK, PIX0, M0), F32, True),
            ((8, 128), F32, False),
            ((2, M0 + 128), F32, False),
        ],
    )

    s1 = shared(st)
    (v2,) = unpack(meta, pin(params, st), [(9 * M1, M1)], ([], [(0, 524288)]), 7)
    s1[0] = pin(s1[0], v2, evens[1], w3[1], v1[1])
    v2 = sent_from(1, v2)
    tot1, a1, z2, z2b, st = single(
        front_two,
        meta,
        near(*s1, z1, hw, n0) + weight(w2),
        [
            ((2, M0 + 128), F32, False),
            ((WORK, PIX0, M0), BF16, True),
            ((WORK, PIX0, M0), F32, False),
            ((WORK, PIX0, M0), F32, True),
            ((2, M0), F32, False),
        ],
        [vmem(9 * M0, M0), vmem(2, PIX0 + 2 * WB, 3 * M0), DMA],
    )
    s2 = shared(st)
    (v3,) = unpack(meta, pin(params, st), [(M1, C1)], ([], [(0, 2883584)]), 4)
    s2[0] = pin(s2[0], v3, vs[1], evens[2])
    v3 = sent_from(1, v3)
    tot2, a2, a2b, st = single(
        front_three,
        meta,
        near(*s2, tot1, z2, hw, n0) + weight(w3),
        [
            ((2, M0), F32, False),
            ((WORK, PIX0, M0), BF16, False),
            ((WORK, PIX0, M0), BF16, True),
            ((2, C0), F32, False),
        ],
        [vmem(M0, C0), DMA],
    )
    s3 = shared(st)
    s3[0] = pin(s3[0], v2[1], evens[3])

    tile = lambda s, meta: (0, s)
    tot3, src, p_even, z3_even, y1, y1b, ys, st, sts = call(
        join,
        [
            shape_of((2, C0), F32),
            hbm_of((ROWS1, C0), BF16),
            hbm_of((ROWS1, C0), F32),
            hbm_of((ROWS1, C0), F32),
            shape_of((ROWS1, M1), F32),
            hbm_of((ROWS1, M1), F32),
            hbm_of((ROWS1, C1), F32),
            shape_of((2, M1), F32),
            shape_of((2, C1), F32),
        ],
        (4,),
        [full(2, C0)] * 4
        + [full(2, M0 + 128), full(WORK, PIX0, M0)]
        + [full(PIX1, C0)] * 4
        + [full(8, 128), full(2, CN)]
        + [ANYWHERE] * 6,
        [
            full(2, C0),
            full(ROWS1, C0),
            full(ROWS1, C0),
            full(ROWS1, C0),
            full(ROWS1, M1),
            full(ROWS1, M1),
            pl.BlockSpec((ROWS1, SIDE_PART), tile),
            full(2, M1),
            pl.BlockSpec((2, SIDE_PART), tile),
        ],
        [vmem(M0, C0), vmem(C0, M1), vmem(4, C0, SIDE_PART), DMA((6,))],
    )(meta, *s3, tot1, a2, *evens, hw, n0, *w3, *v1, *vs)

    s4 = shared(st)
    s4[0] = pin(s4[0], v3[1], cots[1])
    conv_scratch = [vmem(9 * M1, M1), DMA((3,))]
    last_scratch = [vmem(M1, C1), DMA]
    row = ((2, M1), F32, False)
    tot4, b1, y2, y2b, st = single(
        mid_one,
        meta,
        near(*s4, tot1, y1, hw, n1) + weight(v2),
        [row, ((ROWS1, M1), BF16, True), ((ROWS1, M1), F32, False), ((ROWS1, M1), F32, True), row],
        conv_scratch,
    )
    s5 = shared(st)
    s5[0] = pin(s5[0], cots[2])
    t5 = shared(sts)
    tot5, b2, y3, st = single(
        mid_two,
        meta,
        near(*s5, tot1, y2, hw, n1) + weight(v3),
        [row, ((ROWS1, M1), BF16, True), ((ROWS1, C1), F32, False), ((2, C1), F32, False)],
        last_scratch,
    )
    s6 = shared(st)
    s6[0] = pin(s6[0], cots[3], *t5)
    made = call(
        turn,
        [shape_of((2, C1), F32)] * 2
        + some((PIX1, C1), BF16)
        + [shape_of((WORK, PIX1, C1), F32), shape_of((3, C1), F32)],
        (WORK,),
        [full(2, C1)] * 8
        + [full(2, M0 + 128), per_image(PIX1, C1), per_image(PIX1, C1), full(8, 128), full(2, CN)]
        + [full(PIX1, C1)] * 4,
        [full(2, C1)] * 2 + [full(PIX1, C1)] * 4 + [per_image(PIX1, C1), full(3, C1)],
    )(
        meta, *s6, *t5, tot1, y3.reshape(WORK, PIX1, C1), in_hbm(ys.reshape(WORK, PIX1, C1)), hw,
        n1, *cots,
    )
    tot6, tots, y_out, grad_y, st = made[0], made[1], made[2:6], made[6], made[7]
    grad_y = grad_y.reshape(ROWS1, C1)

    s7 = shared(st)
    others = [swap_cores(array) for array in (src, b1, b2)]
    s7[0] = pin(s7[0], *others)
    tot7, er, es, g2, st = single(
        back_one,
        meta,
        near(*s7, tot6, tots, tot5, tot1, y3) + far(ys) + near(grad_y) + far(y2b)
        + near(hw, n1) + weight(v3),
        [
            ((3, C1), F32, False),
            ((2, ROWS1, C1), BF16, False),
            ((ROWS1, C1), BF16, False),
            ((ROWS1, M1), F32, False),
            row,
        ],
        last_scratch,
        limit=36,
    )
    s8 = shared(st)
    other = swap_cores(er[1:])
    sides = single(
        sides_grad,
        meta,
        far(src, others[0], b2, others[2]) + near(er, other),
        [((16 * SIDES, 128), BF16, False)],
        limit=40,
    )[0]
    s8[0] = pin(s8[0], sides)
    low, high = level & 1, level >> 1
    sides = added(part_at(sides, low, 2), xor_permute(part_at(sides, 1 - low, 2), 4))
    tot8, e2r, g1, st = single(
        back_two,
        meta,
        near(*s8, tot5, tot4, tot1) + far(y2b) + near(g2) + far(y1b) + near(hw, n1) + weight(v2),
        [row, ((2, ROWS1, M1 // 2), BF16, False), ((ROWS1, M1), F32, False), row],
        conv_scratch,
    )
    s9 = shared(st)
    made = single(
        back_three,
        meta,
        near(*s9, tot4, tot1) + far(y1b) + near(g1, es, tot3) + far(p_even, z3_even)
        + near(hw, n1) + weight(v1) + weight(vs),
        [row, ((2, ROWS1, M1 // 2), BF16, False), ((ROWS1, C0), F32, False), ((2, C0), F32, False)],
        [vmem(C0, M1), vmem(C0, C1), DMA((2,))],
    )
    tot9, e1r, g0, st = made

    s10 = shared(st)
    other2, other1 = swap_cores(e2r[1:]), swap_cores(e1r[1:])
    s10[0] = pin(s10[0], other2, other1, sides)
    half_there = xor_permute(part_at(sides, 1 - high, 2), 8)
    tot10, d3, g2, st = call(
        last_one,
        [
            shape_of((2, C0), F32),
            hbm_of((WORK, PIX0, C0), BF16),
            shape_of((WORK, PIX0, M0), F32),
            shape_of((2, M0), F32),
        ],
        (WORK,),
        [full(2, C0)] * 5
        + [
            full(2, M0), full(2, M0 + 128), per_image(PIX0, M0), per_image(PIX1, C0),
            per_image(PIX0, M0), full(8, 128), full(2, CN), ANYWHERE, ANYWHERE,
        ],
        [full(2, C0), per_image(PIX0, C0), per_image(PIX0, M0), full(2, M0)],
        [vmem(M0, C0), DMA],
    )(
        meta, *s10, tot3, tot2, tot1, in_hbm(a2b), g0.reshape(WORK, PIX1, C0), in_hbm(z2b), hw, n0,
        *w3,
    )
    s11 = shared(st)
    middle = single(
        middle_grad,
        meta,
        far(src, others[0], b1, others[1]) + [(pin(e2r, st), False)] + near(other2, e1r, other1),
        [((16 * MIDDLE, 128), BF16, False)],
        limit=40,
    )[0]
    s11[0] = pin(s11[0], middle)
    tot11, d2, g1, st = call(
        last_two,
        [
            shape_of((2, M0), F32),
            hbm_of((WORK, PIX0, M0), BF16),
            shape_of((WORK, PIX0, M0), F32),
            shape_of((2, M0), F32),
        ],
        (WORK,),
        [full(2, M0)] * 5
        + [full(2, M0 + 128)]
        + [per_image(PIX0, M0)] * 3
        + [full(8, 128), full(2, CN), ANYWHERE, ANYWHERE],
        [full(2, M0), per_image(PIX0, M0), per_image(PIX0, M0), full(2, M0)],
        [vmem(9 * M0, M0), DMA],
    )(meta, *s11, tot2, tot1, in_hbm(z2b), g2, in_hbm(z1b), hw, n0, *w2)
    s12 = shared(st)
    front = call(
        front_grad_two,
        shape_of((2 * 9 * M0 + 8 * M0, 128), BF16),
        (WORK,),
        [per_image(PIX0, M0)] * 3 + [per_image(PIX0, C0)],
        full(2 * 9 * M0 + 8 * M0, 128),
        [pltpu.VMEM((M0, 9 * M0), F32), pltpu.VMEM((M0, C0), F32)],
    )(meta, in_hbm(a1), in_hbm(d2), in_hbm(a2b), in_hbm(d3))
    s12[0] = pin(s12[0], front)
    made = single(
        last_three,
        meta,
        near(*s12, tot1) + far(z1b) + near(g1) + far(g0) + near(hw, n0),
        [((2, M0), F32, False)] + [((PIX0 + C0 // M0 * PIX1, M0), BF16, False)] * 4,
    )
    tot12, backs = made[0], over_levels(made[1:])
    middle = pin(middle, s12[1])
    sides = added(pin(part_at(sides, high, 2), tot12), half_there)
    middle = added(part_at(middle, place >> 1, 2), plane_turn(part_at(middle, 1 - (place >> 1), 2), 1))
    for bit in upper_bits():
        sides = added(sides, xor_permute(sides, bit))
    backs[0] = pin(backs[0], middle, sides)
    gx, first = call(
        leave,
        [shape_of((WORK, PIX0, C0), BF16), shape_of((2 * C0, 128), BF16)],
        (WORK,),
        [own_image(HB, WB, C0), ANYWHERE, ANYWHERE] + [full(PIX0 + C0 // M0 * PIX1, M0)] * 4,
        [per_image(PIX0, C0), full(2 * C0, 128)],
        [vmem(C0, M0), pltpu.VMEM((C0, M0), F32), DMA],
    )(meta, images, *w1, *backs)

    middle = added(part_at(middle, place & 1, 2), plane_turn(part_at(middle, 1 - (place & 1), 2), 2))
    sides = plane_sum(sides, place)
    sides = level_gather(pin(sides, first))
    front = jnp.concatenate([first, front], axis=0)
    front = added(part_at(front, core, 2), swap_cores(part_at(front, 1 - core, 2)))
    front = plane_sum(pin(front, middle), place)
    middle = level_sum(pin(middle, front), level)
    front = level_gather(level_sum(front, level))
    sides_two = jnp.concatenate([sides, plane_turn(sides, 2)], axis=0)
    middle = level_gather(pin(middle, sides_two))
    sides = to_core(sides_two, 1)
    front = jnp.concatenate([front, plane_turn(front, 2)], axis=0)
    fronts = to_core(front, 0)

    whole = shape_of((GRAD_ROWS, 128), F32)
    block_at = lambda at: pl.BlockSpec((PACK_ROWS, 128), lambda s, meta: (s + at, 0))
    side_spec, mid_spec = full(8 * SIDES, 128), full(8 * MIDDLE, 128)
    steps = GRAD_ROWS // PACK_ROWS - 11
    grads = call(pack_sides, whole, (steps,), [side_spec] * 4, block_at(11), micros=8)(meta, *sides)
    middle = pin(middle, grads)
    x_there = lax.ppermute(gx, "pipe", [(1, 0)])
    y_back = jnp.stack(over_levels([pin(array, middle) for array in y_out]))
    y_there = lax.ppermute(y_back, "pipe", [(0, 1)])
    strip = lambda s, meta: (0, s, 0)
    strip_y = lambda s, meta: (0, jnp.minimum(s, 7), 0)
    boundary = call(
        rows_out,
        shape_of((2 * WORK, HB * WB * C0), BF16),
        (HB,),
        [pl.BlockSpec((WORK, WB, C0), strip)] * 2
        + [pl.BlockSpec((WORK, WB // 2, C1), strip_y)] * 2,
        pl.BlockSpec((2 * WORK, WB * C0), lambda s, meta: (0, s)),
        micros=9,
    )(meta, gx, x_there, y_back, y_there)
    middle = to_core(jnp.concatenate([middle, plane_turn(middle, 2)], axis=0), 1)
    grads = call(
        pack_rest, whole, (6,), [ANYWHERE] + [mid_spec] * 4, block_at(5), aliases={1: 0}
    )(meta, grads, *middle)
    front_rows = fronts[0].shape[0]
    grads = call(
        pack_front,
        whole,
        (5,),
        [ANYWHERE] + [mid_spec] * 4 + [full(front_rows, 128)] * 4,
        block_at(0),
        [pltpu.VMEM((4 * front_rows, 128), BF16)],
        aliases={1: 0},
    )(meta, grads, *middle, *fronts)
    weight_grads = grads.reshape(1, P_SIZE)

    def gain_shift(table, second=1):
        return jnp.concatenate([table[second : second + 1], table[0:1]], axis=0)

    line0 = jnp.concatenate(
        [gain_shift(tot12), gain_shift(tot11), gain_shift(tot10), jnp.zeros((2, CN - 1536), F32)],
        axis=1,
    )
    line1 = jnp.concatenate(
        [gain_shift(tot9), gain_shift(tot8), gain_shift(tot7), gain_shift(tot7, 2)], axis=1
    )
    line = jnp.where(first_core, line0, line1) + swap_cores(jnp.where(first_core, line1, line0))
    for bit in (4, 8):
        line = line + xor_permute(line, bit)

    return boundary[None], weight_grads, line[None]


def solution(mesh):
    placed_as = (
        P("dp", None, None, None),
        P("dp", None),
        P("dp"),
        P("pipe", None),
        P("pipe", None, None),
        P("dp", None, None, None),
    )
    return jax.shard_map(
        on_device,
        mesh=mesh,
        in_specs=placed_as,
        out_specs=(P("pipe", "dp", None), P("pipe", None), P("pipe", None, None)),
        check_vma=False,
    )
```

```python
import functools

import jax
import jax.numpy as jnp
from jax import lax
from jax.experimental import pallas as pl
from jax.experimental.pallas import tpu as pltpu
from jax.sharding import PartitionSpec as P

C0 = 1024
M0 = 256
M1 = 512
C1 = 2048
HB = 16
WB = 16
P_SIZE = 6029312
CN = 5120
WORK = 4
PIX0 = 256
PIX1 = 64
ROWS0 = WORK * PIX0
ROWS1 = WORK * PIX1
EPSILON = 1e-05
MIB = 1 << 20

F32 = jnp.float32
BF16 = jnp.bfloat16
CORE, PLANE, LEVEL, HIGH, WIDE = 4, 5, 6, 7, 11


def shape_of(dims, kind):
    return jax.ShapeDtypeStruct(dims, kind)


def hbm_of(dims, kind):
    return pltpu.HBM(dims, kind)


def dot_nn(left, right):
    return lax.dot_general(left, right, (((1,), (0,)), ((), ())), preferred_element_type=F32)


def dot_nt(left, right):
    return lax.dot_general(left, right, (((1,), (1,)), ((), ())), preferred_element_type=F32)


def dot_tn(left, right):
    return lax.dot_general(left, right, (((0,), (0,)), ((), ())), preferred_element_type=F32)


def over_lanes(column, width):
    return jnp.concatenate([column] * (width // 128), axis=1)


def pixel_mask(high, wide, breadth, rows):
    index = lax.broadcasted_iota(jnp.int32, (rows, 128), 0)
    row = (index >> (breadth.bit_length() - 1)).astype(F32)
    col = (index & (breadth - 1)).astype(F32)
    return jnp.where((row < high) & (col < wide), 1.0, 0.0)


def mask0(hw_ref, image):
    return pixel_mask(hw_ref[image : image + 1, :], hw_ref[4 + image : 5 + image, :], WB, PIX0)


def mask1(hw_ref, image):
    high, wide = hw_ref[image : image + 1, :] * 0.5, hw_ref[4 + image : 5 + image, :] * 0.5
    return pixel_mask(high, wide, WB // 2, PIX1)


def mask1_all(hw_ref, width):
    return over_lanes(jnp.concatenate([mask1(hw_ref, k) for k in range(WORK)], axis=0), width)


def sigmoid(values):
    return 1.0 / (1.0 + jnp.exp(-values))


def silu(values):
    return values * sigmoid(values)


def slope(values):
    sig = sigmoid(values)
    return sig * (1.0 + values * (1.0 - sig))


def total_rows(values):
    return jnp.sum(values, axis=0, keepdims=True)


def put_sums(ref, first, second):
    ref[0:1, :] = total_rows(first)
    ref[1:2, :] = total_rows(second)


def plane_total(refs):
    return (refs[0][...] + refs[1][...]) + (refs[2][...] + refs[3][...])


def mean_scale(table, count):
    mean = table[0:1, :] / count
    spread = table[1:2, :] / count - mean * mean
    return mean, lax.rsqrt(spread + EPSILON)


def count_of(tot_ref):
    return tot_ref[0:1, M0 : M0 + 1]


def side_columns(values, breadth):
    rows, width = values.shape
    column = lax.broadcasted_iota(jnp.int32, (rows, width), 0) & (breadth - 1)
    left = jnp.where(column == 0, 0.0, pltpu.roll(values, 1, 0))
    right = jnp.where(column == breadth - 1, 0.0, pltpu.roll(values, rows - 1, 0))
    return left, right


def later_rows(values, step, height, breadth):
    if step == 0:
        return values
    rows, width = values.shape
    images = values.reshape(rows // (height * breadth), height * breadth, width)
    gap = jnp.zeros((images.shape[0], breadth, width), values.dtype)
    if step > 0:
        moved = jnp.concatenate([gap, images[:, :-breadth]], axis=1)
    else:
        moved = jnp.concatenate([images[:, breadth:], gap], axis=1)
    return moved.reshape(rows, width)


def even_picker():
    row = lax.broadcasted_iota(jnp.int32, (PIX1, PIX0), 0)
    col = lax.broadcasted_iota(jnp.int32, (PIX1, PIX0), 1)
    return jnp.where(col == 32 * (row >> 3) + 2 * (row & 7), 1.0, 0.0).astype(BF16)


def even_placer():
    row = lax.broadcasted_iota(jnp.int32, (PIX0, PIX1), 0)
    col = lax.broadcasted_iota(jnp.int32, (PIX0, PIX1), 1)
    return jnp.where(row == 32 * (col >> 3) + 2 * (col & 7), 1.0, 0.0).astype(BF16)


def placed(values):
    placer = even_placer()
    high = values.astype(BF16)
    rest = (values - high.astype(F32)).astype(BF16)
    return dot_nn(placer, high) + dot_nn(placer, rest)


def call(body, outs, grid, in_specs, out_specs, scratch=(), limit=28, aliases={}, micros=5):
    size = int(micros * 3.6e6)
    return pl.pallas_call(
        body,
        out_shape=outs,
        grid_spec=pltpu.PrefetchScalarGridSpec(
            num_scalar_prefetch=1,
            grid=grid,
            in_specs=in_specs,
            out_specs=out_specs,
            scratch_shapes=list(scratch),
        ),
        input_output_aliases=aliases,
        cost_estimate=pl.CostEstimate(flops=0, bytes_accessed=size, transcendentals=0),
        compiler_params=pltpu.CompilerParams(vmem_limit_bytes=limit * MIB),
    )


ANYWHERE = pl.BlockSpec(memory_space=pltpu.HBM)
DMA = pltpu.SemaphoreType.DMA


def in_hbm(array):
    return pltpu.with_memory_space_constraint(array, pltpu.HBM)


def vmem(*dims):
    return pltpu.VMEM(dims, BF16)


def full(*dims):
    return pl.BlockSpec(dims, lambda *_: (0,) * len(dims), pipeline_mode=pl.Buffered(1))


def per_image(*dims):
    return pl.BlockSpec((1,) + dims, lambda s, meta: (s,) + (0,) * len(dims))


def own_image(*dims):
    return pl.BlockSpec((1,) + dims, lambda s, meta: (meta[s],) + (0,) * len(dims))


def single(body, meta, ins, outs, scratch=(), limit=28, micros=5):
    in_specs = [ANYWHERE if whole else full(*array.shape) for array, whole in ins]
    shapes = [(hbm_of if far else shape_of)(dims, kind) for dims, kind, far in outs]
    out_specs = [full(*dims) for dims, _, _ in outs]
    made = call(body, shapes, (1,), in_specs, out_specs, scratch, limit, micros=micros)
    return made(meta, *[array for array, _ in ins])


def near(*arrays):
    return [(array, False) for array in arrays]


def far(*arrays):
    return [(in_hbm(array), False) for array in arrays]


def weight(pair):
    return [(array, True) for array in pair]


W1 = (0, 0, C0, M0)
W2 = (0, 0, 9 * M0, M0)
W3 = (0, 2304, M0, C0)
V1 = (1, 0, C0, M1)
VS = (1, 2048, C0, C1)
V2 = (1, 0, 9 * M1, M1)
V3 = (1, 9216, M1, C1)


def fetch(meta, weight, own_ref, got_ref, here, sem, rows=None, cols=None):
    owner, base, height, width = weight
    first, some = rows or (0, height)
    left, wide = cols or (0, width)

    def start(ref):
        for k in range(wide // 256):
            source = ref.at[pl.ds(base + (left // 256 + k) * height + first, some)]
            pltpu.make_async_copy(source, here.at[:, pl.ds(256 * k, 256)], sem).start()

    pl.when(meta[CORE] == owner)(functools.partial(start, own_ref))
    pl.when(meta[CORE] != owner)(functools.partial(start, got_ref))


def await_copy(here, sem):
    pltpu.make_async_copy(here, here, sem).wait()


def enter(meta, x_ref, cot_ref, wa_ref, wb_ref, *refs):
    pays, evens, cots, w_ref, sem = refs[0:4], refs[4:8], refs[8:12], refs[12], refs[13]
    step = pl.program_id(0)

    @pl.when(step == 0)
    def _():
        fetch(meta, W1, wa_ref, wb_ref, w_ref, sem)
        await_copy(w_ref, sem)

    x = x_ref[0].reshape(PIX0, C0)
    z = dot_nn(x, w_ref[...])
    even = dot_nn(even_picker(), x).astype(BF16)
    row = lax.broadcasted_iota(jnp.int32, (16, M0), 0)
    high, wide = meta[HIGH + step].astype(F32), meta[WIDE + step].astype(F32)
    sizes = jnp.where(row == 0, high, jnp.where(row == 1, wide, 0.0))
    middle = total_rows(z) * (1.0 / PIX0)
    rest = middle
    for k in range(3):
        part = rest.astype(BF16).astype(F32)
        sizes = jnp.where(row == 2 + k, part, sizes)
        rest = rest - part
    z = z - middle
    for k in range(WORK):

        @pl.when(step == k)
        def _(k=k):
            pays[k][0:PIX0, :] = z.astype(BF16)
            pays[k][PIX0 : PIX0 + 16, :] = sizes.astype(BF16)
            evens[k][...] = even
            cots[k][...] = cot_ref[0].reshape(PIX1, C1)


def arrive(meta, *refs):
    pays, z_ref, z_far_ref, hw_ref, st_ref = refs[0:4], *refs[4:]
    first, second, count = 0.0, 0.0, 0.0
    for k in range(WORK):
        rows = pays[k][PIX0 : PIX0 + 16, :].astype(F32)
        sizes = rows[:, 0:128]
        hw_ref[k : k + 1, :] = sizes[0:1, :]
        hw_ref[4 + k : 5 + k, :] = sizes[1:2, :]
        count = count + sizes[0:1, :] * sizes[1:2, :]
        z = pays[k][0:PIX0, :].astype(F32) + ((rows[2:3, :] + rows[3:4, :]) + rows[4:5, :])
        z_ref[k] = z
        z_far_ref[k] = z
        zm = z * over_lanes(pixel_mask(sizes[0:1, :], sizes[1:2, :], WB, PIX0), M0)
        first = first + total_rows(zm)
        second = second + total_rows(zm * z)
    st_ref[0:1, :] = jnp.concatenate([first, count], axis=1)
    st_ref[1:2, :] = jnp.concatenate([second, count], axis=1)


def front_two(meta, *refs):
    stats, (z_ref, hw_ref, n_ref, wa_ref, wb_ref) = refs[0:4], refs[4:9]
    tot_ref, a1_ref, z2_ref, z2b_ref, st_ref, w_ref, act_ref, sem = refs[9:]
    fetch(meta, W2, wa_ref, wb_ref, w_ref, sem)
    table = plane_total(stats)
    tot_ref[...] = table
    mean, scale = mean_scale(table[:, :M0], count_of(tot_ref))
    act_ref[:, 0:WB, :] = jnp.zeros((2, WB, 3 * M0), BF16)
    act_ref[:, WB + PIX0 : 2 * WB + PIX0, :] = jnp.zeros((2, WB, 3 * M0), BF16)
    first, second = 0.0, 0.0
    for k in range(WORK):
        mask = over_lanes(mask0(hw_ref, k), M0)
        pre = (z_ref[k] - mean) * scale * n_ref[0:1, :M0] + n_ref[1:2, :M0]
        act = silu(pre) * mask
        left, right = side_columns(act, WB)
        wide = jnp.concatenate([left, act, right], axis=1).astype(BF16)
        act_ref[k % 2, WB : WB + PIX0, :] = wide
        a1_ref[k] = wide[:, M0 : 2 * M0]
        if k == 0:
            await_copy(w_ref, sem)
        z2 = dot_nn(act_ref[k % 2, 0:PIX0, :], w_ref[0 : 3 * M0, :])
        z2 = z2 + dot_nn(wide, w_ref[3 * M0 : 6 * M0, :])
        z2 = z2 + dot_nn(act_ref[k % 2, 2 * WB : 2 * WB + PIX0, :], w_ref[6 * M0 :, :])
        z2_ref[k] = z2
        z2b_ref[k] = z2
        zm = z2 * mask
        first = first + total_rows(zm)
        second = second + total_rows(zm * z2)
    st_ref[0:1, :] = first
    st_ref[1:2, :] = second


def front_three(meta, *refs):
    stats, (tot_ref, z2_ref, hw_ref, n_ref, wa_ref, wb_ref) = refs[0:4], refs[4:10]
    tot2_ref, a2_ref, a2b_ref, st_ref, w_ref, sem = refs[10:]
    fetch(meta, W3, wa_ref, wb_ref, w_ref, sem)
    table = plane_total(stats)
    tot2_ref[...] = table
    mean, scale = mean_scale(table, count_of(tot_ref))
    first, second = 0.0, 0.0
    for k in range(WORK):
        pre = (z2_ref[k] - mean) * scale * n_ref[0:1, M0 : 2 * M0] + n_ref[1:2, M0 : 2 * M0]
        act = (silu(pre) * over_lanes(mask0(hw_ref, k), M0)).astype(BF16)
        a2_ref[k] = act
        a2b_ref[k] = act
        if k == 0:
            await_copy(w_ref, sem)
        z3 = dot_nn(act, w_ref[...])
        first = first + total_rows(z3)
        second = second + total_rows(z3 * z3)
    st_ref[0:1, :] = first
    st_ref[1:2, :] = second


def even_picker():
    row = lax.broadcasted_iota(jnp.int32, (PIX1, PIX0), 0)
    col = lax.broadcasted_iota(jnp.int32, (PIX1, PIX0), 1)
    return jnp.where(col == 32 * (row >> 3) + 2 * (row & 7), 1.0, 0.0).astype(BF16)


def even_placer():
    row = lax.broadcasted_iota(jnp.int32, (PIX0, PIX1), 0)
    col = lax.broadcasted_iota(jnp.int32, (PIX0, PIX1), 1)
    return jnp.where(row == 32 * (col >> 3) + 2 * (col & 7), 1.0, 0.0).astype(BF16)


def placed(values):
    placer = even_placer()
    high = values.astype(BF16)
    rest = (values - high.astype(F32)).astype(BF16)
    return dot_nn(placer, high) + dot_nn(placer, rest)


SIDE_PART = C1 // 4


def join(meta, *refs):
    stats, (tot_ref, a2_ref), evens, (hw_ref, n_ref) = refs[0:4], refs[4:6], refs[6:10], refs[10:12]
    wa_ref, wb_ref = refs[12:14]
    tot3_ref, s_ref, p_ref, z3_ref, z1_ref, z1b_ref, zs_ref, st_ref, sts_ref = refs[14:23]
    w3_ref, w1_ref, ws_ref, sems = refs[23:]
    step = pl.program_id(0)

    @pl.when(step == 0)
    def _():
        fetch(meta, W3, wa_ref, wb_ref, w3_ref, sems.at[0])
        fetch(meta, V1, wa_ref, wb_ref, w1_ref, sems.at[1])
        for k in range(4):
            cols = (k * SIDE_PART, SIDE_PART)
            fetch(meta, VS, wa_ref, wb_ref, ws_ref.at[k], sems.at[2 + k], cols=cols)
        table = plane_total(stats)
        tot3_ref[...] = table
        mean, scale = mean_scale(table, count_of(tot_ref))
        picker = even_picker()
        await_copy(w3_ref, sems.at[0])
        for k in range(WORK):
            act = dot_nn(picker, a2_ref[k]).astype(BF16)
            z3 = dot_nn(act, w3_ref[...])
            here = slice(k * PIX1, (k + 1) * PIX1)
            z3_ref[here, :] = z3
            pre = (z3 - mean) * scale * n_ref[0:1, 2 * M0 : 2 * M0 + C0]
            pre = pre + n_ref[1:2, 2 * M0 : 2 * M0 + C0]
            pre = pre + evens[k][...].astype(F32)
            p_ref[here, :] = pre
            s_ref[here, :] = (silu(pre) * over_lanes(mask1(hw_ref, k), C0)).astype(BF16)
        await_copy(w1_ref, sems.at[1])
        z1 = dot_nn(s_ref[...], w1_ref[...])
        z1_ref[...] = z1
        z1b_ref[...] = z1
        put_sums(st_ref, z1, z1 * z1)

    for k in range(4):

        @pl.when(step == k)
        def _(k=k):
            await_copy(ws_ref.at[k], sems.at[2 + k])
            zs = dot_nn(s_ref[...], ws_ref[k])
            zs_ref[...] = zs
            put_sums(sts_ref, zs, zs * zs)


def fetch_conv(meta, wa_ref, wb_ref, w_ref, sems):
    for k in range(3):
        rows = (k * 3 * M1, 3 * M1)
        fetch(meta, V2, wa_ref, wb_ref, w_ref.at[pl.ds(*rows)], sems.at[k], rows=rows)


def await_conv(w_ref, sems, k):
    await_copy(w_ref.at[pl.ds(k * 3 * M1, 3 * M1)], sems.at[k])


def mid_one(meta, *refs):
    stats, (tot_ref, z1_ref, hw_ref, n_ref, wa_ref, wb_ref) = refs[0:4], refs[4:10]
    tot4_ref, a1_ref, z2_ref, z2b_ref, st_ref, w_ref, sems = refs[10:]
    fetch_conv(meta, wa_ref, wb_ref, w_ref, sems)
    table = plane_total(stats)
    tot4_ref[...] = table
    mean, scale = mean_scale(table, count_of(tot_ref) * 0.25)
    mask = mask1_all(hw_ref, M1)
    act = silu((z1_ref[...] - mean) * scale * n_ref[0:1, :M1] + n_ref[1:2, :M1]) * mask
    left, right = side_columns(act, WB // 2)
    wide = jnp.concatenate([left, act, right], axis=1).astype(BF16)
    a1_ref[...] = wide[:, M1 : 2 * M1]
    await_conv(w_ref, sems, 0)
    z2 = later_rows(dot_nn(wide, w_ref[0 : 3 * M1, :]), 1, HB // 2, WB // 2)
    await_conv(w_ref, sems, 1)
    z2 = z2 + dot_nn(wide, w_ref[3 * M1 : 6 * M1, :])
    await_conv(w_ref, sems, 2)
    z2 = z2 + later_rows(dot_nn(wide, w_ref[6 * M1 :, :]), -1, HB // 2, WB // 2)
    z2_ref[...] = z2
    z2b_ref[...] = z2
    zm = z2 * mask
    put_sums(st_ref, zm, zm * z2)


def mid_two(meta, *refs):
    stats, (tot_ref, z2_ref, hw_ref, n_ref, wa_ref, wb_ref) = refs[0:4], refs[4:10]
    tot5_ref, a2_ref, z3_ref, st_ref, w_ref, sem = refs[10:]
    fetch(meta, V3, wa_ref, wb_ref, w_ref, sem)
    table = plane_total(stats)
    tot5_ref[...] = table
    mean, scale = mean_scale(table, count_of(tot_ref) * 0.25)
    pre = (z2_ref[...] - mean) * scale * n_ref[0:1, M1 : 2 * M1] + n_ref[1:2, M1 : 2 * M1]
    act = (silu(pre) * mask1_all(hw_ref, M1)).astype(BF16)
    a2_ref[...] = act
    await_copy(w_ref, sem)
    z3 = dot_nn(act, w_ref[...])
    z3_ref[...] = z3
    put_sums(st_ref, z3, z3 * z3)


AT3, ATS = 2 * M1, 2 * M1 + C1


def turn(meta, *refs):
    stats, sides, (tot_ref, z3_ref, zs_ref, hw_ref, n_ref) = refs[0:4], refs[4:8], refs[8:13]
    cots, (tot6_ref, tots_ref), ys, (g_ref, st_ref) = refs[13:17], refs[17:19], refs[19:23], refs[23:]
    step = pl.program_id(0)

    @pl.when(step == 0)
    def _():
        tot6_ref[...] = plane_total(stats)
        tots_ref[...] = plane_total(sides)
        st_ref[...] = jnp.zeros_like(st_ref)

    count = count_of(tot_ref) * 0.25
    mean, scale = mean_scale(tot6_ref[...], count)
    mean_s, scale_s = mean_scale(tots_ref[...], count)
    normed = (z3_ref[0] - mean) * scale
    normed_s = (zs_ref[0] - mean_s) * scale_s
    pre = normed * n_ref[0:1, AT3:ATS] + n_ref[1:2, AT3:ATS]
    pre = pre + (normed_s * n_ref[0:1, ATS : ATS + C1] + n_ref[1:2, ATS : ATS + C1])
    sig = sigmoid(pre)
    value = pre * sig
    change = sig * (1.0 + pre * (1.0 - sig))
    for k in range(WORK):

        @pl.when(step == k)
        def _(k=k):
            mask = over_lanes(mask1(hw_ref, k), C1)
            ys[k][...] = (value * mask).astype(BF16)
            g_ref[0] = cots[k][...].astype(F32) * change * mask

    grad = g_ref[0]
    st_ref[0:1, :] += total_rows(grad)
    st_ref[1:2, :] += total_rows(grad * normed)
    st_ref[2:3, :] += total_rows(grad * normed_s)


def norm_back(grad, normed, scale, gain, first, second, mask):
    return (mask * (scale * gain) * (grad - first - normed * second)).astype(BF16)


def back_one(meta, *refs):
    stats, (tot6_ref, tots_ref, tot5_ref, tot_ref) = refs[0:4], refs[4:8]
    z3_ref, zs_ref, g_ref, z2_ref, hw_ref, n_ref, wa_ref, wb_ref = refs[8:16]
    tot7_ref, er_ref, es_ref, g2_ref, st_ref, w_ref, sem = refs[16:]
    fetch(meta, V3, wa_ref, wb_ref, w_ref, sem)
    table = plane_total(stats)
    tot7_ref[...] = table
    count = count_of(tot_ref) * 0.25
    table = table / count
    mask = mask1_all(hw_ref, C1)
    grad = g_ref[...]
    mean, scale = mean_scale(tot6_ref[...], count)
    normed = (z3_ref[...] - mean) * scale
    d3 = norm_back(grad, normed, scale, n_ref[0:1, AT3:ATS], table[0:1], table[1:2], mask)
    mean2, scale2 = mean_scale(tot5_ref[...], count)
    normed2 = (z2_ref[...] - mean2) * scale2
    pre2 = normed2 * n_ref[0:1, M1 : 2 * M1] + n_ref[1:2, M1 : 2 * M1]
    await_copy(w_ref, sem)
    g2 = dot_nt(d3, w_ref[...]) * mask[:, :M1] * slope(pre2)
    g2_ref[...] = g2
    put_sums(st_ref, g2, g2 * normed2)
    mean_s, scale_s = mean_scale(tots_ref[...], count)
    normed_s = (zs_ref[...] - mean_s) * scale_s
    ds = norm_back(grad, normed_s, scale_s, n_ref[0:1, ATS : ATS + C1], table[0:1], table[2:3], mask)
    es_ref[...] = ds
    half = C1 // 2
    for p in range(2):
        cols = slice(p * half, (p + 1) * half)
        er_ref[meta[CORE] ^ p] = jnp.concatenate([d3[:, cols], ds[:, cols]], axis=1)


def back_two(meta, *refs):
    stats, (tot5_ref, tot4_ref, tot_ref, z2_ref, g2_ref, z1_ref) = refs[0:4], refs[4:10]
    hw_ref, n_ref, wa_ref, wb_ref, tot8_ref, er_ref, g1_ref, st_ref, w_ref, sems = refs[10:]
    fetch_conv(meta, wa_ref, wb_ref, w_ref, sems)
    table = plane_total(stats)
    tot8_ref[...] = table
    count = count_of(tot_ref) * 0.25
    table = table / count
    mask = mask1_all(hw_ref, M1)
    mean, scale = mean_scale(tot5_ref[...], count)
    normed = (z2_ref[...] - mean) * scale
    d2 = norm_back(
        g2_ref[...], normed, scale, n_ref[0:1, M1 : 2 * M1], table[0:1], table[1:2], mask
    )
    for p in range(2):
        er_ref[meta[CORE] ^ p] = d2[:, p * (M1 // 2) : (p + 1) * (M1 // 2)]
    mean1, scale1 = mean_scale(tot4_ref[...], count)
    normed1 = (z1_ref[...] - mean1) * scale1
    pre1 = normed1 * n_ref[0:1, :M1] + n_ref[1:2, :M1]
    await_conv(w_ref, sems, 0)
    wide = later_rows(dot_nt(d2, w_ref[0 : 3 * M1, :]), -1, HB // 2, WB // 2)
    await_conv(w_ref, sems, 1)
    wide = wide + dot_nt(d2, w_ref[3 * M1 : 6 * M1, :])
    await_conv(w_ref, sems, 2)
    wide = wide + later_rows(dot_nt(d2, w_ref[6 * M1 :, :]), 1, HB // 2, WB // 2)
    left, _ = side_columns(wide[:, 2 * M1 :], WB // 2)
    _, right = side_columns(wide[:, :M1], WB // 2)
    g1 = (wide[:, M1 : 2 * M1] + left + right) * mask * slope(pre1)
    g1_ref[...] = g1
    put_sums(st_ref, g1, g1 * normed1)


def back_three(meta, *refs):
    stats, (tot4_ref, tot_ref, z1_ref, g1_ref, es_ref, tot3_ref, p_ref, z3_ref) = refs[0:4], refs[4:12]
    hw_ref, n_ref, wa_ref, wb_ref = refs[12:16]
    tot9_ref, er_ref, g0_ref, st_ref, w1_ref, ws_ref, sems = refs[16:]
    fetch(meta, V1, wa_ref, wb_ref, w1_ref, sems.at[0])
    fetch(meta, VS, wa_ref, wb_ref, ws_ref, sems.at[1])
    table = plane_total(stats)
    tot9_ref[...] = table
    count = count_of(tot_ref) * 0.25
    table = table / count
    mask = mask1_all(hw_ref, C0)
    mean, scale = mean_scale(tot4_ref[...], count)
    normed = (z1_ref[...] - mean) * scale
    d1 = norm_back(
        g1_ref[...], normed, scale, n_ref[0:1, :M1], table[0:1], table[1:2], mask[:, :M1]
    )
    for p in range(2):
        er_ref[meta[CORE] ^ p] = d1[:, p * (M1 // 2) : (p + 1) * (M1 // 2)]
    await_copy(w1_ref, sems.at[0])
    grad = dot_nt(d1, w1_ref[...])
    await_copy(ws_ref, sems.at[1])
    grad = grad + dot_nt(es_ref[...], ws_ref[...])
    grad = grad.astype(BF16).astype(F32)
    g0 = grad * slope(p_ref[...]) * mask
    g0_ref[...] = g0
    mean3, scale3 = mean_scale(tot3_ref[...], count * 4.0)
    put_sums(st_ref, g0, g0 * ((z3_ref[...] - mean3) * scale3))


def last_one(meta, *refs):
    stats, (tot3_ref, tot2_ref, tot_ref, a2_ref, g0_ref, z2_ref, hw_ref, n_ref) = refs[0:4], refs[4:12]
    wa_ref, wb_ref, tot10_ref, d3_ref, g2_ref, st_ref, w_ref, sem = refs[12:]
    step = pl.program_id(0)

    @pl.when(step == 0)
    def _():
        fetch(meta, W3, wa_ref, wb_ref, w_ref, sem)
        tot10_ref[...] = plane_total(stats)
        st_ref[...] = jnp.zeros_like(st_ref)
        await_copy(w_ref, sem)

    count = count_of(tot_ref)
    table = tot10_ref[...] / count
    mean, scale = mean_scale(tot3_ref[...], count)
    mean2, scale2 = mean_scale(tot2_ref[...], count)
    high = pl.ds(step, 1)
    wide = pl.ds(4 + step, 1)
    mask = over_lanes(pixel_mask(hw_ref[high, :], hw_ref[wide, :], WB, PIX0), C0)
    normed = (dot_nn(a2_ref[0], w_ref[...]) - mean) * scale
    grad = placed(g0_ref[0])
    gain = n_ref[0:1, 2 * M0 : 2 * M0 + C0]
    d3 = norm_back(grad, normed, scale, gain, table[0:1], table[1:2], mask)
    d3_ref[0] = d3
    normed2 = (z2_ref[0] - mean2) * scale2
    pre2 = normed2 * n_ref[0:1, M0 : 2 * M0] + n_ref[1:2, M0 : 2 * M0]
    g2 = dot_nt(d3, w_ref[...]) * mask[:, :M0] * slope(pre2)
    g2_ref[0] = g2
    st_ref[0:1, :] += total_rows(g2)
    st_ref[1:2, :] += total_rows(g2 * normed2)


def last_two(meta, *refs):
    stats, (tot2_ref, tot_ref, z2_ref, g2_ref, z1_ref, hw_ref, n_ref) = refs[0:4], refs[4:11]
    wa_ref, wb_ref, tot11_ref, d2_ref, g1_ref, st_ref, w_ref, sem = refs[11:]
    step = pl.program_id(0)

    @pl.when(step == 0)
    def _():
        fetch(meta, W2, wa_ref, wb_ref, w_ref, sem)
        tot11_ref[...] = plane_total(stats)
        st_ref[...] = jnp.zeros_like(st_ref)

    count = count_of(tot_ref)
    table = tot11_ref[...] / count
    mask = pixel_mask(hw_ref[pl.ds(step, 1), :], hw_ref[pl.ds(4 + step, 1), :], WB, PIX0)
    mask = over_lanes(mask, M0)
    mean2, scale2 = mean_scale(tot2_ref[...], count)
    normed2 = (z2_ref[0] - mean2) * scale2
    gain = n_ref[0:1, M0 : 2 * M0]
    d2 = norm_back(g2_ref[0], normed2, scale2, gain, table[0:1], table[1:2], mask)
    d2_ref[0] = d2
    mean1, scale1 = mean_scale(tot_ref[:, :M0], count)
    normed1 = (z1_ref[0] - mean1) * scale1
    pre1 = normed1 * n_ref[0:1, :M0] + n_ref[1:2, :M0]

    @pl.when(step == 0)
    def _():
        await_copy(w_ref, sem)

    wide = dot_nt(d2, w_ref[3 * M0 : 6 * M0, :])
    wide = wide + later_rows(dot_nt(d2, w_ref[0 : 3 * M0, :]), -1, HB, WB)
    wide = wide + later_rows(dot_nt(d2, w_ref[6 * M0 :, :]), 1, HB, WB)
    left, _ = side_columns(wide[:, 2 * M0 :], WB)
    _, right = side_columns(wide[:, :M0], WB)
    g1 = (wide[:, M0 : 2 * M0] + left + right) * mask * slope(pre1)
    g1_ref[0] = g1
    st_ref[0:1, :] += total_rows(g1)
    st_ref[1:2, :] += total_rows(g1 * normed1)


def last_three(meta, *refs):
    stats, (tot_ref, z1_ref, g1_ref, g0_ref, hw_ref, n_ref) = refs[0:4], refs[4:10]
    tot12_ref, backs = refs[10], refs[11:15]
    table = plane_total(stats)
    tot12_ref[...] = table
    count = count_of(tot_ref)
    table = table / count
    mean, scale = mean_scale(tot_ref[:, :M0], count)
    for k in range(WORK):
        mask = over_lanes(mask0(hw_ref, k), M0)
        normed = (z1_ref[k] - mean) * scale
        backs[k][0:PIX0, :] = norm_back(
            g1_ref[k], normed, scale, n_ref[0:1, :M0], table[0:1], table[1:2], mask
        )
        grad = g0_ref[k * PIX1 : (k + 1) * PIX1, :].astype(BF16)
        for part in range(C0 // M0):
            here = slice(PIX0 + part * PIX1, PIX0 + (part + 1) * PIX1)
            backs[k][here, :] = grad[:, part * M0 : (part + 1) * M0]


def leave(meta, x_ref, wa_ref, wb_ref, *refs):
    backs, gx_ref, out_ref = refs[0:4], refs[5], refs[6]
    w_ref, acc_ref, stage_ref, sem, out_sem = refs[7:]
    step = pl.program_id(0)

    @pl.when(step == 0)
    def _():
        fetch(meta, W1, wa_ref, wb_ref, w_ref, sem)
        acc_ref[...] = jnp.zeros_like(acc_ref)
        await_copy(w_ref, sem)

    for k in range(WORK):

        @pl.when(step == k)
        def _(k=k):
            d1 = backs[k][0:PIX0, :]
            grad = jnp.concatenate(
                [backs[k][PIX0 + n * PIX1 : PIX0 + (n + 1) * PIX1, :] for n in range(C0 // M0)], axis=1
            )
            acc_ref[...] += dot_tn(x_ref[0].reshape(PIX0, C0), d1)
            gx_ref[0] = (dot_nt(d1, w_ref[...]) + dot_nn(even_placer(), grad)).astype(BF16)

    @pl.when(step == WORK - 1)
    def _():
        put_tiles(stage_ref, 0, acc_ref[...])
        copy = pltpu.make_async_copy(stage_ref, out_ref.at[pl.ds(0, 2 * C0)], out_sem)
        copy.start()
        copy.wait()


def put_tiles(ref, start, values):
    rows, width = values.shape
    for k in range(width // 128):
        here = slice(start + k * rows, start + (k + 1) * rows)
        ref[here, :] = values[:, 128 * k : 128 * (k + 1)].astype(BF16)


def nine_shifts(delta, height, breadth):
    pieces = []
    left, right = side_columns(delta, breadth)
    for a in range(3):
        for moved in (right, delta, left):
            pieces.append(later_rows(moved, a - 1, height, breadth).astype(BF16))
    return jnp.concatenate(pieces, axis=1)


SIDES, MIDDLE = 768, 704
SWAPPED = (0, 2, 1, 3)


def place_of(core, chip):
    return jnp.where(core == 0, 2 * (chip & 1) + (chip >> 1), chip)


def spot_of(level):
    return 2 * (level & 1) + (level >> 1)


def put_shards(ref, shard, start, core, level_first, values):
    rows = values.shape[0] // 16
    values = values.astype(BF16)
    for chip in range(4):
        place = place_of(core, chip)
        for z in range(4):
            at = (SWAPPED[z] * 4 + place if level_first else place * 4 + SWAPPED[z]) * shard + start
            part = values[(4 * chip + z) * rows : (4 * chip + z + 1) * rows]
            for k in range(values.shape[1] // 128):
                here = pl.ds(pl.multiple_of(at + k * rows, 16), rows)
                ref[here, :] = part[:, 128 * k : 128 * (k + 1)]


def sides_grad(meta, sa_ref, sb_ref, la_ref, lb_ref, ea_ref, eb_ref, out_ref):
    half = C1 // 2
    side = dot_tn(sa_ref[...], ea_ref[0][:, half:]) + dot_tn(sb_ref[...], eb_ref[0][:, half:])
    put_shards(out_ref, SIDES, 0, meta[CORE], True, side)
    last = dot_tn(la_ref[...], ea_ref[0][:, :half]) + dot_tn(lb_ref[...], eb_ref[0][:, :half])
    put_shards(out_ref, SIDES, C0 // 2, meta[CORE], True, last)


def middle_grad(meta, sa_ref, sb_ref, la_ref, lb_ref, ma_ref, mb_ref, fa_ref, fb_ref, out_ref):
    conv = dot_tn(la_ref[...], nine_shifts(ma_ref[0].astype(F32), HB // 2, WB // 2))
    conv = conv + dot_tn(lb_ref[...], nine_shifts(mb_ref[0].astype(F32), HB // 2, WB // 2))
    put_shards(out_ref, MIDDLE, 0, meta[CORE], False, conv)
    first = dot_tn(sa_ref[...], fa_ref[0]) + dot_tn(sb_ref[...], fb_ref[0])
    put_shards(out_ref, MIDDLE, 9 * M1 // 8, meta[CORE], False, first)


def front_grad_two(meta, a1_ref, d2_ref, a2_ref, d3_ref, out_ref, acc2_ref, acc3_ref):
    slot = pl.program_id(0)
    conv = dot_tn(a1_ref[0], nine_shifts(d2_ref[0].astype(F32), HB, WB))
    last = dot_tn(a2_ref[0], d3_ref[0])

    @pl.when(slot == 0)
    def _():
        acc2_ref[...] = conv
        acc3_ref[...] = last

    @pl.when(slot > 0)
    def _():
        acc2_ref[...] += conv
        acc3_ref[...] += last

    @pl.when(slot == WORK - 1)
    def _():
        for tap in range(9):
            for tile in range(2):
                start = 2 * C0 + tile * 9 * M0 + tap * M0
                lanes = tap * M0 + tile * 128
                out_ref[start : start + M0, :] = acc2_ref[:, lanes : lanes + 128].astype(BF16)
        out_ref[0 : 2 * C0, :] = jnp.zeros((2 * C0, 128), BF16)
        put_tiles(out_ref, 2 * C0 + 2 * 9 * M0, acc3_ref[...])


def unpack_kernel(jobs, chunk, meta, raw_ref, out_ref, *refs):
    raws, flat_ref, sem_in, sem_out = refs[0:3], refs[3], refs[4], refs[5]
    stages = dict(zip(sorted({weight[3] for listed in jobs for _, weight in listed}), refs[6:]))

    def run(listed):
        loads, stores, waits, sizes = [], [], [], []
        for offset, (_, base, height, cols) in listed:
            for row in range(0, height, chunk // cols):
                some = min(chunk // cols, height - row)
                k = len(loads)
                source = raw_ref.at[:, pl.ds(offset + row * cols, some * cols)]
                here = raws[k % 3].at[:, pl.ds(0, some * cols)]
                loads.append(pltpu.make_async_copy(source, here, sem_in.at[k % 3]))
                stage = stages[cols].at[k % 2, pl.ds(0, some)]
                panels = []
                for panel in range(cols // 256):
                    there = out_ref.at[pl.ds(base + panel * height + row, some)]
                    lanes = stage.at[:, pl.ds(256 * panel, 256)]
                    panels.append(pltpu.make_async_copy(lanes, there, sem_out.at[k % 2]))
                stores.append(panels)
                waits.append(pltpu.make_async_copy(stage, stage, sem_out.at[k % 2]))
                sizes.append((some, cols))
        for load in loads[:2]:
            load.start()
        for k, (rows, cols) in enumerate(sizes):
            if k + 2 < len(sizes):
                loads[k + 2].start()
            loads[k].wait()
            flat_ref[:, : rows * cols] = raws[k % 3][:, : rows * cols].astype(F32)
            lines = flat_ref.reshape(chunk // 128, 128)
            if k >= 2:
                waits[k - 2].wait()
            for tile in range(cols // 128):
                values = lines[pl.ds(tile, rows, stride=cols // 128), :].astype(BF16)
                stages[cols][k % 2, 0:rows, tile * 128 : (tile + 1) * 128] = values
            for store in stores[k]:
                store.start()
        for wait in waits[-2:]:
            wait.wait()

    for core in range(2):
        if jobs[core]:
            pl.when(meta[CORE] == core)(functools.partial(run, jobs[core]))


def unpack(meta, packed, rows, jobs, micros, chunk=262144):
    widths = sorted({weight[3] for listed in jobs for _, weight in listed})
    return call(
        functools.partial(unpack_kernel, jobs, chunk),
        pltpu.HBM((rows, 256), BF16),
        (1,),
        [ANYWHERE],
        ANYWHERE,
        [pltpu.VMEM((1, chunk), BF16)] * 3
        + [pltpu.VMEM((1, chunk), F32), DMA((3,)), DMA((2,))]
        + [pltpu.VMEM((2, chunk // cols, cols), BF16) for cols in widths],
        micros=micros,
    )(meta, in_hbm(packed))


PACK_ROWS = 2048
GRAD_ROWS = P_SIZE // 128
ARRIVED = ((1, (0, 1)), (0, (0, 2)), (0, (1, 3)), (1, (2, 3)))


def quarters(bufs, target):
    found = []
    for buf, (p, masks) in zip(bufs, ARRIVED):
        if target == 0:
            p, masks = 1 - p, tuple(SWAPPED[m] for m in masks)
        for k, mask in enumerate(masks):
            found.append((p, mask, buf, k * (buf.shape[0] // 2)))
    return found


def pack_sides(meta, *refs):
    bufs, out_ref = refs[:4], refs[4]
    step = pl.program_id(0)
    level, plane = meta[LEVEL], meta[PLANE]

    @pl.when(meta[CORE] == 0)
    def _():
        out_ref[...] = jnp.zeros_like(out_ref)

    for p, mask, buf, start in quarters(bufs, 1):
        here = meta[CORE] == 1

        @pl.when(here & (step < 4) & (step == (plane ^ mask)))
        def _(p=p, buf=buf, start=start):
            for z in range(4):
                for k in range(8):
                    row = start + spot_of(level ^ z) * SIDES + C0 // 2 + 32 * k
                    rows = buf[pl.ds(pl.multiple_of(row, 32), 32), :].astype(F32)
                    out_ref[pl.ds(512 * z + 8 * p + k, 32, stride=16), :] = rows

        @pl.when(here & (step >= 4) & (((step - 4) >> 1) == (plane ^ mask)))
        def _(p=p, buf=buf, start=start):
            for j in range(2):
                z = 2 * (step & 1) + j
                for k in range(8):
                    row = start + spot_of(level ^ z) * SIDES + 64 * k
                    rows = buf[pl.ds(pl.multiple_of(row, 64), 64), :].astype(F32)
                    out_ref[pl.ds(1024 * j + 8 * p + k, 64, stride=16), :] = rows


def pack_middle(first_step, meta, *refs):
    bufs, out_ref = refs[1:5], refs[-1]
    step = pl.program_id(0) + first_step
    plane, level = meta[PLANE], meta[LEVEL]

    for p, mask, buf, start in quarters(bufs, 1):
        chip = plane ^ mask

        @pl.when((meta[CORE] == 1) & (step < 2) & (step == (chip >> 1)))
        def _(p=p, buf=buf, start=start, chip=chip):
            for z in range(4):
                for k in range(2):
                    row = start + spot_of(level ^ z) * MIDDLE + 9 * M1 // 8 + 64 * k
                    rows = buf[pl.ds(pl.multiple_of(row, 64), 64), :].astype(F32)
                    at = 256 * (4 * (chip & 1) + z) + 2 * p + k
                    out_ref[pl.ds(at, 64, stride=4), :] = rows

        @pl.when((meta[CORE] == 1) & (step > 1))
        def _(p=p, buf=buf, start=start, chip=chip):
            for z in range(4):
                for k in range(2):
                    row = start + spot_of(level ^ z) * MIDDLE + 64 * (step - 2) + 32 * k
                    rows = buf[pl.ds(pl.multiple_of(row, 32), 32), :].astype(F32)
                    at = 128 * (4 * chip + z) + 2 * p + k
                    out_ref[pl.ds(at, 32, stride=4), :] = rows


def pack_rest(meta, *refs):
    out_ref = refs[-1]

    @pl.when(meta[CORE] == 0)
    def _():
        out_ref[...] = jnp.zeros_like(out_ref)

    pack_middle(5, meta, *refs)


def pack_front(meta, *refs):
    fronts, out_ref, whole_ref = refs[5:9], refs[9], refs[10]
    step = pl.program_id(0)
    core, plane, level = meta[CORE], meta[PLANE], meta[LEVEL]
    part = fronts[0].shape[0] // 8

    @pl.when((core == 0) & (step == 0))
    def _():
        for p, mask, buf, start in quarters(fronts, 0):
            for z in range(4):
                there = (16 * p + 4 * place_of(p, plane ^ mask) + spot_of(level ^ z)) * part
                at = start + SWAPPED[z] * part
                rows = buf[at : at + part, :]
                whole_ref[pl.ds(pl.multiple_of(there, 16), part), :] = rows

    at2, at3 = 2 * C0, 2 * C0 + 2 * 9 * M0

    def piece(start, rows):
        return whole_ref[start : start + rows, :].astype(F32)

    @pl.when((core == 0) & (step == 0))
    def _():
        for tile in range(2):
            out_ref[pl.ds(tile, C0, stride=2), :] = piece(tile * C0, C0)

    for k in range(2):

        @pl.when((core == 0) & (step == 1 + k))
        def _(k=k):
            for tile in range(2):
                out_ref[pl.ds(tile, C0, stride=2), :] = piece(at2 + tile * 9 * M0 + k * C0, C0)

    @pl.when((core == 0) & (step == 3))
    def _():
        for tile in range(2):
            out_ref[pl.ds(tile, 256, stride=2), :] = piece(at2 + tile * 9 * M0 + 2 * C0, 256)
        for tile in range(8):
            out_ref[pl.ds(512 + tile, 192, stride=8), :] = piece(at3 + tile * 256, 192)

    @pl.when((core == 0) & (step == 4))
    def _():
        out_ref[...] = jnp.zeros_like(out_ref)
        for tile in range(8):
            out_ref[pl.ds(tile, 64, stride=8), :] = piece(at3 + tile * 256 + 192, 64)

    pack_middle(0, meta, *refs[:5], out_ref)


def rows_out(meta, x_ref, xg_ref, y_ref, yg_ref, out_ref):
    step = pl.program_id(0)
    row = lax.broadcasted_iota(jnp.int32, (128, 128), 0)
    col = lax.broadcasted_iota(jnp.int32, (128, 128), 1)

    def put(first, second, source):
        values = jnp.concatenate([first.reshape(-1, C0), second.reshape(-1, C0)], axis=0)
        mover = jnp.where(col == source, 1.0, 0.0).astype(BF16)
        moved = dot_nn(mover, values).astype(BF16)
        for k in range(16):
            out_ref[:, k * C0 : (k + 1) * C0] = moved[8 * k : 8 * (k + 1), :]

    image, stand = row & 7, row * 0
    for k in range(WORK):
        stand = jnp.where(image == meta[k], k, jnp.where(image == (meta[k] ^ 1), WORK + k, stand))

    @pl.when(meta[CORE] == 0)
    def _():
        put(x_ref[...], xg_ref[...], 16 * stand + (row >> 3))

    @pl.when((meta[CORE] == 1) & (step < HB // 2))
    def _():
        def split(ref):
            pieces = []
            for k in range(WORK):
                wide = ref[k].astype(F32)
                pieces += [wide[:, :C0], wide[:, C0:]]
            return jnp.concatenate(pieces, axis=0).astype(BF16)

        put(split(y_ref), split(yg_ref), 16 * stand + 8 * ((row >> 3) & 1) + (row >> 4))

    @pl.when((meta[CORE] == 1) & (step >= HB // 2))
    def _():
        out_ref[...] = jnp.zeros_like(out_ref)


def pin(value, *others):
    return lax.optimization_barrier((value,) + others)[0]


def swap_cores(value):
    return lax.ppermute(value, "pipe", [(0, 1), (1, 0)])


def xor_permute(value, mask):
    count = lax.axis_size("dp")
    return lax.ppermute(value, "dp", [(i, i ^ mask) for i in range(count)])


def upper_bits():
    return [bit for bit in (16, 32, 64, 128, 256, 512) if bit < lax.axis_size("dp")]


def plane_turn(value, turn_no):
    count = lax.axis_size("dp")
    pairs = []
    for p in range(2):
        mask = SWAPPED[turn_no] if p else turn_no
        pairs += [(p * count + i, p * count + (i ^ mask)) for i in range(count)]
    return lax.ppermute(value, ("pipe", "dp"), pairs)


def shared(value):
    for bit in upper_bits():
        value = value + xor_permute(value, bit)
    return [value] + [plane_turn(value, k) for k in (1, 2, 3)]


def over_levels(values):
    return [values[0]] + [xor_permute(values[k], 4 * k) for k in (1, 2, 3)]


def part_at(value, index, parts):
    rows = value.shape[0] // parts
    return lax.optimization_barrier(lax.dynamic_slice_in_dim(value, index * rows, rows, 0))


def added(*parts):
    total = parts[0].astype(F32)
    for part in parts[1:]:
        total = total + part.astype(F32)
    return total.astype(BF16)


def upper_sum(value):
    for bit in upper_bits():
        value = added(value, xor_permute(value, bit))
    return value


def to_core(both, target):
    count = lax.axis_size("dp")
    other = 1 - target
    close, away = (1, 2) if target == 1 else (2, 1)
    arrived = [both]
    for p, mask in ((other, 0), (other, close), (target, away)):
        pairs = [(p * count + i, target * count + (i ^ mask)) for i in range(count)]
        arrived.append(lax.ppermute(both, ("pipe", "dp"), pairs))
    return arrived


def on_device(images, extents, views, params, norms, cotangent):
    images, cotangent, params = in_hbm(images), in_hbm(cotangent), in_hbm(params)
    core = lax.axis_index("pipe")
    first_core = core == 0
    plane = lax.axis_index("dp") % 4
    level = (lax.axis_index("dp") // 4) % 4
    place = place_of(core, plane)

    pair = 2 * (level ^ jnp.arange(WORK, dtype=jnp.int32))
    hot = (pair[:, None] == jnp.arange(2 * WORK, dtype=jnp.int32)[None, :]).astype(jnp.int32)
    view = jnp.sum(hot * views[None, :], axis=1)
    order = pair + (view != core).astype(jnp.int32)
    hot = (order[:, None] == jnp.arange(2 * WORK, dtype=jnp.int32)[None, :]).astype(jnp.int32)
    sizes = jnp.sum(hot[:, :, None] * extents[None], axis=1)
    spot = jnp.stack([core, plane, level]).astype(jnp.int32)
    meta = jnp.concatenate([order, spot, sizes[:, 0], sizes[:, 1]]).astype(jnp.int32)

    w1 = unpack(meta, params, C0, ([(0, W1)], []), 3, 65536)
    w1 = (in_hbm(w1), in_hbm(lax.ppermute(w1, "pipe", [(0, 1)])))
    norms_there = swap_cores(norms[0])
    n0 = jnp.where(first_core, norms[0], norms_there)
    n1 = jnp.where(first_core, norms_there, norms[0])

    some = lambda dims, kind: [shape_of(dims, kind)] * WORK
    made = call(
        enter,
        some((PIX0 + 16, M0), BF16) + some((PIX1, C0), BF16) + some((PIX1, C1), BF16),
        (WORK,),
        [own_image(HB, WB, C0), own_image(HB // 2, WB // 2, C1), ANYWHERE, ANYWHERE],
        [full(PIX0 + 16, M0)] * 4 + [full(PIX1, C0)] * 4 + [full(PIX1, C1)] * 4,
        [vmem(C0, M0), DMA],
    )(meta, images, cotangent, *w1)
    pays, evens, cots = over_levels(made[0:4]), made[4:8], made[8:12]
    first_weights = unpack(
        meta,
        pin(params, made[0]),
        10240,
        ([(262144, W2), (851968, W3)], [(0, V1), (3932160, VS)]),
        8,
    )
    pays[0] = pin(pays[0], first_weights, norms_there)
    z1, z1b, hw, st = single(
        arrive,
        meta,
        near(*pays),
        [
            ((WORK, PIX0, M0), F32, False),
            ((WORK, PIX0, M0), F32, True),
            ((8, 128), F32, False),
            ((2, M0 + 128), F32, False),
        ],
    )

    s1 = shared(st)
    got = swap_cores(first_weights)
    evens = over_levels(evens)
    second_weights = unpack(
        meta, pin(params, st), 13312, ([], [(524288, V2), (2883584, V3)]), 10
    )
    s1[0] = pin(s1[0], got, evens[1], second_weights)
    wa = (in_hbm(first_weights), in_hbm(got))
    tot1, a1, z2, z2b, st = single(
        front_two,
        meta,
        near(*s1, z1, hw, n0) + weight(wa),
        [
            ((2, M0 + 128), F32, False),
            ((WORK, PIX0, M0), BF16, True),
            ((WORK, PIX0, M0), F32, False),
            ((WORK, PIX0, M0), F32, True),
            ((2, M0), F32, False),
        ],
        [vmem(9 * M0, M0), vmem(2, PIX0 + 2 * WB, 3 * M0), DMA],
    )
    s2 = shared(st)
    got = lax.ppermute(second_weights, "pipe", [(1, 0)])
    s2[0] = pin(s2[0], evens[2])
    tot2, a2, a2b, st = single(
        front_three,
        meta,
        near(*s2, tot1, z2, hw, n0) + weight(wa),
        [
            ((2, M0), F32, False),
            ((WORK, PIX0, M0), BF16, False),
            ((WORK, PIX0, M0), BF16, True),
            ((2, C0), F32, False),
        ],
        [vmem(M0, C0), DMA],
    )
    s3 = shared(st)
    cots = over_levels(cots)
    s3[0] = pin(s3[0], evens[3])

    tile = lambda s, meta: (0, s)
    tot3, src, p_even, z3_even, y1, y1b, ys, st, sts = call(
        join,
        [
            shape_of((2, C0), F32),
            hbm_of((ROWS1, C0), BF16),
            hbm_of((ROWS1, C0), F32),
            hbm_of((ROWS1, C0), F32),
            shape_of((ROWS1, M1), F32),
            hbm_of((ROWS1, M1), F32),
            hbm_of((ROWS1, C1), F32),
            shape_of((2, M1), F32),
            shape_of((2, C1), F32),
        ],
        (4,),
        [full(2, C0)] * 4
        + [full(2, M0 + 128), full(WORK, PIX0, M0)]
        + [full(PIX1, C0)] * 4
        + [full(8, 128), full(2, CN)]
        + [ANYWHERE] * 2,
        [
            full(2, C0),
            full(ROWS1, C0),
            full(ROWS1, C0),
            full(ROWS1, C0),
            full(ROWS1, M1),
            full(ROWS1, M1),
            pl.BlockSpec((ROWS1, SIDE_PART), tile),
            full(2, M1),
            pl.BlockSpec((2, SIDE_PART), tile),
        ],
        [vmem(M0, C0), vmem(C0, M1), vmem(4, C0, SIDE_PART), DMA((6,))],
    )(meta, *s3, tot1, a2, *evens, hw, n0, *wa)

    s4 = shared(st)
    src_there = swap_cores(src)
    s4[0] = pin(s4[0], got, src_there)
    wb = (in_hbm(second_weights), in_hbm(got))
    conv_scratch = [vmem(9 * M1, M1), DMA((3,))]
    last_scratch = [vmem(M1, C1), DMA]
    row = ((2, M1), F32, False)
    tot4, b1, y2, y2b, st = single(
        mid_one,
        meta,
        near(*s4, tot1, y1, hw, n1) + weight(wb),
        [row, ((ROWS1, M1), BF16, True), ((ROWS1, M1), F32, False), ((ROWS1, M1), F32, True), row],
        conv_scratch,
    )
    s5 = shared(st)
    b1_there = swap_cores(b1)
    t5 = shared(sts)
    s5[0] = pin(s5[0], cots[1], b1_there, *t5)
    tot5, b2, y3, st = single(
        mid_two,
        meta,
        near(*s5, tot1, y2, hw, n1) + weight(wb),
        [row, ((ROWS1, M1), BF16, True), ((ROWS1, C1), F32, False), ((2, C1), F32, False)],
        last_scratch,
    )
    s6 = shared(st)
    b2_there = swap_cores(b2)
    s6[0] = pin(s6[0], cots[2], cots[3], b2_there)
    made = call(
        turn,
        [shape_of((2, C1), F32)] * 2
        + some((PIX1, C1), BF16)
        + [shape_of((WORK, PIX1, C1), F32), shape_of((3, C1), F32)],
        (WORK,),
        [full(2, C1)] * 8
        + [full(2, M0 + 128), per_image(PIX1, C1), per_image(PIX1, C1), full(8, 128), full(2, CN)]
        + [full(PIX1, C1)] * 4,
        [full(2, C1)] * 2 + [full(PIX1, C1)] * 4 + [per_image(PIX1, C1), full(3, C1)],
    )(
        meta, *s6, *t5, tot1, y3.reshape(WORK, PIX1, C1), in_hbm(ys.reshape(WORK, PIX1, C1)), hw,
        n1, *cots,
    )
    tot6, tots, y_out, grad_y, st = made[0], made[1], made[2:6], made[6], made[7]
    grad_y = grad_y.reshape(ROWS1, C1)

    s7 = shared(st)
    tot7, er, es, g2, st = single(
        back_one,
        meta,
        near(*s7, tot6, tots, tot5, tot1, y3) + far(ys) + near(grad_y) + far(y2b)
        + near(hw, n1) + weight(wb),
        [
            ((3, C1), F32, False),
            ((2, ROWS1, C1), BF16, False),
            ((ROWS1, C1), BF16, False),
            ((ROWS1, M1), F32, False),
            row,
        ],
        last_scratch,
        limit=36,
    )
    s8 = shared(st)
    other = swap_cores(er[1:])
    sides = single(
        sides_grad,
        meta,
        far(src, src_there, b2, b2_there) + near(er, other),
        [((16 * SIDES, 128), BF16, False)],
        limit=40,
    )[0]
    s8[0] = pin(s8[0], sides)
    low, high = level & 1, level >> 1
    sides = added(part_at(sides, low, 2), xor_permute(part_at(sides, 1 - low, 2), 4))
    tot8, e2r, g1, st = single(
        back_two,
        meta,
        near(*s8, tot5, tot4, tot1) + far(y2b) + near(g2) + far(y1b) + near(hw, n1) + weight(wb),
        [row, ((2, ROWS1, M1 // 2), BF16, False), ((ROWS1, M1), F32, False), row],
        conv_scratch,
    )
    s9 = shared(st)
    other2 = swap_cores(e2r[1:])
    s9[0] = pin(s9[0], other2)
    made = single(
        back_three,
        meta,
        near(*s9, tot4, tot1) + far(y1b) + near(g1, es, tot3) + far(p_even, z3_even)
        + near(hw, n1) + weight(wa),
        [row, ((2, ROWS1, M1 // 2), BF16, False), ((ROWS1, C0), F32, False), ((2, C0), F32, False)],
        [vmem(C0, M1), vmem(C0, C1), DMA((2,))],
    )
    tot9, e1r, g0, st = made

    s10 = shared(st)
    other1 = swap_cores(e1r[1:])
    s10[0] = pin(s10[0], other1, sides)
    half_there = xor_permute(part_at(sides, 1 - high, 2), 8)
    tot10, d3, g2, st = call(
        last_one,
        [
            shape_of((2, C0), F32),
            hbm_of((WORK, PIX0, C0), BF16),
            shape_of((WORK, PIX0, M0), F32),
            shape_of((2, M0), F32),
        ],
        (WORK,),
        [full(2, C0)] * 5
        + [
            full(2, M0), full(2, M0 + 128), per_image(PIX0, M0), per_image(PIX1, C0),
            per_image(PIX0, M0), full(8, 128), full(2, CN), ANYWHERE, ANYWHERE,
        ],
        [full(2, C0), per_image(PIX0, C0), per_image(PIX0, M0), full(2, M0)],
        [vmem(M0, C0), DMA],
    )(
        meta, *s10, tot3, tot2, tot1, in_hbm(a2b), g0.reshape(WORK, PIX1, C0), in_hbm(z2b), hw, n0,
        *wa,
    )
    s11 = shared(st)
    middle = single(
        middle_grad,
        meta,
        far(src, src_there, b1, b1_there) + [(pin(e2r, st), False)] + near(other2, e1r, other1),
        [((16 * MIDDLE, 128), BF16, False)],
        limit=40,
    )[0]
    s11[0] = pin(s11[0], middle)
    tot11, d2, g1, st = call(
        last_two,
        [
            shape_of((2, M0), F32),
            hbm_of((WORK, PIX0, M0), BF16),
            shape_of((WORK, PIX0, M0), F32),
            shape_of((2, M0), F32),
        ],
        (WORK,),
        [full(2, M0)] * 5
        + [full(2, M0 + 128)]
        + [per_image(PIX0, M0)] * 3
        + [full(8, 128), full(2, CN), ANYWHERE, ANYWHERE],
        [full(2, M0), per_image(PIX0, M0), per_image(PIX0, M0), full(2, M0)],
        [vmem(9 * M0, M0), DMA],
    )(meta, *s11, tot2, tot1, in_hbm(z2b), g2, in_hbm(z1b), hw, n0, *wa)
    s12 = shared(st)
    front = call(
        front_grad_two,
        hbm_of((2 * C0 + 2 * 9 * M0 + 8 * M0, 128), BF16),
        (WORK,),
        [per_image(PIX0, M0)] * 3 + [per_image(PIX0, C0)],
        full(2 * C0 + 2 * 9 * M0 + 8 * M0, 128),
        [pltpu.VMEM((M0, 9 * M0), F32), pltpu.VMEM((M0, C0), F32)],
    )(meta, in_hbm(a1), in_hbm(d2), in_hbm(a2b), in_hbm(d3))
    sides = upper_sum(added(part_at(sides, high, 2), half_there))
    s12[0] = pin(s12[0], front, sides)
    made = single(
        last_three,
        meta,
        near(*s12, tot1) + far(z1b) + near(g1) + far(g0) + near(hw, n0),
        [((2, M0), F32, False)] + [((PIX0 + C0 // M0 * PIX1, M0), BF16, False)] * 4,
    )
    tot12, backs = made[0], over_levels(made[1:])

    last = [tot12]

    def after(value):
        return pin(value, last[0])

    def step(value):
        last[0] = value
        return value

    def half_sum(value, bit, got):
        return step(added(after(part_at(value, bit, 2)), got))

    def other_half(value, bit):
        return part_at(value, 1 - bit, 2)

    def joined(value, got):
        return step(lax.optimization_barrier(jnp.concatenate([after(value), got], axis=0)))

    one, two = place >> 1, place & 1
    middle = pin(middle, *s12[1:])
    middle_got = plane_turn(other_half(middle, one), 1)
    sides_got = plane_turn(pin(other_half(sides, one), *s12[1:]), 1)
    sides = half_sum(sides, one, sides_got)
    sides_got = plane_turn(other_half(sides, two), 2)
    middle = half_sum(middle, one, middle_got)
    middle_got = plane_turn(other_half(middle, two), 2)
    sides = half_sum(sides, two, sides_got)
    sides_got = xor_permute(sides, 8)
    backs[0] = after(backs[0])
    rows = front.shape[0]
    gx, front = call(
        leave,
        [shape_of((WORK, PIX0, C0), BF16), hbm_of((rows, 128), BF16)],
        (WORK,),
        [own_image(HB, WB, C0), ANYWHERE, ANYWHERE]
        + [full(PIX0 + C0 // M0 * PIX1, M0)] * 4
        + [ANYWHERE],
        [per_image(PIX0, C0), ANYWHERE],
        [vmem(C0, M0), pltpu.VMEM((C0, M0), F32), vmem(2 * C0, 128), DMA, DMA],
        aliases={8: 1},
    )(meta, images, *w1, *backs, front)
    step(front)
    front_got = swap_cores(other_half(front, core))
    middle = half_sum(middle, two, middle_got)
    middle_got = xor_permute(other_half(middle, low), 4)
    x_there = lax.ppermute(gx, "pipe", [(1, 0)])
    middle = half_sum(middle, low, middle_got)
    middle_got = xor_permute(other_half(middle, high), 8)
    front = half_sum(front, core, front_got)
    front_got = plane_turn(other_half(front, one), 1)
    sides = joined(sides, sides_got)
    sides_got = xor_permute(sides, 4)
    middle = upper_sum(half_sum(middle, high, middle_got))
    middle_got = xor_permute(middle, 8)
    front = half_sum(front, one, front_got)
    front_got = plane_turn(other_half(front, two), 2)
    sides = joined(sides, sides_got)
    sides_got = plane_turn(sides, 2)
    front = half_sum(front, two, front_got)
    front_got = xor_permute(other_half(front, low), 4)
    middle = joined(middle, middle_got)
    middle_got = xor_permute(middle, 4)
    sides = to_core(joined(sides, sides_got), 1)
    y_back = [y_out[0]] + [xor_permute(after(y_out[k]), 4 * k) for k in (1, 2, 3)]
    front = half_sum(front, low, front_got)
    front_got = xor_permute(other_half(front, high), 8)
    middle = joined(middle, middle_got)
    middle_got = plane_turn(middle, 2)
    front = upper_sum(half_sum(front, high, front_got))
    front_got = xor_permute(front, 8)
    front = joined(front, front_got)
    front_got = xor_permute(front, 4)

    whole = shape_of((GRAD_ROWS, 128), F32)
    block_at = lambda at: pl.BlockSpec((PACK_ROWS, 128), lambda s, meta: (s + at, 0))
    side_spec, mid_spec = full(8 * SIDES, 128), full(8 * MIDDLE, 128)
    middle = to_core(joined(middle, middle_got), 1)
    sides[0] = after(sides[0])
    steps = GRAD_ROWS // PACK_ROWS - 11
    grads = call(pack_sides, whole, (steps,), [side_spec] * 4, block_at(11), micros=8)(meta, *sides)
    step(grads)
    y_back = step(lax.optimization_barrier(jnp.stack([after(y_back[0])] + y_back[1:])))
    y_there = lax.ppermute(y_back, "pipe", [(0, 1)])
    front = joined(front, front_got)
    front_got = plane_turn(front, 2)
    strip = lambda s, meta: (0, s, 0)
    strip_y = lambda s, meta: (0, jnp.minimum(s, 7), 0)
    boundary = call(
        rows_out,
        shape_of((2 * WORK, HB * WB * C0), BF16),
        (HB,),
        [pl.BlockSpec((WORK, WB, C0), strip)] * 2
        + [pl.BlockSpec((WORK, WB // 2, C1), strip_y)] * 2,
        pl.BlockSpec((2 * WORK, WB * C0), lambda s, meta: (0, s)),
        micros=9,
    )(meta, after(gx), x_there, y_back, y_there)
    step(boundary)
    fronts = to_core(joined(front, front_got), 0)
    middle[0] = after(middle[0])
    grads = call(
        pack_rest, whole, (6,), [ANYWHERE] + [mid_spec] * 4, block_at(5), aliases={1: 0}
    )(meta, grads, *middle)
    front_rows = fronts[0].shape[0]
    grads = call(
        pack_front,
        whole,
        (5,),
        [ANYWHERE] + [mid_spec] * 4 + [full(front_rows, 128)] * 4,
        block_at(0),
        [pltpu.VMEM((4 * front_rows, 128), BF16)],
        aliases={1: 0},
    )(meta, grads, *middle, *fronts)
    weight_grads = grads.reshape(1, P_SIZE)

    def gain_shift(table, second=1):
        return jnp.concatenate([table[second : second + 1], table[0:1]], axis=0)

    line0 = jnp.concatenate(
        [gain_shift(tot12), gain_shift(tot11), gain_shift(tot10), jnp.zeros((2, CN - 1536), F32)],
        axis=1,
    )
    line1 = jnp.concatenate(
        [gain_shift(tot9), gain_shift(tot8), gain_shift(tot7), gain_shift(tot7, 2)], axis=1
    )
    line = jnp.where(first_core, line0, line1) + swap_cores(jnp.where(first_core, line1, line0))
    for bit in (4, 8):
        line = line + xor_permute(line, bit)

    return boundary[None], weight_grads, line[None]


def solution(mesh):
    placed_as = (
        P("dp", None, None, None),
        P("dp", None),
        P("dp"),
        P("pipe", None),
        P("pipe", None, None),
        P("dp", None, None, None),
    )
    return jax.shard_map(
        on_device,
        mesh=mesh,
        in_specs=placed_as,
        out_specs=(P("pipe", "dp", None), P("pipe", None), P("pipe", None, None)),
        check_vma=False,
    )
```

```python
import functools

import jax
import jax.numpy as jnp
from jax import lax
from jax.experimental import pallas as pl
from jax.experimental.pallas import tpu as pltpu
from jax.sharding import PartitionSpec as P

C0 = 1024
M0 = 256
M1 = 512
C1 = 2048
HB = 16
WB = 16
P_SIZE = 6029312
CN = 5120
WORK = 4
PIX0 = 256
PIX1 = 64
ROWS0 = WORK * PIX0
ROWS1 = WORK * PIX1
EPSILON = 1e-05
MIB = 1 << 20

F32 = jnp.float32
BF16 = jnp.bfloat16
CORE, PLANE, LEVEL, HIGH, WIDE = 4, 5, 6, 7, 11


def shape_of(dims, kind):
    return jax.ShapeDtypeStruct(dims, kind)


def hbm_of(dims, kind):
    return pltpu.HBM(dims, kind)


def dot_nn(left, right):
    return lax.dot_general(left, right, (((1,), (0,)), ((), ())), preferred_element_type=F32)


def dot_nt(left, right):
    return lax.dot_general(left, right, (((1,), (1,)), ((), ())), preferred_element_type=F32)


def dot_tn(left, right):
    return lax.dot_general(left, right, (((0,), (0,)), ((), ())), preferred_element_type=F32)


def over_lanes(column, width):
    return jnp.concatenate([column] * (width // 128), axis=1)


def pixel_mask(high, wide, breadth, rows):
    index = lax.broadcasted_iota(jnp.int32, (rows, 128), 0)
    row = (index >> (breadth.bit_length() - 1)).astype(F32)
    col = (index & (breadth - 1)).astype(F32)
    return jnp.where((row < high) & (col < wide), 1.0, 0.0)


def mask0(hw_ref, image):
    return pixel_mask(hw_ref[image : image + 1, :], hw_ref[4 + image : 5 + image, :], WB, PIX0)


def mask1(hw_ref, image):
    high, wide = hw_ref[image : image + 1, :] * 0.5, hw_ref[4 + image : 5 + image, :] * 0.5
    return pixel_mask(high, wide, WB // 2, PIX1)


def mask1_all(hw_ref, width):
    return over_lanes(jnp.concatenate([mask1(hw_ref, k) for k in range(WORK)], axis=0), width)


def sigmoid(values):
    return 1.0 / (1.0 + jnp.exp(-values))


def silu(values):
    return values * sigmoid(values)


def slope(values):
    sig = sigmoid(values)
    return sig * (1.0 + values * (1.0 - sig))


def total_rows(values):
    return jnp.sum(values, axis=0, keepdims=True)


def put_sums(ref, first, second):
    ref[0:1, :] = total_rows(first)
    ref[1:2, :] = total_rows(second)


def plane_total(refs):
    return (refs[0][...] + refs[1][...]) + (refs[2][...] + refs[3][...])


def mean_scale(table, count):
    mean = table[0:1, :] / count
    spread = table[1:2, :] / count - mean * mean
    return mean, lax.rsqrt(spread + EPSILON)


def count_of(tot_ref):
    return tot_ref[0:1, M0 : M0 + 1]


def side_columns(values, breadth):
    rows, width = values.shape
    column = lax.broadcasted_iota(jnp.int32, (rows, width), 0) & (breadth - 1)
    left = jnp.where(column == 0, 0.0, pltpu.roll(values, 1, 0))
    right = jnp.where(column == breadth - 1, 0.0, pltpu.roll(values, rows - 1, 0))
    return left, right


def later_rows(values, step, height, breadth):
    if step == 0:
        return values
    rows, width = values.shape
    images = values.reshape(rows // (height * breadth), height * breadth, width)
    gap = jnp.zeros((images.shape[0], breadth, width), values.dtype)
    if step > 0:
        moved = jnp.concatenate([gap, images[:, :-breadth]], axis=1)
    else:
        moved = jnp.concatenate([images[:, breadth:], gap], axis=1)
    return moved.reshape(rows, width)


def even_picker():
    row = lax.broadcasted_iota(jnp.int32, (PIX1, PIX0), 0)
    col = lax.broadcasted_iota(jnp.int32, (PIX1, PIX0), 1)
    return jnp.where(col == 32 * (row >> 3) + 2 * (row & 7), 1.0, 0.0).astype(BF16)


def even_placer():
    row = lax.broadcasted_iota(jnp.int32, (PIX0, PIX1), 0)
    col = lax.broadcasted_iota(jnp.int32, (PIX0, PIX1), 1)
    return jnp.where(row == 32 * (col >> 3) + 2 * (col & 7), 1.0, 0.0).astype(BF16)


def placed(values):
    placer = even_placer()
    high = values.astype(BF16)
    rest = (values - high.astype(F32)).astype(BF16)
    return dot_nn(placer, high) + dot_nn(placer, rest)


def call(body, outs, grid, in_specs, out_specs, scratch=(), limit=28, aliases={}, micros=5):
    size = int(micros * 3.6e6)
    return pl.pallas_call(
        body,
        out_shape=outs,
        grid_spec=pltpu.PrefetchScalarGridSpec(
            num_scalar_prefetch=1,
            grid=grid,
            in_specs=in_specs,
            out_specs=out_specs,
            scratch_shapes=list(scratch),
        ),
        input_output_aliases=aliases,
        cost_estimate=pl.CostEstimate(flops=0, bytes_accessed=size, transcendentals=0),
        compiler_params=pltpu.CompilerParams(vmem_limit_bytes=limit * MIB),
    )


ANYWHERE = pl.BlockSpec(memory_space=pltpu.HBM)
DMA = pltpu.SemaphoreType.DMA


def in_hbm(array):
    return pltpu.with_memory_space_constraint(array, pltpu.HBM)


def vmem(*dims):
    return pltpu.VMEM(dims, BF16)


def full(*dims):
    return pl.BlockSpec(dims, lambda *_: (0,) * len(dims), pipeline_mode=pl.Buffered(1))


def per_image(*dims):
    return pl.BlockSpec((1,) + dims, lambda s, meta: (s,) + (0,) * len(dims))


def own_image(*dims):
    return pl.BlockSpec((1,) + dims, lambda s, meta: (meta[s],) + (0,) * len(dims))


def single(body, meta, ins, outs, scratch=(), limit=28, micros=5):
    in_specs = [ANYWHERE if whole else full(*array.shape) for array, whole in ins]
    shapes = [(hbm_of if far else shape_of)(dims, kind) for dims, kind, far in outs]
    out_specs = [full(*dims) for dims, _, _ in outs]
    made = call(body, shapes, (1,), in_specs, out_specs, scratch, limit, micros=micros)
    return made(meta, *[array for array, _ in ins])


def near(*arrays):
    return [(array, False) for array in arrays]


def far(*arrays):
    return [(in_hbm(array), False) for array in arrays]


def weight(pair):
    return [(array, True) for array in pair]


W1 = (0, 0, C0, M0)
W2 = (0, 0, 9 * M0, M0)
W3 = (0, 2304, M0, C0)
V1 = (1, 0, C0, M1)
VS = (1, 2048, C0, C1)
V2 = (1, 0, 9 * M1, M1)
V3 = (1, 9216, M1, C1)


def fetch(meta, weight, own_ref, got_ref, here, sem, rows=None, cols=None):
    owner, base, height, width = weight
    first, some = rows or (0, height)
    left, wide = cols or (0, width)

    def start(ref):
        for k in range(wide // 256):
            source = ref.at[pl.ds(base + (left // 256 + k) * height + first, some)]
            pltpu.make_async_copy(source, here.at[:, pl.ds(256 * k, 256)], sem).start()

    pl.when(meta[CORE] == owner)(functools.partial(start, own_ref))
    pl.when(meta[CORE] != owner)(functools.partial(start, got_ref))


def await_copy(here, sem):
    pltpu.make_async_copy(here, here, sem).wait()


def enter(meta, x_ref, cot_ref, wa_ref, wb_ref, *refs):
    pays, evens, cots, w_ref, sem = refs[0:4], refs[4:8], refs[8:12], refs[12], refs[13]
    step = pl.program_id(0)

    @pl.when(step == 0)
    def _():
        fetch(meta, W1, wa_ref, wb_ref, w_ref, sem)
        await_copy(w_ref, sem)

    x = x_ref[0].reshape(PIX0, C0)
    z = dot_nn(x, w_ref[...])
    even = dot_nn(even_picker(), x).astype(BF16)
    row = lax.broadcasted_iota(jnp.int32, (16, M0), 0)
    high, wide = meta[HIGH + step].astype(F32), meta[WIDE + step].astype(F32)
    sizes = jnp.where(row == 0, high, jnp.where(row == 1, wide, 0.0))
    middle = total_rows(z) * (1.0 / PIX0)
    rest = middle
    for k in range(3):
        part = rest.astype(BF16).astype(F32)
        sizes = jnp.where(row == 2 + k, part, sizes)
        rest = rest - part
    z = z - middle
    for k in range(WORK):

        @pl.when(step == k)
        def _(k=k):
            pays[k][0:PIX0, :] = z.astype(BF16)
            pays[k][PIX0 : PIX0 + 16, :] = sizes.astype(BF16)
            evens[k][...] = even
            cots[k][...] = cot_ref[0].reshape(PIX1, C1)


def arrive(meta, *refs):
    pays, z_ref, z_far_ref, hw_ref, st_ref = refs[0:4], *refs[4:]
    first, second, count = 0.0, 0.0, 0.0
    for k in range(WORK):
        rows = pays[k][PIX0 : PIX0 + 16, :].astype(F32)
        sizes = rows[:, 0:128]
        hw_ref[k : k + 1, :] = sizes[0:1, :]
        hw_ref[4 + k : 5 + k, :] = sizes[1:2, :]
        count = count + sizes[0:1, :] * sizes[1:2, :]
        z = pays[k][0:PIX0, :].astype(F32) + ((rows[2:3, :] + rows[3:4, :]) + rows[4:5, :])
        z_ref[k] = z
        z_far_ref[k] = z
        zm = z * over_lanes(pixel_mask(sizes[0:1, :], sizes[1:2, :], WB, PIX0), M0)
        first = first + total_rows(zm)
        second = second + total_rows(zm * z)
    st_ref[0:1, :] = jnp.concatenate([first, count], axis=1)
    st_ref[1:2, :] = jnp.concatenate([second, count], axis=1)


def front_two(meta, *refs):
    stats, (z_ref, hw_ref, n_ref, wa_ref, wb_ref) = refs[0:4], refs[4:9]
    tot_ref, a1_ref, z2_ref, z2b_ref, st_ref, w_ref, act_ref, sem = refs[9:]
    fetch(meta, W2, wa_ref, wb_ref, w_ref, sem)
    table = plane_total(stats)
    tot_ref[...] = table
    mean, scale = mean_scale(table[:, :M0], count_of(tot_ref))
    act_ref[:, 0:WB, :] = jnp.zeros((2, WB, 3 * M0), BF16)
    act_ref[:, WB + PIX0 : 2 * WB + PIX0, :] = jnp.zeros((2, WB, 3 * M0), BF16)
    first, second = 0.0, 0.0
    for k in range(WORK):
        mask = over_lanes(mask0(hw_ref, k), M0)
        pre = (z_ref[k] - mean) * scale * n_ref[0:1, :M0] + n_ref[1:2, :M0]
        act = silu(pre) * mask
        left, right = side_columns(act, WB)
        wide = jnp.concatenate([left, act, right], axis=1).astype(BF16)
        act_ref[k % 2, WB : WB + PIX0, :] = wide
        a1_ref[k] = wide[:, M0 : 2 * M0]
        if k == 0:
            await_copy(w_ref, sem)
        z2 = dot_nn(act_ref[k % 2, 0:PIX0, :], w_ref[0 : 3 * M0, :])
        z2 = z2 + dot_nn(wide, w_ref[3 * M0 : 6 * M0, :])
        z2 = z2 + dot_nn(act_ref[k % 2, 2 * WB : 2 * WB + PIX0, :], w_ref[6 * M0 :, :])
        z2_ref[k] = z2
        z2b_ref[k] = z2
        zm = z2 * mask
        first = first + total_rows(zm)
        second = second + total_rows(zm * z2)
    st_ref[0:1, :] = first
    st_ref[1:2, :] = second


def front_three(meta, *refs):
    stats, (tot_ref, z2_ref, hw_ref, n_ref, wa_ref, wb_ref) = refs[0:4], refs[4:10]
    tot2_ref, a2_ref, a2b_ref, st_ref, w_ref, sem = refs[10:]
    fetch(meta, W3, wa_ref, wb_ref, w_ref, sem)
    table = plane_total(stats)
    tot2_ref[...] = table
    mean, scale = mean_scale(table, count_of(tot_ref))
    first, second = 0.0, 0.0
    for k in range(WORK):
        pre = (z2_ref[k] - mean) * scale * n_ref[0:1, M0 : 2 * M0] + n_ref[1:2, M0 : 2 * M0]
        act = (silu(pre) * over_lanes(mask0(hw_ref, k), M0)).astype(BF16)
        a2_ref[k] = act
        a2b_ref[k] = act
        if k == 0:
            await_copy(w_ref, sem)
        z3 = dot_nn(act, w_ref[...])
        first = first + total_rows(z3)
        second = second + total_rows(z3 * z3)
    st_ref[0:1, :] = first
    st_ref[1:2, :] = second


def even_picker():
    row = lax.broadcasted_iota(jnp.int32, (PIX1, PIX0), 0)
    col = lax.broadcasted_iota(jnp.int32, (PIX1, PIX0), 1)
    return jnp.where(col == 32 * (row >> 3) + 2 * (row & 7), 1.0, 0.0).astype(BF16)


def even_placer():
    row = lax.broadcasted_iota(jnp.int32, (PIX0, PIX1), 0)
    col = lax.broadcasted_iota(jnp.int32, (PIX0, PIX1), 1)
    return jnp.where(row == 32 * (col >> 3) + 2 * (col & 7), 1.0, 0.0).astype(BF16)


def placed(values):
    placer = even_placer()
    high = values.astype(BF16)
    rest = (values - high.astype(F32)).astype(BF16)
    return dot_nn(placer, high) + dot_nn(placer, rest)


SIDE_PART = C1 // 4


def join(meta, *refs):
    stats, (tot_ref, a2_ref), evens, (hw_ref, n_ref) = refs[0:4], refs[4:6], refs[6:10], refs[10:12]
    wa_ref, wb_ref = refs[12:14]
    tot3_ref, s_ref, p_ref, z3_ref, z1_ref, z1b_ref, zs_ref, st_ref, sts_ref = refs[14:23]
    w3_ref, w1_ref, ws_ref, sems = refs[23:]
    step = pl.program_id(0)

    @pl.when(step == 0)
    def _():
        fetch(meta, W3, wa_ref, wb_ref, w3_ref, sems.at[0])
        fetch(meta, V1, wa_ref, wb_ref, w1_ref, sems.at[1])
        for k in range(4):
            cols = (k * SIDE_PART, SIDE_PART)
            fetch(meta, VS, wa_ref, wb_ref, ws_ref.at[k], sems.at[2 + k], cols=cols)
        table = plane_total(stats)
        tot3_ref[...] = table
        mean, scale = mean_scale(table, count_of(tot_ref))
        picker = even_picker()
        await_copy(w3_ref, sems.at[0])
        for k in range(WORK):
            act = dot_nn(picker, a2_ref[k]).astype(BF16)
            z3 = dot_nn(act, w3_ref[...])
            here = slice(k * PIX1, (k + 1) * PIX1)
            z3_ref[here, :] = z3
            pre = (z3 - mean) * scale * n_ref[0:1, 2 * M0 : 2 * M0 + C0]
            pre = pre + n_ref[1:2, 2 * M0 : 2 * M0 + C0]
            pre = pre + evens[k][...].astype(F32)
            p_ref[here, :] = pre
            s_ref[here, :] = (silu(pre) * over_lanes(mask1(hw_ref, k), C0)).astype(BF16)
        await_copy(w1_ref, sems.at[1])
        z1 = dot_nn(s_ref[...], w1_ref[...])
        z1_ref[...] = z1
        z1b_ref[...] = z1
        put_sums(st_ref, z1, z1 * z1)

    for k in range(4):

        @pl.when(step == k)
        def _(k=k):
            await_copy(ws_ref.at[k], sems.at[2 + k])
            zs = dot_nn(s_ref[...], ws_ref[k])
            zs_ref[...] = zs
            put_sums(sts_ref, zs, zs * zs)


def fetch_conv(meta, wa_ref, wb_ref, w_ref, sems):
    for k in range(3):
        rows = (k * 3 * M1, 3 * M1)
        fetch(meta, V2, wa_ref, wb_ref, w_ref.at[pl.ds(*rows)], sems.at[k], rows=rows)


def await_conv(w_ref, sems, k):
    await_copy(w_ref.at[pl.ds(k * 3 * M1, 3 * M1)], sems.at[k])


def mid_one(meta, *refs):
    stats, (tot_ref, z1_ref, hw_ref, n_ref, wa_ref, wb_ref) = refs[0:4], refs[4:10]
    tot4_ref, a1_ref, z2_ref, z2b_ref, st_ref, w_ref, sems = refs[10:]
    fetch_conv(meta, wa_ref, wb_ref, w_ref, sems)
    table = plane_total(stats)
    tot4_ref[...] = table
    mean, scale = mean_scale(table, count_of(tot_ref) * 0.25)
    mask = mask1_all(hw_ref, M1)
    act = silu((z1_ref[...] - mean) * scale * n_ref[0:1, :M1] + n_ref[1:2, :M1]) * mask
    left, right = side_columns(act, WB // 2)
    wide = jnp.concatenate([left, act, right], axis=1).astype(BF16)
    a1_ref[...] = wide[:, M1 : 2 * M1]
    await_conv(w_ref, sems, 0)
    z2 = later_rows(dot_nn(wide, w_ref[0 : 3 * M1, :]), 1, HB // 2, WB // 2)
    await_conv(w_ref, sems, 1)
    z2 = z2 + dot_nn(wide, w_ref[3 * M1 : 6 * M1, :])
    await_conv(w_ref, sems, 2)
    z2 = z2 + later_rows(dot_nn(wide, w_ref[6 * M1 :, :]), -1, HB // 2, WB // 2)
    z2_ref[...] = z2
    z2b_ref[...] = z2
    zm = z2 * mask
    put_sums(st_ref, zm, zm * z2)


def mid_two(meta, *refs):
    stats, (tot_ref, z2_ref, hw_ref, n_ref, wa_ref, wb_ref) = refs[0:4], refs[4:10]
    tot5_ref, a2_ref, z3_ref, st_ref, w_ref, sem = refs[10:]
    fetch(meta, V3, wa_ref, wb_ref, w_ref, sem)
    table = plane_total(stats)
    tot5_ref[...] = table
    mean, scale = mean_scale(table, count_of(tot_ref) * 0.25)
    pre = (z2_ref[...] - mean) * scale * n_ref[0:1, M1 : 2 * M1] + n_ref[1:2, M1 : 2 * M1]
    act = (silu(pre) * mask1_all(hw_ref, M1)).astype(BF16)
    a2_ref[...] = act
    await_copy(w_ref, sem)
    z3 = dot_nn(act, w_ref[...])
    z3_ref[...] = z3
    put_sums(st_ref, z3, z3 * z3)


AT3, ATS = 2 * M1, 2 * M1 + C1


def turn(meta, *refs):
    stats, sides, (tot_ref, z3_ref, zs_ref, hw_ref, n_ref) = refs[0:4], refs[4:8], refs[8:13]
    cots, (tot6_ref, tots_ref), ys, (g_ref, st_ref) = refs[13:17], refs[17:19], refs[19:23], refs[23:]
    step = pl.program_id(0)

    @pl.when(step == 0)
    def _():
        tot6_ref[...] = plane_total(stats)
        tots_ref[...] = plane_total(sides)
        st_ref[...] = jnp.zeros_like(st_ref)

    count = count_of(tot_ref) * 0.25
    mean, scale = mean_scale(tot6_ref[...], count)
    mean_s, scale_s = mean_scale(tots_ref[...], count)
    normed = (z3_ref[0] - mean) * scale
    normed_s = (zs_ref[0] - mean_s) * scale_s
    pre = normed * n_ref[0:1, AT3:ATS] + n_ref[1:2, AT3:ATS]
    pre = pre + (normed_s * n_ref[0:1, ATS : ATS + C1] + n_ref[1:2, ATS : ATS + C1])
    sig = sigmoid(pre)
    value = pre * sig
    change = sig * (1.0 + pre * (1.0 - sig))
    for k in range(WORK):

        @pl.when(step == k)
        def _(k=k):
            mask = over_lanes(mask1(hw_ref, k), C1)
            ys[k][...] = (value * mask).astype(BF16)
            g_ref[0] = cots[k][...].astype(F32) * change * mask

    grad = g_ref[0]
    st_ref[0:1, :] += total_rows(grad)
    st_ref[1:2, :] += total_rows(grad * normed)
    st_ref[2:3, :] += total_rows(grad * normed_s)


def norm_back(grad, normed, scale, gain, first, second, mask):
    return (mask * (scale * gain) * (grad - first - normed * second)).astype(BF16)


def back_one(meta, *refs):
    stats, (tot6_ref, tots_ref, tot5_ref, tot_ref) = refs[0:4], refs[4:8]
    z3_ref, zs_ref, g_ref, z2_ref, hw_ref, n_ref, wa_ref, wb_ref = refs[8:16]
    tot7_ref, er_ref, es_ref, g2_ref, st_ref, w_ref, sem = refs[16:]
    fetch(meta, V3, wa_ref, wb_ref, w_ref, sem)
    table = plane_total(stats)
    tot7_ref[...] = table
    count = count_of(tot_ref) * 0.25
    table = table / count
    mask = mask1_all(hw_ref, C1)
    grad = g_ref[...]
    mean, scale = mean_scale(tot6_ref[...], count)
    normed = (z3_ref[...] - mean) * scale
    d3 = norm_back(grad, normed, scale, n_ref[0:1, AT3:ATS], table[0:1], table[1:2], mask)
    mean2, scale2 = mean_scale(tot5_ref[...], count)
    normed2 = (z2_ref[...] - mean2) * scale2
    pre2 = normed2 * n_ref[0:1, M1 : 2 * M1] + n_ref[1:2, M1 : 2 * M1]
    await_copy(w_ref, sem)
    g2 = dot_nt(d3, w_ref[...]) * mask[:, :M1] * slope(pre2)
    g2_ref[...] = g2
    put_sums(st_ref, g2, g2 * normed2)
    mean_s, scale_s = mean_scale(tots_ref[...], count)
    normed_s = (zs_ref[...] - mean_s) * scale_s
    ds = norm_back(grad, normed_s, scale_s, n_ref[0:1, ATS : ATS + C1], table[0:1], table[2:3], mask)
    es_ref[...] = ds
    half = C1 // 2
    for p in range(2):
        cols = slice(p * half, (p + 1) * half)
        er_ref[meta[CORE] ^ p] = jnp.concatenate([d3[:, cols], ds[:, cols]], axis=1)


def back_two(meta, *refs):
    stats, (tot5_ref, tot4_ref, tot_ref, z2_ref, g2_ref, z1_ref) = refs[0:4], refs[4:10]
    hw_ref, n_ref, wa_ref, wb_ref, tot8_ref, er_ref, g1_ref, st_ref, w_ref, sems = refs[10:]
    fetch_conv(meta, wa_ref, wb_ref, w_ref, sems)
    table = plane_total(stats)
    tot8_ref[...] = table
    count = count_of(tot_ref) * 0.25
    table = table / count
    mask = mask1_all(hw_ref, M1)
    mean, scale = mean_scale(tot5_ref[...], count)
    normed = (z2_ref[...] - mean) * scale
    d2 = norm_back(
        g2_ref[...], normed, scale, n_ref[0:1, M1 : 2 * M1], table[0:1], table[1:2], mask
    )
    for p in range(2):
        er_ref[meta[CORE] ^ p] = d2[:, p * (M1 // 2) : (p + 1) * (M1 // 2)]
    mean1, scale1 = mean_scale(tot4_ref[...], count)
    normed1 = (z1_ref[...] - mean1) * scale1
    pre1 = normed1 * n_ref[0:1, :M1] + n_ref[1:2, :M1]
    await_conv(w_ref, sems, 0)
    wide = later_rows(dot_nt(d2, w_ref[0 : 3 * M1, :]), -1, HB // 2, WB // 2)
    await_conv(w_ref, sems, 1)
    wide = wide + dot_nt(d2, w_ref[3 * M1 : 6 * M1, :])
    await_conv(w_ref, sems, 2)
    wide = wide + later_rows(dot_nt(d2, w_ref[6 * M1 :, :]), 1, HB // 2, WB // 2)
    left, _ = side_columns(wide[:, 2 * M1 :], WB // 2)
    _, right = side_columns(wide[:, :M1], WB // 2)
    g1 = (wide[:, M1 : 2 * M1] + left + right) * mask * slope(pre1)
    g1_ref[...] = g1
    put_sums(st_ref, g1, g1 * normed1)


def back_three(meta, *refs):
    stats, (tot4_ref, tot_ref, z1_ref, g1_ref, es_ref, tot3_ref, p_ref, z3_ref) = refs[0:4], refs[4:12]
    hw_ref, n_ref, wa_ref, wb_ref = refs[12:16]
    tot9_ref, er_ref, g0_ref, st_ref, w1_ref, ws_ref, sems = refs[16:]
    fetch(meta, V1, wa_ref, wb_ref, w1_ref, sems.at[0])
    fetch(meta, VS, wa_ref, wb_ref, ws_ref, sems.at[1])
    table = plane_total(stats)
    tot9_ref[...] = table
    count = count_of(tot_ref) * 0.25
    table = table / count
    mask = mask1_all(hw_ref, C0)
    mean, scale = mean_scale(tot4_ref[...], count)
    normed = (z1_ref[...] - mean) * scale
    d1 = norm_back(
        g1_ref[...], normed, scale, n_ref[0:1, :M1], table[0:1], table[1:2], mask[:, :M1]
    )
    for p in range(2):
        er_ref[meta[CORE] ^ p] = d1[:, p * (M1 // 2) : (p + 1) * (M1 // 2)]
    await_copy(w1_ref, sems.at[0])
    grad = dot_nt(d1, w1_ref[...])
    await_copy(ws_ref, sems.at[1])
    grad = grad + dot_nt(es_ref[...], ws_ref[...])
    grad = grad.astype(BF16).astype(F32)
    g0 = grad * slope(p_ref[...]) * mask
    g0_ref[...] = g0
    mean3, scale3 = mean_scale(tot3_ref[...], count * 4.0)
    put_sums(st_ref, g0, g0 * ((z3_ref[...] - mean3) * scale3))


def last_one(meta, *refs):
    stats, (tot3_ref, tot2_ref, tot_ref, a2_ref, g0_ref, z2_ref, hw_ref, n_ref) = refs[0:4], refs[4:12]
    wa_ref, wb_ref, tot10_ref, d3_ref, g2_ref, st_ref, w_ref, sem = refs[12:]
    step = pl.program_id(0)

    @pl.when(step == 0)
    def _():
        fetch(meta, W3, wa_ref, wb_ref, w_ref, sem)
        tot10_ref[...] = plane_total(stats)
        st_ref[...] = jnp.zeros_like(st_ref)
        await_copy(w_ref, sem)

    count = count_of(tot_ref)
    table = tot10_ref[...] / count
    mean, scale = mean_scale(tot3_ref[...], count)
    mean2, scale2 = mean_scale(tot2_ref[...], count)
    high = pl.ds(step, 1)
    wide = pl.ds(4 + step, 1)
    mask = over_lanes(pixel_mask(hw_ref[high, :], hw_ref[wide, :], WB, PIX0), C0)
    normed = (dot_nn(a2_ref[0], w_ref[...]) - mean) * scale
    grad = placed(g0_ref[0])
    gain = n_ref[0:1, 2 * M0 : 2 * M0 + C0]
    d3 = norm_back(grad, normed, scale, gain, table[0:1], table[1:2], mask)
    d3_ref[0] = d3
    normed2 = (z2_ref[0] - mean2) * scale2
    pre2 = normed2 * n_ref[0:1, M0 : 2 * M0] + n_ref[1:2, M0 : 2 * M0]
    g2 = dot_nt(d3, w_ref[...]) * mask[:, :M0] * slope(pre2)
    g2_ref[0] = g2
    st_ref[0:1, :] += total_rows(g2)
    st_ref[1:2, :] += total_rows(g2 * normed2)


def last_two(meta, *refs):
    stats, (tot2_ref, tot_ref, z2_ref, g2_ref, z1_ref, hw_ref, n_ref) = refs[0:4], refs[4:11]
    wa_ref, wb_ref, tot11_ref, d2_ref, g1_ref, st_ref, w_ref, sem = refs[11:]
    step = pl.program_id(0)

    @pl.when(step == 0)
    def _():
        fetch(meta, W2, wa_ref, wb_ref, w_ref, sem)
        tot11_ref[...] = plane_total(stats)
        st_ref[...] = jnp.zeros_like(st_ref)

    count = count_of(tot_ref)
    table = tot11_ref[...] / count
    mask = pixel_mask(hw_ref[pl.ds(step, 1), :], hw_ref[pl.ds(4 + step, 1), :], WB, PIX0)
    mask = over_lanes(mask, M0)
    mean2, scale2 = mean_scale(tot2_ref[...], count)
    normed2 = (z2_ref[0] - mean2) * scale2
    gain = n_ref[0:1, M0 : 2 * M0]
    d2 = norm_back(g2_ref[0], normed2, scale2, gain, table[0:1], table[1:2], mask)
    d2_ref[0] = d2
    mean1, scale1 = mean_scale(tot_ref[:, :M0], count)
    normed1 = (z1_ref[0] - mean1) * scale1
    pre1 = normed1 * n_ref[0:1, :M0] + n_ref[1:2, :M0]

    @pl.when(step == 0)
    def _():
        await_copy(w_ref, sem)

    wide = dot_nt(d2, w_ref[3 * M0 : 6 * M0, :])
    wide = wide + later_rows(dot_nt(d2, w_ref[0 : 3 * M0, :]), -1, HB, WB)
    wide = wide + later_rows(dot_nt(d2, w_ref[6 * M0 :, :]), 1, HB, WB)
    left, _ = side_columns(wide[:, 2 * M0 :], WB)
    _, right = side_columns(wide[:, :M0], WB)
    g1 = (wide[:, M0 : 2 * M0] + left + right) * mask * slope(pre1)
    g1_ref[0] = g1
    st_ref[0:1, :] += total_rows(g1)
    st_ref[1:2, :] += total_rows(g1 * normed1)


def last_three(meta, *refs):
    stats, (tot_ref, z1_ref, g1_ref, g0_ref, hw_ref, n_ref) = refs[0:4], refs[4:10]
    tot12_ref, backs = refs[10], refs[11:15]
    table = plane_total(stats)
    tot12_ref[...] = table
    count = count_of(tot_ref)
    table = table / count
    mean, scale = mean_scale(tot_ref[:, :M0], count)
    for k in range(WORK):
        mask = over_lanes(mask0(hw_ref, k), M0)
        normed = (z1_ref[k] - mean) * scale
        backs[k][0:PIX0, :] = norm_back(
            g1_ref[k], normed, scale, n_ref[0:1, :M0], table[0:1], table[1:2], mask
        )
        grad = g0_ref[k * PIX1 : (k + 1) * PIX1, :].astype(BF16)
        for part in range(C0 // M0):
            here = slice(PIX0 + part * PIX1, PIX0 + (part + 1) * PIX1)
            backs[k][here, :] = grad[:, part * M0 : (part + 1) * M0]


def leave(meta, x_ref, wa_ref, wb_ref, *refs):
    backs, gx_ref, out_ref = refs[0:4], refs[5], refs[6]
    w_ref, acc_ref, stage_ref, sem, out_sem = refs[7:]
    step = pl.program_id(0)

    @pl.when(step == 0)
    def _():
        fetch(meta, W1, wa_ref, wb_ref, w_ref, sem)
        acc_ref[...] = jnp.zeros_like(acc_ref)
        await_copy(w_ref, sem)

    for k in range(WORK):

        @pl.when(step == k)
        def _(k=k):
            d1 = backs[k][0:PIX0, :]
            grad = jnp.concatenate(
                [backs[k][PIX0 + n * PIX1 : PIX0 + (n + 1) * PIX1, :] for n in range(C0 // M0)], axis=1
            )
            acc_ref[...] += dot_tn(x_ref[0].reshape(PIX0, C0), d1)
            gx_ref[0] = (dot_nt(d1, w_ref[...]) + dot_nn(even_placer(), grad)).astype(BF16)

    @pl.when(step == WORK - 1)
    def _():
        put_tiles(stage_ref, 0, acc_ref[...])
        copy = pltpu.make_async_copy(stage_ref, out_ref.at[pl.ds(0, 2 * C0)], out_sem)
        copy.start()
        copy.wait()


def put_tiles(ref, start, values):
    rows, width = values.shape
    for k in range(width // 128):
        here = slice(start + k * rows, start + (k + 1) * rows)
        ref[here, :] = values[:, 128 * k : 128 * (k + 1)].astype(BF16)


def nine_shifts(delta, height, breadth):
    pieces = []
    left, right = side_columns(delta, breadth)
    for a in range(3):
        for moved in (right, delta, left):
            pieces.append(later_rows(moved, a - 1, height, breadth).astype(BF16))
    return jnp.concatenate(pieces, axis=1)


SIDES, MIDDLE = 768, 704
SWAPPED = (0, 2, 1, 3)


def place_of(core, chip):
    return jnp.where(core == 0, 2 * (chip & 1) + (chip >> 1), chip)


def spot_of(level):
    return 2 * (level & 1) + (level >> 1)


def put_shards(ref, shard, start, core, level_first, values):
    rows = values.shape[0] // 16
    values = values.astype(BF16)
    for chip in range(4):
        place = place_of(core, chip)
        for z in range(4):
            at = (SWAPPED[z] * 4 + place if level_first else place * 4 + SWAPPED[z]) * shard + start
            part = values[(4 * chip + z) * rows : (4 * chip + z + 1) * rows]
            for k in range(values.shape[1] // 128):
                here = pl.ds(pl.multiple_of(at + k * rows, 16), rows)
                ref[here, :] = part[:, 128 * k : 128 * (k + 1)]


def sides_grad(meta, sa_ref, sb_ref, la_ref, lb_ref, ea_ref, eb_ref, out_ref):
    half = C1 // 2
    side = dot_tn(sa_ref[...], ea_ref[0][:, half:]) + dot_tn(sb_ref[...], eb_ref[0][:, half:])
    put_shards(out_ref, SIDES, 0, meta[CORE], False, side)
    last = dot_tn(la_ref[...], ea_ref[0][:, :half]) + dot_tn(lb_ref[...], eb_ref[0][:, :half])
    put_shards(out_ref, SIDES, C0 // 2, meta[CORE], False, last)


def middle_grad(meta, sa_ref, sb_ref, la_ref, lb_ref, ma_ref, mb_ref, fa_ref, fb_ref, out_ref):
    conv = dot_tn(la_ref[...], nine_shifts(ma_ref[0].astype(F32), HB // 2, WB // 2))
    conv = conv + dot_tn(lb_ref[...], nine_shifts(mb_ref[0].astype(F32), HB // 2, WB // 2))
    put_shards(out_ref, MIDDLE, 0, meta[CORE], False, conv)
    first = dot_tn(sa_ref[...], fa_ref[0]) + dot_tn(sb_ref[...], fb_ref[0])
    put_shards(out_ref, MIDDLE, 9 * M1 // 8, meta[CORE], False, first)


def front_grad_two(meta, a1_ref, d2_ref, a2_ref, d3_ref, out_ref, acc2_ref, acc3_ref):
    slot = pl.program_id(0)
    conv = dot_tn(a1_ref[0], nine_shifts(d2_ref[0].astype(F32), HB, WB))
    last = dot_tn(a2_ref[0], d3_ref[0])

    @pl.when(slot == 0)
    def _():
        acc2_ref[...] = conv
        acc3_ref[...] = last

    @pl.when(slot > 0)
    def _():
        acc2_ref[...] += conv
        acc3_ref[...] += last

    @pl.when(slot == WORK - 1)
    def _():
        for tap in range(9):
            for tile in range(2):
                start = 2 * C0 + tile * 9 * M0 + tap * M0
                lanes = tap * M0 + tile * 128
                out_ref[start : start + M0, :] = acc2_ref[:, lanes : lanes + 128].astype(BF16)
        out_ref[0 : 2 * C0, :] = jnp.zeros((2 * C0, 128), BF16)
        put_tiles(out_ref, 2 * C0 + 2 * 9 * M0, acc3_ref[...])


def unpack_kernel(jobs, chunk, meta, raw_ref, out_ref, *refs):
    raws, flat_ref, sem_in, sem_out = refs[0:3], refs[3], refs[4], refs[5]
    stages = dict(zip(sorted({weight[3] for listed in jobs for _, weight in listed}), refs[6:]))

    def run(listed):
        loads, stores, waits, sizes = [], [], [], []
        for offset, (_, base, height, cols) in listed:
            for row in range(0, height, chunk // cols):
                some = min(chunk // cols, height - row)
                k = len(loads)
                source = raw_ref.at[:, pl.ds(offset + row * cols, some * cols)]
                here = raws[k % 3].at[:, pl.ds(0, some * cols)]
                loads.append(pltpu.make_async_copy(source, here, sem_in.at[k % 3]))
                stage = stages[cols].at[k % 2, pl.ds(0, some)]
                panels = []
                for panel in range(cols // 256):
                    there = out_ref.at[pl.ds(base + panel * height + row, some)]
                    lanes = stage.at[:, pl.ds(256 * panel, 256)]
                    panels.append(pltpu.make_async_copy(lanes, there, sem_out.at[k % 2]))
                stores.append(panels)
                waits.append(pltpu.make_async_copy(stage, stage, sem_out.at[k % 2]))
                sizes.append((some, cols))
        for load in loads[:2]:
            load.start()
        for k, (rows, cols) in enumerate(sizes):
            if k + 2 < len(sizes):
                loads[k + 2].start()
            loads[k].wait()
            flat_ref[:, : rows * cols] = raws[k % 3][:, : rows * cols].astype(F32)
            lines = flat_ref.reshape(chunk // 128, 128)
            if k >= 2:
                waits[k - 2].wait()
            for tile in range(cols // 128):
                values = lines[pl.ds(tile, rows, stride=cols // 128), :].astype(BF16)
                stages[cols][k % 2, 0:rows, tile * 128 : (tile + 1) * 128] = values
            for store in stores[k]:
                store.start()
        for wait in waits[-2:]:
            wait.wait()

    for core in range(2):
        if jobs[core]:
            pl.when(meta[CORE] == core)(functools.partial(run, jobs[core]))


def unpack(meta, packed, rows, jobs, micros, chunk=262144):
    widths = sorted({weight[3] for listed in jobs for _, weight in listed})
    return call(
        functools.partial(unpack_kernel, jobs, chunk),
        pltpu.HBM((rows, 256), BF16),
        (1,),
        [ANYWHERE],
        ANYWHERE,
        [pltpu.VMEM((1, chunk), BF16)] * 3
        + [pltpu.VMEM((1, chunk), F32), DMA((3,)), DMA((2,))]
        + [pltpu.VMEM((2, chunk // cols, cols), BF16) for cols in widths],
        micros=micros,
    )(meta, in_hbm(packed))


PACK_ROWS = 2048
GRAD_ROWS = P_SIZE // 128
ARRIVED = ((1, (0, 1)), (0, (0, 2)), (0, (1, 3)), (1, (2, 3)))


def quarters(bufs, target):
    found = []
    for buf, (p, masks) in zip(bufs, ARRIVED):
        if target == 0:
            p, masks = 1 - p, tuple(SWAPPED[m] for m in masks)
        for k, mask in enumerate(masks):
            found.append((p, mask, buf, k * (buf.shape[0] // 2)))
    return found


def pack_sides(meta, *refs):
    bufs, out_ref = refs[:4], refs[4]
    step = pl.program_id(0)
    level, plane = meta[LEVEL], meta[PLANE]

    @pl.when(meta[CORE] == 0)
    def _():
        out_ref[...] = jnp.zeros_like(out_ref)

    for p, mask, buf, start in quarters(bufs, 1):
        here = meta[CORE] == 1

        @pl.when(here & (step < 4) & (step == (plane ^ mask)))
        def _(p=p, buf=buf, start=start):
            for z in range(4):
                for k in range(8):
                    row = start + spot_of(level ^ z) * SIDES + C0 // 2 + 32 * k
                    rows = buf[pl.ds(pl.multiple_of(row, 32), 32), :].astype(F32)
                    out_ref[pl.ds(512 * z + 8 * p + k, 32, stride=16), :] = rows

        @pl.when(here & (step >= 4) & (((step - 4) >> 1) == (plane ^ mask)))
        def _(p=p, buf=buf, start=start):
            for j in range(2):
                z = 2 * (step & 1) + j
                for k in range(8):
                    row = start + spot_of(level ^ z) * SIDES + 64 * k
                    rows = buf[pl.ds(pl.multiple_of(row, 64), 64), :].astype(F32)
                    out_ref[pl.ds(1024 * j + 8 * p + k, 64, stride=16), :] = rows


def pack_middle(first_step, meta, *refs):
    bufs, out_ref = refs[1:5], refs[-1]
    step = pl.program_id(0) + first_step
    plane, level = meta[PLANE], meta[LEVEL]

    for p, mask, buf, start in quarters(bufs, 1):
        chip = plane ^ mask

        @pl.when((meta[CORE] == 1) & (step < 2) & (step == (chip >> 1)))
        def _(p=p, buf=buf, start=start, chip=chip):
            for z in range(4):
                for k in range(2):
                    row = start + spot_of(level ^ z) * MIDDLE + 9 * M1 // 8 + 64 * k
                    rows = buf[pl.ds(pl.multiple_of(row, 64), 64), :].astype(F32)
                    at = 256 * (4 * (chip & 1) + z) + 2 * p + k
                    out_ref[pl.ds(at, 64, stride=4), :] = rows

        @pl.when((meta[CORE] == 1) & (step > 1))
        def _(p=p, buf=buf, start=start, chip=chip):
            for z in range(4):
                for k in range(2):
                    row = start + spot_of(level ^ z) * MIDDLE + 64 * (step - 2) + 32 * k
                    rows = buf[pl.ds(pl.multiple_of(row, 32), 32), :].astype(F32)
                    at = 128 * (4 * chip + z) + 2 * p + k
                    out_ref[pl.ds(at, 32, stride=4), :] = rows


def pack_rest(meta, *refs):
    out_ref = refs[-1]

    @pl.when(meta[CORE] == 0)
    def _():
        out_ref[...] = jnp.zeros_like(out_ref)

    pack_middle(5, meta, *refs)


def pack_front(meta, *refs):
    fronts, out_ref, whole_ref = refs[5:9], refs[9], refs[10]
    step = pl.program_id(0)
    core, plane, level = meta[CORE], meta[PLANE], meta[LEVEL]
    part = fronts[0].shape[0] // 8

    @pl.when((core == 0) & (step == 0))
    def _():
        for p, mask, buf, start in quarters(fronts, 0):
            for z in range(4):
                there = (16 * p + 4 * place_of(p, plane ^ mask) + spot_of(level ^ z)) * part
                at = start + SWAPPED[z] * part
                rows = buf[at : at + part, :]
                whole_ref[pl.ds(pl.multiple_of(there, 16), part), :] = rows

    at2, at3 = 2 * C0, 2 * C0 + 2 * 9 * M0

    def piece(start, rows):
        return whole_ref[start : start + rows, :].astype(F32)

    @pl.when((core == 0) & (step == 0))
    def _():
        for tile in range(2):
            out_ref[pl.ds(tile, C0, stride=2), :] = piece(tile * C0, C0)

    for k in range(2):

        @pl.when((core == 0) & (step == 1 + k))
        def _(k=k):
            for tile in range(2):
                out_ref[pl.ds(tile, C0, stride=2), :] = piece(at2 + tile * 9 * M0 + k * C0, C0)

    @pl.when((core == 0) & (step == 3))
    def _():
        for tile in range(2):
            out_ref[pl.ds(tile, 256, stride=2), :] = piece(at2 + tile * 9 * M0 + 2 * C0, 256)
        for tile in range(8):
            out_ref[pl.ds(512 + tile, 192, stride=8), :] = piece(at3 + tile * 256, 192)

    @pl.when((core == 0) & (step == 4))
    def _():
        out_ref[...] = jnp.zeros_like(out_ref)
        for tile in range(8):
            out_ref[pl.ds(tile, 64, stride=8), :] = piece(at3 + tile * 256 + 192, 64)

    pack_middle(0, meta, *refs[:5], out_ref)


def rows_out(meta, x_ref, xg_ref, y_ref, yg_ref, out_ref):
    step = pl.program_id(0)
    row = lax.broadcasted_iota(jnp.int32, (128, 128), 0)
    col = lax.broadcasted_iota(jnp.int32, (128, 128), 1)

    def put(first, second, source):
        values = jnp.concatenate([first.reshape(-1, C0), second.reshape(-1, C0)], axis=0)
        mover = jnp.where(col == source, 1.0, 0.0).astype(BF16)
        moved = dot_nn(mover, values).astype(BF16)
        for k in range(16):
            out_ref[:, k * C0 : (k + 1) * C0] = moved[8 * k : 8 * (k + 1), :]

    image, stand = row & 7, row * 0
    for k in range(WORK):
        stand = jnp.where(image == meta[k], k, jnp.where(image == (meta[k] ^ 1), WORK + k, stand))

    @pl.when(meta[CORE] == 0)
    def _():
        put(x_ref[...], xg_ref[...], 16 * stand + (row >> 3))

    @pl.when((meta[CORE] == 1) & (step < HB // 2))
    def _():
        def split(ref):
            pieces = []
            for k in range(WORK):
                wide = ref[k].astype(F32)
                pieces += [wide[:, :C0], wide[:, C0:]]
            return jnp.concatenate(pieces, axis=0).astype(BF16)

        put(split(y_ref), split(yg_ref), 16 * stand + 8 * ((row >> 3) & 1) + (row >> 4))

    @pl.when((meta[CORE] == 1) & (step >= HB // 2))
    def _():
        out_ref[...] = jnp.zeros_like(out_ref)


def pin(value, *others):
    return lax.optimization_barrier((value,) + others)[0]


def swap_cores(value):
    return lax.ppermute(value, "pipe", [(0, 1), (1, 0)])


def xor_permute(value, mask):
    count = lax.axis_size("dp")
    return lax.ppermute(value, "dp", [(i, i ^ mask) for i in range(count)])


def upper_bits():
    return [bit for bit in (16, 32, 64, 128, 256, 512) if bit < lax.axis_size("dp")]


def plane_turn(value, turn_no):
    count = lax.axis_size("dp")
    pairs = []
    for p in range(2):
        mask = SWAPPED[turn_no] if p else turn_no
        pairs += [(p * count + i, p * count + (i ^ mask)) for i in range(count)]
    return lax.ppermute(value, ("pipe", "dp"), pairs)


def shared(value):
    for bit in upper_bits():
        value = value + xor_permute(value, bit)
    return [value] + [plane_turn(value, k) for k in (1, 2, 3)]


def over_levels(values):
    return [values[0]] + [xor_permute(values[k], 4 * k) for k in (1, 2, 3)]


def part_at(value, index, parts):
    rows = value.shape[0] // parts
    return lax.optimization_barrier(lax.dynamic_slice_in_dim(value, index * rows, rows, 0))


def added(*parts):
    total = parts[0].astype(F32)
    for part in parts[1:]:
        total = total + part.astype(F32)
    return total.astype(BF16)


def upper_sum(value):
    for bit in upper_bits():
        value = added(value, xor_permute(value, bit))
    return value


def to_core(both, target):
    count = lax.axis_size("dp")
    other = 1 - target
    close, away = (1, 2) if target == 1 else (2, 1)
    arrived = [both]
    for p, mask in ((other, 0), (other, close), (target, away)):
        pairs = [(p * count + i, target * count + (i ^ mask)) for i in range(count)]
        arrived.append(lax.ppermute(both, ("pipe", "dp"), pairs))
    return arrived


def on_device(images, extents, views, params, norms, cotangent):
    images, cotangent, params = in_hbm(images), in_hbm(cotangent), in_hbm(params)
    core = lax.axis_index("pipe")
    first_core = core == 0
    plane = lax.axis_index("dp") % 4
    level = (lax.axis_index("dp") // 4) % 4
    place = place_of(core, plane)

    pair = 2 * (level ^ jnp.arange(WORK, dtype=jnp.int32))
    hot = (pair[:, None] == jnp.arange(2 * WORK, dtype=jnp.int32)[None, :]).astype(jnp.int32)
    view = jnp.sum(hot * views[None, :], axis=1)
    order = pair + (view != core).astype(jnp.int32)
    hot = (order[:, None] == jnp.arange(2 * WORK, dtype=jnp.int32)[None, :]).astype(jnp.int32)
    sizes = jnp.sum(hot[:, :, None] * extents[None], axis=1)
    spot = jnp.stack([core, plane, level]).astype(jnp.int32)
    meta = jnp.concatenate([order, spot, sizes[:, 0], sizes[:, 1]]).astype(jnp.int32)

    w1 = unpack(meta, params, C0, ([(0, W1)], []), 3, 65536)
    w1 = (in_hbm(w1), in_hbm(lax.ppermute(w1, "pipe", [(0, 1)])))
    norms_there = swap_cores(norms[0])
    n0 = jnp.where(first_core, norms[0], norms_there)
    n1 = jnp.where(first_core, norms_there, norms[0])

    some = lambda dims, kind: [shape_of(dims, kind)] * WORK
    made = call(
        enter,
        some((PIX0 + 16, M0), BF16) + some((PIX1, C0), BF16) + some((PIX1, C1), BF16),
        (WORK,),
        [own_image(HB, WB, C0), own_image(HB // 2, WB // 2, C1), ANYWHERE, ANYWHERE],
        [full(PIX0 + 16, M0)] * 4 + [full(PIX1, C0)] * 4 + [full(PIX1, C1)] * 4,
        [vmem(C0, M0), DMA],
    )(meta, images, cotangent, *w1)
    pays, evens, cots = over_levels(made[0:4]), made[4:8], made[8:12]
    first_weights = unpack(
        meta,
        pin(params, made[0]),
        10240,
        ([(262144, W2), (851968, W3)], [(0, V1), (3932160, VS)]),
        8,
    )
    pays[0] = pin(pays[0], first_weights, norms_there)
    z1, z1b, hw, st = single(
        arrive,
        meta,
        near(*pays),
        [
            ((WORK, PIX0, M0), F32, False),
            ((WORK, PIX0, M0), F32, True),
            ((8, 128), F32, False),
            ((2, M0 + 128), F32, False),
        ],
    )

    s1 = shared(st)
    got = swap_cores(first_weights)
    evens = over_levels(evens)
    second_weights = unpack(
        meta, pin(params, st), 13312, ([], [(524288, V2), (2883584, V3)]), 10
    )
    s1[0] = pin(s1[0], got, evens[1], second_weights)
    wa = (in_hbm(first_weights), in_hbm(got))
    tot1, a1, z2, z2b, st = single(
        front_two,
        meta,
        near(*s1, z1, hw, n0) + weight(wa),
        [
            ((2, M0 + 128), F32, False),
            ((WORK, PIX0, M0), BF16, True),
            ((WORK, PIX0, M0), F32, False),
            ((WORK, PIX0, M0), F32, True),
            ((2, M0), F32, False),
        ],
        [vmem(9 * M0, M0), vmem(2, PIX0 + 2 * WB, 3 * M0), DMA],
    )
    s2 = shared(st)
    got = lax.ppermute(second_weights, "pipe", [(1, 0)])
    s2[0] = pin(s2[0], evens[2])
    tot2, a2, a2b, st = single(
        front_three,
        meta,
        near(*s2, tot1, z2, hw, n0) + weight(wa),
        [
            ((2, M0), F32, False),
            ((WORK, PIX0, M0), BF16, False),
            ((WORK, PIX0, M0), BF16, True),
            ((2, C0), F32, False),
        ],
        [vmem(M0, C0), DMA],
    )
    s3 = shared(st)
    cots = over_levels(cots)
    s3[0] = pin(s3[0], evens[3])

    tile = lambda s, meta: (0, s)
    tot3, src, p_even, z3_even, y1, y1b, ys, st, sts = call(
        join,
        [
            shape_of((2, C0), F32),
            hbm_of((ROWS1, C0), BF16),
            hbm_of((ROWS1, C0), F32),
            hbm_of((ROWS1, C0), F32),
            shape_of((ROWS1, M1), F32),
            hbm_of((ROWS1, M1), F32),
            hbm_of((ROWS1, C1), F32),
            shape_of((2, M1), F32),
            shape_of((2, C1), F32),
        ],
        (4,),
        [full(2, C0)] * 4
        + [full(2, M0 + 128), full(WORK, PIX0, M0)]
        + [full(PIX1, C0)] * 4
        + [full(8, 128), full(2, CN)]
        + [ANYWHERE] * 2,
        [
            full(2, C0),
            full(ROWS1, C0),
            full(ROWS1, C0),
            full(ROWS1, C0),
            full(ROWS1, M1),
            full(ROWS1, M1),
            pl.BlockSpec((ROWS1, SIDE_PART), tile),
            full(2, M1),
            pl.BlockSpec((2, SIDE_PART), tile),
        ],
        [vmem(M0, C0), vmem(C0, M1), vmem(4, C0, SIDE_PART), DMA((6,))],
    )(meta, *s3, tot1, a2, *evens, hw, n0, *wa)

    s4 = shared(st)
    src_there = swap_cores(src)
    s4[0] = pin(s4[0], got, src_there)
    wb = (in_hbm(second_weights), in_hbm(got))
    conv_scratch = [vmem(9 * M1, M1), DMA((3,))]
    last_scratch = [vmem(M1, C1), DMA]
    row = ((2, M1), F32, False)
    tot4, b1, y2, y2b, st = single(
        mid_one,
        meta,
        near(*s4, tot1, y1, hw, n1) + weight(wb),
        [row, ((ROWS1, M1), BF16, True), ((ROWS1, M1), F32, False), ((ROWS1, M1), F32, True), row],
        conv_scratch,
    )
    s5 = shared(st)
    b1_there = swap_cores(b1)
    t5 = shared(sts)
    s5[0] = pin(s5[0], cots[1], b1_there, *t5)
    tot5, b2, y3, st = single(
        mid_two,
        meta,
        near(*s5, tot1, y2, hw, n1) + weight(wb),
        [row, ((ROWS1, M1), BF16, True), ((ROWS1, C1), F32, False), ((2, C1), F32, False)],
        last_scratch,
    )
    s6 = shared(st)
    b2_there = swap_cores(b2)
    s6[0] = pin(s6[0], cots[2], cots[3], b2_there)
    made = call(
        turn,
        [shape_of((2, C1), F32)] * 2
        + some((PIX1, C1), BF16)
        + [shape_of((WORK, PIX1, C1), F32), shape_of((3, C1), F32)],
        (WORK,),
        [full(2, C1)] * 8
        + [full(2, M0 + 128), per_image(PIX1, C1), per_image(PIX1, C1), full(8, 128), full(2, CN)]
        + [full(PIX1, C1)] * 4,
        [full(2, C1)] * 2 + [full(PIX1, C1)] * 4 + [per_image(PIX1, C1), full(3, C1)],
    )(
        meta, *s6, *t5, tot1, y3.reshape(WORK, PIX1, C1), in_hbm(ys.reshape(WORK, PIX1, C1)), hw,
        n1, *cots,
    )
    tot6, tots, y_out, grad_y, st = made[0], made[1], made[2:6], made[6], made[7]
    grad_y = grad_y.reshape(ROWS1, C1)

    s7 = shared(st)
    tot7, er, es, g2, st = single(
        back_one,
        meta,
        near(*s7, tot6, tots, tot5, tot1, y3) + far(ys) + near(grad_y) + far(y2b)
        + near(hw, n1) + weight(wb),
        [
            ((3, C1), F32, False),
            ((2, ROWS1, C1), BF16, False),
            ((ROWS1, C1), BF16, False),
            ((ROWS1, M1), F32, False),
            row,
        ],
        last_scratch,
        limit=36,
    )
    s8 = shared(st)
    other = swap_cores(er[1:])
    s8[0] = pin(s8[0], other)
    low, high = level & 1, level >> 1
    tot8, e2r, g1, st = single(
        back_two,
        meta,
        near(*s8, tot5, tot4, tot1) + far(y2b) + near(g2) + far(y1b) + near(hw, n1) + weight(wb),
        [row, ((2, ROWS1, M1 // 2), BF16, False), ((ROWS1, M1), F32, False), row],
        conv_scratch,
    )
    s9 = shared(st)
    other2 = swap_cores(e2r[1:])
    sides = single(
        sides_grad,
        meta,
        far(src, src_there, b2, b2_there) + [(pin(er, st), False), (other, False)],
        [((16 * SIDES, 128), BF16, False)],
        limit=40,
    )[0]
    s9[0] = pin(s9[0], other2, sides)
    made = single(
        back_three,
        meta,
        near(*s9, tot4, tot1) + far(y1b) + near(g1, es, tot3) + far(p_even, z3_even)
        + near(hw, n1) + weight(wa),
        [row, ((2, ROWS1, M1 // 2), BF16, False), ((ROWS1, C0), F32, False), ((2, C0), F32, False)],
        [vmem(C0, M1), vmem(C0, C1), DMA((2,))],
    )
    tot9, e1r, g0, st = made

    s10 = shared(st)
    other1 = swap_cores(e1r[1:])
    y_back = [y_out[0], xor_permute(y_out[1], 4), xor_permute(y_out[2], 8)]
    s10[0] = pin(s10[0], other1, y_back[1])
    tot10, d3, g2, st = call(
        last_one,
        [
            shape_of((2, C0), F32),
            hbm_of((WORK, PIX0, C0), BF16),
            shape_of((WORK, PIX0, M0), F32),
            shape_of((2, M0), F32),
        ],
        (WORK,),
        [full(2, C0)] * 5
        + [
            full(2, M0), full(2, M0 + 128), per_image(PIX0, M0), per_image(PIX1, C0),
            per_image(PIX0, M0), full(8, 128), full(2, CN), ANYWHERE, ANYWHERE,
        ],
        [full(2, C0), per_image(PIX0, C0), per_image(PIX0, M0), full(2, M0)],
        [vmem(M0, C0), DMA],
    )(
        meta, *s10, tot3, tot2, tot1, in_hbm(a2b), g0.reshape(WORK, PIX1, C0), in_hbm(z2b), hw, n0,
        *wa,
    )
    s11 = shared(st)
    middle = single(
        middle_grad,
        meta,
        far(src, src_there, b1, b1_there) + [(pin(e2r, st), False)] + near(other2, e1r, other1),
        [((16 * MIDDLE, 128), BF16, False)],
        limit=40,
    )[0]
    y_back.append(xor_permute(pin(y_out[3], tot9), 12))
    s11[0] = pin(s11[0], middle, y_back[2])
    tot11, d2, g1, st = call(
        last_two,
        [
            shape_of((2, M0), F32),
            hbm_of((WORK, PIX0, M0), BF16),
            shape_of((WORK, PIX0, M0), F32),
            shape_of((2, M0), F32),
        ],
        (WORK,),
        [full(2, M0)] * 5
        + [full(2, M0 + 128)]
        + [per_image(PIX0, M0)] * 3
        + [full(8, 128), full(2, CN), ANYWHERE, ANYWHERE],
        [full(2, M0), per_image(PIX0, M0), per_image(PIX0, M0), full(2, M0)],
        [vmem(9 * M0, M0), DMA],
    )(meta, *s11, tot2, tot1, in_hbm(z2b), g2, in_hbm(z1b), hw, n0, *wa)
    s12 = shared(st)
    front = call(
        front_grad_two,
        hbm_of((2 * C0 + 2 * 9 * M0 + 8 * M0, 128), BF16),
        (WORK,),
        [per_image(PIX0, M0)] * 3 + [per_image(PIX0, C0)],
        full(2 * C0 + 2 * 9 * M0 + 8 * M0, 128),
        [pltpu.VMEM((M0, 9 * M0), F32), pltpu.VMEM((M0, C0), F32)],
    )(meta, in_hbm(a1), in_hbm(d2), in_hbm(a2b), in_hbm(d3))
    one, two = place >> 1, place & 1
    kept, sent = part_at(middle, one, 2), part_at(middle, 1 - one, 2)
    s12[0] = pin(s12[0], front, y_back[3], kept, sent)
    made = single(
        last_three,
        meta,
        near(*s12, tot1) + far(z1b) + near(g1) + far(g0) + near(hw, n0),
        [((2, M0), F32, False)] + [((PIX0 + C0 // M0 * PIX1, M0), BF16, False)] * 4,
    )
    tot12, backs = made[0], over_levels(made[1:])

    last = [tot12]

    def after(value):
        return pin(value, last[0])

    def step(value):
        last[0] = value
        return value

    def half_sum(value, bit, got):
        return step(added(after(part_at(value, bit, 2)), got))

    def other_half(value, bit):
        return part_at(value, 1 - bit, 2)

    def joined(value, got):
        return step(lax.optimization_barrier(jnp.concatenate([after(value), got], axis=0)))

    sides = pin(sides, *s12[1:])
    sides_got = plane_turn(other_half(sides, one), 1)
    sides = half_sum(sides, one, sides_got)
    sides_got = plane_turn(other_half(sides, two), 2)
    middle_got = plane_turn(after(sent), 1)
    y_back = step(lax.optimization_barrier(jnp.stack([after(y_back[0])] + y_back[1:])))
    y_there = lax.ppermute(y_back, "pipe", [(0, 1)])
    sides = half_sum(sides, two, sides_got)
    sides_got = xor_permute(other_half(sides, low), 4)
    backs[0] = after(backs[0])
    rows = front.shape[0]
    gx, front = call(
        leave,
        [shape_of((WORK, PIX0, C0), BF16), hbm_of((rows, 128), BF16)],
        (WORK,),
        [own_image(HB, WB, C0), ANYWHERE, ANYWHERE]
        + [full(PIX0 + C0 // M0 * PIX1, M0)] * 4
        + [ANYWHERE],
        [per_image(PIX0, C0), ANYWHERE],
        [vmem(C0, M0), pltpu.VMEM((C0, M0), F32), vmem(2 * C0, 128), DMA, DMA],
        aliases={8: 1},
    )(meta, images, *w1, *backs, front)
    step(front)
    front_got = swap_cores(other_half(front, core))
    x_there = lax.ppermute(gx, "pipe", [(1, 0)])
    sides = half_sum(sides, low, sides_got)
    sides_got = xor_permute(other_half(sides, high), 8)
    middle = step(added(after(kept), middle_got))
    middle_got = plane_turn(other_half(middle, two), 2)
    front = half_sum(front, core, front_got)
    front_got = plane_turn(other_half(front, one), 1)
    sides = upper_sum(half_sum(sides, high, sides_got))
    sides_got = xor_permute(sides, 8)
    middle = half_sum(middle, two, middle_got)
    middle_got = xor_permute(other_half(middle, low), 4)
    sides = joined(sides, sides_got)
    sides_got = xor_permute(sides, 4)
    front = half_sum(front, one, front_got)
    front_got = plane_turn(other_half(front, two), 2)
    middle = half_sum(middle, low, middle_got)
    middle_got = xor_permute(other_half(middle, high), 8)
    front = half_sum(front, two, front_got)
    front_got = xor_permute(other_half(front, low), 4)
    sides = joined(sides, sides_got)
    sides_got = plane_turn(sides, 2)
    middle = upper_sum(half_sum(middle, high, middle_got))
    middle_got = xor_permute(middle, 8)
    front = half_sum(front, low, front_got)
    front_got = xor_permute(other_half(front, high), 8)
    sides = to_core(joined(sides, sides_got), 1)
    middle = joined(middle, middle_got)
    middle_got = xor_permute(middle, 4)
    front = upper_sum(half_sum(front, high, front_got))
    front_got = xor_permute(front, 8)
    middle = joined(middle, middle_got)
    middle_got = plane_turn(middle, 2)
    front = joined(front, front_got)
    front_got = xor_permute(front, 4)
    strip = lambda s, meta: (0, s, 0)
    strip_y = lambda s, meta: (0, jnp.minimum(s, 7), 0)
    boundary = call(
        rows_out,
        shape_of((2 * WORK, HB * WB * C0), BF16),
        (HB,),
        [pl.BlockSpec((WORK, WB, C0), strip)] * 2
        + [pl.BlockSpec((WORK, WB // 2, C1), strip_y)] * 2,
        pl.BlockSpec((2 * WORK, WB * C0), lambda s, meta: (0, s)),
        micros=9,
    )(meta, after(gx), x_there, y_back, y_there)
    step(boundary)
    middle = joined(middle, middle_got)
    front = joined(front, front_got)
    front_got = plane_turn(front, 2)
    middle = to_core(middle, 1)

    whole = shape_of((GRAD_ROWS, 128), F32)
    block_at = lambda at: pl.BlockSpec((PACK_ROWS, 128), lambda s, meta: (s + at, 0))
    side_spec, mid_spec = full(8 * SIDES, 128), full(8 * MIDDLE, 128)
    steps = GRAD_ROWS // PACK_ROWS - 11
    sides[0] = after(sides[0])
    grads = call(pack_sides, whole, (steps,), [side_spec] * 4, block_at(11), micros=8)(meta, *sides)
    step(grads)
    fronts = to_core(joined(front, front_got), 0)
    middle[0] = after(middle[0])
    grads = call(
        pack_rest, whole, (6,), [ANYWHERE] + [mid_spec] * 4, block_at(5), aliases={1: 0}
    )(meta, grads, *middle)
    front_rows = fronts[0].shape[0]
    grads = call(
        pack_front,
        whole,
        (5,),
        [ANYWHERE] + [mid_spec] * 4 + [full(front_rows, 128)] * 4,
        block_at(0),
        [pltpu.VMEM((4 * front_rows, 128), BF16)],
        aliases={1: 0},
    )(meta, grads, *middle, *fronts)
    weight_grads = grads.reshape(1, P_SIZE)

    def gain_shift(table, second=1):
        return jnp.concatenate([table[second : second + 1], table[0:1]], axis=0)

    line0 = jnp.concatenate(
        [gain_shift(tot12), gain_shift(tot11), gain_shift(tot10), jnp.zeros((2, CN - 1536), F32)],
        axis=1,
    )
    line1 = jnp.concatenate(
        [gain_shift(tot9), gain_shift(tot8), gain_shift(tot7), gain_shift(tot7, 2)], axis=1
    )
    line = jnp.where(first_core, line0, line1) + swap_cores(jnp.where(first_core, line1, line0))
    for bit in (4, 8):
        line = line + xor_permute(line, bit)

    return boundary[None], weight_grads, line[None]


def solution(mesh):
    placed_as = (
        P("dp", None, None, None),
        P("dp", None),
        P("dp"),
        P("pipe", None),
        P("pipe", None, None),
        P("dp", None, None, None),
    )
    return jax.shard_map(
        on_device,
        mesh=mesh,
        in_specs=placed_as,
        out_specs=(P("pipe", "dp", None), P("pipe", None), P("pipe", None, None)),
        check_vma=False,
    )
```

```python
import functools

import jax
import jax.numpy as jnp
from jax import lax
from jax.experimental import pallas as pl
from jax.experimental.pallas import tpu as pltpu
from jax.sharding import PartitionSpec as P

C0 = 1024
M0 = 256
M1 = 512
C1 = 2048
HB = 16
WB = 16
P_SIZE = 6029312
CN = 5120
WORK = 4
PIX0 = 256
PIX1 = 64
ROWS0 = WORK * PIX0
ROWS1 = WORK * PIX1
EPSILON = 1e-05
MIB = 1 << 20

F32 = jnp.float32
BF16 = jnp.bfloat16
CORE, PLANE, LEVEL, HIGH, WIDE = 4, 5, 6, 7, 11


def shape_of(dims, kind):
    return jax.ShapeDtypeStruct(dims, kind)


def hbm_of(dims, kind):
    return pltpu.HBM(dims, kind)


def dot_nn(left, right):
    return lax.dot_general(left, right, (((1,), (0,)), ((), ())), preferred_element_type=F32)


def dot_nt(left, right):
    return lax.dot_general(left, right, (((1,), (1,)), ((), ())), preferred_element_type=F32)


def dot_tn(left, right):
    return lax.dot_general(left, right, (((0,), (0,)), ((), ())), preferred_element_type=F32)


def over_lanes(column, width):
    return jnp.concatenate([column] * (width // 128), axis=1)


def pixel_mask(high, wide, breadth, rows):
    index = lax.broadcasted_iota(jnp.int32, (rows, 128), 0)
    row = (index >> (breadth.bit_length() - 1)).astype(F32)
    col = (index & (breadth - 1)).astype(F32)
    return jnp.where((row < high) & (col < wide), 1.0, 0.0)


def mask0(hw_ref, image):
    return pixel_mask(hw_ref[image : image + 1, :], hw_ref[4 + image : 5 + image, :], WB, PIX0)


def mask1(hw_ref, image):
    high, wide = hw_ref[image : image + 1, :] * 0.5, hw_ref[4 + image : 5 + image, :] * 0.5
    return pixel_mask(high, wide, WB // 2, PIX1)


def mask1_all(hw_ref, width):
    return over_lanes(jnp.concatenate([mask1(hw_ref, k) for k in range(WORK)], axis=0), width)


def sigmoid(values):
    return 1.0 / (1.0 + jnp.exp(-values))


def silu(values):
    return values * sigmoid(values)


def slope(values):
    sig = sigmoid(values)
    return sig * (1.0 + values * (1.0 - sig))


def total_rows(values):
    return jnp.sum(values, axis=0, keepdims=True)


def put_sums(ref, first, second):
    ref[0:1, :] = total_rows(first)
    ref[1:2, :] = total_rows(second)


def plane_total(refs):
    return (refs[0][...] + refs[1][...]) + (refs[2][...] + refs[3][...])


def mean_scale(table, count):
    mean = table[0:1, :] / count
    spread = table[1:2, :] / count - mean * mean
    return mean, lax.rsqrt(spread + EPSILON)


def count_of(tot_ref):
    return tot_ref[0:1, M0 : M0 + 1]


def side_columns(values, breadth):
    rows, width = values.shape
    column = lax.broadcasted_iota(jnp.int32, (rows, width), 0) & (breadth - 1)
    left = jnp.where(column == 0, 0.0, pltpu.roll(values, 1, 0))
    right = jnp.where(column == breadth - 1, 0.0, pltpu.roll(values, rows - 1, 0))
    return left, right


def later_rows(values, step, height, breadth):
    if step == 0:
        return values
    rows, width = values.shape
    images = values.reshape(rows // (height * breadth), height * breadth, width)
    gap = jnp.zeros((images.shape[0], breadth, width), values.dtype)
    if step > 0:
        moved = jnp.concatenate([gap, images[:, :-breadth]], axis=1)
    else:
        moved = jnp.concatenate([images[:, breadth:], gap], axis=1)
    return moved.reshape(rows, width)


def even_picker():
    row = lax.broadcasted_iota(jnp.int32, (PIX1, PIX0), 0)
    col = lax.broadcasted_iota(jnp.int32, (PIX1, PIX0), 1)
    return jnp.where(col == 32 * (row >> 3) + 2 * (row & 7), 1.0, 0.0).astype(BF16)


def even_placer():
    row = lax.broadcasted_iota(jnp.int32, (PIX0, PIX1), 0)
    col = lax.broadcasted_iota(jnp.int32, (PIX0, PIX1), 1)
    return jnp.where(row == 32 * (col >> 3) + 2 * (col & 7), 1.0, 0.0).astype(BF16)


def placed(values):
    placer = even_placer()
    high = values.astype(BF16)
    rest = (values - high.astype(F32)).astype(BF16)
    return dot_nn(placer, high) + dot_nn(placer, rest)


def call(body, outs, grid, in_specs, out_specs, scratch=(), limit=28, aliases={}, micros=5):
    size = int(micros * 3.6e6)
    return pl.pallas_call(
        body,
        out_shape=outs,
        grid_spec=pltpu.PrefetchScalarGridSpec(
            num_scalar_prefetch=1,
            grid=grid,
            in_specs=in_specs,
            out_specs=out_specs,
            scratch_shapes=list(scratch),
        ),
        input_output_aliases=aliases,
        cost_estimate=pl.CostEstimate(flops=0, bytes_accessed=size, transcendentals=0),
        compiler_params=pltpu.CompilerParams(vmem_limit_bytes=limit * MIB),
    )


ANYWHERE = pl.BlockSpec(memory_space=pltpu.HBM)
DMA = pltpu.SemaphoreType.DMA


def in_hbm(array):
    return pltpu.with_memory_space_constraint(array, pltpu.HBM)


def vmem(*dims):
    return pltpu.VMEM(dims, BF16)


def full(*dims):
    return pl.BlockSpec(dims, lambda *_: (0,) * len(dims), pipeline_mode=pl.Buffered(1))


def per_image(*dims):
    return pl.BlockSpec((1,) + dims, lambda s, meta: (s,) + (0,) * len(dims))


def own_image(*dims):
    return pl.BlockSpec((1,) + dims, lambda s, meta: (meta[s],) + (0,) * len(dims))


def single(body, meta, ins, outs, scratch=(), limit=28, micros=5):
    in_specs = [ANYWHERE if whole else full(*array.shape) for array, whole in ins]
    shapes = [(hbm_of if far else shape_of)(dims, kind) for dims, kind, far in outs]
    out_specs = [full(*dims) for dims, _, _ in outs]
    made = call(body, shapes, (1,), in_specs, out_specs, scratch, limit, micros=micros)
    return made(meta, *[array for array, _ in ins])


def near(*arrays):
    return [(array, False) for array in arrays]


def far(*arrays):
    return [(in_hbm(array), False) for array in arrays]


def weight(pair):
    return [(array, True) for array in pair]


W1 = (0, 0, C0, M0)
W2 = (0, 0, 9 * M0, M0)
W3 = (0, 2304, M0, C0)
V1 = (1, 0, C0, M1)
VS = (1, 2048, C0, C1)
V2 = (1, 0, 9 * M1, M1)
V3 = (1, 9216, M1, C1)


def fetch(meta, weight, own_ref, got_ref, here, sem, rows=None, cols=None):
    owner, base, height, width = weight
    first, some = rows or (0, height)
    left, wide = cols or (0, width)

    def start(ref):
        for k in range(wide // 256):
            source = ref.at[pl.ds(base + (left // 256 + k) * height + first, some)]
            pltpu.make_async_copy(source, here.at[:, pl.ds(256 * k, 256)], sem).start()

    pl.when(meta[CORE] == owner)(functools.partial(start, own_ref))
    pl.when(meta[CORE] != owner)(functools.partial(start, got_ref))


def await_copy(here, sem):
    pltpu.make_async_copy(here, here, sem).wait()


def enter(meta, x_ref, cot_ref, wa_ref, wb_ref, *refs):
    pays, evens, cots, w_ref, sem = refs[0:4], refs[4:8], refs[8:12], refs[12], refs[13]
    step = pl.program_id(0)

    @pl.when(step == 0)
    def _():
        fetch(meta, W1, wa_ref, wb_ref, w_ref, sem)
        await_copy(w_ref, sem)

    x = x_ref[0].reshape(PIX0, C0)
    z = dot_nn(x, w_ref[...])
    even = dot_nn(even_picker(), x).astype(BF16)
    row = lax.broadcasted_iota(jnp.int32, (16, M0), 0)
    high, wide = meta[HIGH + step].astype(F32), meta[WIDE + step].astype(F32)
    sizes = jnp.where(row == 0, high, jnp.where(row == 1, wide, 0.0))
    middle = total_rows(z) * (1.0 / PIX0)
    rest = middle
    for k in range(3):
        part = rest.astype(BF16).astype(F32)
        sizes = jnp.where(row == 2 + k, part, sizes)
        rest = rest - part
    z = z - middle
    for k in range(WORK):

        @pl.when(step == k)
        def _(k=k):
            pays[k][0:PIX0, :] = z.astype(BF16)
            pays[k][PIX0 : PIX0 + 16, :] = sizes.astype(BF16)
            evens[k][...] = even
            cots[k][...] = cot_ref[0].reshape(PIX1, C1)


def arrive(meta, *refs):
    pays, z_ref, z_far_ref, hw_ref, st_ref = refs[0:4], *refs[4:]
    first, second, count = 0.0, 0.0, 0.0
    for k in range(WORK):
        rows = pays[k][PIX0 : PIX0 + 16, :].astype(F32)
        sizes = rows[:, 0:128]
        hw_ref[k : k + 1, :] = sizes[0:1, :]
        hw_ref[4 + k : 5 + k, :] = sizes[1:2, :]
        count = count + sizes[0:1, :] * sizes[1:2, :]
        z = pays[k][0:PIX0, :].astype(F32) + ((rows[2:3, :] + rows[3:4, :]) + rows[4:5, :])
        z_ref[k] = z
        z_far_ref[k] = z
        zm = z * over_lanes(pixel_mask(sizes[0:1, :], sizes[1:2, :], WB, PIX0), M0)
        first = first + total_rows(zm)
        second = second + total_rows(zm * z)
    st_ref[0:1, :] = jnp.concatenate([first, count], axis=1)
    st_ref[1:2, :] = jnp.concatenate([second, count], axis=1)


def front_two(meta, *refs):
    stats, (z_ref, hw_ref, n_ref, wa_ref, wb_ref) = refs[0:4], refs[4:9]
    tot_ref, a1_ref, z2_ref, z2b_ref, st_ref, w_ref, act_ref, sem = refs[9:]
    fetch(meta, W2, wa_ref, wb_ref, w_ref, sem)
    table = plane_total(stats)
    tot_ref[...] = table
    mean, scale = mean_scale(table[:, :M0], count_of(tot_ref))
    act_ref[:, 0:WB, :] = jnp.zeros((2, WB, 3 * M0), BF16)
    act_ref[:, WB + PIX0 : 2 * WB + PIX0, :] = jnp.zeros((2, WB, 3 * M0), BF16)
    first, second = 0.0, 0.0
    for k in range(WORK):
        mask = over_lanes(mask0(hw_ref, k), M0)
        pre = (z_ref[k] - mean) * scale * n_ref[0:1, :M0] + n_ref[1:2, :M0]
        act = silu(pre) * mask
        left, right = side_columns(act, WB)
        wide = jnp.concatenate([left, act, right], axis=1).astype(BF16)
        act_ref[k % 2, WB : WB + PIX0, :] = wide
        a1_ref[k] = wide[:, M0 : 2 * M0]
        if k == 0:
            await_copy(w_ref, sem)
        z2 = dot_nn(act_ref[k % 2, 0:PIX0, :], w_ref[0 : 3 * M0, :])
        z2 = z2 + dot_nn(wide, w_ref[3 * M0 : 6 * M0, :])
        z2 = z2 + dot_nn(act_ref[k % 2, 2 * WB : 2 * WB + PIX0, :], w_ref[6 * M0 :, :])
        z2_ref[k] = z2
        z2b_ref[k] = z2
        zm = z2 * mask
        first = first + total_rows(zm)
        second = second + total_rows(zm * z2)
    st_ref[0:1, :] = first
    st_ref[1:2, :] = second


def front_three(meta, *refs):
    stats, (tot_ref, z2_ref, hw_ref, n_ref, wa_ref, wb_ref) = refs[0:4], refs[4:10]
    tot2_ref, a2_ref, a2b_ref, st_ref, w_ref, sem = refs[10:]
    fetch(meta, W3, wa_ref, wb_ref, w_ref, sem)
    table = plane_total(stats)
    tot2_ref[...] = table
    mean, scale = mean_scale(table, count_of(tot_ref))
    first, second = 0.0, 0.0
    for k in range(WORK):
        pre = (z2_ref[k] - mean) * scale * n_ref[0:1, M0 : 2 * M0] + n_ref[1:2, M0 : 2 * M0]
        act = (silu(pre) * over_lanes(mask0(hw_ref, k), M0)).astype(BF16)
        a2_ref[k] = act
        a2b_ref[k] = act
        if k == 0:
            await_copy(w_ref, sem)
        z3 = dot_nn(act, w_ref[...])
        first = first + total_rows(z3)
        second = second + total_rows(z3 * z3)
    st_ref[0:1, :] = first
    st_ref[1:2, :] = second


def even_picker():
    row = lax.broadcasted_iota(jnp.int32, (PIX1, PIX0), 0)
    col = lax.broadcasted_iota(jnp.int32, (PIX1, PIX0), 1)
    return jnp.where(col == 32 * (row >> 3) + 2 * (row & 7), 1.0, 0.0).astype(BF16)


def even_placer():
    row = lax.broadcasted_iota(jnp.int32, (PIX0, PIX1), 0)
    col = lax.broadcasted_iota(jnp.int32, (PIX0, PIX1), 1)
    return jnp.where(row == 32 * (col >> 3) + 2 * (col & 7), 1.0, 0.0).astype(BF16)


def placed(values):
    placer = even_placer()
    high = values.astype(BF16)
    rest = (values - high.astype(F32)).astype(BF16)
    return dot_nn(placer, high) + dot_nn(placer, rest)


SIDE_PART = C1 // 4


def join(meta, *refs):
    stats, (tot_ref, a2_ref), evens, (hw_ref, n_ref) = refs[0:4], refs[4:6], refs[6:10], refs[10:12]
    wa_ref, wb_ref = refs[12:14]
    tot3_ref, s_ref, p_ref, z3_ref, z1_ref, z1b_ref, zs_ref, st_ref, sts_ref = refs[14:23]
    w3_ref, w1_ref, ws_ref, sems = refs[23:]
    step = pl.program_id(0)

    @pl.when(step == 0)
    def _():
        fetch(meta, W3, wa_ref, wb_ref, w3_ref, sems.at[0])
        fetch(meta, V1, wa_ref, wb_ref, w1_ref, sems.at[1])
        for k in range(4):
            cols = (k * SIDE_PART, SIDE_PART)
            fetch(meta, VS, wa_ref, wb_ref, ws_ref.at[k], sems.at[2 + k], cols=cols)
        table = plane_total(stats)
        tot3_ref[...] = table
        mean, scale = mean_scale(table, count_of(tot_ref))
        picker = even_picker()
        await_copy(w3_ref, sems.at[0])
        for k in range(WORK):
            act = dot_nn(picker, a2_ref[k]).astype(BF16)
            z3 = dot_nn(act, w3_ref[...])
            here = slice(k * PIX1, (k + 1) * PIX1)
            z3_ref[here, :] = z3
            pre = (z3 - mean) * scale * n_ref[0:1, 2 * M0 : 2 * M0 + C0]
            pre = pre + n_ref[1:2, 2 * M0 : 2 * M0 + C0]
            pre = pre + evens[k][...].astype(F32)
            p_ref[here, :] = pre
            s_ref[here, :] = (silu(pre) * over_lanes(mask1(hw_ref, k), C0)).astype(BF16)
        await_copy(w1_ref, sems.at[1])
        z1 = dot_nn(s_ref[...], w1_ref[...])
        z1_ref[...] = z1
        z1b_ref[...] = z1
        put_sums(st_ref, z1, z1 * z1)

    for k in range(4):

        @pl.when(step == k)
        def _(k=k):
            await_copy(ws_ref.at[k], sems.at[2 + k])
            zs = dot_nn(s_ref[...], ws_ref[k])
            zs_ref[...] = zs
            put_sums(sts_ref, zs, zs * zs)


def fetch_conv(meta, wa_ref, wb_ref, w_ref, sems):
    for k in range(3):
        rows = (k * 3 * M1, 3 * M1)
        fetch(meta, V2, wa_ref, wb_ref, w_ref.at[pl.ds(*rows)], sems.at[k], rows=rows)


def await_conv(w_ref, sems, k):
    await_copy(w_ref.at[pl.ds(k * 3 * M1, 3 * M1)], sems.at[k])


def mid_one(meta, *refs):
    stats, (tot_ref, z1_ref, hw_ref, n_ref, wa_ref, wb_ref) = refs[0:4], refs[4:10]
    tot4_ref, a1_ref, z2_ref, z2b_ref, st_ref, w_ref, sems = refs[10:]
    fetch_conv(meta, wa_ref, wb_ref, w_ref, sems)
    table = plane_total(stats)
    tot4_ref[...] = table
    mean, scale = mean_scale(table, count_of(tot_ref) * 0.25)
    mask = mask1_all(hw_ref, M1)
    act = silu((z1_ref[...] - mean) * scale * n_ref[0:1, :M1] + n_ref[1:2, :M1]) * mask
    left, right = side_columns(act, WB // 2)
    wide = jnp.concatenate([left, act, right], axis=1).astype(BF16)
    a1_ref[...] = wide[:, M1 : 2 * M1]
    await_conv(w_ref, sems, 0)
    z2 = later_rows(dot_nn(wide, w_ref[0 : 3 * M1, :]), 1, HB // 2, WB // 2)
    await_conv(w_ref, sems, 1)
    z2 = z2 + dot_nn(wide, w_ref[3 * M1 : 6 * M1, :])
    await_conv(w_ref, sems, 2)
    z2 = z2 + later_rows(dot_nn(wide, w_ref[6 * M1 :, :]), -1, HB // 2, WB // 2)
    z2_ref[...] = z2
    z2b_ref[...] = z2
    zm = z2 * mask
    put_sums(st_ref, zm, zm * z2)


def mid_two(meta, *refs):
    stats, (tot_ref, z2_ref, hw_ref, n_ref, wa_ref, wb_ref) = refs[0:4], refs[4:10]
    tot5_ref, a2_ref, z3_ref, st_ref, w_ref, sem = refs[10:]
    fetch(meta, V3, wa_ref, wb_ref, w_ref, sem)
    table = plane_total(stats)
    tot5_ref[...] = table
    mean, scale = mean_scale(table, count_of(tot_ref) * 0.25)
    pre = (z2_ref[...] - mean) * scale * n_ref[0:1, M1 : 2 * M1] + n_ref[1:2, M1 : 2 * M1]
    act = (silu(pre) * mask1_all(hw_ref, M1)).astype(BF16)
    a2_ref[...] = act
    await_copy(w_ref, sem)
    z3 = dot_nn(act, w_ref[...])
    z3_ref[...] = z3
    put_sums(st_ref, z3, z3 * z3)


AT3, ATS = 2 * M1, 2 * M1 + C1


def turn(meta, *refs):
    stats, sides, (tot_ref, z3_ref, zs_ref, hw_ref, n_ref) = refs[0:4], refs[4:8], refs[8:13]
    cots, (tot6_ref, tots_ref), ys = refs[13:17], refs[17:19], refs[19:23]
    g_ref, st_ref, cot_ref, y_ref = refs[23:]
    step = pl.program_id(0)

    @pl.when(step == 0)
    def _():
        tot6_ref[...] = plane_total(stats)
        tots_ref[...] = plane_total(sides)
        st_ref[...] = jnp.zeros_like(st_ref)

    count = count_of(tot_ref) * 0.25
    mean, scale = mean_scale(tot6_ref[...], count)
    mean_s, scale_s = mean_scale(tots_ref[...], count)
    normed = (z3_ref[0] - mean) * scale
    normed_s = (zs_ref[0] - mean_s) * scale_s
    pre = normed * n_ref[0:1, AT3:ATS] + n_ref[1:2, AT3:ATS]
    pre = pre + (normed_s * n_ref[0:1, ATS : ATS + C1] + n_ref[1:2, ATS : ATS + C1])
    sig = sigmoid(pre)
    for k in range(WORK):

        @pl.when(step == k)
        def _(k=k):
            cot_ref[...] = cots[k][...]

    high, wide = hw_ref[pl.ds(step, 1), :] * 0.5, hw_ref[pl.ds(4 + step, 1), :] * 0.5
    mask = over_lanes(pixel_mask(high, wide, WB // 2, PIX1), C1)
    y_ref[...] = (pre * sig * mask).astype(BF16)
    g_ref[0] = cot_ref[...].astype(F32) * (sig * (1.0 + pre * (1.0 - sig))) * mask
    for k in range(WORK):

        @pl.when(step == k)
        def _(k=k):
            ys[k][...] = y_ref[...]

    grad = g_ref[0]
    st_ref[0:1, :] += total_rows(grad)
    st_ref[1:2, :] += total_rows(grad * normed)
    st_ref[2:3, :] += total_rows(grad * normed_s)


def norm_back(grad, normed, scale, gain, first, second, mask):
    return (mask * (scale * gain) * (grad - first - normed * second)).astype(BF16)


def back_one(meta, *refs):
    stats, (tot6_ref, tots_ref, tot5_ref, tot_ref) = refs[0:4], refs[4:8]
    z3_ref, zs_ref, g_ref, z2_ref, hw_ref, n_ref, wa_ref, wb_ref = refs[8:16]
    tot7_ref, er_ref, es_ref, g2_ref, st_ref, w_ref, sem = refs[16:]
    fetch(meta, V3, wa_ref, wb_ref, w_ref, sem)
    table = plane_total(stats)
    tot7_ref[...] = table
    count = count_of(tot_ref) * 0.25
    table = table / count
    mask = mask1_all(hw_ref, C1)
    grad = g_ref[...]
    mean, scale = mean_scale(tot6_ref[...], count)
    normed = (z3_ref[...] - mean) * scale
    d3 = norm_back(grad, normed, scale, n_ref[0:1, AT3:ATS], table[0:1], table[1:2], mask)
    mean2, scale2 = mean_scale(tot5_ref[...], count)
    normed2 = (z2_ref[...] - mean2) * scale2
    pre2 = normed2 * n_ref[0:1, M1 : 2 * M1] + n_ref[1:2, M1 : 2 * M1]
    await_copy(w_ref, sem)
    g2 = dot_nt(d3, w_ref[...]) * mask[:, :M1] * slope(pre2)
    g2_ref[...] = g2
    put_sums(st_ref, g2, g2 * normed2)
    mean_s, scale_s = mean_scale(tots_ref[...], count)
    normed_s = (zs_ref[...] - mean_s) * scale_s
    ds = norm_back(grad, normed_s, scale_s, n_ref[0:1, ATS : ATS + C1], table[0:1], table[2:3], mask)
    es_ref[...] = ds
    half = C1 // 2
    for p in range(2):
        cols = slice(p * half, (p + 1) * half)
        er_ref[meta[CORE] ^ p] = jnp.concatenate([d3[:, cols], ds[:, cols]], axis=1)


def back_two(meta, *refs):
    stats, (tot5_ref, tot4_ref, tot_ref, z2_ref, g2_ref, z1_ref) = refs[0:4], refs[4:10]
    hw_ref, n_ref, wa_ref, wb_ref, tot8_ref, er_ref, g1_ref, st_ref, w_ref, sems = refs[10:]
    fetch_conv(meta, wa_ref, wb_ref, w_ref, sems)
    table = plane_total(stats)
    tot8_ref[...] = table
    count = count_of(tot_ref) * 0.25
    table = table / count
    mask = mask1_all(hw_ref, M1)
    mean, scale = mean_scale(tot5_ref[...], count)
    normed = (z2_ref[...] - mean) * scale
    d2 = norm_back(
        g2_ref[...], normed, scale, n_ref[0:1, M1 : 2 * M1], table[0:1], table[1:2], mask
    )
    for p in range(2):
        er_ref[meta[CORE] ^ p] = d2[:, p * (M1 // 2) : (p + 1) * (M1 // 2)]
    mean1, scale1 = mean_scale(tot4_ref[...], count)
    normed1 = (z1_ref[...] - mean1) * scale1
    pre1 = normed1 * n_ref[0:1, :M1] + n_ref[1:2, :M1]
    await_conv(w_ref, sems, 0)
    wide = later_rows(dot_nt(d2, w_ref[0 : 3 * M1, :]), -1, HB // 2, WB // 2)
    await_conv(w_ref, sems, 1)
    wide = wide + dot_nt(d2, w_ref[3 * M1 : 6 * M1, :])
    await_conv(w_ref, sems, 2)
    wide = wide + later_rows(dot_nt(d2, w_ref[6 * M1 :, :]), 1, HB // 2, WB // 2)
    left, _ = side_columns(wide[:, 2 * M1 :], WB // 2)
    _, right = side_columns(wide[:, :M1], WB // 2)
    g1 = (wide[:, M1 : 2 * M1] + left + right) * mask * slope(pre1)
    g1_ref[...] = g1
    put_sums(st_ref, g1, g1 * normed1)


def back_three(meta, *refs):
    stats, (tot4_ref, tot_ref, z1_ref, g1_ref, es_ref, tot3_ref, p_ref, z3_ref) = refs[0:4], refs[4:12]
    hw_ref, n_ref, wa_ref, wb_ref = refs[12:16]
    tot9_ref, er_ref, g0_ref, st_ref, w1_ref, ws_ref, sems = refs[16:]
    fetch(meta, V1, wa_ref, wb_ref, w1_ref, sems.at[0])
    fetch(meta, VS, wa_ref, wb_ref, ws_ref, sems.at[1])
    table = plane_total(stats)
    tot9_ref[...] = table
    count = count_of(tot_ref) * 0.25
    table = table / count
    mask = mask1_all(hw_ref, C0)
    mean, scale = mean_scale(tot4_ref[...], count)
    normed = (z1_ref[...] - mean) * scale
    d1 = norm_back(
        g1_ref[...], normed, scale, n_ref[0:1, :M1], table[0:1], table[1:2], mask[:, :M1]
    )
    for p in range(2):
        er_ref[meta[CORE] ^ p] = d1[:, p * (M1 // 2) : (p + 1) * (M1 // 2)]
    await_copy(w1_ref, sems.at[0])
    grad = dot_nt(d1, w1_ref[...])
    await_copy(ws_ref, sems.at[1])
    grad = grad + dot_nt(es_ref[...], ws_ref[...])
    grad = grad.astype(BF16).astype(F32)
    g0 = grad * slope(p_ref[...]) * mask
    g0_ref[...] = g0
    mean3, scale3 = mean_scale(tot3_ref[...], count * 4.0)
    put_sums(st_ref, g0, g0 * ((z3_ref[...] - mean3) * scale3))


def last_one(meta, *refs):
    stats, (tot3_ref, tot2_ref, tot_ref, a2_ref, g0_ref, z2_ref, hw_ref, n_ref) = refs[0:4], refs[4:12]
    wa_ref, wb_ref, tot10_ref, d3_ref, g2_ref, st_ref, w_ref, sem = refs[12:]
    step = pl.program_id(0)

    @pl.when(step == 0)
    def _():
        fetch(meta, W3, wa_ref, wb_ref, w_ref, sem)
        tot10_ref[...] = plane_total(stats)
        st_ref[...] = jnp.zeros_like(st_ref)
        await_copy(w_ref, sem)

    count = count_of(tot_ref)
    table = tot10_ref[...] / count
    mean, scale = mean_scale(tot3_ref[...], count)
    mean2, scale2 = mean_scale(tot2_ref[...], count)
    high = pl.ds(step, 1)
    wide = pl.ds(4 + step, 1)
    mask = over_lanes(pixel_mask(hw_ref[high, :], hw_ref[wide, :], WB, PIX0), C0)
    normed = (dot_nn(a2_ref[0], w_ref[...]) - mean) * scale
    grad = placed(g0_ref[0])
    gain = n_ref[0:1, 2 * M0 : 2 * M0 + C0]
    d3 = norm_back(grad, normed, scale, gain, table[0:1], table[1:2], mask)
    d3_ref[0] = d3
    normed2 = (z2_ref[0] - mean2) * scale2
    pre2 = normed2 * n_ref[0:1, M0 : 2 * M0] + n_ref[1:2, M0 : 2 * M0]
    g2 = dot_nt(d3, w_ref[...]) * mask[:, :M0] * slope(pre2)
    g2_ref[0] = g2
    st_ref[0:1, :] += total_rows(g2)
    st_ref[1:2, :] += total_rows(g2 * normed2)


def last_two(meta, *refs):
    stats, (tot2_ref, tot_ref, z2_ref, g2_ref, z1_ref, hw_ref, n_ref) = refs[0:4], refs[4:11]
    wa_ref, wb_ref, tot11_ref, d2_ref, g1_ref, st_ref, w_ref, sem = refs[11:]
    step = pl.program_id(0)

    @pl.when(step == 0)
    def _():
        fetch(meta, W2, wa_ref, wb_ref, w_ref, sem)
        tot11_ref[...] = plane_total(stats)
        st_ref[...] = jnp.zeros_like(st_ref)

    count = count_of(tot_ref)
    table = tot11_ref[...] / count
    mask = pixel_mask(hw_ref[pl.ds(step, 1), :], hw_ref[pl.ds(4 + step, 1), :], WB, PIX0)
    mask = over_lanes(mask, M0)
    mean2, scale2 = mean_scale(tot2_ref[...], count)
    normed2 = (z2_ref[0] - mean2) * scale2
    gain = n_ref[0:1, M0 : 2 * M0]
    d2 = norm_back(g2_ref[0], normed2, scale2, gain, table[0:1], table[1:2], mask)
    d2_ref[0] = d2
    mean1, scale1 = mean_scale(tot_ref[:, :M0], count)
    normed1 = (z1_ref[0] - mean1) * scale1
    pre1 = normed1 * n_ref[0:1, :M0] + n_ref[1:2, :M0]

    @pl.when(step == 0)
    def _():
        await_copy(w_ref, sem)

    wide = dot_nt(d2, w_ref[3 * M0 : 6 * M0, :])
    wide = wide + later_rows(dot_nt(d2, w_ref[0 : 3 * M0, :]), -1, HB, WB)
    wide = wide + later_rows(dot_nt(d2, w_ref[6 * M0 :, :]), 1, HB, WB)
    left, _ = side_columns(wide[:, 2 * M0 :], WB)
    _, right = side_columns(wide[:, :M0], WB)
    g1 = (wide[:, M0 : 2 * M0] + left + right) * mask * slope(pre1)
    g1_ref[0] = g1
    st_ref[0:1, :] += total_rows(g1)
    st_ref[1:2, :] += total_rows(g1 * normed1)


def last_three(meta, *refs):
    stats, (tot_ref, z1_ref, g1_ref, g0_ref, hw_ref, n_ref) = refs[0:4], refs[4:10]
    tot12_ref, backs = refs[10], refs[11:15]
    table = plane_total(stats)
    tot12_ref[...] = table
    count = count_of(tot_ref)
    table = table / count
    mean, scale = mean_scale(tot_ref[:, :M0], count)
    for k in range(WORK):
        mask = over_lanes(mask0(hw_ref, k), M0)
        normed = (z1_ref[k] - mean) * scale
        backs[k][0:PIX0, :] = norm_back(
            g1_ref[k], normed, scale, n_ref[0:1, :M0], table[0:1], table[1:2], mask
        )
        grad = g0_ref[k * PIX1 : (k + 1) * PIX1, :].astype(BF16)
        for part in range(C0 // M0):
            here = slice(PIX0 + part * PIX1, PIX0 + (part + 1) * PIX1)
            backs[k][here, :] = grad[:, part * M0 : (part + 1) * M0]


def leave(meta, x_ref, wa_ref, wb_ref, *refs):
    backs, gx_ref, out_ref = refs[0:4], refs[5], refs[6]
    w_ref, acc_ref, stage_ref, sem, out_sem = refs[7:]
    step = pl.program_id(0)

    @pl.when(step == 0)
    def _():
        fetch(meta, W1, wa_ref, wb_ref, w_ref, sem)
        acc_ref[...] = jnp.zeros_like(acc_ref)
        await_copy(w_ref, sem)

    for k in range(WORK):

        @pl.when(step == k)
        def _(k=k):
            d1 = backs[k][0:PIX0, :]
            grad = jnp.concatenate(
                [backs[k][PIX0 + n * PIX1 : PIX0 + (n + 1) * PIX1, :] for n in range(C0 // M0)], axis=1
            )
            acc_ref[...] += dot_tn(x_ref[0].reshape(PIX0, C0), d1)
            gx_ref[0] = (dot_nt(d1, w_ref[...]) + dot_nn(even_placer(), grad)).astype(BF16)

    @pl.when(step == WORK - 1)
    def _():
        put_tiles(stage_ref, 0, acc_ref[...])
        copy = pltpu.make_async_copy(stage_ref, out_ref.at[pl.ds(0, 2 * C0)], out_sem)
        copy.start()
        copy.wait()


def put_tiles(ref, start, values):
    rows, width = values.shape
    for k in range(width // 128):
        here = slice(start + k * rows, start + (k + 1) * rows)
        ref[here, :] = values[:, 128 * k : 128 * (k + 1)].astype(BF16)


def nine_shifts(delta, height, breadth):
    pieces = []
    left, right = side_columns(delta, breadth)
    for a in range(3):
        for moved in (right, delta, left):
            pieces.append(later_rows(moved, a - 1, height, breadth).astype(BF16))
    return jnp.concatenate(pieces, axis=1)


SIDES, MIDDLE = 768, 704
SWAPPED = (0, 2, 1, 3)


def place_of(core, chip):
    return jnp.where(core == 0, 2 * (chip & 1) + (chip >> 1), chip)


def spot_of(level):
    return 2 * (level & 1) + (level >> 1)


def put_shards(ref, shard, start, core, level_first, values):
    rows = values.shape[0] // 16
    values = values.astype(BF16)
    for chip in range(4):
        place = place_of(core, chip)
        for z in range(4):
            at = (SWAPPED[z] * 4 + place if level_first else place * 4 + SWAPPED[z]) * shard + start
            part = values[(4 * chip + z) * rows : (4 * chip + z + 1) * rows]
            for k in range(values.shape[1] // 128):
                here = pl.ds(pl.multiple_of(at + k * rows, 16), rows)
                ref[here, :] = part[:, 128 * k : 128 * (k + 1)]


def sides_grad(meta, sa_ref, sb_ref, la_ref, lb_ref, ea_ref, eb_ref, out_ref):
    half = C1 // 2
    side = dot_tn(sa_ref[...], ea_ref[0][:, half:]) + dot_tn(sb_ref[...], eb_ref[0][:, half:])
    put_shards(out_ref, SIDES, 0, meta[CORE], False, side)
    last = dot_tn(la_ref[...], ea_ref[0][:, :half]) + dot_tn(lb_ref[...], eb_ref[0][:, :half])
    put_shards(out_ref, SIDES, C0 // 2, meta[CORE], False, last)


def middle_grad(meta, sa_ref, sb_ref, la_ref, lb_ref, ma_ref, mb_ref, fa_ref, fb_ref, out_ref):
    conv = dot_tn(la_ref[...], nine_shifts(ma_ref[0].astype(F32), HB // 2, WB // 2))
    conv = conv + dot_tn(lb_ref[...], nine_shifts(mb_ref[0].astype(F32), HB // 2, WB // 2))
    put_shards(out_ref, MIDDLE, 0, meta[CORE], False, conv)
    first = dot_tn(sa_ref[...], fa_ref[0]) + dot_tn(sb_ref[...], fb_ref[0])
    put_shards(out_ref, MIDDLE, 9 * M1 // 8, meta[CORE], False, first)


def front_grad_two(meta, a1_ref, d2_ref, a2_ref, d3_ref, out_ref, acc2_ref, acc3_ref):
    slot = pl.program_id(0)
    conv = dot_tn(a1_ref[0], nine_shifts(d2_ref[0].astype(F32), HB, WB))
    last = dot_tn(a2_ref[0], d3_ref[0])

    @pl.when(slot == 0)
    def _():
        acc2_ref[...] = conv
        acc3_ref[...] = last

    @pl.when(slot > 0)
    def _():
        acc2_ref[...] += conv
        acc3_ref[...] += last

    @pl.when(slot == WORK - 1)
    def _():
        for tap in range(9):
            for tile in range(2):
                start = 2 * C0 + tile * 9 * M0 + tap * M0
                lanes = tap * M0 + tile * 128
                out_ref[start : start + M0, :] = acc2_ref[:, lanes : lanes + 128].astype(BF16)
        out_ref[0 : 2 * C0, :] = jnp.zeros((2 * C0, 128), BF16)
        put_tiles(out_ref, 2 * C0 + 2 * 9 * M0, acc3_ref[...])


def unpack_kernel(jobs, chunk, meta, raw_ref, out_ref, *refs):
    raws, flat_ref, sem_in, sem_out = refs[0:3], refs[3], refs[4], refs[5]
    stages = dict(zip(sorted({weight[3] for listed in jobs for _, weight in listed}), refs[6:]))

    def run(listed):
        loads, stores, waits, sizes = [], [], [], []
        for offset, (_, base, height, cols) in listed:
            for row in range(0, height, chunk // cols):
                some = min(chunk // cols, height - row)
                k = len(loads)
                source = raw_ref.at[:, pl.ds(offset + row * cols, some * cols)]
                here = raws[k % 3].at[:, pl.ds(0, some * cols)]
                loads.append(pltpu.make_async_copy(source, here, sem_in.at[k % 3]))
                stage = stages[cols].at[k % 2, pl.ds(0, some)]
                panels = []
                for panel in range(cols // 256):
                    there = out_ref.at[pl.ds(base + panel * height + row, some)]
                    lanes = stage.at[:, pl.ds(256 * panel, 256)]
                    panels.append(pltpu.make_async_copy(lanes, there, sem_out.at[k % 2]))
                stores.append(panels)
                waits.append(pltpu.make_async_copy(stage, stage, sem_out.at[k % 2]))
                sizes.append((some, cols))
        for load in loads[:2]:
            load.start()
        for k, (rows, cols) in enumerate(sizes):
            if k + 2 < len(sizes):
                loads[k + 2].start()
            loads[k].wait()
            flat_ref[:, : rows * cols] = raws[k % 3][:, : rows * cols].astype(F32)
            lines = flat_ref.reshape(chunk // 128, 128)
            if k >= 2:
                waits[k - 2].wait()
            for tile in range(cols // 128):
                values = lines[pl.ds(tile, rows, stride=cols // 128), :].astype(BF16)
                stages[cols][k % 2, 0:rows, tile * 128 : (tile + 1) * 128] = values
            for store in stores[k]:
                store.start()
        for wait in waits[-2:]:
            wait.wait()

    for core in range(2):
        if jobs[core]:
            pl.when(meta[CORE] == core)(functools.partial(run, jobs[core]))


def unpack(meta, packed, rows, jobs, micros, chunk=524288):
    widths = sorted({weight[3] for listed in jobs for _, weight in listed})
    return call(
        functools.partial(unpack_kernel, jobs, chunk),
        pltpu.HBM((rows, 256), BF16),
        (1,),
        [ANYWHERE],
        ANYWHERE,
        [pltpu.VMEM((1, chunk), BF16)] * 3
        + [pltpu.VMEM((1, chunk), F32), DMA((3,)), DMA((2,))]
        + [pltpu.VMEM((2, chunk // cols, cols), BF16) for cols in widths],
        micros=micros,
    )(meta, in_hbm(packed))


PACK_ROWS = 2048
GRAD_ROWS = P_SIZE // 128
ARRIVED = ((1, (0, 1)), (0, (0, 2)), (0, (1, 3)), (1, (2, 3)))


def quarters(bufs, target):
    found = []
    for buf, (p, masks) in zip(bufs, ARRIVED):
        if target == 0:
            p, masks = 1 - p, tuple(SWAPPED[m] for m in masks)
        for k, mask in enumerate(masks):
            found.append((p, mask, buf, k * (buf.shape[0] // 2)))
    return found


def pack_sides(meta, *refs):
    bufs, out_ref = refs[:4], refs[4]
    step = pl.program_id(0)
    level, plane = meta[LEVEL], meta[PLANE]

    @pl.when(meta[CORE] == 0)
    def _():
        out_ref[...] = jnp.zeros_like(out_ref)

    for p, mask, buf, start in quarters(bufs, 1):
        here = meta[CORE] == 1

        @pl.when(here & (step < 4) & (step == (plane ^ mask)))
        def _(p=p, buf=buf, start=start):
            for z in range(4):
                for k in range(8):
                    row = start + spot_of(level ^ z) * SIDES + C0 // 2 + 32 * k
                    rows = buf[pl.ds(pl.multiple_of(row, 32), 32), :].astype(F32)
                    out_ref[pl.ds(512 * z + 8 * p + k, 32, stride=16), :] = rows

        @pl.when(here & (step >= 4) & (((step - 4) >> 1) == (plane ^ mask)))
        def _(p=p, buf=buf, start=start):
            for j in range(2):
                z = 2 * (step & 1) + j
                for k in range(8):
                    row = start + spot_of(level ^ z) * SIDES + 64 * k
                    rows = buf[pl.ds(pl.multiple_of(row, 64), 64), :].astype(F32)
                    out_ref[pl.ds(1024 * j + 8 * p + k, 64, stride=16), :] = rows


def pack_middle(first_step, meta, *refs):
    bufs, out_ref = refs[1:5], refs[-1]
    step = pl.program_id(0) + first_step
    plane, level = meta[PLANE], meta[LEVEL]

    for p, mask, buf, start in quarters(bufs, 1):
        chip = plane ^ mask

        @pl.when((meta[CORE] == 1) & (step < 2) & (step == (chip >> 1)))
        def _(p=p, buf=buf, start=start, chip=chip):
            for z in range(4):
                for k in range(2):
                    row = start + spot_of(level ^ z) * MIDDLE + 9 * M1 // 8 + 64 * k
                    rows = buf[pl.ds(pl.multiple_of(row, 64), 64), :].astype(F32)
                    at = 256 * (4 * (chip & 1) + z) + 2 * p + k
                    out_ref[pl.ds(at, 64, stride=4), :] = rows

        @pl.when((meta[CORE] == 1) & (step > 1))
        def _(p=p, buf=buf, start=start, chip=chip):
            for z in range(4):
                for k in range(2):
                    row = start + spot_of(level ^ z) * MIDDLE + 64 * (step - 2) + 32 * k
                    rows = buf[pl.ds(pl.multiple_of(row, 32), 32), :].astype(F32)
                    at = 128 * (4 * chip + z) + 2 * p + k
                    out_ref[pl.ds(at, 32, stride=4), :] = rows


def pack_rest(meta, *refs):
    out_ref = refs[-1]

    @pl.when(meta[CORE] == 0)
    def _():
        out_ref[...] = jnp.zeros_like(out_ref)

    pack_middle(5, meta, *refs)


def pack_front(meta, *refs):
    fronts, out_ref, whole_ref = refs[5:9], refs[9], refs[10]
    step = pl.program_id(0)
    core, plane, level = meta[CORE], meta[PLANE], meta[LEVEL]
    part = fronts[0].shape[0] // 8

    @pl.when((core == 0) & (step == 0))
    def _():
        for p, mask, buf, start in quarters(fronts, 0):
            for z in range(4):
                there = (16 * p + 4 * place_of(p, plane ^ mask) + spot_of(level ^ z)) * part
                at = start + SWAPPED[z] * part
                rows = buf[at : at + part, :]
                whole_ref[pl.ds(pl.multiple_of(there, 16), part), :] = rows

    at2, at3 = 2 * C0, 2 * C0 + 2 * 9 * M0

    def piece(start, rows):
        return whole_ref[start : start + rows, :].astype(F32)

    @pl.when((core == 0) & (step == 0))
    def _():
        for tile in range(2):
            out_ref[pl.ds(tile, C0, stride=2), :] = piece(tile * C0, C0)

    for k in range(2):

        @pl.when((core == 0) & (step == 1 + k))
        def _(k=k):
            for tile in range(2):
                out_ref[pl.ds(tile, C0, stride=2), :] = piece(at2 + tile * 9 * M0 + k * C0, C0)

    @pl.when((core == 0) & (step == 3))
    def _():
        for tile in range(2):
            out_ref[pl.ds(tile, 256, stride=2), :] = piece(at2 + tile * 9 * M0 + 2 * C0, 256)
        for tile in range(8):
            out_ref[pl.ds(512 + tile, 192, stride=8), :] = piece(at3 + tile * 256, 192)

    @pl.when((core == 0) & (step == 4))
    def _():
        out_ref[...] = jnp.zeros_like(out_ref)
        for tile in range(8):
            out_ref[pl.ds(tile, 64, stride=8), :] = piece(at3 + tile * 256 + 192, 64)

    pack_middle(0, meta, *refs[:5], out_ref)


def rows_out(meta, x_ref, xg_ref, y_ref, yg_ref, out_ref):
    step = pl.program_id(0)
    row = lax.broadcasted_iota(jnp.int32, (128, 128), 0)
    col = lax.broadcasted_iota(jnp.int32, (128, 128), 1)

    def put(first, second, source):
        values = jnp.concatenate([first.reshape(-1, C0), second.reshape(-1, C0)], axis=0)
        mover = jnp.where(col == source, 1.0, 0.0).astype(BF16)
        moved = dot_nn(mover, values).astype(BF16)
        for k in range(16):
            out_ref[:, k * C0 : (k + 1) * C0] = moved[8 * k : 8 * (k + 1), :]

    image, stand = row & 7, row * 0
    for k in range(WORK):
        stand = jnp.where(image == meta[k], k, jnp.where(image == (meta[k] ^ 1), WORK + k, stand))

    @pl.when(meta[CORE] == 0)
    def _():
        put(x_ref[...], xg_ref[...], 16 * stand + (row >> 3))

    @pl.when((meta[CORE] == 1) & (step < HB // 2))
    def _():
        def split(ref):
            pieces = []
            for k in range(WORK):
                wide = ref[k].astype(F32)
                pieces += [wide[:, :C0], wide[:, C0:]]
            return jnp.concatenate(pieces, axis=0).astype(BF16)

        put(split(y_ref), split(yg_ref), 16 * stand + 8 * ((row >> 3) & 1) + (row >> 4))

    @pl.when((meta[CORE] == 1) & (step >= HB // 2))
    def _():
        out_ref[...] = jnp.zeros_like(out_ref)


def pin(value, *others):
    return lax.optimization_barrier((value,) + others)[0]


def swap_cores(value):
    return lax.ppermute(value, "pipe", [(0, 1), (1, 0)])


def xor_permute(value, mask):
    count = lax.axis_size("dp")
    return lax.ppermute(value, "dp", [(i, i ^ mask) for i in range(count)])


def upper_bits():
    return [bit for bit in (16, 32, 64, 128, 256, 512) if bit < lax.axis_size("dp")]


def plane_turn(value, turn_no):
    count = lax.axis_size("dp")
    pairs = []
    for p in range(2):
        mask = SWAPPED[turn_no] if p else turn_no
        pairs += [(p * count + i, p * count + (i ^ mask)) for i in range(count)]
    return lax.ppermute(value, ("pipe", "dp"), pairs)


def shared(value):
    for bit in upper_bits():
        value = value + xor_permute(value, bit)
    return [value] + [plane_turn(value, k) for k in (1, 2, 3)]


def over_levels(values):
    return [values[0]] + [xor_permute(values[k], 4 * k) for k in (1, 2, 3)]


def part_at(value, index, parts):
    rows = value.shape[0] // parts
    return lax.optimization_barrier(lax.dynamic_slice_in_dim(value, index * rows, rows, 0))


def added(*parts):
    total = parts[0].astype(F32)
    for part in parts[1:]:
        total = total + part.astype(F32)
    return total.astype(BF16)


def upper_sum(value):
    for bit in upper_bits():
        value = added(value, xor_permute(value, bit))
    return value


def to_core(both, target):
    count = lax.axis_size("dp")
    other = 1 - target
    close, away = (1, 2) if target == 1 else (2, 1)
    arrived = [both]
    for p, mask in ((other, 0), (other, close), (target, away)):
        pairs = [(p * count + i, target * count + (i ^ mask)) for i in range(count)]
        arrived.append(lax.ppermute(both, ("pipe", "dp"), pairs))
    return arrived


def on_device(images, extents, views, params, norms, cotangent):
    images, cotangent, params = in_hbm(images), in_hbm(cotangent), in_hbm(params)
    core = lax.axis_index("pipe")
    first_core = core == 0
    plane = lax.axis_index("dp") % 4
    level = (lax.axis_index("dp") // 4) % 4
    place = place_of(core, plane)

    pair = 2 * (level ^ jnp.arange(WORK, dtype=jnp.int32))
    hot = (pair[:, None] == jnp.arange(2 * WORK, dtype=jnp.int32)[None, :]).astype(jnp.int32)
    view = jnp.sum(hot * views[None, :], axis=1)
    order = pair + (view != core).astype(jnp.int32)
    hot = (order[:, None] == jnp.arange(2 * WORK, dtype=jnp.int32)[None, :]).astype(jnp.int32)
    sizes = jnp.sum(hot[:, :, None] * extents[None], axis=1)
    spot = jnp.stack([core, plane, level]).astype(jnp.int32)
    meta = jnp.concatenate([order, spot, sizes[:, 0], sizes[:, 1]]).astype(jnp.int32)

    w1 = unpack(meta, params, C0, ([(0, W1)], []), 3, 131072)
    w1 = (in_hbm(w1), in_hbm(lax.ppermute(w1, "pipe", [(0, 1)])))
    norms_there = swap_cores(norms[0])
    n0 = jnp.where(first_core, norms[0], norms_there)
    n1 = jnp.where(first_core, norms_there, norms[0])

    some = lambda dims, kind: [shape_of(dims, kind)] * WORK
    made = call(
        enter,
        some((PIX0 + 16, M0), BF16) + some((PIX1, C0), BF16) + some((PIX1, C1), BF16),
        (WORK,),
        [own_image(HB, WB, C0), own_image(HB // 2, WB // 2, C1), ANYWHERE, ANYWHERE],
        [full(PIX0 + 16, M0)] * 4 + [full(PIX1, C0)] * 4 + [full(PIX1, C1)] * 4,
        [vmem(C0, M0), DMA],
    )(meta, images, cotangent, *w1)
    pays, evens, cots = over_levels(made[0:4]), made[4:8], made[8:12]
    first_weights = unpack(
        meta,
        pin(params, made[0]),
        10240,
        ([(262144, W2), (851968, W3)], [(0, V1), (3932160, VS)]),
        8,
    )
    pays[0] = pin(pays[0], first_weights, norms_there)
    z1, z1b, hw, st = single(
        arrive,
        meta,
        near(*pays),
        [
            ((WORK, PIX0, M0), F32, False),
            ((WORK, PIX0, M0), F32, True),
            ((8, 128), F32, False),
            ((2, M0 + 128), F32, False),
        ],
    )

    s1 = shared(st)
    got = swap_cores(first_weights)
    evens = over_levels(evens)
    second_weights = unpack(
        meta, pin(params, st), 13312, ([], [(524288, V2), (2883584, V3)]), 10
    )
    s1[0] = pin(s1[0], got, evens[1], second_weights)
    wa = (in_hbm(first_weights), in_hbm(got))
    tot1, a1, z2, z2b, st = single(
        front_two,
        meta,
        near(*s1, z1, hw, n0) + weight(wa),
        [
            ((2, M0 + 128), F32, False),
            ((WORK, PIX0, M0), BF16, True),
            ((WORK, PIX0, M0), F32, False),
            ((WORK, PIX0, M0), F32, True),
            ((2, M0), F32, False),
        ],
        [vmem(9 * M0, M0), vmem(2, PIX0 + 2 * WB, 3 * M0), DMA],
    )
    s2 = shared(st)
    got = lax.ppermute(second_weights, "pipe", [(1, 0)])
    s2[0] = pin(s2[0], evens[2])
    tot2, a2, a2b, st = single(
        front_three,
        meta,
        near(*s2, tot1, z2, hw, n0) + weight(wa),
        [
            ((2, M0), F32, False),
            ((WORK, PIX0, M0), BF16, False),
            ((WORK, PIX0, M0), BF16, True),
            ((2, C0), F32, False),
        ],
        [vmem(M0, C0), DMA],
    )
    s3 = shared(st)
    cots = over_levels(cots)
    s3[0] = pin(s3[0], evens[3])

    tile = lambda s, meta: (0, s)
    tot3, src, p_even, z3_even, y1, y1b, ys, st, sts = call(
        join,
        [
            shape_of((2, C0), F32),
            hbm_of((ROWS1, C0), BF16),
            hbm_of((ROWS1, C0), F32),
            hbm_of((ROWS1, C0), F32),
            shape_of((ROWS1, M1), F32),
            hbm_of((ROWS1, M1), F32),
            hbm_of((ROWS1, C1), F32),
            shape_of((2, M1), F32),
            shape_of((2, C1), F32),
        ],
        (4,),
        [full(2, C0)] * 4
        + [full(2, M0 + 128), full(WORK, PIX0, M0)]
        + [full(PIX1, C0)] * 4
        + [full(8, 128), full(2, CN)]
        + [ANYWHERE] * 2,
        [
            full(2, C0),
            full(ROWS1, C0),
            full(ROWS1, C0),
            full(ROWS1, C0),
            full(ROWS1, M1),
            full(ROWS1, M1),
            pl.BlockSpec((ROWS1, SIDE_PART), tile),
            full(2, M1),
            pl.BlockSpec((2, SIDE_PART), tile),
        ],
        [vmem(M0, C0), vmem(C0, M1), vmem(4, C0, SIDE_PART), DMA((6,))],
    )(meta, *s3, tot1, a2, *evens, hw, n0, *wa)

    s4 = shared(st)
    src_there = swap_cores(src)
    s4[0] = pin(s4[0], got, src_there)
    wb = (in_hbm(second_weights), in_hbm(got))
    conv_scratch = [vmem(9 * M1, M1), DMA((3,))]
    last_scratch = [vmem(M1, C1), DMA]
    row = ((2, M1), F32, False)
    tot4, b1, y2, y2b, st = single(
        mid_one,
        meta,
        near(*s4, tot1, y1, hw, n1) + weight(wb),
        [row, ((ROWS1, M1), BF16, True), ((ROWS1, M1), F32, False), ((ROWS1, M1), F32, True), row],
        conv_scratch,
    )
    s5 = shared(st)
    b1_there = swap_cores(b1)
    t5 = shared(sts)
    s5[0] = pin(s5[0], cots[1], b1_there, *t5)
    tot5, b2, y3, st = single(
        mid_two,
        meta,
        near(*s5, tot1, y2, hw, n1) + weight(wb),
        [row, ((ROWS1, M1), BF16, True), ((ROWS1, C1), F32, False), ((2, C1), F32, False)],
        last_scratch,
    )
    s6 = shared(st)
    b2_there = swap_cores(b2)
    s6[0] = pin(s6[0], cots[2], cots[3], b2_there)
    made = call(
        turn,
        [shape_of((2, C1), F32)] * 2
        + some((PIX1, C1), BF16)
        + [shape_of((WORK, PIX1, C1), F32), shape_of((3, C1), F32)],
        (WORK,),
        [full(2, C1)] * 8
        + [full(2, M0 + 128), per_image(PIX1, C1), per_image(PIX1, C1), full(8, 128), full(2, CN)]
        + [full(PIX1, C1)] * 4,
        [full(2, C1)] * 2 + [full(PIX1, C1)] * 4 + [per_image(PIX1, C1), full(3, C1)],
        [vmem(PIX1, C1), vmem(PIX1, C1)],
    )(
        meta, *s6, *t5, tot1, y3.reshape(WORK, PIX1, C1), in_hbm(ys.reshape(WORK, PIX1, C1)), hw,
        n1, *cots,
    )
    tot6, tots, y_out, grad_y, st = made[0], made[1], made[2:6], made[6], made[7]
    grad_y = grad_y.reshape(ROWS1, C1)

    s7 = shared(st)
    tot7, er, es, g2, st = single(
        back_one,
        meta,
        near(*s7, tot6, tots, tot5, tot1, y3) + far(ys) + near(grad_y) + far(y2b)
        + near(hw, n1) + weight(wb),
        [
            ((3, C1), F32, False),
            ((2, ROWS1, C1), BF16, False),
            ((ROWS1, C1), BF16, False),
            ((ROWS1, M1), F32, False),
            row,
        ],
        last_scratch,
        limit=36,
    )
    s8 = shared(st)
    other = swap_cores(er[1:])
    s8[0] = pin(s8[0], other)
    low, high = level & 1, level >> 1
    tot8, e2r, g1, st = single(
        back_two,
        meta,
        near(*s8, tot5, tot4, tot1) + far(y2b) + near(g2) + far(y1b) + near(hw, n1) + weight(wb),
        [row, ((2, ROWS1, M1 // 2), BF16, False), ((ROWS1, M1), F32, False), row],
        conv_scratch,
    )
    s9 = shared(st)
    other2 = swap_cores(e2r[1:])
    sides = single(
        sides_grad,
        meta,
        far(src, src_there, b2, b2_there) + [(pin(er, st), False), (other, False)],
        [((16 * SIDES, 128), BF16, False)],
        limit=40,
    )[0]
    s9[0] = pin(s9[0], other2, sides)
    made = single(
        back_three,
        meta,
        near(*s9, tot4, tot1) + far(y1b) + near(g1, es, tot3) + far(p_even, z3_even)
        + near(hw, n1) + weight(wa),
        [row, ((2, ROWS1, M1 // 2), BF16, False), ((ROWS1, C0), F32, False), ((2, C0), F32, False)],
        [vmem(C0, M1), vmem(C0, C1), DMA((2,))],
    )
    tot9, e1r, g0, st = made

    s10 = shared(st)
    other1 = swap_cores(e1r[1:])
    y_back = [y_out[0], xor_permute(y_out[1], 4), xor_permute(y_out[2], 8)]
    s10[0] = pin(s10[0], other1, y_back[1])
    tot10, d3, g2, st = call(
        last_one,
        [
            shape_of((2, C0), F32),
            hbm_of((WORK, PIX0, C0), BF16),
            shape_of((WORK, PIX0, M0), F32),
            shape_of((2, M0), F32),
        ],
        (WORK,),
        [full(2, C0)] * 5
        + [
            full(2, M0), full(2, M0 + 128), per_image(PIX0, M0), per_image(PIX1, C0),
            per_image(PIX0, M0), full(8, 128), full(2, CN), ANYWHERE, ANYWHERE,
        ],
        [full(2, C0), per_image(PIX0, C0), per_image(PIX0, M0), full(2, M0)],
        [vmem(M0, C0), DMA],
    )(
        meta, *s10, tot3, tot2, tot1, in_hbm(a2b), g0.reshape(WORK, PIX1, C0), in_hbm(z2b), hw, n0,
        *wa,
    )
    s11 = shared(st)
    middle = single(
        middle_grad,
        meta,
        far(src, src_there, b1, b1_there) + [(pin(e2r, st), False)] + near(other2, e1r, other1),
        [((16 * MIDDLE, 128), BF16, False)],
        limit=40,
    )[0]
    y_back.append(xor_permute(pin(y_out[3], tot9), 12))
    s11[0] = pin(s11[0], middle, y_back[2])
    tot11, d2, g1, st = call(
        last_two,
        [
            shape_of((2, M0), F32),
            hbm_of((WORK, PIX0, M0), BF16),
            shape_of((WORK, PIX0, M0), F32),
            shape_of((2, M0), F32),
        ],
        (WORK,),
        [full(2, M0)] * 5
        + [full(2, M0 + 128)]
        + [per_image(PIX0, M0)] * 3
        + [full(8, 128), full(2, CN), ANYWHERE, ANYWHERE],
        [full(2, M0), per_image(PIX0, M0), per_image(PIX0, M0), full(2, M0)],
        [vmem(9 * M0, M0), DMA],
    )(meta, *s11, tot2, tot1, in_hbm(z2b), g2, in_hbm(z1b), hw, n0, *wa)
    s12 = shared(st)
    front = call(
        front_grad_two,
        hbm_of((2 * C0 + 2 * 9 * M0 + 8 * M0, 128), BF16),
        (WORK,),
        [per_image(PIX0, M0)] * 3 + [per_image(PIX0, C0)],
        full(2 * C0 + 2 * 9 * M0 + 8 * M0, 128),
        [pltpu.VMEM((M0, 9 * M0), F32), pltpu.VMEM((M0, C0), F32)],
    )(meta, in_hbm(a1), in_hbm(d2), in_hbm(a2b), in_hbm(d3))
    one, two = place >> 1, place & 1
    kept, sent = part_at(middle, one, 2), part_at(middle, 1 - one, 2)
    s12[0] = pin(s12[0], front, y_back[3], kept, sent)
    made = single(
        last_three,
        meta,
        near(*s12, tot1) + far(z1b) + near(g1) + far(g0) + near(hw, n0),
        [((2, M0), F32, False)] + [((PIX0 + C0 // M0 * PIX1, M0), BF16, False)] * 4,
    )
    tot12, backs = made[0], over_levels(made[1:])

    last = [tot12]

    def after(value):
        return pin(value, last[0])

    def step(value):
        last[0] = value
        return value

    def half_sum(value, bit, got):
        return step(added(after(part_at(value, bit, 2)), got))

    def other_half(value, bit):
        return part_at(value, 1 - bit, 2)

    def joined(value, got):
        return step(lax.optimization_barrier(jnp.concatenate([after(value), got], axis=0)))

    sides = pin(sides, *s12[1:])
    sides_got = plane_turn(other_half(sides, one), 1)
    sides = half_sum(sides, one, sides_got)
    sides_got = plane_turn(other_half(sides, two), 2)
    middle_got = plane_turn(after(sent), 1)
    y_back = step(lax.optimization_barrier(jnp.stack([after(y_back[0])] + y_back[1:])))
    y_there = lax.ppermute(y_back, "pipe", [(0, 1)])
    sides = half_sum(sides, two, sides_got)
    sides_got = xor_permute(other_half(sides, low), 4)
    backs[0] = after(backs[0])
    rows = front.shape[0]
    gx, front = call(
        leave,
        [shape_of((WORK, PIX0, C0), BF16), hbm_of((rows, 128), BF16)],
        (WORK,),
        [own_image(HB, WB, C0), ANYWHERE, ANYWHERE]
        + [full(PIX0 + C0 // M0 * PIX1, M0)] * 4
        + [ANYWHERE],
        [per_image(PIX0, C0), ANYWHERE],
        [vmem(C0, M0), pltpu.VMEM((C0, M0), F32), vmem(2 * C0, 128), DMA, DMA],
        aliases={8: 1},
    )(meta, images, *w1, *backs, front)
    step(front)
    front_got = swap_cores(other_half(front, core))
    x_there = lax.ppermute(gx, "pipe", [(1, 0)])
    sides = half_sum(sides, low, sides_got)
    sides_got = xor_permute(other_half(sides, high), 8)
    middle = step(added(after(kept), middle_got))
    middle_got = plane_turn(other_half(middle, two), 2)
    front = half_sum(front, core, front_got)
    front_got = plane_turn(other_half(front, one), 1)
    sides = upper_sum(half_sum(sides, high, sides_got))
    sides_got = xor_permute(sides, 8)
    middle = half_sum(middle, two, middle_got)
    middle_got = xor_permute(other_half(middle, low), 4)
    sides = joined(sides, sides_got)
    sides_got = xor_permute(sides, 4)
    front = half_sum(front, one, front_got)
    front_got = plane_turn(other_half(front, two), 2)
    middle = half_sum(middle, low, middle_got)
    middle_got = xor_permute(other_half(middle, high), 8)
    front = half_sum(front, two, front_got)
    front_got = xor_permute(other_half(front, low), 4)
    sides = joined(sides, sides_got)
    sides_got = plane_turn(sides, 2)
    middle = upper_sum(half_sum(middle, high, middle_got))
    middle_got = xor_permute(middle, 8)
    front = half_sum(front, low, front_got)
    front_got = xor_permute(other_half(front, high), 8)
    sides = to_core(joined(sides, sides_got), 1)
    middle = joined(middle, middle_got)
    middle_got = xor_permute(middle, 4)
    front = upper_sum(half_sum(front, high, front_got))
    front_got = xor_permute(front, 8)
    middle = joined(middle, middle_got)
    middle_got = plane_turn(middle, 2)
    front = joined(front, front_got)
    front_got = xor_permute(front, 4)
    strip = lambda s, meta: (0, s, 0)
    strip_y = lambda s, meta: (0, jnp.minimum(s, 7), 0)
    boundary = call(
        rows_out,
        shape_of((2 * WORK, HB * WB * C0), BF16),
        (HB,),
        [pl.BlockSpec((WORK, WB, C0), strip)] * 2
        + [pl.BlockSpec((WORK, WB // 2, C1), strip_y)] * 2,
        pl.BlockSpec((2 * WORK, WB * C0), lambda s, meta: (0, s)),
        micros=9,
    )(meta, after(gx), x_there, y_back, y_there)
    step(boundary)
    middle = to_core(joined(middle, middle_got), 1)
    front = joined(front, front_got)
    front_got = plane_turn(front, 2)

    whole = shape_of((GRAD_ROWS, 128), F32)
    block_at = lambda at: pl.BlockSpec((PACK_ROWS, 128), lambda s, meta: (s + at, 0))
    side_spec, mid_spec = full(8 * SIDES, 128), full(8 * MIDDLE, 128)
    steps = GRAD_ROWS // PACK_ROWS - 11
    sides[0] = after(sides[0])
    grads = call(pack_sides, whole, (steps,), [side_spec] * 4, block_at(11), micros=8)(meta, *sides)
    step(grads)
    fronts = to_core(joined(front, front_got), 0)
    middle[0] = after(middle[0])
    grads = call(
        pack_rest, whole, (6,), [ANYWHERE] + [mid_spec] * 4, block_at(5), aliases={1: 0}
    )(meta, grads, *middle)
    front_rows = fronts[0].shape[0]
    grads = call(
        pack_front,
        whole,
        (5,),
        [ANYWHERE] + [mid_spec] * 4 + [full(front_rows, 128)] * 4,
        block_at(0),
        [pltpu.VMEM((4 * front_rows, 128), BF16)],
        aliases={1: 0},
    )(meta, grads, *middle, *fronts)
    weight_grads = grads.reshape(1, P_SIZE)

    def gain_shift(table, second=1):
        return jnp.concatenate([table[second : second + 1], table[0:1]], axis=0)

    line0 = jnp.concatenate(
        [gain_shift(tot12), gain_shift(tot11), gain_shift(tot10), jnp.zeros((2, CN - 1536), F32)],
        axis=1,
    )
    line1 = jnp.concatenate(
        [gain_shift(tot9), gain_shift(tot8), gain_shift(tot7), gain_shift(tot7, 2)], axis=1
    )
    line = jnp.where(first_core, line0, line1) + swap_cores(jnp.where(first_core, line1, line0))
    for bit in (4, 8):
        line = line + xor_permute(line, bit)

    return boundary[None], weight_grads, line[None]


def solution(mesh):
    placed_as = (
        P("dp", None, None, None),
        P("dp", None),
        P("dp"),
        P("pipe", None),
        P("pipe", None, None),
        P("dp", None, None, None),
    )
    return jax.shard_map(
        on_device,
        mesh=mesh,
        in_specs=placed_as,
        out_specs=(P("pipe", "dp", None), P("pipe", None), P("pipe", None, None)),
        check_vma=False,
    )
```

```python
import functools

import jax
import jax.numpy as jnp
from jax import lax
from jax.experimental import pallas as pl
from jax.experimental.pallas import tpu as pltpu
from jax.sharding import PartitionSpec as P

C0 = 1024
M0 = 256
M1 = 512
C1 = 2048
HB = 16
WB = 16
P_SIZE = 6029312
CN = 5120
WORK = 4
PIX0 = 256
PIX1 = 64
ROWS0 = WORK * PIX0
ROWS1 = WORK * PIX1
EPSILON = 1e-05
MIB = 1 << 20

F32 = jnp.float32
BF16 = jnp.bfloat16
CORE, PLANE, LEVEL, HIGH, WIDE = 4, 5, 6, 7, 11


def shape_of(dims, kind):
    return jax.ShapeDtypeStruct(dims, kind)


def hbm_of(dims, kind):
    return pltpu.HBM(dims, kind)


def dot_nn(left, right):
    return lax.dot_general(left, right, (((1,), (0,)), ((), ())), preferred_element_type=F32)


def dot_nt(left, right):
    return lax.dot_general(left, right, (((1,), (1,)), ((), ())), preferred_element_type=F32)


def dot_tn(left, right):
    return lax.dot_general(left, right, (((0,), (0,)), ((), ())), preferred_element_type=F32)


def over_lanes(column, width):
    return jnp.concatenate([column] * (width // 128), axis=1)


def pixel_mask(high, wide, breadth, rows):
    index = lax.broadcasted_iota(jnp.int32, (rows, 128), 0)
    row = (index >> (breadth.bit_length() - 1)).astype(F32)
    col = (index & (breadth - 1)).astype(F32)
    return jnp.where((row < high) & (col < wide), 1.0, 0.0)


def mask0(hw_ref, image):
    return pixel_mask(hw_ref[image : image + 1, :], hw_ref[4 + image : 5 + image, :], WB, PIX0)


def mask1(hw_ref, image):
    high, wide = hw_ref[image : image + 1, :] * 0.5, hw_ref[4 + image : 5 + image, :] * 0.5
    return pixel_mask(high, wide, WB // 2, PIX1)


def mask1_all(hw_ref, width):
    return over_lanes(jnp.concatenate([mask1(hw_ref, k) for k in range(WORK)], axis=0), width)


def sigmoid(values):
    return 1.0 / (1.0 + jnp.exp(-values))


def silu(values):
    return values * sigmoid(values)


def slope(values):
    sig = sigmoid(values)
    return sig * (1.0 + values * (1.0 - sig))


def total_rows(values):
    return jnp.sum(values, axis=0, keepdims=True)


def put_sums(ref, first, second):
    ref[0:1, :] = total_rows(first)
    ref[1:2, :] = total_rows(second)


def plane_total(refs):
    return (refs[0][...] + refs[1][...]) + (refs[2][...] + refs[3][...])


def mean_scale(table, count):
    mean = table[0:1, :] / count
    spread = table[1:2, :] / count - mean * mean
    return mean, lax.rsqrt(spread + EPSILON)


def count_of(tot_ref):
    return tot_ref[0:1, M0 : M0 + 1]


def side_columns(values, breadth):
    rows, width = values.shape
    column = lax.broadcasted_iota(jnp.int32, (rows, width), 0) & (breadth - 1)
    left = jnp.where(column == 0, 0.0, pltpu.roll(values, 1, 0))
    right = jnp.where(column == breadth - 1, 0.0, pltpu.roll(values, rows - 1, 0))
    return left, right


def later_rows(values, step, height, breadth):
    if step == 0:
        return values
    rows, width = values.shape
    images = values.reshape(rows // (height * breadth), height * breadth, width)
    gap = jnp.zeros((images.shape[0], breadth, width), values.dtype)
    if step > 0:
        moved = jnp.concatenate([gap, images[:, :-breadth]], axis=1)
    else:
        moved = jnp.concatenate([images[:, breadth:], gap], axis=1)
    return moved.reshape(rows, width)


def even_picker():
    row = lax.broadcasted_iota(jnp.int32, (PIX1, PIX0), 0)
    col = lax.broadcasted_iota(jnp.int32, (PIX1, PIX0), 1)
    return jnp.where(col == 32 * (row >> 3) + 2 * (row & 7), 1.0, 0.0).astype(BF16)


def even_placer():
    row = lax.broadcasted_iota(jnp.int32, (PIX0, PIX1), 0)
    col = lax.broadcasted_iota(jnp.int32, (PIX0, PIX1), 1)
    return jnp.where(row == 32 * (col >> 3) + 2 * (col & 7), 1.0, 0.0).astype(BF16)


def placed(values):
    placer = even_placer()
    high = values.astype(BF16)
    rest = (values - high.astype(F32)).astype(BF16)
    return dot_nn(placer, high) + dot_nn(placer, rest)


def call(body, outs, grid, in_specs, out_specs, scratch=(), limit=28, aliases={}, micros=5):
    size = int(micros * 3.6e6)
    return pl.pallas_call(
        body,
        out_shape=outs,
        grid_spec=pltpu.PrefetchScalarGridSpec(
            num_scalar_prefetch=1,
            grid=grid,
            in_specs=in_specs,
            out_specs=out_specs,
            scratch_shapes=list(scratch),
        ),
        input_output_aliases=aliases,
        cost_estimate=pl.CostEstimate(flops=0, bytes_accessed=size, transcendentals=0),
        compiler_params=pltpu.CompilerParams(vmem_limit_bytes=limit * MIB),
    )


ANYWHERE = pl.BlockSpec(memory_space=pltpu.HBM)
DMA = pltpu.SemaphoreType.DMA


def in_hbm(array):
    return pltpu.with_memory_space_constraint(array, pltpu.HBM)


def vmem(*dims):
    return pltpu.VMEM(dims, BF16)


def full(*dims):
    return pl.BlockSpec(dims, lambda *_: (0,) * len(dims), pipeline_mode=pl.Buffered(1))


def per_image(*dims):
    return pl.BlockSpec((1,) + dims, lambda s, meta: (s,) + (0,) * len(dims))


def own_image(*dims):
    return pl.BlockSpec((1,) + dims, lambda s, meta: (meta[s],) + (0,) * len(dims))


def single(body, meta, ins, outs, scratch=(), limit=28, micros=5):
    in_specs = [ANYWHERE if whole else full(*array.shape) for array, whole in ins]
    shapes = [(hbm_of if far else shape_of)(dims, kind) for dims, kind, far in outs]
    out_specs = [full(*dims) for dims, _, _ in outs]
    made = call(body, shapes, (1,), in_specs, out_specs, scratch, limit, micros=micros)
    return made(meta, *[array for array, _ in ins])


def near(*arrays):
    return [(array, False) for array in arrays]


def far(*arrays):
    return [(in_hbm(array), False) for array in arrays]


def weight(pair):
    return [(array, True) for array in pair]


W1 = (0, 0, C0, M0)
W2 = (0, 0, 9 * M0, M0)
W3 = (0, 2304, M0, C0)
V1 = (1, 0, C0, M1)
VS = (1, 2048, C0, C1)
V2 = (1, 0, 9 * M1, M1)
V3 = (1, 9216, M1, C1)


def fetch(meta, weight, own_ref, got_ref, here, sem, rows=None, cols=None):
    owner, base, height, width = weight
    first, some = rows or (0, height)
    left, wide = cols or (0, width)

    def start(ref):
        for k in range(wide // 256):
            source = ref.at[pl.ds(base + (left // 256 + k) * height + first, some)]
            pltpu.make_async_copy(source, here.at[:, pl.ds(256 * k, 256)], sem).start()

    pl.when(meta[CORE] == owner)(functools.partial(start, own_ref))
    pl.when(meta[CORE] != owner)(functools.partial(start, got_ref))


def await_copy(here, sem):
    pltpu.make_async_copy(here, here, sem).wait()


def enter(meta, x_ref, cot_ref, wa_ref, wb_ref, *refs):
    pays, evens, cots, w_ref, sem = refs[0:4], refs[4:8], refs[8:12], refs[12], refs[13]
    step = pl.program_id(0)

    @pl.when(step == 0)
    def _():
        fetch(meta, W1, wa_ref, wb_ref, w_ref, sem)
        await_copy(w_ref, sem)

    x = x_ref[0].reshape(PIX0, C0)
    z = dot_nn(x, w_ref[...])
    even = dot_nn(even_picker(), x).astype(BF16)
    row = lax.broadcasted_iota(jnp.int32, (16, M0), 0)
    high, wide = meta[HIGH + step].astype(F32), meta[WIDE + step].astype(F32)
    sizes = jnp.where(row == 0, high, jnp.where(row == 1, wide, 0.0))
    middle = total_rows(z) * (1.0 / PIX0)
    rest = middle
    for k in range(3):
        part = rest.astype(BF16).astype(F32)
        sizes = jnp.where(row == 2 + k, part, sizes)
        rest = rest - part
    z = z - middle
    for k in range(WORK):

        @pl.when(step == k)
        def _(k=k):
            pays[k][0:PIX0, :] = z.astype(BF16)
            pays[k][PIX0 : PIX0 + 16, :] = sizes.astype(BF16)
            evens[k][...] = even
            cots[k][...] = cot_ref[0].reshape(PIX1, C1)


def arrive(meta, *refs):
    pays, z_ref, z_far_ref, hw_ref, st_ref = refs[0:4], *refs[4:]
    first, second, count = 0.0, 0.0, 0.0
    for k in range(WORK):
        rows = pays[k][PIX0 : PIX0 + 16, :].astype(F32)
        sizes = rows[:, 0:128]
        hw_ref[k : k + 1, :] = sizes[0:1, :]
        hw_ref[4 + k : 5 + k, :] = sizes[1:2, :]
        count = count + sizes[0:1, :] * sizes[1:2, :]
        z = pays[k][0:PIX0, :].astype(F32) + ((rows[2:3, :] + rows[3:4, :]) + rows[4:5, :])
        z_ref[k] = z
        z_far_ref[k] = z
        zm = z * over_lanes(pixel_mask(sizes[0:1, :], sizes[1:2, :], WB, PIX0), M0)
        first = first + total_rows(zm)
        second = second + total_rows(zm * z)
    st_ref[0:1, :] = jnp.concatenate([first, count], axis=1)
    st_ref[1:2, :] = jnp.concatenate([second, count], axis=1)


def front_two(meta, *refs):
    stats, (z_ref, hw_ref, n_ref, wa_ref, wb_ref) = refs[0:4], refs[4:9]
    tot_ref, a1_ref, z2_ref, z2b_ref, st_ref, w_ref, act_ref, sem = refs[9:]
    fetch(meta, W2, wa_ref, wb_ref, w_ref, sem)
    table = plane_total(stats)
    tot_ref[...] = table
    mean, scale = mean_scale(table[:, :M0], count_of(tot_ref))
    act_ref[:, 0:WB, :] = jnp.zeros((2, WB, 3 * M0), BF16)
    act_ref[:, WB + PIX0 : 2 * WB + PIX0, :] = jnp.zeros((2, WB, 3 * M0), BF16)
    first, second = 0.0, 0.0
    for k in range(WORK):
        mask = over_lanes(mask0(hw_ref, k), M0)
        pre = (z_ref[k] - mean) * scale * n_ref[0:1, :M0] + n_ref[1:2, :M0]
        act = silu(pre) * mask
        left, right = side_columns(act, WB)
        wide = jnp.concatenate([left, act, right], axis=1).astype(BF16)
        act_ref[k % 2, WB : WB + PIX0, :] = wide
        a1_ref[k] = wide[:, M0 : 2 * M0]
        if k == 0:
            await_copy(w_ref, sem)
        z2 = dot_nn(act_ref[k % 2, 0:PIX0, :], w_ref[0 : 3 * M0, :])
        z2 = z2 + dot_nn(wide, w_ref[3 * M0 : 6 * M0, :])
        z2 = z2 + dot_nn(act_ref[k % 2, 2 * WB : 2 * WB + PIX0, :], w_ref[6 * M0 :, :])
        z2_ref[k] = z2
        z2b_ref[k] = z2
        zm = z2 * mask
        first = first + total_rows(zm)
        second = second + total_rows(zm * z2)
    st_ref[0:1, :] = first
    st_ref[1:2, :] = second


def front_three(meta, *refs):
    stats, (tot_ref, z2_ref, hw_ref, n_ref, wa_ref, wb_ref) = refs[0:4], refs[4:10]
    tot2_ref, a2_ref, a2b_ref, st_ref, w_ref, sem = refs[10:]
    fetch(meta, W3, wa_ref, wb_ref, w_ref, sem)
    table = plane_total(stats)
    tot2_ref[...] = table
    mean, scale = mean_scale(table, count_of(tot_ref))
    first, second = 0.0, 0.0
    for k in range(WORK):
        pre = (z2_ref[k] - mean) * scale * n_ref[0:1, M0 : 2 * M0] + n_ref[1:2, M0 : 2 * M0]
        act = (silu(pre) * over_lanes(mask0(hw_ref, k), M0)).astype(BF16)
        a2_ref[k] = act
        a2b_ref[k] = act
        if k == 0:
            await_copy(w_ref, sem)
        z3 = dot_nn(act, w_ref[...])
        first = first + total_rows(z3)
        second = second + total_rows(z3 * z3)
    st_ref[0:1, :] = first
    st_ref[1:2, :] = second


def even_picker():
    row = lax.broadcasted_iota(jnp.int32, (PIX1, PIX0), 0)
    col = lax.broadcasted_iota(jnp.int32, (PIX1, PIX0), 1)
    return jnp.where(col == 32 * (row >> 3) + 2 * (row & 7), 1.0, 0.0).astype(BF16)


def even_placer():
    row = lax.broadcasted_iota(jnp.int32, (PIX0, PIX1), 0)
    col = lax.broadcasted_iota(jnp.int32, (PIX0, PIX1), 1)
    return jnp.where(row == 32 * (col >> 3) + 2 * (col & 7), 1.0, 0.0).astype(BF16)


def placed(values):
    placer = even_placer()
    high = values.astype(BF16)
    rest = (values - high.astype(F32)).astype(BF16)
    return dot_nn(placer, high) + dot_nn(placer, rest)


SIDE_PART = C1 // 4


def join(meta, *refs):
    stats, (tot_ref, a2_ref), evens, (hw_ref, n_ref) = refs[0:4], refs[4:6], refs[6:10], refs[10:12]
    wa_ref, wb_ref = refs[12:14]
    tot3_ref, s_ref, p_ref, z3_ref, z1_ref, z1b_ref, zs_ref, st_ref, sts_ref = refs[14:23]
    w3_ref, w1_ref, ws_ref, sems = refs[23:]
    step = pl.program_id(0)

    @pl.when(step == 0)
    def _():
        fetch(meta, W3, wa_ref, wb_ref, w3_ref, sems.at[0])
        fetch(meta, V1, wa_ref, wb_ref, w1_ref, sems.at[1])
        for k in range(4):
            cols = (k * SIDE_PART, SIDE_PART)
            fetch(meta, VS, wa_ref, wb_ref, ws_ref.at[k], sems.at[2 + k], cols=cols)
        table = plane_total(stats)
        tot3_ref[...] = table
        mean, scale = mean_scale(table, count_of(tot_ref))
        picker = even_picker()
        await_copy(w3_ref, sems.at[0])
        for k in range(WORK):
            act = dot_nn(picker, a2_ref[k]).astype(BF16)
            z3 = dot_nn(act, w3_ref[...])
            here = slice(k * PIX1, (k + 1) * PIX1)
            z3_ref[here, :] = z3
            pre = (z3 - mean) * scale * n_ref[0:1, 2 * M0 : 2 * M0 + C0]
            pre = pre + n_ref[1:2, 2 * M0 : 2 * M0 + C0]
            pre = pre + evens[k][...].astype(F32)
            p_ref[here, :] = pre
            s_ref[here, :] = (silu(pre) * over_lanes(mask1(hw_ref, k), C0)).astype(BF16)
        await_copy(w1_ref, sems.at[1])
        z1 = dot_nn(s_ref[...], w1_ref[...])
        z1_ref[...] = z1
        z1b_ref[...] = z1
        put_sums(st_ref, z1, z1 * z1)

    for k in range(4):

        @pl.when(step == k)
        def _(k=k):
            await_copy(ws_ref.at[k], sems.at[2 + k])
            zs = dot_nn(s_ref[...], ws_ref[k])
            zs_ref[...] = zs
            put_sums(sts_ref, zs, zs * zs)


def fetch_conv(meta, wa_ref, wb_ref, w_ref, sems):
    for k in range(3):
        rows = (k * 3 * M1, 3 * M1)
        fetch(meta, V2, wa_ref, wb_ref, w_ref.at[pl.ds(*rows)], sems.at[k], rows=rows)


def await_conv(w_ref, sems, k):
    await_copy(w_ref.at[pl.ds(k * 3 * M1, 3 * M1)], sems.at[k])


def mid_one(meta, *refs):
    stats, (tot_ref, z1_ref, hw_ref, n_ref, wa_ref, wb_ref) = refs[0:4], refs[4:10]
    tot4_ref, a1_ref, z2_ref, z2b_ref, st_ref, w_ref, sems = refs[10:]
    fetch_conv(meta, wa_ref, wb_ref, w_ref, sems)
    table = plane_total(stats)
    tot4_ref[...] = table
    mean, scale = mean_scale(table, count_of(tot_ref) * 0.25)
    mask = mask1_all(hw_ref, M1)
    act = silu((z1_ref[...] - mean) * scale * n_ref[0:1, :M1] + n_ref[1:2, :M1]) * mask
    left, right = side_columns(act, WB // 2)
    wide = jnp.concatenate([left, act, right], axis=1).astype(BF16)
    a1_ref[...] = wide[:, M1 : 2 * M1]
    await_conv(w_ref, sems, 0)
    z2 = later_rows(dot_nn(wide, w_ref[0 : 3 * M1, :]), 1, HB // 2, WB // 2)
    await_conv(w_ref, sems, 1)
    z2 = z2 + dot_nn(wide, w_ref[3 * M1 : 6 * M1, :])
    await_conv(w_ref, sems, 2)
    z2 = z2 + later_rows(dot_nn(wide, w_ref[6 * M1 :, :]), -1, HB // 2, WB // 2)
    z2_ref[...] = z2
    z2b_ref[...] = z2
    zm = z2 * mask
    put_sums(st_ref, zm, zm * z2)


def mid_two(meta, *refs):
    stats, (tot_ref, z2_ref, hw_ref, n_ref, wa_ref, wb_ref) = refs[0:4], refs[4:10]
    tot5_ref, a2_ref, z3_ref, st_ref, w_ref, sem = refs[10:]
    fetch(meta, V3, wa_ref, wb_ref, w_ref, sem)
    table = plane_total(stats)
    tot5_ref[...] = table
    mean, scale = mean_scale(table, count_of(tot_ref) * 0.25)
    pre = (z2_ref[...] - mean) * scale * n_ref[0:1, M1 : 2 * M1] + n_ref[1:2, M1 : 2 * M1]
    act = (silu(pre) * mask1_all(hw_ref, M1)).astype(BF16)
    a2_ref[...] = act
    await_copy(w_ref, sem)
    z3 = dot_nn(act, w_ref[...])
    z3_ref[...] = z3
    put_sums(st_ref, z3, z3 * z3)


AT3, ATS = 2 * M1, 2 * M1 + C1


def turn(meta, *refs):
    stats, sides, (tot_ref, z3_ref, zs_ref, hw_ref, n_ref) = refs[0:4], refs[4:8], refs[8:13]
    cots, (tot6_ref, tots_ref), ys = refs[13:17], refs[17:19], refs[19:23]
    g_ref, st_ref, cot_ref, y_ref = refs[23:]
    step = pl.program_id(0)

    @pl.when(step == 0)
    def _():
        tot6_ref[...] = plane_total(stats)
        tots_ref[...] = plane_total(sides)
        st_ref[...] = jnp.zeros_like(st_ref)

    count = count_of(tot_ref) * 0.25
    mean, scale = mean_scale(tot6_ref[...], count)
    mean_s, scale_s = mean_scale(tots_ref[...], count)
    normed = (z3_ref[0] - mean) * scale
    normed_s = (zs_ref[0] - mean_s) * scale_s
    pre = normed * n_ref[0:1, AT3:ATS] + n_ref[1:2, AT3:ATS]
    pre = pre + (normed_s * n_ref[0:1, ATS : ATS + C1] + n_ref[1:2, ATS : ATS + C1])
    sig = sigmoid(pre)
    for k in range(WORK):

        @pl.when(step == k)
        def _(k=k):
            cot_ref[...] = cots[k][...]

    high, wide = hw_ref[pl.ds(step, 1), :] * 0.5, hw_ref[pl.ds(4 + step, 1), :] * 0.5
    mask = over_lanes(pixel_mask(high, wide, WB // 2, PIX1), C1)
    y_ref[...] = (pre * sig * mask).astype(BF16)
    g_ref[0] = cot_ref[...].astype(F32) * (sig * (1.0 + pre * (1.0 - sig))) * mask
    for k in range(WORK):

        @pl.when(step == k)
        def _(k=k):
            ys[k][...] = y_ref[...]

    grad = g_ref[0]
    st_ref[0:1, :] += total_rows(grad)
    st_ref[1:2, :] += total_rows(grad * normed)
    st_ref[2:3, :] += total_rows(grad * normed_s)


def norm_back(grad, normed, scale, gain, first, second, mask):
    return (mask * (scale * gain) * (grad - first - normed * second)).astype(BF16)


def back_one(meta, *refs):
    stats, (tot6_ref, tots_ref, tot5_ref, tot_ref) = refs[0:4], refs[4:8]
    z3_ref, zs_ref, g_ref, z2_ref, hw_ref, n_ref, wa_ref, wb_ref = refs[8:16]
    tot7_ref, er_ref, es_ref, g2_ref, st_ref, w_ref, sem = refs[16:]
    fetch(meta, V3, wa_ref, wb_ref, w_ref, sem)
    table = plane_total(stats)
    tot7_ref[...] = table
    count = count_of(tot_ref) * 0.25
    table = table / count
    mask = mask1_all(hw_ref, C1)
    grad = g_ref[...]
    mean, scale = mean_scale(tot6_ref[...], count)
    normed = (z3_ref[...] - mean) * scale
    d3 = norm_back(grad, normed, scale, n_ref[0:1, AT3:ATS], table[0:1], table[1:2], mask)
    mean2, scale2 = mean_scale(tot5_ref[...], count)
    normed2 = (z2_ref[...] - mean2) * scale2
    pre2 = normed2 * n_ref[0:1, M1 : 2 * M1] + n_ref[1:2, M1 : 2 * M1]
    await_copy(w_ref, sem)
    g2 = dot_nt(d3, w_ref[...]) * mask[:, :M1] * slope(pre2)
    g2_ref[...] = g2
    put_sums(st_ref, g2, g2 * normed2)
    mean_s, scale_s = mean_scale(tots_ref[...], count)
    normed_s = (zs_ref[...] - mean_s) * scale_s
    ds = norm_back(grad, normed_s, scale_s, n_ref[0:1, ATS : ATS + C1], table[0:1], table[2:3], mask)
    es_ref[...] = ds
    half = C1 // 2
    for p in range(2):
        cols = slice(p * half, (p + 1) * half)
        er_ref[meta[CORE] ^ p] = jnp.concatenate([d3[:, cols], ds[:, cols]], axis=1)


def back_two(meta, *refs):
    stats, (tot5_ref, tot4_ref, tot_ref, z2_ref, g2_ref, z1_ref) = refs[0:4], refs[4:10]
    hw_ref, n_ref, wa_ref, wb_ref, tot8_ref, er_ref, g1_ref, st_ref, w_ref, sems = refs[10:]
    fetch_conv(meta, wa_ref, wb_ref, w_ref, sems)
    table = plane_total(stats)
    tot8_ref[...] = table
    count = count_of(tot_ref) * 0.25
    table = table / count
    mask = mask1_all(hw_ref, M1)
    mean, scale = mean_scale(tot5_ref[...], count)
    normed = (z2_ref[...] - mean) * scale
    d2 = norm_back(
        g2_ref[...], normed, scale, n_ref[0:1, M1 : 2 * M1], table[0:1], table[1:2], mask
    )
    for p in range(2):
        er_ref[meta[CORE] ^ p] = d2[:, p * (M1 // 2) : (p + 1) * (M1 // 2)]
    mean1, scale1 = mean_scale(tot4_ref[...], count)
    normed1 = (z1_ref[...] - mean1) * scale1
    pre1 = normed1 * n_ref[0:1, :M1] + n_ref[1:2, :M1]
    await_conv(w_ref, sems, 0)
    wide = later_rows(dot_nt(d2, w_ref[0 : 3 * M1, :]), -1, HB // 2, WB // 2)
    await_conv(w_ref, sems, 1)
    wide = wide + dot_nt(d2, w_ref[3 * M1 : 6 * M1, :])
    await_conv(w_ref, sems, 2)
    wide = wide + later_rows(dot_nt(d2, w_ref[6 * M1 :, :]), 1, HB // 2, WB // 2)
    left, _ = side_columns(wide[:, 2 * M1 :], WB // 2)
    _, right = side_columns(wide[:, :M1], WB // 2)
    g1 = (wide[:, M1 : 2 * M1] + left + right) * mask * slope(pre1)
    g1_ref[...] = g1
    put_sums(st_ref, g1, g1 * normed1)


def back_three(meta, *refs):
    stats, (tot4_ref, tot_ref, z1_ref, g1_ref, es_ref, tot3_ref, p_ref, z3_ref) = refs[0:4], refs[4:12]
    hw_ref, n_ref, wa_ref, wb_ref = refs[12:16]
    tot9_ref, er_ref, g0_ref, st_ref, w1_ref, ws_ref, sems = refs[16:]
    fetch(meta, V1, wa_ref, wb_ref, w1_ref, sems.at[0])
    fetch(meta, VS, wa_ref, wb_ref, ws_ref, sems.at[1])
    table = plane_total(stats)
    tot9_ref[...] = table
    count = count_of(tot_ref) * 0.25
    table = table / count
    mask = mask1_all(hw_ref, C0)
    mean, scale = mean_scale(tot4_ref[...], count)
    normed = (z1_ref[...] - mean) * scale
    d1 = norm_back(
        g1_ref[...], normed, scale, n_ref[0:1, :M1], table[0:1], table[1:2], mask[:, :M1]
    )
    for p in range(2):
        er_ref[meta[CORE] ^ p] = d1[:, p * (M1 // 2) : (p + 1) * (M1 // 2)]
    await_copy(w1_ref, sems.at[0])
    grad = dot_nt(d1, w1_ref[...])
    await_copy(ws_ref, sems.at[1])
    grad = grad + dot_nt(es_ref[...], ws_ref[...])
    grad = grad.astype(BF16).astype(F32)
    g0 = grad * slope(p_ref[...]) * mask
    g0_ref[...] = g0
    mean3, scale3 = mean_scale(tot3_ref[...], count * 4.0)
    put_sums(st_ref, g0, g0 * ((z3_ref[...] - mean3) * scale3))


def last_one(meta, *refs):
    stats, (tot3_ref, tot2_ref, tot_ref, a2_ref, g0_ref, z2_ref, hw_ref, n_ref) = refs[0:4], refs[4:12]
    wa_ref, wb_ref, tot10_ref, d3_ref, g2_ref, st_ref, w_ref, sem = refs[12:]
    step = pl.program_id(0)

    @pl.when(step == 0)
    def _():
        fetch(meta, W3, wa_ref, wb_ref, w_ref, sem)
        tot10_ref[...] = plane_total(stats)
        st_ref[...] = jnp.zeros_like(st_ref)
        await_copy(w_ref, sem)

    count = count_of(tot_ref)
    table = tot10_ref[...] / count
    mean, scale = mean_scale(tot3_ref[...], count)
    mean2, scale2 = mean_scale(tot2_ref[...], count)
    high = pl.ds(step, 1)
    wide = pl.ds(4 + step, 1)
    mask = over_lanes(pixel_mask(hw_ref[high, :], hw_ref[wide, :], WB, PIX0), C0)
    normed = (dot_nn(a2_ref[0], w_ref[...]) - mean) * scale
    grad = placed(g0_ref[0])
    gain = n_ref[0:1, 2 * M0 : 2 * M0 + C0]
    d3 = norm_back(grad, normed, scale, gain, table[0:1], table[1:2], mask)
    d3_ref[0] = d3
    normed2 = (z2_ref[0] - mean2) * scale2
    pre2 = normed2 * n_ref[0:1, M0 : 2 * M0] + n_ref[1:2, M0 : 2 * M0]
    g2 = dot_nt(d3, w_ref[...]) * mask[:, :M0] * slope(pre2)
    g2_ref[0] = g2
    st_ref[0:1, :] += total_rows(g2)
    st_ref[1:2, :] += total_rows(g2 * normed2)


def last_two(meta, *refs):
    stats, (tot2_ref, tot_ref, z2_ref, g2_ref, z1_ref, hw_ref, n_ref) = refs[0:4], refs[4:11]
    wa_ref, wb_ref, tot11_ref, d2_ref, g1_ref, st_ref, w_ref, sem = refs[11:]
    step = pl.program_id(0)

    @pl.when(step == 0)
    def _():
        fetch(meta, W2, wa_ref, wb_ref, w_ref, sem)
        tot11_ref[...] = plane_total(stats)
        st_ref[...] = jnp.zeros_like(st_ref)

    count = count_of(tot_ref)
    table = tot11_ref[...] / count
    mask = pixel_mask(hw_ref[pl.ds(step, 1), :], hw_ref[pl.ds(4 + step, 1), :], WB, PIX0)
    mask = over_lanes(mask, M0)
    mean2, scale2 = mean_scale(tot2_ref[...], count)
    normed2 = (z2_ref[0] - mean2) * scale2
    gain = n_ref[0:1, M0 : 2 * M0]
    d2 = norm_back(g2_ref[0], normed2, scale2, gain, table[0:1], table[1:2], mask)
    d2_ref[0] = d2
    mean1, scale1 = mean_scale(tot_ref[:, :M0], count)
    normed1 = (z1_ref[0] - mean1) * scale1
    pre1 = normed1 * n_ref[0:1, :M0] + n_ref[1:2, :M0]

    @pl.when(step == 0)
    def _():
        await_copy(w_ref, sem)

    wide = dot_nt(d2, w_ref[3 * M0 : 6 * M0, :])
    wide = wide + later_rows(dot_nt(d2, w_ref[0 : 3 * M0, :]), -1, HB, WB)
    wide = wide + later_rows(dot_nt(d2, w_ref[6 * M0 :, :]), 1, HB, WB)
    left, _ = side_columns(wide[:, 2 * M0 :], WB)
    _, right = side_columns(wide[:, :M0], WB)
    g1 = (wide[:, M0 : 2 * M0] + left + right) * mask * slope(pre1)
    g1_ref[0] = g1
    st_ref[0:1, :] += total_rows(g1)
    st_ref[1:2, :] += total_rows(g1 * normed1)


def last_three(meta, *refs):
    stats, (tot_ref, z1_ref, g1_ref, g0_ref, hw_ref, n_ref) = refs[0:4], refs[4:10]
    tot12_ref, backs = refs[10], refs[11:15]
    table = plane_total(stats)
    tot12_ref[...] = table
    count = count_of(tot_ref)
    table = table / count
    mean, scale = mean_scale(tot_ref[:, :M0], count)
    for k in range(WORK):
        mask = over_lanes(mask0(hw_ref, k), M0)
        normed = (z1_ref[k] - mean) * scale
        backs[k][0:PIX0, :] = norm_back(
            g1_ref[k], normed, scale, n_ref[0:1, :M0], table[0:1], table[1:2], mask
        )
        grad = g0_ref[k * PIX1 : (k + 1) * PIX1, :].astype(BF16)
        for part in range(C0 // M0):
            here = slice(PIX0 + part * PIX1, PIX0 + (part + 1) * PIX1)
            backs[k][here, :] = grad[:, part * M0 : (part + 1) * M0]


def leave(meta, x_ref, wa_ref, wb_ref, *refs):
    backs, gx_ref, out_ref = refs[0:4], refs[5], refs[6]
    w_ref, acc_ref, stage_ref, sem, out_sem = refs[7:]
    step = pl.program_id(0)

    @pl.when(step == 0)
    def _():
        fetch(meta, W1, wa_ref, wb_ref, w_ref, sem)
        acc_ref[...] = jnp.zeros_like(acc_ref)
        await_copy(w_ref, sem)

    for k in range(WORK):

        @pl.when(step == k)
        def _(k=k):
            d1 = backs[k][0:PIX0, :]
            grad = jnp.concatenate(
                [backs[k][PIX0 + n * PIX1 : PIX0 + (n + 1) * PIX1, :] for n in range(C0 // M0)], axis=1
            )
            acc_ref[...] += dot_tn(x_ref[0].reshape(PIX0, C0), d1)
            gx_ref[0] = (dot_nt(d1, w_ref[...]) + dot_nn(even_placer(), grad)).astype(BF16)

    @pl.when(step == WORK - 1)
    def _():
        put_tiles(stage_ref, 0, acc_ref[...])
        copy = pltpu.make_async_copy(stage_ref, out_ref.at[pl.ds(0, 2 * C0)], out_sem)
        copy.start()
        copy.wait()


def put_tiles(ref, start, values):
    rows, width = values.shape
    for k in range(width // 128):
        here = slice(start + k * rows, start + (k + 1) * rows)
        ref[here, :] = values[:, 128 * k : 128 * (k + 1)].astype(BF16)


def nine_shifts(delta, height, breadth):
    pieces = []
    left, right = side_columns(delta, breadth)
    for a in range(3):
        for moved in (right, delta, left):
            pieces.append(later_rows(moved, a - 1, height, breadth).astype(BF16))
    return jnp.concatenate(pieces, axis=1)


SIDES, MIDDLE = 768, 704
SWAPPED = (0, 2, 1, 3)


def place_of(core, chip):
    return jnp.where(core == 0, 2 * (chip & 1) + (chip >> 1), chip)


def spot_of(level):
    return 2 * (level & 1) + (level >> 1)


def put_shards(ref, shard, start, core, level_first, values):
    rows = values.shape[0] // 16
    values = values.astype(BF16)
    for chip in range(4):
        place = place_of(core, chip)
        for z in range(4):
            at = (SWAPPED[z] * 4 + place if level_first else place * 4 + SWAPPED[z]) * shard + start
            part = values[(4 * chip + z) * rows : (4 * chip + z + 1) * rows]
            for k in range(values.shape[1] // 128):
                here = pl.ds(pl.multiple_of(at + k * rows, 16), rows)
                ref[here, :] = part[:, 128 * k : 128 * (k + 1)]


def sides_grad(meta, sa_ref, sb_ref, la_ref, lb_ref, ea_ref, eb_ref, out_ref):
    half = C1 // 2
    side = dot_tn(sa_ref[...], ea_ref[0][:, half:]) + dot_tn(sb_ref[...], eb_ref[0][:, half:])
    put_shards(out_ref, SIDES, 0, meta[CORE], False, side)
    last = dot_tn(la_ref[...], ea_ref[0][:, :half]) + dot_tn(lb_ref[...], eb_ref[0][:, :half])
    put_shards(out_ref, SIDES, C0 // 2, meta[CORE], False, last)


def middle_grad(meta, sa_ref, sb_ref, la_ref, lb_ref, ma_ref, mb_ref, fa_ref, fb_ref, out_ref):
    conv = dot_tn(la_ref[...], nine_shifts(ma_ref[0].astype(F32), HB // 2, WB // 2))
    conv = conv + dot_tn(lb_ref[...], nine_shifts(mb_ref[0].astype(F32), HB // 2, WB // 2))
    put_shards(out_ref, MIDDLE, 0, meta[CORE], False, conv)
    first = dot_tn(sa_ref[...], fa_ref[0]) + dot_tn(sb_ref[...], fb_ref[0])
    put_shards(out_ref, MIDDLE, 9 * M1 // 8, meta[CORE], False, first)


def front_grad_two(meta, a1_ref, d2_ref, a2_ref, d3_ref, out_ref):
    last = dot_tn(a2_ref[...].reshape(ROWS0, M0), d3_ref[...].reshape(ROWS0, C0))
    put_tiles(out_ref, 2 * C0 + 2 * 9 * M0, last)
    shifted = nine_shifts(d2_ref[...].reshape(ROWS0, M0).astype(F32), HB, WB)
    left = a1_ref[...].reshape(ROWS0, M0)
    out_ref[0 : 2 * C0, :] = jnp.zeros((2 * C0, 128), BF16)
    for tap in range(9):
        conv = dot_tn(left, shifted[:, tap * M0 : (tap + 1) * M0])
        for tile in range(2):
            start = 2 * C0 + tile * 9 * M0 + tap * M0
            out_ref[start : start + M0, :] = conv[:, tile * 128 : (tile + 1) * 128].astype(BF16)


def unpack_kernel(jobs, chunk, meta, raw_ref, out_ref, *refs):
    raws, flat_ref, sem_in, sem_out = refs[0:3], refs[3], refs[4], refs[5]
    stages = dict(zip(sorted({weight[3] for listed in jobs for _, weight in listed}), refs[6:]))

    def run(listed):
        loads, stores, waits, sizes = [], [], [], []
        for offset, (_, base, height, cols) in listed:
            for row in range(0, height, chunk // cols):
                some = min(chunk // cols, height - row)
                k = len(loads)
                source = raw_ref.at[:, pl.ds(offset + row * cols, some * cols)]
                here = raws[k % 3].at[:, pl.ds(0, some * cols)]
                loads.append(pltpu.make_async_copy(source, here, sem_in.at[k % 3]))
                stage = stages[cols].at[k % 2, pl.ds(0, some)]
                panels = []
                for panel in range(cols // 256):
                    there = out_ref.at[pl.ds(base + panel * height + row, some)]
                    lanes = stage.at[:, pl.ds(256 * panel, 256)]
                    panels.append(pltpu.make_async_copy(lanes, there, sem_out.at[k % 2]))
                stores.append(panels)
                waits.append(pltpu.make_async_copy(stage, stage, sem_out.at[k % 2]))
                sizes.append((some, cols))
        for load in loads[:2]:
            load.start()
        for k, (rows, cols) in enumerate(sizes):
            if k + 2 < len(sizes):
                loads[k + 2].start()
            loads[k].wait()
            flat_ref[:, : rows * cols] = raws[k % 3][:, : rows * cols].astype(F32)
            lines = flat_ref.reshape(chunk // 128, 128)
            if k >= 2:
                waits[k - 2].wait()
            for tile in range(cols // 128):
                values = lines[pl.ds(tile, rows, stride=cols // 128), :].astype(BF16)
                stages[cols][k % 2, 0:rows, tile * 128 : (tile + 1) * 128] = values
            for store in stores[k]:
                store.start()
        for wait in waits[-2:]:
            wait.wait()

    for core in range(2):
        if jobs[core]:
            pl.when(meta[CORE] == core)(functools.partial(run, jobs[core]))


def unpack(meta, packed, rows, jobs, micros, chunk=524288):
    widths = sorted({weight[3] for listed in jobs for _, weight in listed})
    return call(
        functools.partial(unpack_kernel, jobs, chunk),
        pltpu.HBM((rows, 256), BF16),
        (1,),
        [ANYWHERE],
        ANYWHERE,
        [pltpu.VMEM((1, chunk), BF16)] * 3
        + [pltpu.VMEM((1, chunk), F32), DMA((3,)), DMA((2,))]
        + [pltpu.VMEM((2, chunk // cols, cols), BF16) for cols in widths],
        micros=micros,
    )(meta, in_hbm(packed))


PACK_ROWS = 2048
GRAD_ROWS = P_SIZE // 128
ARRIVED = ((1, (0, 1)), (0, (0, 2)), (0, (1, 3)), (1, (2, 3)))


def quarters(bufs, target):
    found = []
    for buf, (p, masks) in zip(bufs, ARRIVED):
        if target == 0:
            p, masks = 1 - p, tuple(SWAPPED[m] for m in masks)
        for k, mask in enumerate(masks):
            found.append((p, mask, buf, k * (buf.shape[0] // 2)))
    return found


def pack_sides(meta, *refs):
    bufs, out_ref = refs[:4], refs[4]
    step = pl.program_id(0)
    level, plane = meta[LEVEL], meta[PLANE]

    @pl.when(meta[CORE] == 0)
    def _():
        out_ref[...] = jnp.zeros_like(out_ref)

    for p, mask, buf, start in quarters(bufs, 1):
        here = meta[CORE] == 1

        @pl.when(here & (step < 4) & (step == (plane ^ mask)))
        def _(p=p, buf=buf, start=start):
            for z in range(4):
                for k in range(8):
                    row = start + spot_of(level ^ z) * SIDES + C0 // 2 + 32 * k
                    rows = buf[pl.ds(pl.multiple_of(row, 32), 32), :].astype(F32)
                    out_ref[pl.ds(512 * z + 8 * p + k, 32, stride=16), :] = rows

        @pl.when(here & (step >= 4) & (((step - 4) >> 1) == (plane ^ mask)))
        def _(p=p, buf=buf, start=start):
            for j in range(2):
                z = 2 * (step & 1) + j
                for k in range(8):
                    row = start + spot_of(level ^ z) * SIDES + 64 * k
                    rows = buf[pl.ds(pl.multiple_of(row, 64), 64), :].astype(F32)
                    out_ref[pl.ds(1024 * j + 8 * p + k, 64, stride=16), :] = rows


def pack_middle(first_step, meta, *refs):
    bufs, out_ref = refs[1:5], refs[-1]
    step = pl.program_id(0) + first_step
    plane, level = meta[PLANE], meta[LEVEL]

    for p, mask, buf, start in quarters(bufs, 1):
        chip = plane ^ mask

        @pl.when((meta[CORE] == 1) & (step < 2) & (step == (chip >> 1)))
        def _(p=p, buf=buf, start=start, chip=chip):
            for z in range(4):
                for k in range(2):
                    row = start + spot_of(level ^ z) * MIDDLE + 9 * M1 // 8 + 64 * k
                    rows = buf[pl.ds(pl.multiple_of(row, 64), 64), :].astype(F32)
                    at = 256 * (4 * (chip & 1) + z) + 2 * p + k
                    out_ref[pl.ds(at, 64, stride=4), :] = rows

        @pl.when((meta[CORE] == 1) & (step > 1))
        def _(p=p, buf=buf, start=start, chip=chip):
            for z in range(4):
                for k in range(2):
                    row = start + spot_of(level ^ z) * MIDDLE + 64 * (step - 2) + 32 * k
                    rows = buf[pl.ds(pl.multiple_of(row, 32), 32), :].astype(F32)
                    at = 128 * (4 * chip + z) + 2 * p + k
                    out_ref[pl.ds(at, 32, stride=4), :] = rows


def pack_rest(meta, *refs):
    out_ref = refs[-1]

    @pl.when(meta[CORE] == 0)
    def _():
        out_ref[...] = jnp.zeros_like(out_ref)

    pack_middle(5, meta, *refs)


def pack_front(meta, *refs):
    fronts, out_ref, whole_ref = refs[5:9], refs[9], refs[10]
    step = pl.program_id(0)
    core, plane, level = meta[CORE], meta[PLANE], meta[LEVEL]
    part = fronts[0].shape[0] // 8

    @pl.when((core == 0) & (step == 0))
    def _():
        for p, mask, buf, start in quarters(fronts, 0):
            for z in range(4):
                there = (16 * p + 4 * place_of(p, plane ^ mask) + spot_of(level ^ z)) * part
                at = start + SWAPPED[z] * part
                rows = buf[at : at + part, :]
                whole_ref[pl.ds(pl.multiple_of(there, 16), part), :] = rows

    at2, at3 = 2 * C0, 2 * C0 + 2 * 9 * M0

    def piece(start, rows):
        return whole_ref[start : start + rows, :].astype(F32)

    @pl.when((core == 0) & (step == 0))
    def _():
        for tile in range(2):
            out_ref[pl.ds(tile, C0, stride=2), :] = piece(tile * C0, C0)

    for k in range(2):

        @pl.when((core == 0) & (step == 1 + k))
        def _(k=k):
            for tile in range(2):
                out_ref[pl.ds(tile, C0, stride=2), :] = piece(at2 + tile * 9 * M0 + k * C0, C0)

    @pl.when((core == 0) & (step == 3))
    def _():
        for tile in range(2):
            out_ref[pl.ds(tile, 256, stride=2), :] = piece(at2 + tile * 9 * M0 + 2 * C0, 256)
        for tile in range(8):
            out_ref[pl.ds(512 + tile, 192, stride=8), :] = piece(at3 + tile * 256, 192)

    @pl.when((core == 0) & (step == 4))
    def _():
        out_ref[...] = jnp.zeros_like(out_ref)
        for tile in range(8):
            out_ref[pl.ds(tile, 64, stride=8), :] = piece(at3 + tile * 256 + 192, 64)

    pack_middle(0, meta, *refs[:5], out_ref)


def rows_out(meta, x_ref, xg_ref, y_ref, yg_ref, out_ref):
    step = pl.program_id(0)
    row = lax.broadcasted_iota(jnp.int32, (128, 128), 0)
    col = lax.broadcasted_iota(jnp.int32, (128, 128), 1)

    def put(first, second, source):
        values = jnp.concatenate([first.reshape(-1, C0), second.reshape(-1, C0)], axis=0)
        mover = jnp.where(col == source, 1.0, 0.0).astype(BF16)
        moved = dot_nn(mover, values).astype(BF16)
        for k in range(16):
            out_ref[:, k * C0 : (k + 1) * C0] = moved[8 * k : 8 * (k + 1), :]

    image, stand = row & 7, row * 0
    for k in range(WORK):
        stand = jnp.where(image == meta[k], k, jnp.where(image == (meta[k] ^ 1), WORK + k, stand))

    @pl.when(meta[CORE] == 0)
    def _():
        put(x_ref[...], xg_ref[...], 16 * stand + (row >> 3))

    @pl.when((meta[CORE] == 1) & (step < HB // 2))
    def _():
        def split(ref):
            pieces = []
            for k in range(WORK):
                wide = ref[k].astype(F32)
                pieces += [wide[:, :C0], wide[:, C0:]]
            return jnp.concatenate(pieces, axis=0).astype(BF16)

        put(split(y_ref), split(yg_ref), 16 * stand + 8 * ((row >> 3) & 1) + (row >> 4))

    @pl.when((meta[CORE] == 1) & (step >= HB // 2))
    def _():
        out_ref[...] = jnp.zeros_like(out_ref)


def pin(value, *others):
    return lax.optimization_barrier((value,) + others)[0]


def swap_cores(value):
    return lax.ppermute(value, "pipe", [(0, 1), (1, 0)])


def xor_permute(value, mask):
    count = lax.axis_size("dp")
    return lax.ppermute(value, "dp", [(i, i ^ mask) for i in range(count)])


def upper_bits():
    return [bit for bit in (16, 32, 64, 128, 256, 512) if bit < lax.axis_size("dp")]


def plane_turn(value, turn_no):
    count = lax.axis_size("dp")
    pairs = []
    for p in range(2):
        mask = SWAPPED[turn_no] if p else turn_no
        pairs += [(p * count + i, p * count + (i ^ mask)) for i in range(count)]
    return lax.ppermute(value, ("pipe", "dp"), pairs)


def shared(value):
    for bit in upper_bits():
        value = value + xor_permute(value, bit)
    return [value] + [plane_turn(value, k) for k in (1, 2, 3)]


def over_levels(values):
    return [values[0]] + [xor_permute(values[k], 4 * k) for k in (1, 2, 3)]


def part_at(value, index, parts):
    rows = value.shape[0] // parts
    return lax.optimization_barrier(lax.dynamic_slice_in_dim(value, index * rows, rows, 0))


def added(*parts):
    total = parts[0].astype(F32)
    for part in parts[1:]:
        total = total + part.astype(F32)
    return total.astype(BF16)


def upper_sum(value):
    for bit in upper_bits():
        value = added(value, xor_permute(value, bit))
    return value


def to_core(both, target):
    count = lax.axis_size("dp")
    other = 1 - target
    close, away = (1, 2) if target == 1 else (2, 1)
    arrived = [both]
    for p, mask in ((other, 0), (other, close), (target, away)):
        pairs = [(p * count + i, target * count + (i ^ mask)) for i in range(count)]
        arrived.append(lax.ppermute(both, ("pipe", "dp"), pairs))
    return arrived


def on_device(images, extents, views, params, norms, cotangent):
    images, cotangent, params = in_hbm(images), in_hbm(cotangent), in_hbm(params)
    core = lax.axis_index("pipe")
    first_core = core == 0
    plane = lax.axis_index("dp") % 4
    level = (lax.axis_index("dp") // 4) % 4
    place = place_of(core, plane)

    pair = 2 * (level ^ jnp.arange(WORK, dtype=jnp.int32))
    hot = (pair[:, None] == jnp.arange(2 * WORK, dtype=jnp.int32)[None, :]).astype(jnp.int32)
    view = jnp.sum(hot * views[None, :], axis=1)
    order = pair + (view != core).astype(jnp.int32)
    hot = (order[:, None] == jnp.arange(2 * WORK, dtype=jnp.int32)[None, :]).astype(jnp.int32)
    sizes = jnp.sum(hot[:, :, None] * extents[None], axis=1)
    spot = jnp.stack([core, plane, level]).astype(jnp.int32)
    meta = jnp.concatenate([order, spot, sizes[:, 0], sizes[:, 1]]).astype(jnp.int32)

    w1 = unpack(meta, params, C0, ([(0, W1)], []), 3, 131072)
    w1 = (in_hbm(w1), in_hbm(lax.ppermute(w1, "pipe", [(0, 1)])))
    norms_there = swap_cores(norms[0])
    n0 = jnp.where(first_core, norms[0], norms_there)
    n1 = jnp.where(first_core, norms_there, norms[0])

    some = lambda dims, kind: [shape_of(dims, kind)] * WORK
    made = call(
        enter,
        some((PIX0 + 16, M0), BF16) + some((PIX1, C0), BF16) + some((PIX1, C1), BF16),
        (WORK,),
        [own_image(HB, WB, C0), own_image(HB // 2, WB // 2, C1), ANYWHERE, ANYWHERE],
        [full(PIX0 + 16, M0)] * 4 + [full(PIX1, C0)] * 4 + [full(PIX1, C1)] * 4,
        [vmem(C0, M0), DMA],
    )(meta, images, cotangent, *w1)
    pays, evens, cots = over_levels(made[0:4]), made[4:8], made[8:12]
    first_weights = unpack(
        meta,
        pin(params, made[0]),
        10240,
        ([(262144, W2), (851968, W3)], [(0, V1), (3932160, VS)]),
        8,
    )
    pays[0] = pin(pays[0], first_weights, norms_there)
    z1, z1b, hw, st = single(
        arrive,
        meta,
        near(*pays),
        [
            ((WORK, PIX0, M0), F32, False),
            ((WORK, PIX0, M0), F32, True),
            ((8, 128), F32, False),
            ((2, M0 + 128), F32, False),
        ],
    )

    s1 = shared(st)
    got = swap_cores(first_weights)
    evens = over_levels(evens)
    second_weights = unpack(
        meta, pin(params, st), 13312, ([], [(524288, V2), (2883584, V3)]), 10
    )
    s1[0] = pin(s1[0], got, evens[1], second_weights)
    wa = (in_hbm(first_weights), in_hbm(got))
    tot1, a1, z2, z2b, st = single(
        front_two,
        meta,
        near(*s1, z1, hw, n0) + weight(wa),
        [
            ((2, M0 + 128), F32, False),
            ((WORK, PIX0, M0), BF16, True),
            ((WORK, PIX0, M0), F32, False),
            ((WORK, PIX0, M0), F32, True),
            ((2, M0), F32, False),
        ],
        [vmem(9 * M0, M0), vmem(2, PIX0 + 2 * WB, 3 * M0), DMA],
    )
    s2 = shared(st)
    got = lax.ppermute(second_weights, "pipe", [(1, 0)])
    s2[0] = pin(s2[0], evens[2])
    tot2, a2, a2b, st = single(
        front_three,
        meta,
        near(*s2, tot1, z2, hw, n0) + weight(wa),
        [
            ((2, M0), F32, False),
            ((WORK, PIX0, M0), BF16, False),
            ((WORK, PIX0, M0), BF16, True),
            ((2, C0), F32, False),
        ],
        [vmem(M0, C0), DMA],
    )
    s3 = shared(st)
    cots = over_levels(cots)
    s3[0] = pin(s3[0], evens[3])

    tile = lambda s, meta: (0, s)
    tot3, src, p_even, z3_even, y1, y1b, ys, st, sts = call(
        join,
        [
            shape_of((2, C0), F32),
            hbm_of((ROWS1, C0), BF16),
            hbm_of((ROWS1, C0), F32),
            hbm_of((ROWS1, C0), F32),
            shape_of((ROWS1, M1), F32),
            hbm_of((ROWS1, M1), F32),
            hbm_of((ROWS1, C1), F32),
            shape_of((2, M1), F32),
            shape_of((2, C1), F32),
        ],
        (4,),
        [full(2, C0)] * 4
        + [full(2, M0 + 128), full(WORK, PIX0, M0)]
        + [full(PIX1, C0)] * 4
        + [full(8, 128), full(2, CN)]
        + [ANYWHERE] * 2,
        [
            full(2, C0),
            full(ROWS1, C0),
            full(ROWS1, C0),
            full(ROWS1, C0),
            full(ROWS1, M1),
            full(ROWS1, M1),
            pl.BlockSpec((ROWS1, SIDE_PART), tile),
            full(2, M1),
            pl.BlockSpec((2, SIDE_PART), tile),
        ],
        [vmem(M0, C0), vmem(C0, M1), vmem(4, C0, SIDE_PART), DMA((6,))],
    )(meta, *s3, tot1, a2, *evens, hw, n0, *wa)

    s4 = shared(st)
    src_there = swap_cores(src)
    s4[0] = pin(s4[0], got, src_there)
    wb = (in_hbm(second_weights), in_hbm(got))
    conv_scratch = [vmem(9 * M1, M1), DMA((3,))]
    last_scratch = [vmem(M1, C1), DMA]
    row = ((2, M1), F32, False)
    tot4, b1, y2, y2b, st = single(
        mid_one,
        meta,
        near(*s4, tot1, y1, hw, n1) + weight(wb),
        [row, ((ROWS1, M1), BF16, True), ((ROWS1, M1), F32, False), ((ROWS1, M1), F32, True), row],
        conv_scratch,
    )
    s5 = shared(st)
    b1_there = swap_cores(b1)
    t5 = shared(sts)
    s5[0] = pin(s5[0], cots[1], b1_there, *t5)
    tot5, b2, y3, st = single(
        mid_two,
        meta,
        near(*s5, tot1, y2, hw, n1) + weight(wb),
        [row, ((ROWS1, M1), BF16, True), ((ROWS1, C1), F32, False), ((2, C1), F32, False)],
        last_scratch,
    )
    s6 = shared(st)
    b2_there = swap_cores(b2)
    s6[0] = pin(s6[0], cots[2], cots[3], b2_there)
    made = call(
        turn,
        [shape_of((2, C1), F32)] * 2
        + some((PIX1, C1), BF16)
        + [shape_of((WORK, PIX1, C1), F32), shape_of((3, C1), F32)],
        (WORK,),
        [full(2, C1)] * 8
        + [full(2, M0 + 128), per_image(PIX1, C1), per_image(PIX1, C1), full(8, 128), full(2, CN)]
        + [full(PIX1, C1)] * 4,
        [full(2, C1)] * 2 + [full(PIX1, C1)] * 4 + [per_image(PIX1, C1), full(3, C1)],
        [vmem(PIX1, C1), vmem(PIX1, C1)],
    )(
        meta, *s6, *t5, tot1, y3.reshape(WORK, PIX1, C1), in_hbm(ys.reshape(WORK, PIX1, C1)), hw,
        n1, *cots,
    )
    tot6, tots, y_out, grad_y, st = made[0], made[1], made[2:6], made[6], made[7]
    grad_y = grad_y.reshape(ROWS1, C1)

    s7 = shared(st)
    tot7, er, es, g2, st = single(
        back_one,
        meta,
        near(*s7, tot6, tots, tot5, tot1, y3) + far(ys) + near(grad_y) + far(y2b)
        + near(hw, n1) + weight(wb),
        [
            ((3, C1), F32, False),
            ((2, ROWS1, C1), BF16, False),
            ((ROWS1, C1), BF16, False),
            ((ROWS1, M1), F32, False),
            row,
        ],
        last_scratch,
        limit=36,
    )
    s8 = shared(st)
    other = swap_cores(er[1:])
    s8[0] = pin(s8[0], other)
    low, high = level & 1, level >> 1
    tot8, e2r, g1, st = single(
        back_two,
        meta,
        near(*s8, tot5, tot4, tot1) + far(y2b) + near(g2) + far(y1b) + near(hw, n1) + weight(wb),
        [row, ((2, ROWS1, M1 // 2), BF16, False), ((ROWS1, M1), F32, False), row],
        conv_scratch,
    )
    s9 = shared(st)
    other2 = swap_cores(e2r[1:])
    sides = single(
        sides_grad,
        meta,
        far(src, src_there, b2, b2_there) + [(pin(er, st), False), (other, False)],
        [((16 * SIDES, 128), BF16, False)],
        limit=40,
    )[0]
    s9[0] = pin(s9[0], other2, sides)
    made = single(
        back_three,
        meta,
        near(*s9, tot4, tot1) + far(y1b) + near(g1, es, tot3) + far(p_even, z3_even)
        + near(hw, n1) + weight(wa),
        [row, ((2, ROWS1, M1 // 2), BF16, False), ((ROWS1, C0), F32, False), ((2, C0), F32, False)],
        [vmem(C0, M1), vmem(C0, C1), DMA((2,))],
    )
    tot9, e1r, g0, st = made

    s10 = shared(st)
    other1 = swap_cores(e1r[1:])
    y_back = [y_out[0], xor_permute(y_out[1], 4), xor_permute(y_out[2], 8)]
    s10[0] = pin(s10[0], other1, y_back[1])
    tot10, d3, g2, st = call(
        last_one,
        [
            shape_of((2, C0), F32),
            hbm_of((WORK, PIX0, C0), BF16),
            shape_of((WORK, PIX0, M0), F32),
            shape_of((2, M0), F32),
        ],
        (WORK,),
        [full(2, C0)] * 5
        + [
            full(2, M0), full(2, M0 + 128), per_image(PIX0, M0), per_image(PIX1, C0),
            per_image(PIX0, M0), full(8, 128), full(2, CN), ANYWHERE, ANYWHERE,
        ],
        [full(2, C0), per_image(PIX0, C0), per_image(PIX0, M0), full(2, M0)],
        [vmem(M0, C0), DMA],
    )(
        meta, *s10, tot3, tot2, tot1, in_hbm(a2b), g0.reshape(WORK, PIX1, C0), in_hbm(z2b), hw, n0,
        *wa,
    )
    s11 = shared(st)
    middle = single(
        middle_grad,
        meta,
        far(src, src_there, b1, b1_there) + [(pin(e2r, st), False)] + near(other2, e1r, other1),
        [((16 * MIDDLE, 128), BF16, False)],
        limit=40,
    )[0]
    y_back.append(xor_permute(pin(y_out[3], tot9), 12))
    s11[0] = pin(s11[0], middle, y_back[2])
    tot11, d2, g1, st = call(
        last_two,
        [
            shape_of((2, M0), F32),
            hbm_of((WORK, PIX0, M0), BF16),
            shape_of((WORK, PIX0, M0), F32),
            shape_of((2, M0), F32),
        ],
        (WORK,),
        [full(2, M0)] * 5
        + [full(2, M0 + 128)]
        + [per_image(PIX0, M0)] * 3
        + [full(8, 128), full(2, CN), ANYWHERE, ANYWHERE],
        [full(2, M0), per_image(PIX0, M0), per_image(PIX0, M0), full(2, M0)],
        [vmem(9 * M0, M0), DMA],
    )(meta, *s11, tot2, tot1, in_hbm(z2b), g2, in_hbm(z1b), hw, n0, *wa)
    s12 = shared(st)
    front = call(
        front_grad_two,
        hbm_of((2 * C0 + 2 * 9 * M0 + 8 * M0, 128), BF16),
        (1,),
        [full(WORK, PIX0, M0)] * 3 + [full(WORK, PIX0, C0)],
        full(2 * C0 + 2 * 9 * M0 + 8 * M0, 128),
        limit=40,
    )(meta, in_hbm(a1), in_hbm(d2), in_hbm(a2b), in_hbm(d3))
    one, two = place >> 1, place & 1
    kept, sent = part_at(middle, one, 2), part_at(middle, 1 - one, 2)
    s12[0] = pin(s12[0], front, y_back[3], kept, sent)
    made = single(
        last_three,
        meta,
        near(*s12, tot1) + far(z1b) + near(g1) + far(g0) + near(hw, n0),
        [((2, M0), F32, False)] + [((PIX0 + C0 // M0 * PIX1, M0), BF16, False)] * 4,
    )
    tot12, backs = made[0], over_levels(made[1:])

    last = [tot12]

    def after(value):
        return pin(value, last[0])

    def step(value):
        last[0] = value
        return value

    def half_sum(value, bit, got):
        return step(added(after(part_at(value, bit, 2)), got))

    def other_half(value, bit):
        return part_at(value, 1 - bit, 2)

    def joined(value, got):
        return step(lax.optimization_barrier(jnp.concatenate([after(value), got], axis=0)))

    sides = pin(sides, *s12[1:])
    sides_got = plane_turn(other_half(sides, one), 1)
    sides = half_sum(sides, one, sides_got)
    sides_got = plane_turn(other_half(sides, two), 2)
    middle_got = plane_turn(after(sent), 1)
    y_back = step(lax.optimization_barrier(jnp.stack([after(y_back[0])] + y_back[1:])))
    y_there = lax.ppermute(y_back, "pipe", [(0, 1)])
    sides = half_sum(sides, two, sides_got)
    sides_got = xor_permute(other_half(sides, low), 4)
    backs[0] = after(backs[0])
    rows = front.shape[0]
    gx, front = call(
        leave,
        [shape_of((WORK, PIX0, C0), BF16), hbm_of((rows, 128), BF16)],
        (WORK,),
        [own_image(HB, WB, C0), ANYWHERE, ANYWHERE]
        + [full(PIX0 + C0 // M0 * PIX1, M0)] * 4
        + [ANYWHERE],
        [per_image(PIX0, C0), ANYWHERE],
        [vmem(C0, M0), pltpu.VMEM((C0, M0), F32), vmem(2 * C0, 128), DMA, DMA],
        aliases={8: 1},
    )(meta, images, *w1, *backs, front)
    step(front)
    front_got = swap_cores(other_half(front, core))
    x_there = lax.ppermute(gx, "pipe", [(1, 0)])
    sides = half_sum(sides, low, sides_got)
    sides_got = xor_permute(other_half(sides, high), 8)
    middle = step(added(after(kept), middle_got))
    middle_got = plane_turn(other_half(middle, two), 2)
    front = half_sum(front, core, front_got)
    front_got = plane_turn(other_half(front, one), 1)
    sides = upper_sum(half_sum(sides, high, sides_got))
    sides_got = xor_permute(sides, 8)
    middle = half_sum(middle, two, middle_got)
    middle_got = xor_permute(other_half(middle, low), 4)
    sides = joined(sides, sides_got)
    sides_got = xor_permute(sides, 4)
    front = half_sum(front, one, front_got)
    front_got = plane_turn(other_half(front, two), 2)
    middle = half_sum(middle, low, middle_got)
    middle_got = xor_permute(other_half(middle, high), 8)
    front = half_sum(front, two, front_got)
    front_got = xor_permute(other_half(front, low), 4)
    sides = joined(sides, sides_got)
    sides_got = plane_turn(sides, 2)
    middle = upper_sum(half_sum(middle, high, middle_got))
    middle_got = xor_permute(middle, 8)
    front = half_sum(front, low, front_got)
    front_got = xor_permute(other_half(front, high), 8)
    sides = to_core(joined(sides, sides_got), 1)
    middle = joined(middle, middle_got)
    middle_got = xor_permute(middle, 4)
    front = upper_sum(half_sum(front, high, front_got))
    front_got = xor_permute(front, 8)
    middle = joined(middle, middle_got)
    middle_got = plane_turn(middle, 2)
    front = joined(front, front_got)
    front_got = xor_permute(front, 4)
    strip = lambda s, meta: (0, s, 0)
    strip_y = lambda s, meta: (0, jnp.minimum(s, 7), 0)
    boundary = call(
        rows_out,
        shape_of((2 * WORK, HB * WB * C0), BF16),
        (HB,),
        [pl.BlockSpec((WORK, WB, C0), strip)] * 2
        + [pl.BlockSpec((WORK, WB // 2, C1), strip_y)] * 2,
        pl.BlockSpec((2 * WORK, WB * C0), lambda s, meta: (0, s)),
        micros=9,
    )(meta, after(gx), x_there, y_back, y_there)
    step(boundary)
    middle = to_core(joined(middle, middle_got), 1)
    front = joined(front, front_got)
    front_got = plane_turn(front, 2)

    whole = shape_of((GRAD_ROWS, 128), F32)
    block_at = lambda at: pl.BlockSpec((PACK_ROWS, 128), lambda s, meta: (s + at, 0))
    side_spec, mid_spec = full(8 * SIDES, 128), full(8 * MIDDLE, 128)
    steps = GRAD_ROWS // PACK_ROWS - 11
    sides[0] = after(sides[0])
    grads = call(pack_sides, whole, (steps,), [side_spec] * 4, block_at(11), micros=8)(meta, *sides)
    step(grads)
    fronts = to_core(joined(front, front_got), 0)
    middle[0] = after(middle[0])
    grads = call(
        pack_rest, whole, (6,), [ANYWHERE] + [mid_spec] * 4, block_at(5), aliases={1: 0}
    )(meta, grads, *middle)
    front_rows = fronts[0].shape[0]
    grads = call(
        pack_front,
        whole,
        (5,),
        [ANYWHERE] + [mid_spec] * 4 + [full(front_rows, 128)] * 4,
        block_at(0),
        [pltpu.VMEM((4 * front_rows, 128), BF16)],
        aliases={1: 0},
    )(meta, grads, *middle, *fronts)
    weight_grads = grads.reshape(1, P_SIZE)

    def gain_shift(table, second=1):
        return jnp.concatenate([table[second : second + 1], table[0:1]], axis=0)

    line0 = jnp.concatenate(
        [gain_shift(tot12), gain_shift(tot11), gain_shift(tot10), jnp.zeros((2, CN - 1536), F32)],
        axis=1,
    )
    line1 = jnp.concatenate(
        [gain_shift(tot9), gain_shift(tot8), gain_shift(tot7), gain_shift(tot7, 2)], axis=1
    )
    line = jnp.where(first_core, line0, line1) + swap_cores(jnp.where(first_core, line1, line0))
    for bit in (4, 8):
        line = line + xor_permute(line, bit)

    return boundary[None], weight_grads, line[None]


def solution(mesh):
    placed_as = (
        P("dp", None, None, None),
        P("dp", None),
        P("dp"),
        P("pipe", None),
        P("pipe", None, None),
        P("dp", None, None, None),
    )
    return jax.shard_map(
        on_device,
        mesh=mesh,
        in_specs=placed_as,
        out_specs=(P("pipe", "dp", None), P("pipe", None), P("pipe", None, None)),
        check_vma=False,
    )
```
